128 devices in a mesh: dp: 8 (over z_lo, y), ctx: 16 (over z_hi, x, core).
Axes of the slice: x: 4, y: 4, z: 4 (z_hi: 2, z_lo: 2; z = z_hi * 2 + z_lo), core: 2. Of those that a mesh axis runs over, the one named last changes fastest.
Arguments:
- tokens: bfloat16 [16, 1024, 1536], P('dp', 'ctx'), may hold values from -6 to 6
- doc_start: int32 [16, 1024], P('dp'), may hold values from 0 to 1, as said below
- gain_attn: bfloat16 [1536], P(('dp', 'ctx')), may hold values from 0.5 to 1.5
- w_query: bfloat16 [1536, 1536], P(('dp', 'ctx')), may hold values from -0.15625 to 0.15625
- w_key: bfloat16 [1536, 1536], P(('dp', 'ctx')), may hold values from -0.15625 to 0.15625
- w_value: bfloat16 [1536, 1536], P(('dp', 'ctx')), may hold values from -0.15625 to 0.15625
- w_path: bfloat16 [1536, 1536], P(('dp', 'ctx')), may hold values from -0.15625 to 0.15625
- conv_path: bfloat16 [4, 1536], P(None, ('dp', 'ctx')), may hold values from -3 to 3
- w_beta: bfloat16 [1536, 12], P(('dp', 'ctx')), may hold values from -0.15625 to 0.15625
- w_out: bfloat16 [1536, 1536], P(('dp', 'ctx')), may hold values from -0.625 to 0.625
- gain_ffn: bfloat16 [1536], P(('dp', 'ctx')), may hold values from 0.5 to 1.5
- w_gate: bfloat16 [1536, 4096], P(('dp', 'ctx')), may hold values from -0.15625 to 0.15625
- w_up: bfloat16 [1536, 4096], P(('dp', 'ctx')), may hold values from -0.15625 to 0.15625
- w_down: bfloat16 [4096, 1536], P(('dp', 'ctx')), may hold values from -0.09375 to 0.09375
- grad_out: bfloat16 [16, 1024, 1536], P('dp', 'ctx'), may hold values from -6 to 6
Outputs:
- output: bfloat16 [16, 1024, 1536], P('dp', 'ctx')
- d_tokens: bfloat16 [16, 1024, 1536], P('dp', 'ctx')
- d_gain_attn: float32 [1536], P(('dp', 'ctx'))
- d_w_query: float32 [1536, 1536], P(('dp', 'ctx'))
- d_w_key: float32 [1536, 1536], P(('dp', 'ctx'))
- d_w_value: float32 [1536, 1536], P(('dp', 'ctx'))
- d_w_path: float32 [1536, 1536], P(('dp', 'ctx'))
- d_conv_path: float32 [4, 1536], P(None, ('dp', 'ctx'))
- d_w_beta: float32 [1536, 12], P(('dp', 'ctx'))
- d_w_out: float32 [1536, 1536], P(('dp', 'ctx'))
- d_gain_ffn: float32 [1536], P(('dp', 'ctx'))
- d_w_gate: float32 [1536, 4096], P(('dp', 'ctx'))
- d_w_up: float32 [1536, 4096], P(('dp', 'ctx'))
- d_w_down: float32 [4096, 1536], P(('dp', 'ctx'))
The draws below stay inside these ranges and needn't reach their ends.
Inputs may be any that keep to these rules, and one draw needn't show every extreme that they name: `doc_start`: position 0 of every row is 1. Of the 2 rows held by each index of dp, one has a document that begins within the first 64 positions and ends within the last 64.
All inputs are finite; a program needn't handle non-finite values.
Results may differ from the reference program's by a relative error of at most 0.025.
Values may be sent and summed in bfloat16 or wider, within the bound.
A program may use at most 384 MiB of HBM per device.

```python
import jax
import jax.numpy as jnp
from jax import lax

D = 1536
HEADS = 12
HEAD_DIM = 128
FF = 4096
KW = 4
MICRO = 2
SEQ = 1024
TOKB = 64
ROWS = 16
N_DP = 8


def draw_doc_start(key, part):
    key = jax.random.fold_in(key, 11)
    key_starts, key_pick, key_left, key_right = jax.random.split(key, 4)
    positions = jnp.arange(SEQ, dtype=jnp.int32)
    starts = jax.random.randint(key_starts, (ROWS, SEQ), 0, 3 * TOKB) == 0
    chosen = jax.random.randint(key_pick, (N_DP, 1), 0, MICRO)
    spanning = (jnp.arange(MICRO, dtype=jnp.int32)[None, :] == chosen).reshape(ROWS, 1)
    left_edge = jax.random.randint(key_left, (ROWS, 1), 0, TOKB)
    right_edge = jax.random.randint(key_right, (ROWS, 1), SEQ - TOKB + 1, SEQ + 1)
    inside = (positions[None, :] > left_edge) & (positions[None, :] < right_edge)
    starts = jnp.where(spanning & inside, False, starts)
    starts = starts | spanning & ((positions[None, :] == left_edge) | (positions[None, :] == right_edge))
    starts = starts | (positions[None, :] == 0)
    return starts.astype(jnp.int32)


def level_of(rng, dims, cuts, smallest, high):
    def one(axis_at, parts):
        steps = jax.random.uniform(jax.random.fold_in(jax.random.fold_in(rng, 6), axis_at), (parts,), jnp.float32, smallest / len(cuts), high / len(cuts))
        return jnp.repeat(jnp.exp(steps), dims[axis_at] // parts).reshape((-1,) + (1,) * (len(dims) - axis_at - 1))

    factor_of = one(*cuts[0])
    for cut in cuts[1:]:
        factor_of = factor_of * one(*cut)
    return factor_of


def scatter_about(rng, shape, spread, most, pieces=(), held_as=jnp.bfloat16):
    array = jax.random.normal(rng, shape, jnp.float32) * spread
    if len(pieces) > 0:
        array = level_of(rng, shape, pieces, -0.22, 0.18) * array
    return jnp.clip(array, min=-most, max=most).astype(held_as)


def setup_inputs(seed: int = 0) -> dict:
    splits = jax.random.split(jax.random.key(seed), 16)
    return {
        "tokens": scatter_about(splits[0], (ROWS, SEQ, D), 1.0, 6.0, ((0, 8), (1, 16))),
        "doc_start": draw_doc_start(jax.random.fold_in(splits[15], 71), 0),
        "gain_attn": jnp.clip(1.0 + 0.1 * jax.random.normal(splits[2], (D,), jnp.float32), 0.5, 1.5).astype(jnp.bfloat16),
        "w_query": scatter_about(splits[3], (D, D), D ** -0.5, 0.15625, ((0, 128),)),
        "w_key": scatter_about(splits[4], (D, D), D ** -0.5, 0.15625, ((0, 128),)),
        "w_value": scatter_about(splits[5], (D, D), D ** -0.5, 0.15625, ((0, 128),)),
        "w_path": scatter_about(splits[6], (D, D), D ** -0.5, 0.15625, ((0, 128),)),
        "conv_path": scatter_about(splits[7], (KW, D), KW ** -0.5, 3.0, ((1, 128),)),
        "w_beta": scatter_about(splits[8], (D, HEADS), D ** -0.5, 0.15625, ((0, 128),)),
        "w_out": scatter_about(splits[9], (D, D), (D // 16) ** -0.5, 0.625, ((0, 128),)),
        "gain_ffn": jnp.clip(1.0 + 0.1 * jax.random.normal(splits[10], (D,), jnp.float32), 0.5, 1.5).astype(jnp.bfloat16),
        "w_gate": scatter_about(splits[11], (D, FF), D ** -0.5, 0.15625, ((0, 128),)),
        "w_up": scatter_about(splits[12], (D, FF), D ** -0.5, 0.15625, ((0, 128),)),
        "w_down": scatter_about(splits[13], (FF, D), FF ** -0.5, 0.09375, ((0, 128),)),
        "grad_out": scatter_about(splits[14], (ROWS, SEQ, D), 1.0, 6.0, ((0, 8), (1, 16))),
    }


PRECISE = lax.Precision.HIGHEST
EPS_NORM = 1e-05
EPS_UNIT = 1e-06

@jax.custom_vjp
def low(v):
    return lax.optimization_barrier(v.astype(jnp.bfloat16)).astype(jnp.float32)

@jax.custom_vjp
def low_back(v):
    return v

def low_keep(v):
    return (low(v), None)

def low_pass(kept, grad):
    return (grad,)

def back_keep(v):
    return (v, None)

def back_low(kept, grad):
    return (low(grad),)
low.defvjp(low_keep, low_pass)
low_back.defvjp(back_keep, back_low)

def mix_dot(left_rows, right_rows):
    return jnp.dot(left_rows, right_rows, precision=PRECISE)

def rms_scale(values, gain_vec):
    return values * lax.rsqrt(lax.optimization_barrier(jnp.mean(values * values, axis=-1, keepdims=True)) + EPS_NORM) * gain_vec

def short_conv(row_vals, conv_w, doc_ids):
    length = row_vals.shape[0]
    conved = conv_w[0] * row_vals
    for tap_index in range(1, conv_w.shape[0]):
        earlier = jnp.concatenate([jnp.zeros((tap_index, row_vals.shape[1]), row_vals.dtype), row_vals[:length - tap_index]], axis=0)
        earlier_docs = jnp.concatenate([jnp.full((tap_index,), -1, jnp.int32), doc_ids[:length - tap_index]])
        same_doc = (earlier_docs == doc_ids)[:, None]
        conved = conved + conv_w[tap_index] * jnp.where(same_doc, earlier, 0.0)
    return conved

def path_scores(queries, key_rows, vectors, beta_vals):
    length = queries.shape[1]
    strict = jnp.tril(jnp.ones((length, length), bool), -1)
    closed = jnp.tril(jnp.ones((length, length), bool))
    inner_ww = jnp.einsum('hsd,htd->hst', vectors, vectors, precision=PRECISE)
    system = jnp.eye(length, dtype=queries.dtype) + jnp.where(strict, inner_ww * beta_vals[:, None, :], 0.0)
    inner_wk = jnp.where(strict, jnp.einsum('hsd,hjd->hsj', vectors, key_rows, precision=PRECISE), 0.0)
    coeffs = jax.scipy.linalg.solve_triangular(system, inner_wk, lower=True, unit_diagonal=True)
    inner_qw = jnp.where(closed, jnp.einsum('hid,hsd->his', queries, vectors, precision=PRECISE), 0.0) * beta_vals[:, None, :]
    direct = jnp.einsum('hid,hjd->hij', queries, key_rows, precision=PRECISE)
    return direct - jnp.einsum('his,hsj->hij', inner_qw, coeffs, precision=PRECISE)

def layer_row(inputs, doc_ids, params):
    gain_attn, w_query, w_key, w_value, w_path, conv_path, w_beta, w_out, gain_ffn, w_gate, w_up, w_down = params
    length = inputs.shape[0]

    def split_heads(flat_rows):
        return flat_rows.reshape(length, HEADS, HEAD_DIM).transpose(1, 0, 2)
    normed = low(rms_scale(inputs, gain_attn))
    queries = low(low_back(mix_dot(normed, w_query)))
    key_rows = low(low_back(mix_dot(normed, w_key)))
    value_rows = low(low_back(mix_dot(normed, w_value)))
    path_raw = low(low_back(mix_dot(normed, w_path)))
    beta_raw = low_back(mix_dot(normed, w_beta))
    conved = short_conv(path_raw, conv_path, doc_ids).reshape(length, HEADS, HEAD_DIM)
    vectors = low(conved * lax.rsqrt(lax.optimization_barrier(jnp.sum(conved * conved, axis=-1, keepdims=True)) + EPS_UNIT))
    beta_vals = 2.0 * jax.nn.sigmoid(beta_raw)
    scores = path_scores(split_heads(queries), split_heads(key_rows), vectors.transpose(1, 0, 2), beta_vals.T) * HEAD_DIM ** (-0.5)
    visible = (doc_ids[:, None] == doc_ids[None, :]) & jnp.tril(jnp.ones((length, length), bool))
    scores = jnp.where(visible[None], scores, -1e+30)
    attn_probs = jax.nn.softmax(scores, axis=-1)
    mixed_heads = jnp.einsum('hij,hjd->hid', attn_probs, split_heads(value_rows), precision=PRECISE)
    attended = low(mixed_heads.transpose(1, 0, 2).reshape(length, HEADS * HEAD_DIM))
    hidden = inputs + low_back(mix_dot(attended, w_out))
    normed_ffn = low(rms_scale(hidden, gain_ffn))
    gate_pre = low_back(mix_dot(normed_ffn, w_gate))
    up_pre = low_back(mix_dot(normed_ffn, w_up))
    activation = low(jax.nn.silu(gate_pre) * up_pre)
    return hidden + mix_dot(activation, w_down)

def reference(tokens, doc_start, gain_attn, w_query, w_key, w_value, w_path, conv_path, w_beta, w_out, gain_ffn, w_gate, w_up, w_down, grad_out):
    params = tuple((weight.astype(jnp.float32) for weight in (gain_attn, w_query, w_key, w_value, w_path, conv_path, w_beta, w_out, gain_ffn, w_gate, w_up, w_down)))
    doc_ids = jnp.cumsum(doc_start, axis=1).astype(jnp.int32)

    def whole_layer(inputs, weights):

        def one_row(row_pair):
            return jax.checkpoint(layer_row)(row_pair[0], row_pair[1], weights)
        return lax.map(one_row, (inputs, doc_ids))
    result, pullback = jax.vjp(whole_layer, tokens.astype(jnp.float32), params)
    d_inputs, d_params = pullback(grad_out.astype(jnp.float32))
    return (result.astype(jnp.bfloat16), d_inputs.astype(jnp.bfloat16), d_params[0], d_params[1], d_params[2], d_params[3], d_params[4], d_params[5], d_params[6], d_params[7], d_params[8], d_params[9], d_params[10], d_params[11])
```

```python
import jax, jax.numpy as jnp
from jax import lax
from jax.experimental import pallas as pl
from jax.experimental.pallas import tpu as pltpu
from jax.sharding import Mesh, PartitionSpec as P

F32, BF16 = jnp.float32, jnp.bfloat16
SEQ, HD, BLK = 1024, 128, 128
NB = SEQ // BLK
NQC = (NB * (NB - 1) // 2) * BLK
SCALE = HD ** (-0.5)
GROUP = 4


def mm(a, b, dims=((1,), (0,))):
    return lax.dot_general(
        a.astype(BF16), b.astype(BF16), (dims, ((), ())), preferred_element_type=F32
    )


def mm_nt(a, b):
    return mm(a, b, ((1,), (1,)))


def mm_tn(a, b):
    return mm(a, b, ((0,), (0,)))


def split(a):
    high = a.astype(BF16)
    return high, (a - high.astype(F32)).astype(BF16)


def mm3(a, b):
    ah, al = split(a)
    bh, bl = split(b)
    return mm(ah, bh) + (mm(ah, bl) + mm(al, bh))


def iota2(axis):
    return lax.broadcasted_iota(jnp.int32, (BLK, BLK), axis)


BASE = 16


def unit_inverses(lowers):
    row, col = iota2(0), iota2(1)
    eye = (row == col).astype(F32)
    in_base = (row // BASE) == (col // BASE)
    narrow = [jnp.where(in_base, low, 0.0) for low in lowers]
    inv = [eye for _ in lowers]
    for u in range(BASE - 1):
        pick = (col % BASE) == u
        coef = [jnp.sum(jnp.where(pick, low, 0.0), axis=1, keepdims=True) for low in narrow]
        for n, (t, c) in enumerate(zip(inv, coef)):
            t3 = t.reshape(BLK // BASE, BASE, BLK)
            lead = jnp.broadcast_to(t3[:, u : u + 1, :], t3.shape).reshape(BLK, BLK)
            inv[n] = t - c * lead
    size = BASE
    while size < BLK:
        off = ((row // (2 * size)) == (col // (2 * size))) & ((row // size) != (col // size))
        mid = [mm3(t, jnp.where(off, low, 0.0)) for t, low in zip(inv, lowers)]
        inv = [t - mm3(m, t) for t, m in zip(inv, mid)]
        size *= 2
    return inv


def fwd_kernel(q, k, v, w, bcol, brow, dcol, drow, o, probs, qc, t_out, a_out, z_out, m_out, kp_out, s_buf, x_buf, qm_buf):
    row, col = iota2(0), iota2(1)
    strict, closed = row > col, row >= col
    eye = (row == col).astype(F32)

    def group(g, carry):
        sl = [pl.ds(pl.multiple_of((g * GROUP + n) * BLK, BLK), BLK) for n in range(GROUP)]
        qs = [q[s, :] for s in sl]
        ks = [k[s, :] for s in sl]
        ws = [w[s, :] for s in sl]
        bc = [bcol[0, s, :] for s in sl]
        br = [brow[0, :, s] for s in sl]
        low = [jnp.where(strict, mm_nt(x, x), 0.0) * b for x, b in zip(ws, br)]
        inv = unit_inverses(low)
        m1 = [jnp.where(strict, mm_nt(x, y), 0.0) for x, y in zip(ws, ks)]
        gq = [jnp.where(closed, mm_nt(x, y), 0.0) * b for x, y, b in zip(qs, ws, br)]
        a = [mm(x, t) for x, t in zip(gq, inv)]
        z = [mm_tn(t, b * x.astype(F32)) for t, b, x in zip(inv, bc, ws)]
        sd = [mm_nt(x, y) - mm(p, m) for x, y, p, m in zip(qs, ks, a, m1)]
        qm = [x.astype(F32) - mm(p, y) for x, p, y in zip(qs, a, ws)]
        kmt = [x.astype(F32).T - mm_tn(zz, m) for x, zz, m in zip(ks, z, m1)]
        pm = [eye - mm_tn(zz, x) for zz, x in zip(z, ws)]
        for n, s in enumerate(sl):
            b = g * GROUP + n
            t_out[0, s, :] = inv[n].astype(t_out.dtype)
            a_out[0, s, :] = a[n].astype(a_out.dtype)
            z_out[0, s, :] = z[n].astype(z_out.dtype)
            m_out[0, s, :] = m1[n].astype(m_out.dtype)
            kp_out[0, s, :HD] = kmt[n].astype(BF16)
            kp_out[0, s, HD:] = pm[n].astype(BF16)
            qm_buf[s, :] = qm[n]
            s_buf[s, s] = sd[n]
        return carry

    lax.fori_loop(0, NB // GROUP, group, 0)
    at = NQC
    for j in range(NB - 2, -1, -1):
        r0 = (j + 1) * BLK
        rows = SEQ - r0
        x_buf[r0 : r0 + BLK, :] = qm_buf[r0 : r0 + BLK, :]
        x = x_buf[r0:, :].astype(BF16)
        at -= rows
        qc[0, at : at + rows, :] = x
        both = mm(x, kp_out[0, j * BLK : r0, :])
        s_buf[r0:, j * BLK : r0] = both[:, :HD]
        x_buf[r0:, :] = both[:, HD:]
    for i in range(NB):
        lo, width = i * BLK, (i + 1) * BLK
        s = s_buf[lo:width, :width] * SCALE
        seen = dcol[lo:width, :] == drow[:, :width]
        seen = seen & (
            lax.broadcasted_iota(jnp.int32, (BLK, width), 0) + lo
            >= lax.broadcasted_iota(jnp.int32, (BLK, width), 1)
        )
        s = jnp.where(seen, s, -1e30)
        e = jnp.exp(s - jnp.max(s, axis=1, keepdims=True))
        p = e * (1.0 / jnp.sum(e, axis=1, keepdims=True))
        pb = p.astype(BF16)
        probs[0, lo:width, :width] = pb
        o[lo:width, :] = mm(pb, v[:width, :])


def bwd_kernel(q, k, v, w, bcol, brow, o, do, probs, qc, t_in, a_in, z_in, m_in, kp, dq, dk, dv, dw, dbc, dbr, ds_buf, x_buf, dkm_buf, dpm_buf, ):
    row, col = iota2(0), iota2(1)
    strict, closed = row > col, row >= col
    for i in range(NB):
        lo, width = i * BLK, (i + 1) * BLK
        p = probs[0, lo:width, :width].astype(F32)
        g = do[lo:width, :]
        delta = jnp.sum(g * o[lo:width, :], axis=1, keepdims=True)
        ds = p * (mm_nt(g, v[:width, :]) - delta) * SCALE
        ds_buf[lo:width, :width] = ds.astype(BF16)
    for j in range(NB):
        lo = j * BLK
        dv[lo : lo + BLK, :] = mm_tn(probs[0, lo:, lo : lo + BLK], do[lo:, :]).astype(dv.dtype)
    x_buf[...] = jnp.zeros_like(x_buf)
    dkm_buf[SEQ - BLK :, :] = jnp.zeros((BLK, HD), F32)
    dpm_buf[SEQ - BLK :, :] = jnp.zeros((BLK, HD), F32)
    at = 0
    for j in range(NB - 1):
        lo, r0 = j * BLK, (j + 1) * BLK
        rows = SEQ - r0
        x = x_buf[r0:, :].astype(BF16)
        ds = ds_buf[r0:, lo:r0]
        qcj = qc[0, at : at + rows, :]
        at += rows
        both = mm_tn(qcj, jnp.concatenate([x, ds], axis=1))
        dpm_buf[lo:r0, :] = both[:, :HD]
        dkm_buf[lo:r0, :] = both[:, HD:].T
        kpj = kp[0, lo:r0, :]
        x_buf[r0:, :] = mm_nt(jnp.concatenate([ds, x], axis=1), kpj)

    def group(g, carry):
        sl = [pl.ds(pl.multiple_of((g * GROUP + n) * BLK, BLK), BLK) for n in range(GROUP)]
        rng = range(GROUP)
        Q = [q[s, :] for s in sl]
        K = [k[s, :] for s in sl]
        W = [w[s, :] for s in sl]
        bc = [bcol[0, s, :] for s in sl]
        br = [brow[0, :, s] for s in sl]
        E = [ds_buf[s, s] for s in sl]
        T = [t_in[0, s, :] for s in sl]
        A = [a_in[0, s, :] for s in sl]
        Z = [z_in[0, s, :] for s in sl]
        M = [m_in[0, s, :] for s in sl]
        dQm = [x_buf[s, :] for s in sl]
        dKm = [dkm_buf[s, :] for s in sl]
        dPm = [dpm_buf[s, :] for s in sl]
        E = [jnp.where(closed, e, jnp.zeros_like(e)) for e in E]
        i1 = [mm_nt(W[n], W[n]) for n in rng]
        qw = [jnp.where(closed, mm_nt(Q[n], W[n]), 0.0) for n in rng]
        dA = [-(mm_nt(E[n], M[n]) + mm_nt(dQm[n], W[n])) for n in rng]
        dM = [jnp.where(strict, -(mm_tn(A[n], E[n]) + mm_nt(Z[n], dKm[n])), 0.0) for n in rng]
        dZ = [-(mm(M[n], dKm[n]) + mm_nt(W[n], dPm[n])) for n in rng]
        dW = [-(mm_tn(A[n], dQm[n]) + mm(Z[n], dPm[n])) for n in rng]
        dG = [jnp.where(closed, mm_nt(dA[n], T[n]), 0.0) for n in rng]
        bw = [bc[n] * W[n].astype(F32) for n in rng]
        dT = [mm_tn(qw[n] * br[n], dA[n]) + mm_nt(bw[n], dZ[n]) for n in rng]
        dBW = [mm(T[n], dZ[n]) for n in rng]
        dL = [mm_tn(T[n], dT[n]) for n in rng]
        dL = [jnp.where(strict, -mm_nt(dL[n], T[n]), 0.0) for n in rng]
        dI = [dL[n] * br[n] for n in rng]
        R = [dG[n] * br[n] for n in rng]
        for n, s in enumerate(sl):
            dbr[0, :, s] = jnp.sum(dL[n] * i1[n] + dG[n] * qw[n], axis=0, keepdims=True)
            dbc[0, s, :] = jnp.sum(dBW[n] * W[n].astype(F32), axis=1, keepdims=True)
            dq[s, :] = (dQm[n] + mm(E[n], K[n]) + mm(R[n], W[n])).astype(dq.dtype)
            dk[s, :] = (dKm[n] + mm_tn(E[n], Q[n]) + mm_tn(dM[n], W[n])).astype(dk.dtype)
            dw[s, :] = (
                dW[n]
                + bc[n] * dBW[n]
                + mm_tn(R[n], Q[n])
                + mm(dM[n], K[n])
                + mm(dI[n] + dI[n].T, W[n])
            )
        return carry

    lax.fori_loop(0, NB // GROUP, group, 0)


def _full(shape):
    return pl.BlockSpec(shape, lambda s: (0,) * len(shape))


def _slot(*shape):
    return pl.BlockSpec((1,) + shape, lambda s: (s,) + (0,) * len(shape))


def _cols(at):
    return pl.BlockSpec((SEQ, HD), lambda s: (0, at + s))


VM = 60 * 1024 * 1024


def attn_fwd(qkv, vec, bcol, brow, dcol, drow):
    slots = bcol.shape[0]
    sds = jax.ShapeDtypeStruct
    return pl.pallas_call(
        fwd_kernel,
        grid=(slots,),
        in_specs=[_cols(0), _cols(2), _cols(4), _cols(0), _slot(SEQ, 1), _slot(1, SEQ), _full((SEQ, 1)), _full((1, SEQ))],
        out_specs=[_cols(0), _slot(SEQ, SEQ), _slot(NQC, HD)] + [_slot(SEQ, BLK)] * 4 + [_slot(SEQ, 2 * HD)],
        out_shape=[
            sds((SEQ, slots * HD), F32),
            sds((slots, SEQ, SEQ), BF16),
            sds((slots, NQC, HD), BF16),
            sds((slots, SEQ, BLK), F32),
            sds((slots, SEQ, BLK), BF16),
            sds((slots, SEQ, BLK), BF16),
            sds((slots, SEQ, BLK), BF16),
            sds((slots, SEQ, 2 * HD), BF16),
        ],
        scratch_shapes=[pltpu.VMEM((SEQ, SEQ), F32), pltpu.VMEM((SEQ, HD), F32), pltpu.VMEM((SEQ, HD), F32)],
        compiler_params=pltpu.CompilerParams(vmem_limit_bytes=VM),
        name="attn_fwd",
    )(qkv, qkv, qkv, vec, bcol, brow, dcol, drow)


def attn_bwd(qkv, vec, bcol, brow, o, do, saved):
    slots = bcol.shape[0]
    sds = jax.ShapeDtypeStruct
    return pl.pallas_call(
        bwd_kernel,
        grid=(slots,),
        in_specs=[_cols(0), _cols(2), _cols(4), _cols(0), _slot(SEQ, 1), _slot(1, SEQ), _cols(0), _cols(0)]
        + [_slot(SEQ, SEQ), _slot(NQC, HD)] + [_slot(SEQ, BLK)] * 4 + [_slot(SEQ, 2 * HD)],
        out_specs=[_cols(0)] * 4 + [_slot(SEQ, 1), _slot(1, SEQ)],
        out_shape=[sds((SEQ, slots * HD), BF16)] * 3 + [sds((SEQ, slots * HD), F32), sds((slots, SEQ, 1), F32), sds((slots, 1, SEQ), F32)],
        scratch_shapes=[pltpu.VMEM((SEQ, SEQ), BF16)] + [pltpu.VMEM((SEQ, HD), F32)] * 3,
        compiler_params=pltpu.CompilerParams(vmem_limit_bytes=VM),
        name="attn_bwd",
    )(qkv, qkv, qkv, vec, bcol, brow, o, do, *saved)


EPS_NORM = 1e-05
EPS_UNIT = 1e-06
GROUPS = ("zl", "y", "zh")
TEAM = ("x", "c")
ALL = GROUPS + TEAM


def rms_scale(values, gain_vec):
    return (
        values * lax.rsqrt(jnp.mean(values * values, axis=-1, keepdims=True) + EPS_NORM) * gain_vec
    )


def dot_nn(a, b):
    return lax.dot_general(a, b, (((1,), (0,)), ((), ())), preferred_element_type=F32)


def dot_nt(a, b):
    return lax.dot_general(a, b, (((1,), (1,)), ((), ())), preferred_element_type=F32)


def dot_tn(a, b):
    return lax.dot_general(a, b, (((0,), (0,)), ((), ())), preferred_element_type=F32)


def gather_rows(block):
    width = block.shape[1]
    whole = lax.all_gather(block.reshape(2, -1, width), TEAM, axis=1)
    return whole.reshape(-1, width)


def scatter_rows(partial):
    width = partial.shape[1]
    parts = partial.astype(BF16).reshape(2, 8, -1, width)
    mine = lax.psum_scatter(parts, TEAM, scatter_dimension=1, tiled=False)
    return mine.reshape(-1, width).astype(F32)


def path_vectors(current, conv_w, same_doc):
    conved = conv_w[0] * current
    for tap in range(1, conv_w.shape[0]):
        earlier = jnp.pad(current, ((tap, 0), (0, 0)))[: current.shape[0]]
        conved = conved + conv_w[tap] * jnp.where(same_doc[tap][:, None], earlier, 0.0)
    heads = conved.reshape(current.shape[0], -1, HD)
    unit = heads * lax.rsqrt(jnp.sum(heads * heads, axis=-1, keepdims=True) + EPS_UNIT)
    return unit.reshape(current.shape)


def per_device(
    tokens,
    doc_start,
    gain_attn,
    w_query,
    w_key,
    w_value,
    w_path,
    conv_path,
    w_beta,
    w_out,
    gain_ffn,
    w_gate,
    w_up,
    w_down,
    grad_out,
):
    zh, chip, core = lax.axis_index("zh"), lax.axis_index("x"), lax.axis_index("c")
    dp = lax.axis_index("zl") * 4 + lax.axis_index("y")
    width = tokens.shape[2]
    share = w_query.shape[0]
    first = zh == 0
    head_a, head_b = 3 * chip + 2 * core, 3 * chip + 1

    pair = jnp.stack([tokens, grad_out])
    mine = jnp.where(first, pair[:, 0], pair[:, 1])
    other = jnp.where(first, pair[:, 1], pair[:, 0])
    got = lax.ppermute(other, "zh", [(0, 1), (1, 0)])
    halves = jnp.stack([jnp.where(first, mine, got), jnp.where(first, got, mine)], axis=1)
    x_rows = halves[0].reshape(-1, width)
    g_rows = halves[1].reshape(-1, width)
    doc_rows = jnp.cumsum(doc_start, axis=1)
    docs = jnp.where(first, doc_rows[0], doc_rows[1])

    small = jnp.concatenate(
        [gain_attn[:, None], gain_ffn[:, None], conv_path.T, w_beta], axis=1
    )
    small = lax.all_gather(small.reshape(1, -1), ALL, axis=0, tiled=True)
    small = small.reshape(width, -1)
    gain_a, gain_f = small[:, 0].astype(F32), small[:, 1].astype(F32)
    conv_full, beta_full = small[:, 2:6].T.astype(F32), small[:, 6:]
    kinds = jnp.stack([w_query, w_key, w_value, w_path], axis=1).reshape(share, 4, 4, 3, HD)
    slot_a = jnp.concatenate([kinds[:, :, :, 0:1], kinds[:, :, :, 2:3]], axis=3)
    slot_b = jnp.broadcast_to(kinds[:, :, :, 1:2], slot_a.shape)
    heads_pack = jnp.stack([slot_a, slot_b], axis=4).transpose(2, 3, 0, 1, 4, 5)
    heads_pack = heads_pack.reshape(8, share, -1)
    ffn_pack = jnp.stack([w_gate, w_up], axis=1).reshape(share, 2, 16, 8, 32)
    ffn_pack = ffn_pack.transpose(3, 0, 1, 2, 4).reshape(8, share, -1)
    packs = jnp.concatenate([heads_pack, ffn_pack], axis=2)
    packs = lax.all_to_all(packs, TEAM, split_axis=0, concat_axis=0, tiled=True)
    packs = packs.reshape(8 * share, -1)
    w_heads = lax.all_gather(packs[:, : 8 * HD], GROUPS, axis=0, tiled=True)
    w_out_full = lax.all_gather(w_out, ALL, axis=0, tiled=True)
    w_ffn = lax.all_gather(packs[:, 8 * HD :], GROUPS, axis=0, tiled=True)
    w_down_t = lax.all_gather(w_down, GROUPS, axis=0, tiled=True)
    out_a = lax.dynamic_slice_in_dim(w_out_full, head_a * HD, HD, 0)
    out_b = lax.dynamic_slice_in_dim(w_out_full, head_b * HD, HD, 0)
    out_b = jnp.where(core == 0, out_b, jnp.zeros_like(out_b))
    w_out_t = jnp.concatenate([out_a, out_b], axis=0)

    def two_heads(full, size):
        return jnp.concatenate(
            [
                lax.dynamic_slice_in_dim(full, head_a * size, size, 1),
                lax.dynamic_slice_in_dim(full, head_b * size, size, 1),
            ],
            axis=1,
        )

    def back_to_all(part, size):
        full = jnp.zeros((part.shape[0], 12 * size), F32)
        full = lax.dynamic_update_slice_in_dim(full, part[:, :size], head_a * size, 1)
        own_b = jnp.where(core == 0, part[:, size:], 0.0)
        return lax.dynamic_update_slice_in_dim(full, own_b, head_b * size, 1)

    w_beta_t = two_heads(beta_full, 1)
    conv_t = two_heads(conv_full, HD)
    same_doc = [
        jnp.concatenate([jnp.zeros((tap,), bool), docs[: SEQ - tap] == docs[tap:]])
        for tap in range(4)
    ]

    x_f = x_rows.astype(F32)
    normed = rms_scale(x_f, gain_a).astype(BF16)
    normed_all = gather_rows(normed)
    g_all = gather_rows(g_rows)
    qkvp = dot_nn(normed_all, w_heads).astype(BF16)
    beta_raw = dot_nn(normed_all, w_beta_t)
    betas = (2.0 * jax.nn.sigmoid(beta_raw)).T
    vec_f, vec_pull = jax.vjp(
        lambda cur, cw: path_vectors(cur, cw, same_doc), qkvp[:, 6 * HD :].astype(F32), conv_t
    )
    vec = vec_f.astype(BF16)
    bcol, brow = betas[:, :, None], betas[:, None, :]
    o, *saved = attn_fwd(qkvp, vec, bcol, brow, docs[:, None], docs[None, :])
    mixed = o.astype(BF16)
    hidden = x_f + scatter_rows(dot_nn(mixed, w_out_t))
    normed_ffn = rms_scale(hidden, gain_f).astype(BF16)
    ffn_all = gather_rows(normed_ffn)
    gate_up = dot_nn(ffn_all, w_ffn)

    def gated(pre):
        return jax.nn.silu(pre[:, :512]) * pre[:, 512:]

    act_f, act_pull = jax.vjp(gated, gate_up)
    act = act_f.astype(BF16)
    out_rows = (hidden + scatter_rows(dot_nn(act, w_down_t))).astype(BF16)

    (d_gate_up,) = act_pull(dot_nt(g_all, w_down_t))
    d_gate_up = d_gate_up.astype(BF16)
    d_normed_ffn = scatter_rows(dot_nt(d_gate_up, w_ffn))
    _, ffn_pull = jax.vjp(rms_scale, hidden, gain_f)
    d_hidden, d_gain_ffn = ffn_pull(d_normed_ffn)
    d_hidden = d_hidden + g_rows.astype(F32)
    branch_all = gather_rows(d_hidden.astype(BF16))
    d_mixed = dot_nt(branch_all, w_out_t)
    d_q, d_k, d_v, d_vec, d_bc, d_br = attn_bwd(qkvp, vec, bcol, brow, o, d_mixed, saved)
    d_path, d_conv = vec_pull(d_vec)
    d_betas = (d_bc[:, :, 0] + d_br[:, 0, :]) * betas * (1.0 - 0.5 * betas)
    d_beta = d_betas.T.astype(BF16)
    d_qkvp = jnp.concatenate([d_q, d_k, d_v, d_path.astype(BF16)], axis=1)
    d_normed = scatter_rows(dot_nt(d_qkvp, w_heads) + dot_nt(d_beta, w_beta_t))
    _, norm_pull = jax.vjp(rms_scale, x_f, gain_a)
    d_x, d_gain_attn = norm_pull(d_normed)
    d_rows = (d_x + d_hidden).astype(BF16)

    def sum_rows(grad):
        return lax.psum_scatter(grad.astype(BF16), GROUPS, scatter_dimension=0, tiled=True)

    d_down = sum_rows(dot_tn(act, g_all)).astype(F32)
    d_ffn = sum_rows(dot_tn(ffn_all, d_gate_up))
    d_out = lax.psum(dot_tn(mixed, branch_all).astype(BF16), GROUPS)
    d_heads = sum_rows(dot_tn(normed_all, d_qkvp))
    none = jnp.zeros((HD, width), BF16)
    own = core == 0
    chip_rows = jnp.concatenate(
        [
            jnp.where(own, d_out[:HD], none),
            jnp.where(own, d_out[HD:], none),
            jnp.where(own, none, d_out[:HD]),
        ],
        axis=0,
    )
    window = lax.dynamic_slice_in_dim(chip_rows, (dp % 2) * 192 + zh * 96, 96, 0)
    window = jnp.where(chip == dp // 2, window, jnp.zeros_like(window))
    back = jnp.concatenate([d_heads, d_ffn, window], axis=1).reshape(8, share, -1)
    back = lax.all_to_all(back, TEAM, split_axis=0, concat_axis=0, tiled=True)
    d_w_out = jnp.sum(back[:, :, 16 * HD :].astype(F32), axis=0)
    heads_back = back[:, :, : 8 * HD].reshape(4, 2, share, 4, 2, HD)
    by_head = jnp.stack(
        [heads_back[:, 0, :, :, 0], heads_back[:, 0, :, :, 1], heads_back[:, 1, :, :, 0]], axis=1
    )
    by_kind = by_head.transpose(3, 2, 0, 1, 4).reshape(4, share, width).astype(F32)
    ffn_back = back[:, :, 8 * HD : 16 * HD].reshape(8, share, 2, 16, 32)
    ffn_back = ffn_back.transpose(2, 1, 3, 0, 4).reshape(2, share, -1).astype(F32)

    d_beta_w = back_to_all(dot_tn(normed_all, d_beta), 1)
    small_back = jnp.concatenate(
        [d_gain_attn[:, None], d_gain_ffn[:, None], back_to_all(d_conv, HD).T, d_beta_w], axis=1
    )
    small_back = lax.psum_scatter(
        small_back.reshape(128, -1), ALL, scatter_dimension=0, tiled=True
    ).reshape(share, -1)

    pair = jnp.stack([out_rows, d_rows]).reshape(2, 2, -1, width)
    mine = jnp.where(first, pair[:, 0], pair[:, 1])
    other = jnp.where(first, pair[:, 1], pair[:, 0])
    got = lax.ppermute(other, "zh", [(0, 1), (1, 0)])
    rows = jnp.stack([jnp.where(first, mine, got), jnp.where(first, got, mine)], axis=1)
    return (
        rows[0],
        rows[1],
        small_back[:, 0],
        by_kind[0],
        by_kind[1],
        by_kind[2],
        by_kind[3],
        small_back[:, 2:6].T,
        small_back[:, 6:],
        d_w_out,
        small_back[:, 1],
        ffn_back[0],
        ffn_back[1],
        d_down,
    )


def solution(mesh):
    fine = Mesh(mesh.devices.reshape(2, 4, 2, 4, 2), ("zl", "y", "zh", "x", "c"))
    dp, ctx = ("zl", "y"), ("zh", "x", "c")
    rows, flat, mat, taps = P(dp, ctx, None), P(ALL), P(ALL, None), P(None, ALL)
    return jax.shard_map(
        per_device,
        mesh=fine,
        in_specs=(
            rows, P(dp, None), flat, mat, mat, mat, mat, taps, mat, mat, flat, mat, mat, mat, rows,
        ),
        out_specs=(
            rows, rows, flat, mat, mat, mat, mat, taps, mat, mat, flat, mat, mat, mat,
        ),
        check_vma=False,
    )
```

```python
import functools

import jax
import jax.numpy as jnp
from jax import lax
from jax.experimental import pallas as pl
from jax.experimental.pallas import tpu as pltpu
from jax.sharding import Mesh, PartitionSpec as P

F32, BF16 = jnp.float32, jnp.bfloat16
VM = 60 * 1024 * 1024

SEQ, HD, BLK = 1024, 128, 128
NB = SEQ // BLK
NQC = (NB * (NB - 1) // 2) * BLK
SCALE = HD ** (-0.5)
GROUP = 4


def mm(a, b, dims=((1,), (0,))):
    return lax.dot_general(
        a.astype(BF16), b.astype(BF16), (dims, ((), ())), preferred_element_type=F32
    )


def mm_nt(a, b):
    return mm(a, b, ((1,), (1,)))


def mm_tn(a, b):
    return mm(a, b, ((0,), (0,)))


def split(a):
    high = a.astype(BF16)
    return high, (a - high.astype(F32)).astype(BF16)


def mm3(a, b):
    ah, al = split(a)
    bh, bl = split(b)
    return mm(ah, bh) + (mm(ah, bl) + mm(al, bh))


def iota2(axis):
    return lax.broadcasted_iota(jnp.int32, (BLK, BLK), axis)


BASE = 16


def unit_inverses(lowers):
    row, col = iota2(0), iota2(1)
    eye = (row == col).astype(F32)
    in_base = (row // BASE) == (col // BASE)
    narrow = [jnp.where(in_base, low, 0.0) for low in lowers]
    inv = [eye for _ in lowers]
    for u in range(BASE - 1):
        pick = (col % BASE) == u
        coef = [jnp.sum(jnp.where(pick, low, 0.0), axis=1, keepdims=True) for low in narrow]
        for n, (t, c) in enumerate(zip(inv, coef)):
            t3 = t.reshape(BLK // BASE, BASE, BLK)
            lead = jnp.broadcast_to(t3[:, u : u + 1, :], t3.shape).reshape(BLK, BLK)
            inv[n] = t - c * lead
    size = BASE
    while size < BLK:
        off = ((row // (2 * size)) == (col // (2 * size))) & ((row // size) != (col // size))
        mid = [mm3(t, jnp.where(off, low, 0.0)) for t, low in zip(inv, lowers)]
        inv = [t - mm3(m, t) for t, m in zip(inv, mid)]
        size *= 2
    return inv


def fwd_kernel(q, k, v, w, bcol, brow, dcol, drow, o, probs, qc, t_out, a_out, z_out, m_out, kp_out, s_buf, x_buf, qm_buf):
    row, col = iota2(0), iota2(1)
    strict, closed = row > col, row >= col
    eye = (row == col).astype(F32)

    def group(g, carry):
        sl = [pl.ds(pl.multiple_of((g * GROUP + n) * BLK, BLK), BLK) for n in range(GROUP)]
        qs = [q[s, :] for s in sl]
        ks = [k[s, :] for s in sl]
        ws = [w[s, :] for s in sl]
        bc = [bcol[0, s, :] for s in sl]
        br = [brow[0, :, s] for s in sl]
        low = [jnp.where(strict, mm_nt(x, x), 0.0) * b for x, b in zip(ws, br)]
        inv = unit_inverses(low)
        m1 = [jnp.where(strict, mm_nt(x, y), 0.0) for x, y in zip(ws, ks)]
        gq = [jnp.where(closed, mm_nt(x, y), 0.0) * b for x, y, b in zip(qs, ws, br)]
        a = [mm(x, t) for x, t in zip(gq, inv)]
        z = [mm_tn(t, b * x.astype(F32)) for t, b, x in zip(inv, bc, ws)]
        sd = [mm_nt(x, y) - mm(p, m) for x, y, p, m in zip(qs, ks, a, m1)]
        qm = [x.astype(F32) - mm(p, y) for x, p, y in zip(qs, a, ws)]
        kmt = [x.astype(F32).T - mm_tn(zz, m) for x, zz, m in zip(ks, z, m1)]
        pm = [eye - mm_tn(zz, x) for zz, x in zip(z, ws)]
        for n, s in enumerate(sl):
            b = g * GROUP + n
            t_out[0, s, :] = inv[n].astype(t_out.dtype)
            a_out[0, s, :] = a[n].astype(a_out.dtype)
            z_out[0, s, :] = z[n].astype(z_out.dtype)
            m_out[0, s, :] = m1[n].astype(m_out.dtype)
            kp_out[0, s, :HD] = kmt[n].astype(BF16)
            kp_out[0, s, HD:] = pm[n].astype(BF16)
            qm_buf[s, :] = qm[n]
            s_buf[s, s] = sd[n]
        return carry

    lax.fori_loop(0, NB // GROUP, group, 0)
    at = NQC
    for j in range(NB - 2, -1, -1):
        r0 = (j + 1) * BLK
        rows = SEQ - r0
        x_buf[r0 : r0 + BLK, :] = qm_buf[r0 : r0 + BLK, :]
        x = x_buf[r0:, :].astype(BF16)
        at -= rows
        qc[0, at : at + rows, :] = x
        both = mm(x, kp_out[0, j * BLK : r0, :])
        s_buf[r0:, j * BLK : r0] = both[:, :HD]
        x_buf[r0:, :] = both[:, HD:]
    for i in range(NB):
        lo, width = i * BLK, (i + 1) * BLK
        s = s_buf[lo:width, :width] * SCALE
        seen = dcol[lo:width, :] == drow[:, :width]
        seen = seen & (
            lax.broadcasted_iota(jnp.int32, (BLK, width), 0) + lo
            >= lax.broadcasted_iota(jnp.int32, (BLK, width), 1)
        )
        s = jnp.where(seen, s, -1e30)
        e = jnp.exp(s - jnp.max(s, axis=1, keepdims=True))
        p = e * (1.0 / jnp.sum(e, axis=1, keepdims=True))
        pb = p.astype(BF16)
        probs[0, lo:width, :width] = pb
        o[lo:width, :] = mm(pb, v[:width, :])


def bwd_kernel(q, k, v, w, bcol, brow, o, do, probs, qc, t_in, a_in, z_in, m_in, kp, dq, dk, dv, dw, dbc, dbr, ds_buf, x_buf, dkm_buf, dpm_buf, ):
    row, col = iota2(0), iota2(1)
    strict, closed = row > col, row >= col
    for i in range(NB):
        lo, width = i * BLK, (i + 1) * BLK
        p = probs[0, lo:width, :width].astype(F32)
        g = do[lo:width, :]
        delta = jnp.sum(g * o[lo:width, :], axis=1, keepdims=True)
        ds = p * (mm_nt(g, v[:width, :]) - delta) * SCALE
        ds_buf[lo:width, :width] = ds.astype(BF16)
    for j in range(NB):
        lo = j * BLK
        dv[lo : lo + BLK, :] = mm_tn(probs[0, lo:, lo : lo + BLK], do[lo:, :]).astype(dv.dtype)
    x_buf[...] = jnp.zeros_like(x_buf)
    dkm_buf[SEQ - BLK :, :] = jnp.zeros((BLK, HD), F32)
    dpm_buf[SEQ - BLK :, :] = jnp.zeros((BLK, HD), F32)
    at = 0
    for j in range(NB - 1):
        lo, r0 = j * BLK, (j + 1) * BLK
        rows = SEQ - r0
        x = x_buf[r0:, :].astype(BF16)
        ds = ds_buf[r0:, lo:r0]
        qcj = qc[0, at : at + rows, :]
        at += rows
        both = mm_tn(qcj, jnp.concatenate([x, ds], axis=1))
        dpm_buf[lo:r0, :] = both[:, :HD]
        dkm_buf[lo:r0, :] = both[:, HD:].T
        kpj = kp[0, lo:r0, :]
        x_buf[r0:, :] = mm_nt(jnp.concatenate([ds, x], axis=1), kpj)

    def group(g, carry):
        sl = [pl.ds(pl.multiple_of((g * GROUP + n) * BLK, BLK), BLK) for n in range(GROUP)]
        rng = range(GROUP)
        Q = [q[s, :] for s in sl]
        K = [k[s, :] for s in sl]
        W = [w[s, :] for s in sl]
        bc = [bcol[0, s, :] for s in sl]
        br = [brow[0, :, s] for s in sl]
        E = [ds_buf[s, s] for s in sl]
        T = [t_in[0, s, :] for s in sl]
        A = [a_in[0, s, :] for s in sl]
        Z = [z_in[0, s, :] for s in sl]
        M = [m_in[0, s, :] for s in sl]
        dQm = [x_buf[s, :] for s in sl]
        dKm = [dkm_buf[s, :] for s in sl]
        dPm = [dpm_buf[s, :] for s in sl]
        E = [jnp.where(closed, e, jnp.zeros_like(e)) for e in E]
        i1 = [mm_nt(W[n], W[n]) for n in rng]
        qw = [jnp.where(closed, mm_nt(Q[n], W[n]), 0.0) for n in rng]
        dA = [-(mm_nt(E[n], M[n]) + mm_nt(dQm[n], W[n])) for n in rng]
        dM = [jnp.where(strict, -(mm_tn(A[n], E[n]) + mm_nt(Z[n], dKm[n])), 0.0) for n in rng]
        dZ = [-(mm(M[n], dKm[n]) + mm_nt(W[n], dPm[n])) for n in rng]
        dW = [-(mm_tn(A[n], dQm[n]) + mm(Z[n], dPm[n])) for n in rng]
        dG = [jnp.where(closed, mm_nt(dA[n], T[n]), 0.0) for n in rng]
        bw = [bc[n] * W[n].astype(F32) for n in rng]
        dT = [mm_tn(qw[n] * br[n], dA[n]) + mm_nt(bw[n], dZ[n]) for n in rng]
        dBW = [mm(T[n], dZ[n]) for n in rng]
        dL = [mm_tn(T[n], dT[n]) for n in rng]
        dL = [jnp.where(strict, -mm_nt(dL[n], T[n]), 0.0) for n in rng]
        dI = [dL[n] * br[n] for n in rng]
        R = [dG[n] * br[n] for n in rng]
        for n, s in enumerate(sl):
            dbr[0, :, s] = jnp.sum(dL[n] * i1[n] + dG[n] * qw[n], axis=0, keepdims=True)
            dbc[0, s, :] = jnp.sum(dBW[n] * W[n].astype(F32), axis=1, keepdims=True)
            dq[s, :] = (dQm[n] + mm(E[n], K[n]) + mm(R[n], W[n])).astype(dq.dtype)
            dk[s, :] = (dKm[n] + mm_tn(E[n], Q[n]) + mm_tn(dM[n], W[n])).astype(dk.dtype)
            dw[s, :] = (
                dW[n]
                + bc[n] * dBW[n]
                + mm_tn(R[n], Q[n])
                + mm(dM[n], K[n])
                + mm(dI[n] + dI[n].T, W[n])
            )
        return carry

    lax.fori_loop(0, NB // GROUP, group, 0)


def _full(shape):
    return pl.BlockSpec(shape, lambda s: (0,) * len(shape))


def _slot(*shape):
    return pl.BlockSpec((1,) + shape, lambda s: (s,) + (0,) * len(shape))


def _cols(at):
    return pl.BlockSpec((SEQ, HD), lambda s: (0, at + s))


def attn_fwd(qkv, vec, bcol, brow, dcol, drow):
    slots = bcol.shape[0]
    sds = jax.ShapeDtypeStruct
    return pl.pallas_call(
        fwd_kernel,
        grid=(slots,),
        in_specs=[_cols(0), _cols(2), _cols(4), _cols(0), _slot(SEQ, 1), _slot(1, SEQ), _full((SEQ, 1)), _full((1, SEQ))],
        out_specs=[_cols(0), _slot(SEQ, SEQ), _slot(NQC, HD)] + [_slot(SEQ, BLK)] * 4 + [_slot(SEQ, 2 * HD)],
        out_shape=[
            sds((SEQ, slots * HD), F32),
            sds((slots, SEQ, SEQ), BF16),
            sds((slots, NQC, HD), BF16),
            sds((slots, SEQ, BLK), F32),
            sds((slots, SEQ, BLK), BF16),
            sds((slots, SEQ, BLK), BF16),
            sds((slots, SEQ, BLK), BF16),
            sds((slots, SEQ, 2 * HD), BF16),
        ],
        scratch_shapes=[pltpu.VMEM((SEQ, SEQ), F32), pltpu.VMEM((SEQ, HD), F32), pltpu.VMEM((SEQ, HD), F32)],
        compiler_params=pltpu.CompilerParams(vmem_limit_bytes=VM),
        name="attn_fwd",
    )(qkv, qkv, qkv, vec, bcol, brow, dcol, drow)


def attn_bwd(qkv, vec, bcol, brow, o, do, saved):
    slots = bcol.shape[0]
    sds = jax.ShapeDtypeStruct
    return pl.pallas_call(
        bwd_kernel,
        grid=(slots,),
        in_specs=[_cols(0), _cols(2), _cols(4), _cols(0), _slot(SEQ, 1), _slot(1, SEQ), _cols(0), _cols(0)]
        + [_slot(SEQ, SEQ), _slot(NQC, HD)] + [_slot(SEQ, BLK)] * 4 + [_slot(SEQ, 2 * HD)],
        out_specs=[_cols(0)] * 4 + [_slot(SEQ, 1), _slot(1, SEQ)],
        out_shape=[sds((SEQ, slots * HD), BF16)] * 3 + [sds((SEQ, slots * HD), F32), sds((slots, SEQ, 1), F32), sds((slots, 1, SEQ), F32)],
        scratch_shapes=[pltpu.VMEM((SEQ, SEQ), BF16)] + [pltpu.VMEM((SEQ, HD), F32)] * 3,
        compiler_params=pltpu.CompilerParams(vmem_limit_bytes=VM),
        name="attn_bwd",
    )(qkv, qkv, qkv, vec, bcol, brow, o, do, *saved)


MESH = pl.DeviceIdType.MESH
ANY = pl.BlockSpec(memory_space=pl.ANY)
VMEM = pl.BlockSpec(memory_space=pltpu.VMEM)


class Place:
    def __init__(self):
        self.x, self.c = lax.axis_index("x"), lax.axis_index("c")
        self.y = lax.axis_index("y")
        self.zl, self.zh = lax.axis_index("zl"), lax.axis_index("zh")
        self.z = self.zh * 2 + self.zl

    def chip(self, d):
        return lax.rem(self.x + d, 4)

    def at_x(self, d):
        return {"x": lax.rem(self.x + d, 4)}

    def at_xc(self, d, k):
        return {"x": lax.rem(self.x + d, 4), "c": lax.rem(self.c + k, 2)}

    def sibling(self):
        return {"c": 1 - self.c}

    def at_y(self, d):
        return {"y": lax.rem(self.y + d, 4)}

    def at_z(self, d):
        z = lax.rem(self.z + d, 4)
        return {"zl": lax.rem(z, 2), "zh": z // 2}


class Net:
    def __init__(self, send_sem, recv_sem, local_sem):
        self.place = Place()
        self.send_sem, self.recv_sem, self.local_sem = send_sem, recv_sem, local_sem
        self.count, self.kept, self.locals, self.sent = 0, 0, [], []

    def prepare(self, src, dst, device):
        k = self.count
        self.count += 1
        return pltpu.make_async_remote_copy(
            src_ref=src,
            dst_ref=dst,
            send_sem=self.send_sem.at[k],
            recv_sem=self.recv_sem.at[k],
            device_id=device,
            device_id_type=MESH,
        )

    def send(self, src, dst, device):
        copy = self.prepare(src, dst, device)
        copy.start()
        self.sent.append(copy)
        return copy

    def local(self, src, dst):
        self.kept += 1
        return pltpu.make_async_copy(src, dst, self.local_sem.at[self.kept - 1])

    def keep(self, src, dst):
        copy = self.local(src, dst)
        copy.start()
        self.locals.append(copy)

    def settle(self):
        for copy in self.locals:
            copy.wait()
        self.locals = []

    def finish(self):
        for copy in self.sent:
            copy.wait_send()
        self.settle()


def meet(devices):
    barrier = pltpu.get_barrier_semaphore()
    for device in devices:
        pl.semaphore_signal(barrier, inc=1, device_id=device, device_id_type=MESH)
    pl.semaphore_wait(barrier, len(devices))


def interleave(*jobs):
    jobs = list(jobs)
    while jobs:
        for job in list(jobs):
            try:
                next(job)
            except StopIteration:
                jobs.remove(job)


def team_peers(p):
    return [p.at_x(1), p.at_x(3), p.sibling()]


def team_all(p):
    return [p.at_xc(d, k) for d in range(4) for k in range(2) if d + k]


def group_peers(p):
    return [p.at_y(d) for d in (1, 2, 3)] + [p.at_z(d) for d in (1, 2, 3)]


def gather_team(net, own, out):
    p = net.place
    me, sib = 2 * p.x + p.c, p.sibling()
    right, left = p.at_x(1), p.at_x(3)
    t_l, t_r, t_2 = (2 * p.chip(d) + p.c for d in (3, 1, 2))
    to_r = net.send(own, out.at[:, me], right)
    to_l = net.send(own, out.at[:, me], left)
    shared = [net.send(own, out.at[:, me], sib)]
    net.keep(own, out.at[:, me])
    yield
    to_r.wait_recv()
    on_r = net.send(out.at[0, t_l], out.at[0, t_l], right)
    shared.append(net.send(out.at[:, t_l], out.at[:, t_l], sib))
    to_l.wait_recv()
    on_l = net.send(out.at[1, t_r], out.at[1, t_r], left)
    shared.append(net.send(out.at[:, t_r], out.at[:, t_r], sib))
    yield
    on_r.wait_recv()
    shared.append(net.send(out.at[0, t_2], out.at[0, t_2], sib))
    on_l.wait_recv()
    shared.append(net.send(out.at[1, t_2], out.at[1, t_2], sib))
    yield
    for copy in shared:
        copy.wait_recv()


GATHER_TEAM = 10


def add(a, b):
    return (a.astype(F32) + b.astype(F32)).astype(BF16)


def scatter_team(net, part, got, total, from_l, from_r, all_l, all_r, finish):
    p = net.place
    sib, right, left = p.sibling(), p.at_x(1), p.at_x(3)
    order = (2, 1, 3, 0)
    swaps = [
        net.send(part.at[:, 2 * p.chip(d) + 1 - p.c], got.at[:, p.chip(d)], sib) for d in order
    ]

    def pair(n):
        swaps[n].wait_recv()
        at = p.chip(order[n])
        total[:, at] = add(part[:, 2 * at + p.c], got[:, at])
        return at

    yield
    x_2 = pair(0)
    half_r = net.send(total.at[0, x_2], from_l, right)
    half_l = net.send(total.at[1, x_2], from_r, left)
    x_r = pair(1)
    rest_r = net.send(total.at[1, x_r], all_l.at[1], right)
    x_l = pair(2)
    rest_l = net.send(total.at[0, x_l], all_r.at[0], left)
    pair(3)
    yield
    half_r.wait_recv()
    total[0, x_r] = add(total[0, x_r], from_l[...])
    last_r = net.send(total.at[0, x_r], all_l.at[0], right)
    half_l.wait_recv()
    total[1, x_l] = add(total[1, x_l], from_r[...])
    last_l = net.send(total.at[1, x_l], all_r.at[1], left)
    yield
    for copy in (rest_r, rest_l, last_r, last_l):
        copy.wait_recv()
    finish(total[:, p.x].astype(F32) + all_l[...].astype(F32) + all_r[...].astype(F32))


SCATTER_TEAM = 10


def scatter_team_scratch(n, w):
    return [
        pltpu.VMEM((2, 4, n, w), BF16),
        pltpu.VMEM((2, 4, n, w), BF16),
        pltpu.VMEM((n, w), BF16),
        pltpu.VMEM((n, w), BF16),
        pltpu.VMEM((2, n, w), BF16),
        pltpu.VMEM((2, n, w), BF16),
    ]


def chunk_rows(y, z, rows):
    zl, zh = (z % 2, z // 2) if isinstance(z, int) else (lax.rem(z, 2), z // 2)
    return pl.ds(pl.multiple_of(((zl * 4 + y) * 2 + zh) * rows, rows), rows)


def gather_groups(net, own, out, cuts):
    p = net.place
    rows = own.shape[0]
    lo, mid, hi = cuts
    first, second = pl.ds(lo, mid - lo), pl.ds(mid, hi - mid)
    net.keep(own, out.at[chunk_rows(p.y, p.z, rows)])

    def spread(cols, y, z, devices, src=None):
        place = out.at[chunk_rows(y, z, rows), cols]
        return [net.send(place if src is None else src.at[:, cols], place, d) for d in devices]

    ys, zs = [p.at_y(d) for d in (1, 3, 2)], [p.at_z(d) for d in (1, 3, 2)]
    y_first = spread(first, p.y, p.z, ys, own)
    z_first = spread(second, p.y, p.z, zs, own)
    last = spread(first, p.y, p.z, zs, own) + spread(second, p.y, p.z, ys, own)
    yield
    for n, d in enumerate((1, 3, 2)):
        y_first[n].wait_recv()
        last += spread(first, lax.rem(p.y + 4 - d, 4), p.z, zs)
        z_first[n].wait_recv()
        last += spread(second, p.y, lax.rem(p.z + 4 - d, 4), ys)
        yield
    for copy in last:
        copy.wait_recv()


GATHER_GROUPS = 30


def scatter_groups(net, part, out, cuts, z_got, z_sum, z_last, y_got, y_sum, y_last):
    p = net.place
    lo, mid, hi = cuts
    first, second = pl.ds(lo, mid - lo), pl.ds(mid, hi - mid)
    rows = z_sum.shape[1]
    flat = len(part.shape) == 2
    order = (2, 1, 3)
    a = []
    b = []
    for n, d in enumerate(order):
        z, y = lax.rem(p.z + d, 4), lax.rem(p.y + d, 4)
        if flat:
            for k in range(4):
                a.append(net.send(part.at[chunk_rows(k, z, rows), first], z_got.at[n, k], p.at_z(d)))
                b.append(net.send(part.at[chunk_rows(y, k, rows), second], y_got.at[n, k % 2, k // 2], p.at_y(d)))
        else:
            a.append(net.send(part.at[lax.rem(z, 2), :, z // 2, :, first], z_got.at[n], p.at_z(d)))
            b.append(net.send(part.at[:, y, :, :, second], y_got.at[n], p.at_y(d)))

    def own(y, zl, zh, cols):
        if flat:
            return part[chunk_rows(y, zh * 2 + zl, rows), cols].astype(F32)
        return part[zl, y, zh, :, cols].astype(F32)

    yield
    for copy in a:
        copy.wait_recv()
    for y in range(4):
        t = own(y, p.zl, p.zh, first)
        for n in range(3):
            t = t + z_got[n, y].astype(F32)
        z_sum[y] = t.astype(BF16)
    a = [
        net.send(z_sum.at[lax.rem(p.y + d, 4)], z_last.at[n], p.at_y(d)) for n, d in enumerate(order)
    ]
    yield
    for copy in b:
        copy.wait_recv()
    for zl in range(2):
        for zh in range(2):
            t = own(p.y, zl, zh, second)
            for n in range(3):
                t = t + y_got[n, zl, zh].astype(F32)
            y_sum[zl, zh] = t.astype(BF16)
    b = []
    for n, d in enumerate(order):
        z = lax.rem(p.z + d, 4)
        b.append(net.send(y_sum.at[lax.rem(z, 2), z // 2], y_last.at[n], p.at_z(d)))
    yield
    for copy in a:
        copy.wait_recv()
    t = z_sum[p.y].astype(F32)
    for n in range(3):
        t = t + z_last[n].astype(F32)
    out[:, first] = t.astype(out.dtype)
    yield
    for copy in b:
        copy.wait_recv()
    t = y_sum[p.zl, p.zh].astype(F32)
    for n in range(3):
        t = t + y_last[n].astype(F32)
    out[:, second] = t.astype(out.dtype)


SCATTER_GROUPS = 12
SCATTER_GROUPS_FLAT = 30


def scatter_groups_scratch(r, cuts):
    a, b = cuts[1] - cuts[0], cuts[2] - cuts[1]
    return [
        pltpu.VMEM((3, 4, r, a), BF16),
        pltpu.VMEM((4, r, a), BF16),
        pltpu.VMEM((3, r, a), BF16),
        pltpu.VMEM((3, 2, 2, r, b), BF16),
        pltpu.VMEM((2, 2, r, b), BF16),
        pltpu.VMEM((3, r, b), BF16),
    ]


def sems(remote, local):
    return [
        pltpu.SemaphoreType.DMA((remote,)),
        pltpu.SemaphoreType.DMA((remote,)),
        pltpu.SemaphoreType.DMA((max(local, 1),)),
    ]


def params(collective_id):
    return pltpu.CompilerParams(
        collective_id=collective_id, has_side_effects=True, vmem_limit_bytes=VM
    )


EPS_NORM = 1e-05
EPS_UNIT = 1e-06
SHAPE = jax.ShapeDtypeStruct


def all_to_team(net, packs, got):
    p = net.place
    me = 2 * p.x + p.c
    net.keep(packs.at[me], got.at[me])
    copies = []
    for d in (2, 1, 3, 0):
        for k in (1, 0):
            if d + k:
                to = 2 * p.chip(d) + lax.rem(p.c + k, 2)
                copies.append(net.send(packs.at[to], got.at[me], p.at_xc(d, k)))
    yield
    for copy in copies:
        copy.wait_recv()


def start_kernel(packs, tokens, grad_out, got, x_rows, g_rows, *sem):
    net = Net(*sem)
    p = net.place
    other = {"zh": 1 - p.zh}
    meet(team_all(p) + [other])
    swaps = []
    for src, dst in ((tokens, x_rows), (grad_out, g_rows)):
        net.keep(src.at[p.zh], dst.at[p.zh])
        swaps.append(net.send(src.at[1 - p.zh], dst.at[p.zh], other))
    interleave(all_to_team(net, packs, got))
    for copy in swaps:
        copy.wait_recv()
    net.finish()


def start(packs, tokens, grad_out):
    rows = SHAPE(tokens.shape, BF16)
    return pl.pallas_call(
        start_kernel,
        out_shape=[SHAPE(packs.shape, BF16), rows, rows],
        in_specs=[ANY] * 3,
        out_specs=[ANY] * 3,
        scratch_shapes=sems(9, 3),
        compiler_params=params(1),
        name="start",
    )(packs, tokens, grad_out)


def lanes(at):
    return pl.ds(pl.multiple_of(at * HD, HD), HD)


OUT_AT = 8


def trade_out(net, whole, w_out):
    p = net.place
    copies = []
    for d in (2, 1, 3, 0):
        for k in (1, 0):
            xd, cd = p.chip(d), lax.rem(p.c + k, 2)
            row_a, row_b = lanes(3 * xd + 2 * cd), lanes(3 * xd + 1)
            row_c = lanes(3 * xd + jnp.where(p.c == 0, 2 * cd, 1))
            col_a, col_b = lanes(3 * p.x + 2 * p.c), lanes(3 * p.x + 1)
            moves = (
                (whole.at[row_a, pl.ds(OUT_AT * HD, HD)], w_out.at[pl.ds(0, HD), col_a]),
                (whole.at[row_b, pl.ds(OUT_AT * HD, HD)], w_out.at[pl.ds(HD, HD), col_a]),
                (whole.at[row_c, pl.ds((OUT_AT + 1) * HD, HD)], w_out.at[lanes(p.c), col_b]),
            )
            for src, dst in moves:
                if d + k:
                    copies.append(net.send(src, dst, p.at_xc(d, k)))
                else:
                    net.keep(src, dst)
    yield
    for copy in copies:
        copy.wait_recv()


def gather_kernel(cuts, x_rows, g_rows, own, x_all, g_all, whole, w_out, *sem):
    net = Net(*sem)
    p = net.place
    meet(team_all(p) + group_peers(p))
    interleave(
        gather_team(net, x_rows, x_all),
        gather_groups(net, own, whole, cuts),
        gather_team(net, g_rows, g_all),
    )
    net.settle()
    interleave(trade_out(net, whole, w_out))
    net.finish()


def gather_all(x_rows, g_rows, own):
    rows, cols = own.shape
    two, n, width = x_rows.shape
    every = SHAPE((two, 8, n, width), BF16)
    return pl.pallas_call(
        functools.partial(gather_kernel, (0, 768, cols)),
        out_shape=[every, every, SHAPE((16 * rows, cols), BF16), SHAPE((2 * HD, width), BF16)],
        in_specs=[ANY] * 3,
        out_specs=[ANY] * 4,
        scratch_shapes=sems(2 * GATHER_TEAM + GATHER_GROUPS + 21, 6),
        compiler_params=params(2),
        name="gather_all",
    )(x_rows, g_rows, own)


def ffn_in_kernel(cuts, part, x_rows, gain, own_ffn, own_down, hidden, ffn_all, w_ffn, w_down, normed, *rest):
    net = Net(*rest[-3:])
    p = net.place
    meet(team_peers(p) + group_peers(p))

    def finish(branch):
        h = x_rows[...].astype(F32) + branch
        hidden[...] = h
        scale = lax.rsqrt(jnp.mean(h * h, axis=-1, keepdims=True) + EPS_NORM)
        normed[...] = (h * scale * gain[...][None]).astype(BF16)

    def team():
        yield from scatter_team(net, part, *rest[:-3], finish)
        yield from gather_team(net, normed, ffn_all)

    interleave(
        team(),
        gather_groups(net, own_ffn, w_ffn, cuts[0]),
        gather_groups(net, own_down, w_down, cuts[1]),
    )
    net.finish()


def ffn_in(part, x_rows, gain, own_ffn, own_down):
    two, n, width = x_rows.shape
    cuts = [(0, a.shape[1] // 2, a.shape[1]) for a in (own_ffn, own_down)]
    return pl.pallas_call(
        functools.partial(ffn_in_kernel, cuts),
        out_shape=[
            SHAPE((two, n, width), F32),
            SHAPE((two, 8, n, width), BF16),
            SHAPE((16 * own_ffn.shape[0], own_ffn.shape[1]), BF16),
            SHAPE((16 * own_down.shape[0], own_down.shape[1]), BF16),
        ],
        in_specs=[VMEM, VMEM, VMEM, ANY, ANY],
        out_specs=[VMEM, ANY, ANY, ANY],
        scratch_shapes=[pltpu.VMEM((two, n, width), BF16)]
        + scatter_team_scratch(n, width)
        + sems(SCATTER_TEAM + GATHER_TEAM + 2 * GATHER_GROUPS, 3),
        compiler_params=params(3),
        name="ffn_in",
    )(part, x_rows, gain, own_ffn, own_down)


def norm_back(v, gain, d_normed):
    scale = lax.rsqrt(jnp.mean(v * v, axis=-1, keepdims=True) + EPS_NORM)
    unit = v * scale
    d_unit = d_normed * gain
    d_v = scale * (d_unit - unit * jnp.mean(d_unit * unit, axis=-1, keepdims=True))
    return d_v, d_normed * unit


def ffn_back_kernel(cuts, part, hidden, gain, g_rows, d_ffn, d_down, d_hidden, d_gain, branch_all, ffn_sum, down_sum, branch, *rest):
    team_scratch, ffn_scratch, down_scratch = rest[:6], rest[6:12], rest[12:18]
    net = Net(*rest[-3:])
    p = net.place
    meet(team_peers(p) + group_peers(p))

    def finish(d_normed):
        d_h, d_g = norm_back(hidden[...], gain[...][None], d_normed)
        d_h = d_h + g_rows[...].astype(F32)
        d_hidden[...] = d_h
        branch[...] = d_h.astype(BF16)
        d_gain[...] = jnp.sum(jnp.sum(d_g, axis=0), axis=0, keepdims=True)

    def team():
        yield from scatter_team(net, part, *team_scratch, finish)
        yield from gather_team(net, branch, branch_all)

    interleave(
        team(),
        scatter_groups(net, d_ffn, ffn_sum, cuts[0], *ffn_scratch),
        scatter_groups(net, d_down, down_sum, cuts[1], *down_scratch),
    )
    net.finish()


def by_group(a):
    return a.reshape(2, 4, 2, a.shape[0] // 16, a.shape[1])


def ffn_back(part, hidden, gain, g_rows, d_ffn, d_down):
    two, n, width = hidden.shape
    d_ffn, d_down = by_group(d_ffn), by_group(d_down)
    sizes = [a.shape[3:] for a in (d_ffn, d_down)]
    cuts = [(0, w // 2, w) for _, w in sizes]
    return pl.pallas_call(
        functools.partial(ffn_back_kernel, cuts),
        out_shape=[
            SHAPE((two, n, width), F32),
            SHAPE((1, width), F32),
            SHAPE((two, 8, n, width), BF16),
            SHAPE(sizes[0], BF16),
            SHAPE(sizes[1], F32),
        ],
        in_specs=[VMEM] * 6,
        out_specs=[VMEM, VMEM, ANY, VMEM, VMEM],
        scratch_shapes=[pltpu.VMEM((two, n, width), BF16)]
        + scatter_team_scratch(n, width)
        + scatter_groups_scratch(sizes[0][0], cuts[0])
        + scatter_groups_scratch(sizes[1][0], cuts[1])
        + sems(SCATTER_TEAM + GATHER_TEAM + 2 * SCATTER_GROUPS, 1),
        compiler_params=params(4),
        name="ffn_back",
    )(part, hidden, gain, g_rows, d_ffn, d_down)


def trade_out_back(net, d_out, whole):
    p = net.place
    rows, middle, own = [], [], []
    cases = [(d, k) for d in (2, 1, 3, 0) for k in (1, 0)]
    for d, k in cases:
        xd, cd = p.chip(d), lax.rem(p.c + k, 2)
        for side, col in enumerate((lanes(3 * xd + 2 * cd), lanes(3 * xd + 1))):
            src = d_out.at[pl.ds(0, HD), col]
            dst = whole.at[lanes(3 * p.x + 2 * p.c), pl.ds(side * HD, HD)]
            if d + k:
                rows.append(net.send(src, dst, p.at_xc(d, k)))
            else:
                own.append(net.local(src, dst))
                own[-1].start()
    for d, k in cases:
        xd, cd = p.chip(d), lax.rem(p.c + k, 2)
        for side, col in enumerate((lanes(3 * xd + 2 * cd), lanes(3 * xd + 1))):
            src = d_out.at[pl.ds(HD, HD), col]
            dst = whole.at[lanes(3 * p.x + 1), pl.ds(side * HD, HD)]
            if d + k:
                middle.append((k, net.prepare(src, dst, p.at_xc(d, k))))
            else:
                middle.append((-1, net.local(src, dst)))

    @pl.when(p.c == 0)
    def _():
        for _, copy in middle:
            copy.start()

    yield
    for copy in rows:
        copy.wait_recv()
    for copy in own:
        copy.wait()
    for core in range(2):

        @pl.when(p.c == core)
        def _(core=core):
            for k, copy in middle:
                if k == core:
                    copy.wait_recv()

    @pl.when(p.c == 0)
    def _():
        for k, copy in middle:
            if k < 0:
                copy.wait()
            else:
                copy.wait_send()

    yield


TRADE_BACK = 28


def last_kernel(cuts, part_n, part_o, x_rows, hidden, d_hidden, gain, d_heads, d_out, out_rows, d_rows, heads_sum, out_sum, whole, *rest):
    n_scratch, o_scratch, h_scratch, w_scratch = rest[:6], rest[6:12], rest[12:18], rest[18:24]
    net = Net(*rest[-3:])
    p = net.place
    meet(team_all(p) + group_peers(p))

    def finish_n(d_normed):
        d_x, _ = norm_back(x_rows[...].astype(F32), gain[...][None], d_normed)
        d_rows[...] = (d_x + d_hidden[...]).astype(BF16)

    def finish_o(branch):
        out_rows[...] = (hidden[...] + branch).astype(BF16)

    def out_grad():
        yield from trade_out_back(net, d_out, whole)
        yield from scatter_groups(net, whole, out_sum, cuts[1], *w_scratch)

    interleave(
        out_grad(),
        scatter_groups(net, d_heads, heads_sum, cuts[0], *h_scratch),
        scatter_team(net, part_n, *n_scratch, finish_n),
        scatter_team(net, part_o, *o_scratch, finish_o),
    )
    net.finish()


def last_sums(part_n, part_o, x_rows, hidden, d_hidden, gain, d_heads, d_out):
    two, n, width = hidden.shape
    d_heads = by_group(d_heads)
    r, w = d_heads.shape[3:]
    cuts = [(0, 640, w), (0, HD, 2 * HD)]
    return pl.pallas_call(
        functools.partial(last_kernel, cuts),
        out_shape=[
            SHAPE((two, n, width), BF16),
            SHAPE((two, n, width), BF16),
            SHAPE((r, w), BF16),
            SHAPE((r, 2 * HD), BF16),
        ],
        in_specs=[VMEM] * 8,
        out_specs=[VMEM] * 4,
        scratch_shapes=[pltpu.VMEM((width, 2 * HD), BF16)]
        + scatter_team_scratch(n, width) * 2
        + scatter_groups_scratch(r, cuts[0])
        + scatter_groups_scratch(r, cuts[1])
        + sems(2 * SCATTER_TEAM + SCATTER_GROUPS + SCATTER_GROUPS_FLAT + TRADE_BACK, 4),
        compiler_params=params(5),
        name="last_sums",
    )(part_n, part_o, x_rows, hidden, d_hidden, gain, d_heads, d_out)


def end_kernel(packs, out_rows, d_rows, got, output, d_tokens, *sem):
    net = Net(*sem)
    p = net.place
    other = {"zh": 1 - p.zh}
    meet(team_all(p) + [other])
    swaps = []
    for src, dst in ((out_rows, output), (d_rows, d_tokens)):
        net.keep(src.at[p.zh], dst.at[p.zh])
        swaps.append(net.send(src.at[1 - p.zh], dst.at[p.zh], other))
    interleave(all_to_team(net, packs, got))
    for copy in swaps:
        copy.wait_recv()
    net.finish()


def end(packs, out_rows, d_rows):
    rows = SHAPE(out_rows.shape, BF16)
    return pl.pallas_call(
        end_kernel,
        out_shape=[SHAPE(packs.shape, BF16), rows, rows],
        in_specs=[ANY] * 3,
        out_specs=[ANY] * 3,
        scratch_shapes=sems(9, 3),
        compiler_params=params(6),
        name="end",
    )(packs, out_rows, d_rows)


def dot_nn(a, b):
    return lax.dot_general(a, b, (((1,), (0,)), ((), ())), preferred_element_type=F32)


def dot_nt(a, b):
    return lax.dot_general(a, b, (((1,), (1,)), ((), ())), preferred_element_type=F32)


def dot_tn(a, b):
    return lax.dot_general(a, b, (((0,), (0,)), ((), ())), preferred_element_type=F32)


def rms_scale(values, gain_vec):
    return (
        values * lax.rsqrt(jnp.mean(values * values, axis=-1, keepdims=True) + EPS_NORM) * gain_vec
    )


def path_vectors(current, conv_w, same_doc):
    conved = conv_w[0] * current
    for tap in range(1, conv_w.shape[0]):
        earlier = jnp.pad(current, ((tap, 0), (0, 0)))[: current.shape[0]]
        conved = conved + conv_w[tap] * jnp.where(same_doc[tap][:, None], earlier, 0.0)
    heads = conved.reshape(current.shape[0], -1, HD)
    unit = heads * lax.rsqrt(jnp.sum(heads * heads, axis=-1, keepdims=True) + EPS_UNIT)
    return unit.reshape(current.shape)


def split_rows(partial):
    return partial.astype(BF16).reshape(2, 8, -1, partial.shape[1])


def pad_rows(a, rows):
    return jnp.pad(a, ((0, 0), (0, rows - a.shape[1]), (0, 0)))


HEADS_W, OUT_W, SMALL_W = 8 * HD, 2 * HD, HD


def per_device(
    tokens,
    doc_start,
    gain_attn,
    w_query,
    w_key,
    w_value,
    w_path,
    conv_path,
    w_beta,
    w_out,
    gain_ffn,
    w_gate,
    w_up,
    w_down,
    grad_out,
):
    zh, chip, core = lax.axis_index("zh"), lax.axis_index("x"), lax.axis_index("c")
    width = tokens.shape[2]
    share = w_query.shape[0]
    head_a, head_b = 3 * chip + 2 * core, 3 * chip + 1
    owns_b = core == 0

    small = jnp.concatenate([gain_attn[:, None], gain_ffn[:, None], conv_path.T, w_beta], axis=1)
    small = jnp.pad(small, ((0, 0), (0, SMALL_W - small.shape[1])))
    small = jnp.broadcast_to(small[None], (8, share, SMALL_W))
    kinds = jnp.stack([w_query, w_key, w_value, w_path, w_out], axis=1).reshape(share, 5, 4, 3, HD)
    slot_a = jnp.concatenate([kinds[:, :, :, 0:1], kinds[:, :, :, 2:3]], axis=3)
    slot_b = jnp.broadcast_to(kinds[:, :, :, 1:2], slot_a.shape)
    heads_pack = jnp.stack([slot_a, slot_b], axis=4).transpose(2, 3, 0, 1, 4, 5)
    heads_pack = heads_pack.reshape(8, share, -1)
    ffn_pack = jnp.stack([w_gate, w_up], axis=1).reshape(share, 2, 16, 8, 32)
    ffn_pack = ffn_pack.transpose(3, 0, 1, 2, 4).reshape(8, share, -1)
    packs = pad_rows(jnp.concatenate([heads_pack, small, ffn_pack], axis=2), 16)
    packs, x_rows, g_rows = start(packs, tokens, grad_out)
    packs = packs[:, :share].reshape(8 * share, -1)
    first_w = HEADS_W + OUT_W + SMALL_W
    x_all, g_all, whole, w_out_t = gather_all(x_rows, g_rows, packs[:, :first_w])
    w_heads = whole[:, :HEADS_W]
    small = whole[:, HEADS_W + OUT_W :]
    gain_a, gain_f = small[:, 0].astype(F32), small[:, 1].astype(F32)
    conv_full, beta_full = small[:, 2:6].T.astype(F32), small[:, 6:18]
    x_all = x_all.reshape(SEQ, width)
    g_all = g_all.reshape(SEQ, width)
    doc_rows = jnp.cumsum(doc_start, axis=1)
    docs = jnp.where(zh == 0, doc_rows[0], doc_rows[1])

    def two_heads(full, size):
        return jnp.concatenate(
            [
                lax.dynamic_slice_in_dim(full, head_a * size, size, 1),
                lax.dynamic_slice_in_dim(full, head_b * size, size, 1),
            ],
            axis=1,
        )

    def back_to_all(part, size):
        full = jnp.zeros((part.shape[0], 12 * size), F32)
        full = lax.dynamic_update_slice_in_dim(full, part[:, :size], head_a * size, 1)
        own_b = jnp.where(owns_b, part[:, size:], 0.0)
        return lax.dynamic_update_slice_in_dim(full, own_b, head_b * size, 1)

    def own_heads(v):
        return jnp.where((jnp.arange(2 * HD) < HD) | owns_b, v, 0.0)

    w_beta_t = two_heads(beta_full, 1)
    conv_t = two_heads(conv_full, HD)
    same_doc = [
        jnp.concatenate([jnp.zeros((tap,), bool), docs[: SEQ - tap] == docs[tap:]])
        for tap in range(4)
    ]

    normed_all = rms_scale(x_all.astype(F32), gain_a).astype(BF16)
    qkvp = dot_nn(normed_all, w_heads).astype(BF16)
    beta_raw = dot_nn(normed_all, w_beta_t)
    betas = (2.0 * jax.nn.sigmoid(beta_raw)).T
    vec_f, vec_pull = jax.vjp(
        lambda cur, cw: path_vectors(cur, cw, same_doc), qkvp[:, 6 * HD :].astype(F32), conv_t
    )
    vec = vec_f.astype(BF16)
    bcol, brow = betas[:, :, None], betas[:, None, :]
    o, *saved = attn_fwd(qkvp, vec, bcol, brow, docs[:, None], docs[None, :])
    mixed = own_heads(o).astype(BF16)
    hidden, ffn_all, w_ffn, w_down_t = ffn_in(
        split_rows(dot_nn(mixed, w_out_t)), x_rows, gain_f[None], packs[:, first_w:], w_down
    )
    ffn_all = ffn_all.reshape(SEQ, width)
    gate_up = dot_nn(ffn_all, w_ffn)
    half = gate_up.shape[1] // 2

    def gated(pre):
        return jax.nn.silu(pre[:, :half]) * pre[:, half:]

    act_f, act_pull = jax.vjp(gated, gate_up)
    act = act_f.astype(BF16)
    out_part = split_rows(dot_nn(act, w_down_t))

    (d_gate_up,) = act_pull(dot_nt(g_all, w_down_t))
    d_gate_up = d_gate_up.astype(BF16)
    d_hidden, d_gain_ffn, branch_all, d_ffn, d_down = ffn_back(
        split_rows(dot_nt(d_gate_up, w_ffn)),
        hidden,
        gain_f[None],
        g_rows,
        dot_tn(ffn_all, d_gate_up).astype(BF16),
        dot_tn(act, g_all).astype(BF16),
    )
    branch_all = branch_all.reshape(SEQ, width)
    d_mixed = own_heads(dot_nt(branch_all, w_out_t))
    d_q, d_k, d_v, d_vec, d_bc, d_br = attn_bwd(qkvp, vec, bcol, brow, o, d_mixed, saved)
    d_path, d_conv = vec_pull(d_vec)
    d_betas = (d_bc[:, :, 0] + d_br[:, 0, :]) * betas * (1.0 - 0.5 * betas)
    d_beta = d_betas.T.astype(BF16)
    d_qkvp = jnp.concatenate([d_q, d_k, d_v, d_path.astype(BF16)], axis=1)
    norm_part = (dot_nt(d_qkvp, w_heads) + dot_nt(d_beta, w_beta_t)).astype(BF16)
    d_gain_attn = jnp.sum(norm_part.astype(F32) * normed_all.astype(F32), axis=0) / gain_a

    small_back = jnp.concatenate(
        [
            d_gain_attn[:, None],
            d_gain_ffn.T,
            back_to_all(d_conv, HD).T,
            back_to_all(dot_tn(normed_all, d_beta), 1),
        ],
        axis=1,
    ).astype(BF16)
    small_back = jnp.pad(small_back, ((0, 0), (0, SMALL_W - small_back.shape[1])))
    d_heads = dot_tn(normed_all, d_qkvp).astype(BF16)
    out_rows, d_rows, heads_sum, out_sum = last_sums(
        split_rows(norm_part),
        out_part,
        x_rows,
        hidden,
        d_hidden,
        gain_a[None],
        jnp.concatenate([d_heads, small_back], axis=1),
        dot_tn(mixed, branch_all).astype(BF16),
    )
    packs = jnp.concatenate([heads_sum, out_sum, d_ffn], axis=1).reshape(8, share, -1)
    packs, output, d_tokens = end(pad_rows(packs, 16), out_rows, d_rows)
    packs = packs[:, :share]
    small = jnp.sum(packs[:, :, HEADS_W : HEADS_W + SMALL_W].astype(F32), axis=0)
    at = HEADS_W + SMALL_W
    heads_back = jnp.concatenate([packs[:, :, :HEADS_W], packs[:, :, at : at + OUT_W]], axis=2)
    heads_back = heads_back.reshape(4, 2, share, 5, 2, HD)
    by_head = jnp.stack(
        [heads_back[:, 0, :, :, 0], heads_back[:, 0, :, :, 1], heads_back[:, 1, :, :, 0]], axis=1
    )
    by_kind = by_head.transpose(3, 2, 0, 1, 4).reshape(5, share, width).astype(F32)
    ffn_sum = packs[:, :, at + OUT_W :].reshape(8, share, 2, 16, 32)
    ffn_sum = ffn_sum.transpose(2, 1, 3, 0, 4).reshape(2, share, -1).astype(F32)
    return (
        output,
        d_tokens,
        small[:, 0],
        by_kind[0],
        by_kind[1],
        by_kind[2],
        by_kind[3],
        small[:, 2:6].T,
        small[:, 6:18],
        by_kind[4],
        small[:, 1],
        ffn_sum[0],
        ffn_sum[1],
        d_down,
    )


def solution(mesh):
    names = ("zl", "y", "zh", "x", "c")
    fine = Mesh(mesh.devices.reshape(2, 4, 2, 4, 2), names)
    dp, ctx = names[:2], names[2:]
    rows, flat, mat, taps = P(dp, ctx, None), P(names), P(names, None), P(None, names)
    return jax.shard_map(
        per_device,
        mesh=fine,
        in_specs=(
            rows, P(dp, None), flat, mat, mat, mat, mat, taps, mat, mat, flat, mat, mat, mat, rows,
        ),
        out_specs=(
            rows, rows, flat, mat, mat, mat, mat, taps, mat, mat, flat, mat, mat, mat,
        ),
        check_vma=False,
    )
```

```python
import functools

import jax
import jax.numpy as jnp
from jax import lax
from jax.experimental import pallas as pl
from jax.experimental.pallas import tpu as pltpu
from jax.sharding import Mesh, PartitionSpec as P

F32, BF16 = jnp.float32, jnp.bfloat16
VM = 60 * 1024 * 1024

SEQ, HD, BLK = 1024, 128, 128
NB = SEQ // BLK
NQC = (NB * (NB - 1) // 2) * BLK
SCALE = HD ** (-0.5)
GROUP = 4


def mm(a, b, dims=((1,), (0,))):
    return lax.dot_general(
        a.astype(BF16), b.astype(BF16), (dims, ((), ())), preferred_element_type=F32
    )


def mm_nt(a, b):
    return mm(a, b, ((1,), (1,)))


def mm_tn(a, b):
    return mm(a, b, ((0,), (0,)))


def split(a):
    high = a.astype(BF16)
    return high, (a - high.astype(F32)).astype(BF16)


def mm3(a, b):
    ah, al = split(a)
    bh, bl = split(b)
    return mm(ah, bh) + (mm(ah, bl) + mm(al, bh))


def iota2(axis):
    return lax.broadcasted_iota(jnp.int32, (BLK, BLK), axis)


BASE = 16


def unit_inverses(lowers):
    row, col = iota2(0), iota2(1)
    eye = (row == col).astype(F32)
    in_base = (row // BASE) == (col // BASE)
    narrow = [jnp.where(in_base, low, 0.0) for low in lowers]
    inv = [eye for _ in lowers]
    for u in range(BASE - 1):
        pick = (col % BASE) == u
        coef = [jnp.sum(jnp.where(pick, low, 0.0), axis=1, keepdims=True) for low in narrow]
        for n, (t, c) in enumerate(zip(inv, coef)):
            t3 = t.reshape(BLK // BASE, BASE, BLK)
            lead = jnp.broadcast_to(t3[:, u : u + 1, :], t3.shape).reshape(BLK, BLK)
            inv[n] = t - c * lead
    size = BASE
    while size < BLK:
        off = ((row // (2 * size)) == (col // (2 * size))) & ((row // size) != (col // size))
        mid = [mm3(t, jnp.where(off, low, 0.0)) for t, low in zip(inv, lowers)]
        inv = [t - mm3(m, t) for t, m in zip(inv, mid)]
        size *= 2
    return inv


def betas_of(raw, head):
    lane = lax.broadcasted_iota(jnp.int32, raw.shape, 1)
    return 2.0 * jax.nn.sigmoid(
        jnp.sum(jnp.where(lane == head + BETA_AT, raw, 0.0), axis=1, keepdims=True)
    )


BETA_AT = 6
CONV_AT = 2
TAPS = 4


def conv_weights(small, head):
    part = small[pl.ds(pl.multiple_of(head * HD, HD), HD), :].astype(F32)
    return part.T[CONV_AT : CONV_AT + TAPS, :]


def convolve(path, taps, marks):
    total = taps[0:1, :] * path
    for m in range(1, TAPS):
        total = total + taps[m : m + 1, :] * (pltpu.roll(path, m, 0) * marks[:, m : m + 1])
    return total


def own_blocks(s, q, k, w, bcol, stores):
    t_out, a_out, z_out, m_out, kp_out, qm_buf, s_buf = stores
    row, col = iota2(0), iota2(1)
    strict, closed = row > col, row >= col
    eye = (row == col).astype(F32)

    def group(g, carry):
        sl = [pl.ds(pl.multiple_of((g * GROUP + n) * BLK, BLK), BLK) for n in range(GROUP)]
        qs = [q[r, :] for r in sl]
        ks = [k[r, :] for r in sl]
        ws = [w[r, :] for r in sl]
        bc = [jnp.broadcast_to(bcol[r, :], (BLK, BLK)) for r in sl]
        br = [b.T for b in bc]
        low = [jnp.where(strict, mm_nt(x, x), 0.0) * b for x, b in zip(ws, br)]
        inv = unit_inverses(low)
        m1 = [jnp.where(strict, mm_nt(x, y), 0.0) for x, y in zip(ws, ks)]
        gq = [jnp.where(closed, mm_nt(x, y), 0.0) * b for x, y, b in zip(qs, ws, br)]
        a = [mm(x, t) for x, t in zip(gq, inv)]
        z = [mm_tn(t, b * x.astype(F32)) for t, b, x in zip(inv, bc, ws)]
        sd = [mm_nt(x, y) - mm(p, m) for x, y, p, m in zip(qs, ks, a, m1)]
        qm = [x.astype(F32) - mm(p, y) for x, p, y in zip(qs, a, ws)]
        kmt = [x.astype(F32).T - mm_tn(zz, m) for x, zz, m in zip(ks, z, m1)]
        pm = [eye - mm_tn(zz, x) for zz, x in zip(z, ws)]
        for n, r in enumerate(sl):
            t_out[s, r, :] = inv[n].astype(t_out.dtype)
            a_out[s, r, :] = a[n].astype(a_out.dtype)
            z_out[s, r, :] = z[n].astype(z_out.dtype)
            m_out[s, r, :] = m1[n].astype(m_out.dtype)
            kp_out[s, r, :HD] = kmt[n].astype(BF16)
            kp_out[s, r, HD:] = pm[n].astype(BF16)
            qm_buf[r, :] = qm[n]
            s_buf[r, r] = sd[n]
        return carry

    lax.fori_loop(0, NB // GROUP, group, 0)


def sweep(s, qc, kp, qm_buf, x_buf, s_buf):
    at = NQC
    for j in range(NB - 2, -1, -1):
        r0 = (j + 1) * BLK
        rows = SEQ - r0
        x_buf[r0 : r0 + BLK, :] = qm_buf[r0 : r0 + BLK, :]
        x = x_buf[r0:, :].astype(BF16)
        at -= rows
        qc[s, at : at + rows, :] = x
        both = mm(x, kp[s, j * BLK : r0, :])
        s_buf[r0:, j * BLK : r0] = both[:, :HD]
        x_buf[r0:, :] = both[:, HD:]


def weigh(s, v, dcol, drow, s_buf, probs, o):
    for i in range(NB):
        lo, width = i * BLK, (i + 1) * BLK
        t = s_buf[lo:width, :width] * SCALE
        seen = dcol[lo:width, 0:1] == drow[0:1, :width]
        seen = seen & (
            lax.broadcasted_iota(jnp.int32, (BLK, width), 0) + lo
            >= lax.broadcasted_iota(jnp.int32, (BLK, width), 1)
        )
        t = jnp.where(seen, t, -1e30)
        e = jnp.exp(t - jnp.max(t, axis=1, keepdims=True))
        p = (e * (1.0 / jnp.sum(e, axis=1, keepdims=True))).astype(BF16)
        probs[s, lo:width, :width] = p
        o[lo:width, :] = mm(p, v[:width, :])


def project(x_all, whole, normed, qkvp, raw):
    rows = 256
    gain = whole[:, 8 * HD : 9 * HD].astype(F32)
    gain = jnp.concatenate(
        [gain[n * HD : (n + 1) * HD, :].T[0:1, :] for n in range(gain.shape[0] // HD)], axis=1
    )

    def block(i, carry):
        at = pl.ds(pl.multiple_of(i * rows, rows), rows)
        x = x_all[at, :].astype(F32)
        scale = lax.rsqrt(jnp.mean(x * x, axis=1, keepdims=True) + 1e-05)
        n = (x * scale * gain).astype(BF16)
        normed[at, :] = n
        y = mm(n, whole[:, : 9 * HD])
        qkvp[at, :] = y[:, : 8 * HD].astype(BF16)
        raw[at, :] = y[:, 8 * HD :]
        return carry

    lax.fori_loop(0, SEQ // rows, block, 0)


def fwd_steps(poke, x_all, whole, marks, drow, normed, qkvp, raw, vec, o, probs, qc, t_out, a_out, z_out, m_out, kp_out, s_buf, x_buf, qm_buf, b_buf):
    chip, core = lax.axis_index("x"), lax.axis_index("c")
    project(x_all, whole, normed, qkvp, raw)
    poke()
    for s, head in enumerate((3 * chip + 2 * core, 3 * chip + 1)):
        cols = slice(s * HD, (s + 1) * HD)
        q, k, v, path = (qkvp.at[:, (2 * n + s) * HD : (2 * n + s + 1) * HD] for n in range(4))
        taps = conv_weights(whole.at[:, 8 * HD : 9 * HD], head)
        conved = convolve(path[...].astype(F32), taps, marks[...])
        unit = conved * lax.rsqrt(jnp.sum(conved * conved, axis=1, keepdims=True) + 1e-06)
        vec[:, cols] = unit.astype(BF16)
        b_buf[...] = betas_of(raw[...], head)
        own_blocks(s, q, k, vec.at[:, cols], b_buf, (t_out, a_out, z_out, m_out, kp_out, qm_buf, s_buf))
        poke()
        sweep(s, qc, kp_out, qm_buf, x_buf, s_buf)
        poke()
        weigh(s, v, marks, drow, s_buf, probs, o.at[:, cols])
        poke()


def score_grads(s, v, o, do, probs, ds_buf, dv):
    for i in range(NB):
        lo, width = i * BLK, (i + 1) * BLK
        p = probs[s, lo:width, :width].astype(F32)
        g = do[lo:width, :]
        delta = jnp.sum(g * o[lo:width, :], axis=1, keepdims=True)
        ds = p * (mm_nt(g, v[:width, :]) - delta) * SCALE
        ds_buf[lo:width, :width] = ds.astype(BF16)
    for j in range(NB):
        lo = j * BLK
        dv[lo : lo + BLK, :] = mm_tn(probs[s, lo:, lo : lo + BLK], do[lo:, :]).astype(dv.dtype)


def sweep_back(s, qc, kp, ds_buf, x_buf, dkm_buf, dpm_buf):
    x_buf[...] = jnp.zeros_like(x_buf)
    dkm_buf[SEQ - BLK :, :] = jnp.zeros((BLK, HD), F32)
    dpm_buf[SEQ - BLK :, :] = jnp.zeros((BLK, HD), F32)
    at = 0
    for j in range(NB - 1):
        lo, r0 = j * BLK, (j + 1) * BLK
        rows = SEQ - r0
        x = x_buf[r0:, :].astype(BF16)
        ds = ds_buf[r0:, lo:r0]
        qcj = qc[s, at : at + rows, :]
        at += rows
        both = mm_tn(qcj, jnp.concatenate([x, ds], axis=1))
        dpm_buf[lo:r0, :] = both[:, :HD]
        dkm_buf[lo:r0, :] = both[:, HD:].T
        x_buf[r0:, :] = mm_nt(jnp.concatenate([ds, x], axis=1), kp[s, lo:r0, :])


def own_blocks_back(s, q, k, w, bcol, saved, bufs, dq, dk, dw, db):
    t_in, a_in, z_in, m_in = saved
    ds_buf, x_buf, dkm_buf, dpm_buf = bufs
    row, col = iota2(0), iota2(1)
    strict, closed = row > col, row >= col

    def group(g, carry):
        sl = [pl.ds(pl.multiple_of((g * GROUP + n) * BLK, BLK), BLK) for n in range(GROUP)]
        rng = range(GROUP)
        Q = [q[r, :] for r in sl]
        K = [k[r, :] for r in sl]
        W = [w[r, :] for r in sl]
        bc = [jnp.broadcast_to(bcol[r, :], (BLK, BLK)) for r in sl]
        br = [b.T for b in bc]
        E = [ds_buf[r, r] for r in sl]
        T = [t_in[s, r, :] for r in sl]
        A = [a_in[s, r, :] for r in sl]
        Z = [z_in[s, r, :] for r in sl]
        M = [m_in[s, r, :] for r in sl]
        dQm = [x_buf[r, :] for r in sl]
        dKm = [dkm_buf[r, :] for r in sl]
        dPm = [dpm_buf[r, :] for r in sl]
        i1 = [mm_nt(W[n], W[n]) for n in rng]
        qw = [jnp.where(closed, mm_nt(Q[n], W[n]), 0.0) for n in rng]
        dA = [-(mm_nt(E[n], M[n]) + mm_nt(dQm[n], W[n])) for n in rng]
        dM = [jnp.where(strict, -(mm_tn(A[n], E[n]) + mm_nt(Z[n], dKm[n])), 0.0) for n in rng]
        dZ = [-(mm(M[n], dKm[n]) + mm_nt(W[n], dPm[n])) for n in rng]
        dW = [-(mm_tn(A[n], dQm[n]) + mm(Z[n], dPm[n])) for n in rng]
        dG = [jnp.where(closed, mm_nt(dA[n], T[n]), 0.0) for n in rng]
        bw = [bc[n] * W[n].astype(F32) for n in rng]
        dT = [mm_tn(qw[n] * br[n], dA[n]) + mm_nt(bw[n], dZ[n]) for n in rng]
        dBW = [mm(T[n], dZ[n]) for n in rng]
        dL = [mm_tn(T[n], dT[n]) for n in rng]
        dL = [jnp.where(strict, -mm_nt(dL[n], T[n]), 0.0) for n in rng]
        dI = [dL[n] * br[n] for n in rng]
        R = [dG[n] * br[n] for n in rng]
        for n, r in enumerate(sl):
            db[r, :] = jnp.sum(
                (dL[n] * i1[n] + dG[n] * qw[n]).T + dBW[n] * W[n].astype(F32), axis=1, keepdims=True
            )
            dq[r, :] = (dQm[n] + mm(E[n], K[n]) + mm(R[n], W[n])).astype(dq.dtype)
            dk[r, :] = (dKm[n] + mm_tn(E[n], Q[n]) + mm_tn(dM[n], W[n])).astype(dk.dtype)
            dw[r, :] = (
                dW[n]
                + bc[n] * dBW[n]
                + mm_tn(R[n], Q[n])
                + mm(dM[n], K[n])
                + mm(dI[n] + dI[n].T, W[n])
            )
        return carry

    lax.fori_loop(0, NB // GROUP, group, 0)


def bwd_steps(poke, qkvp, raw, small, marks, vec, o, do, probs, qc, t_in, a_in, z_in, m_in, kp, d_ext, d_conv, ds_buf, x_buf, dkm_buf, dpm_buf, b_buf, db_buf, dw_buf):
    chip, core = lax.axis_index("x"), lax.axis_index("c")
    lane = lax.broadcasted_iota(jnp.int32, (SEQ, HD), 1)
    d_raw = jnp.zeros((SEQ, HD), F32)
    d_conv[...] = jnp.zeros_like(d_conv)
    for s, head in enumerate((3 * chip + 2 * core, 3 * chip + 1)):
        cols = slice(s * HD, (s + 1) * HD)
        q, k, v, path = (qkvp.at[:, (2 * n + s) * HD : (2 * n + s + 1) * HD] for n in range(4))
        dq, dk, dv, dpath = (d_ext.at[:, (2 * n + s) * HD : (2 * n + s + 1) * HD] for n in range(4))
        beta = betas_of(raw[...], head)
        b_buf[...] = beta
        score_grads(s, v, o.at[:, cols], do.at[:, cols], probs, ds_buf, dv)
        poke()
        sweep_back(s, qc, kp, ds_buf, x_buf, dkm_buf, dpm_buf)
        poke()
        own_blocks_back(
            s, q, k, vec.at[:, cols], b_buf, (t_in, a_in, z_in, m_in), (ds_buf, x_buf, dkm_buf, dpm_buf), dq, dk, dw_buf, db_buf
        )
        poke()
        d_raw = d_raw + jnp.where(
            lane == head + BETA_AT, db_buf[...] * beta * (1.0 - 0.5 * beta), 0.0
        )
        taps = conv_weights(small, head)
        raw_path = path[...].astype(F32)
        conved = convolve(raw_path, taps, marks[...])
        scale = lax.rsqrt(jnp.sum(conved * conved, axis=1, keepdims=True) + 1e-06)
        unit = conved * scale
        dw = dw_buf[...]
        d_conved = scale * (dw - unit * jnp.sum(dw * unit, axis=1, keepdims=True))
        total = taps[0:1, :] * d_conved
        d_conv[s, 0:1, :] = jnp.sum(d_conved * raw_path, axis=0, keepdims=True)
        for m in range(1, TAPS):
            marked = d_conved * marks[:, m : m + 1]
            d_conv[s, m : m + 1, :] = jnp.sum(
                marked * pltpu.roll(raw_path, m, 0), axis=0, keepdims=True
            )
            total = total + taps[m : m + 1, :] * pltpu.roll(marked, SEQ - m, 0)
        dpath[...] = total.astype(dpath.dtype)
    d_ext[:, 8 * HD :] = d_raw.astype(d_ext.dtype)


def fwd_shapes(width):
    sds = jax.ShapeDtypeStruct
    return [
        sds((SEQ, width), BF16),
        sds((SEQ, 8 * HD), BF16),
        sds((SEQ, HD), F32),
        sds((SEQ, 2 * HD), BF16),
        sds((SEQ, 2 * HD), F32),
        sds((2, SEQ, SEQ), BF16),
        sds((2, NQC, HD), BF16),
        sds((2, SEQ, BLK), F32),
        sds((2, SEQ, BLK), BF16),
        sds((2, SEQ, BLK), BF16),
        sds((2, SEQ, BLK), BF16),
        sds((2, SEQ, 2 * HD), BF16),
    ]


def fwd_scratch():
    return [
        pltpu.VMEM((SEQ, SEQ), F32),
        pltpu.VMEM((SEQ, HD), F32),
        pltpu.VMEM((SEQ, HD), F32),
        pltpu.VMEM((SEQ, 1), F32),
    ]


def bwd_shapes():
    sds = jax.ShapeDtypeStruct
    return [sds((SEQ, 9 * HD), BF16), sds((2, 8, HD), F32)]


def bwd_scratch():
    return (
        [pltpu.VMEM((SEQ, SEQ), BF16)]
        + [pltpu.VMEM((SEQ, HD), F32)] * 3
        + [pltpu.VMEM((SEQ, 1), F32)] * 2
        + [pltpu.VMEM((SEQ, HD), F32)]
    )


MESH = pl.DeviceIdType.MESH
ANY = pl.BlockSpec(memory_space=pl.ANY)
VMEM = pl.BlockSpec(memory_space=pltpu.VMEM)


class Place:
    def __init__(self):
        self.x, self.c = lax.axis_index("x"), lax.axis_index("c")
        self.y = lax.axis_index("y")
        self.zl, self.zh = lax.axis_index("zl"), lax.axis_index("zh")
        self.z = self.zh * 2 + self.zl

    def chip(self, d):
        return lax.rem(self.x + d, 4)

    def at_x(self, d):
        return {"x": lax.rem(self.x + d, 4)}

    def at_xc(self, d, k):
        return {"x": lax.rem(self.x + d, 4), "c": lax.rem(self.c + k, 2)}

    def sibling(self):
        return {"c": 1 - self.c}

    def at_y(self, d):
        return {"y": lax.rem(self.y + d, 4)}

    def at_z(self, d):
        z = lax.rem(self.z + d, 4)
        return {"zl": lax.rem(z, 2), "zh": z // 2}


class Net:
    def __init__(self, send_sem, recv_sem, local_sem):
        self.place = Place()
        self.send_sem, self.recv_sem, self.local_sem = send_sem, recv_sem, local_sem
        self.count, self.kept, self.locals, self.sent = 0, 0, [], []

    def prepare(self, src, dst, device):
        k = self.count
        self.count += 1
        return pltpu.make_async_remote_copy(
            src_ref=src,
            dst_ref=dst,
            send_sem=self.send_sem.at[k],
            recv_sem=self.recv_sem.at[k],
            device_id=device,
            device_id_type=MESH,
        )

    def send(self, src, dst, device):
        copy = self.prepare(src, dst, device)
        copy.start()
        self.sent.append(copy)
        return copy

    def local(self, src, dst):
        self.kept += 1
        return pltpu.make_async_copy(src, dst, self.local_sem.at[self.kept - 1])

    def keep(self, src, dst):
        copy = self.local(src, dst)
        copy.start()
        self.locals.append(copy)

    def settle(self):
        for copy in self.locals:
            copy.wait()
        self.locals = []

    def finish(self):
        for copy in self.sent:
            copy.wait_send()
        self.settle()


def meet(devices):
    barrier = pltpu.get_barrier_semaphore()
    for device in devices:
        pl.semaphore_signal(barrier, inc=1, device_id=device, device_id_type=MESH)
    pl.semaphore_wait(barrier, len(devices))


class Jobs:
    def __init__(self, *jobs):
        self.jobs = list(jobs)

    def poke(self):
        for job in list(self.jobs):
            try:
                next(job)
            except StopIteration:
                self.jobs.remove(job)

    def drain(self):
        while self.jobs:
            self.poke()


def interleave(*jobs):
    Jobs(*jobs).drain()


def team_peers(p):
    return [p.at_x(1), p.at_x(3), p.sibling()]


def team_all(p):
    return [p.at_xc(d, k) for d in range(4) for k in range(2) if d + k]


def group_peers(p):
    return [p.at_y(d) for d in (1, 2, 3)] + [p.at_z(d) for d in (1, 2, 3)]


def gather_team(net, own, out):
    p = net.place
    me, sib = 2 * p.x + p.c, p.sibling()
    right, left = p.at_x(1), p.at_x(3)
    t_l, t_r, t_2 = (2 * p.chip(d) + p.c for d in (3, 1, 2))
    to_r = net.send(own, out.at[:, me], right)
    to_l = net.send(own, out.at[:, me], left)
    shared = [net.send(own, out.at[:, me], sib)]
    net.keep(own, out.at[:, me])
    yield
    to_r.wait_recv()
    on_r = net.send(out.at[0, t_l], out.at[0, t_l], right)
    shared.append(net.send(out.at[:, t_l], out.at[:, t_l], sib))
    to_l.wait_recv()
    on_l = net.send(out.at[1, t_r], out.at[1, t_r], left)
    shared.append(net.send(out.at[:, t_r], out.at[:, t_r], sib))
    yield
    on_r.wait_recv()
    shared.append(net.send(out.at[0, t_2], out.at[0, t_2], sib))
    on_l.wait_recv()
    shared.append(net.send(out.at[1, t_2], out.at[1, t_2], sib))
    yield
    for copy in shared:
        copy.wait_recv()


GATHER_TEAM = 10


def add(a, b):
    return (a.astype(F32) + b.astype(F32)).astype(BF16)


def scatter_team(net, part, got, total, from_l, from_r, all_l, all_r, finish):
    p = net.place
    sib, right, left = p.sibling(), p.at_x(1), p.at_x(3)
    order = (2, 1, 3, 0)
    swaps = [
        net.send(part.at[:, 2 * p.chip(d) + 1 - p.c], got.at[:, p.chip(d)], sib) for d in order
    ]

    def pair(n):
        swaps[n].wait_recv()
        at = p.chip(order[n])
        total[:, at] = add(part[:, 2 * at + p.c], got[:, at])
        return at

    yield
    x_2 = pair(0)
    half_r = net.send(total.at[0, x_2], from_l, right)
    half_l = net.send(total.at[1, x_2], from_r, left)
    x_r = pair(1)
    rest_r = net.send(total.at[1, x_r], all_l.at[1], right)
    x_l = pair(2)
    rest_l = net.send(total.at[0, x_l], all_r.at[0], left)
    pair(3)
    yield
    half_r.wait_recv()
    total[0, x_r] = add(total[0, x_r], from_l[...])
    last_r = net.send(total.at[0, x_r], all_l.at[0], right)
    half_l.wait_recv()
    total[1, x_l] = add(total[1, x_l], from_r[...])
    last_l = net.send(total.at[1, x_l], all_r.at[1], left)
    yield
    for copy in (rest_r, rest_l, last_r, last_l):
        copy.wait_recv()
    finish(total[:, p.x].astype(F32) + all_l[...].astype(F32) + all_r[...].astype(F32))


SCATTER_TEAM = 10


def scatter_team_scratch(n, w):
    return [
        pltpu.VMEM((2, 4, n, w), BF16),
        pltpu.VMEM((2, 4, n, w), BF16),
        pltpu.VMEM((n, w), BF16),
        pltpu.VMEM((n, w), BF16),
        pltpu.VMEM((2, n, w), BF16),
        pltpu.VMEM((2, n, w), BF16),
    ]


def chunk_rows(y, z, rows):
    zl, zh = (z % 2, z // 2) if isinstance(z, int) else (lax.rem(z, 2), z // 2)
    return pl.ds(pl.multiple_of(((zl * 4 + y) * 2 + zh) * rows, rows), rows)


def gather_groups(net, own, out, cuts):
    p = net.place
    rows = own.shape[0]
    lo, mid, hi = cuts
    first, second = pl.ds(lo, mid - lo), pl.ds(mid, hi - mid)
    net.keep(own, out.at[chunk_rows(p.y, p.z, rows)])

    def spread(cols, y, z, devices, src=None):
        place = out.at[chunk_rows(y, z, rows), cols]
        return [net.send(place if src is None else src.at[:, cols], place, d) for d in devices]

    ys, zs = [p.at_y(d) for d in (1, 3, 2)], [p.at_z(d) for d in (1, 3, 2)]
    y_first = spread(first, p.y, p.z, ys, own)
    z_first = spread(second, p.y, p.z, zs, own)
    last = spread(first, p.y, p.z, zs, own) + spread(second, p.y, p.z, ys, own)
    yield
    for n, d in enumerate((1, 3, 2)):
        y_first[n].wait_recv()
        last += spread(first, lax.rem(p.y + 4 - d, 4), p.z, zs)
        z_first[n].wait_recv()
        last += spread(second, p.y, lax.rem(p.z + 4 - d, 4), ys)
        yield
    for copy in last:
        copy.wait_recv()


GATHER_GROUPS = 30


def scatter_groups(net, part, out, cuts, z_got, z_sum, z_last, y_got, y_sum, y_last):
    p = net.place
    lo, mid, hi = cuts
    first, second = pl.ds(lo, mid - lo), pl.ds(mid, hi - mid)
    rows = z_sum.shape[1]
    both = hi > mid
    flat = len(part.shape) == 2
    order = (2, 1, 3)
    a = []
    b = []
    for n, d in enumerate(order):
        z, y = lax.rem(p.z + d, 4), lax.rem(p.y + d, 4)
        if flat:
            for k in range(4):
                a.append(net.send(part.at[chunk_rows(k, z, rows), first], z_got.at[n, k], p.at_z(d)))
                b.append(net.send(part.at[chunk_rows(y, k, rows), second], y_got.at[n, k % 2, k // 2], p.at_y(d)))
        else:
            a.append(net.send(part.at[lax.rem(z, 2), :, z // 2, :, first], z_got.at[n], p.at_z(d)))
            if both:
                b.append(net.send(part.at[:, y, :, :, second], y_got.at[n], p.at_y(d)))

    def own(y, zl, zh, cols):
        if flat:
            return part[chunk_rows(y, zh * 2 + zl, rows), cols].astype(F32)
        return part[zl, y, zh, :, cols].astype(F32)

    yield
    for copy in a:
        copy.wait_recv()
    for y in range(4):
        t = own(y, p.zl, p.zh, first)
        for n in range(3):
            t = t + z_got[n, y].astype(F32)
        z_sum[y] = t.astype(BF16)
    a = [
        net.send(z_sum.at[lax.rem(p.y + d, 4)], z_last.at[n], p.at_y(d)) for n, d in enumerate(order)
    ]
    if both:
        yield
        for copy in b:
            copy.wait_recv()
        for zl in range(2):
            for zh in range(2):
                t = own(p.y, zl, zh, second)
                for n in range(3):
                    t = t + y_got[n, zl, zh].astype(F32)
                y_sum[zl, zh] = t.astype(BF16)
        b = []
        for n, d in enumerate(order):
            z = lax.rem(p.z + d, 4)
            b.append(net.send(y_sum.at[lax.rem(z, 2), z // 2], y_last.at[n], p.at_z(d)))
    yield
    for copy in a:
        copy.wait_recv()
    t = z_sum[p.y].astype(F32)
    for n in range(3):
        t = t + z_last[n].astype(F32)
    out[:, first] = t.astype(out.dtype)
    if both:
        yield
        for copy in b:
            copy.wait_recv()
        t = y_sum[p.zl, p.zh].astype(F32)
        for n in range(3):
            t = t + y_last[n].astype(F32)
        out[:, second] = t.astype(out.dtype)


SCATTER_GROUPS = 12
SCATTER_GROUPS_FLAT = 30


def scatter_groups_scratch(r, cuts):
    a, b = cuts[1] - cuts[0], max(cuts[2] - cuts[1], HD)
    return [
        pltpu.VMEM((3, 4, r, a), BF16),
        pltpu.VMEM((4, r, a), BF16),
        pltpu.VMEM((3, r, a), BF16),
        pltpu.VMEM((3, 2, 2, r, b), BF16),
        pltpu.VMEM((2, 2, r, b), BF16),
        pltpu.VMEM((3, r, b), BF16),
    ]


def sems(remote, local):
    return [
        pltpu.SemaphoreType.DMA((remote,)),
        pltpu.SemaphoreType.DMA((remote,)),
        pltpu.SemaphoreType.DMA((max(local, 1),)),
    ]


def params(collective_id):
    return pltpu.CompilerParams(
        collective_id=collective_id, has_side_effects=True, vmem_limit_bytes=VM
    )


EPS_NORM = 1e-05
EPS_UNIT = 1e-06
SHAPE = jax.ShapeDtypeStruct


def all_to_team(net, packs, got):
    p = net.place
    me = 2 * p.x + p.c
    net.keep(packs.at[me], got.at[me])
    copies = []
    for d in (2, 1, 3, 0):
        for k in (1, 0):
            if d + k:
                to = 2 * p.chip(d) + lax.rem(p.c + k, 2)
                copies.append(net.send(packs.at[to], got.at[me], p.at_xc(d, k)))
    yield
    for copy in copies:
        copy.wait_recv()


def start_kernel(packs, tokens, grad_out, got, x_rows, g_rows, *sem):
    net = Net(*sem)
    p = net.place
    other = {"zh": 1 - p.zh}
    meet(team_all(p) + [other])
    swaps = []
    for src, dst in ((tokens, x_rows), (grad_out, g_rows)):
        net.keep(src.at[p.zh], dst.at[p.zh])
        swaps.append(net.send(src.at[1 - p.zh], dst.at[p.zh], other))
    interleave(all_to_team(net, packs, got))
    for copy in swaps:
        copy.wait_recv()
    net.finish()


def start(packs, tokens, grad_out):
    rows = SHAPE(tokens.shape, BF16)
    return pl.pallas_call(
        start_kernel,
        out_shape=[SHAPE(packs.shape, BF16), rows, rows],
        in_specs=[ANY] * 3,
        out_specs=[ANY] * 3,
        scratch_shapes=sems(9, 3),
        compiler_params=params(1),
        name="start",
    )(packs, tokens, grad_out)


def lanes(at):
    return pl.ds(pl.multiple_of(at * HD, HD), HD)


OUT_AT = 9


def trade_out(net, whole, w_out):
    p = net.place
    copies = []
    for d in (2, 1, 3, 0):
        for k in (1, 0):
            xd, cd = p.chip(d), lax.rem(p.c + k, 2)
            row_a, row_b = lanes(3 * xd + 2 * cd), lanes(3 * xd + 1)
            row_c = lanes(3 * xd + jnp.where(p.c == 0, 2 * cd, 1))
            col_a, col_b = lanes(3 * p.x + 2 * p.c), lanes(3 * p.x + 1)
            moves = (
                (whole.at[row_a, pl.ds(OUT_AT * HD, HD)], w_out.at[pl.ds(0, HD), col_a]),
                (whole.at[row_b, pl.ds(OUT_AT * HD, HD)], w_out.at[pl.ds(HD, HD), col_a]),
                (whole.at[row_c, pl.ds((OUT_AT + 1) * HD, HD)], w_out.at[lanes(p.c), col_b]),
            )
            for src, dst in moves:
                if d + k:
                    copies.append(net.send(src, dst, p.at_xc(d, k)))
                else:
                    net.keep(src, dst)
    yield
    for copy in copies:
        copy.wait_recv()


def gather_kernel(cuts, x_rows, own, x_all, whole, *sem):
    net = Net(*sem)
    p = net.place
    meet(team_peers(p) + group_peers(p))
    interleave(gather_team(net, x_rows, x_all), gather_groups(net, own, whole, cuts))
    net.finish()


def gather_all(x_rows, own):
    rows, cols = own.shape
    two, n, width = x_rows.shape
    return pl.pallas_call(
        functools.partial(gather_kernel, (0, 768, cols)),
        out_shape=[SHAPE((two, 8, n, width), BF16), SHAPE((16 * rows, cols), BF16)],
        in_specs=[ANY] * 2,
        out_specs=[ANY] * 2,
        scratch_shapes=sems(GATHER_TEAM + GATHER_GROUPS, 2),
        compiler_params=params(2),
        name="gather_all",
    )(x_rows, own)


def attn_fwd_kernel(cuts, x_all, whole, marks, drow, own_ffn, g_rows, *rest):
    kept, rest = rest[:12], rest[12:]
    w_ffn, g_all, w_out, rest = rest[0], rest[1], rest[2], rest[3:]
    net = Net(*rest[-3:])
    p = net.place
    meet(team_all(p) + group_peers(p))
    jobs = Jobs(
        gather_groups(net, own_ffn, w_ffn, cuts),
        trade_out(net, whole, w_out),
        gather_team(net, g_rows, g_all),
    )
    jobs.poke()
    fwd_steps(jobs.poke, x_all, whole, marks, drow, *kept, *rest[:-3])
    jobs.drain()
    net.finish()


def attn_fwd(x_all, whole, marks, drow, own_ffn, g_rows):
    rows, cols = own_ffn.shape
    two, n, width = g_rows.shape
    kept = fwd_shapes(width)
    return pl.pallas_call(
        functools.partial(attn_fwd_kernel, (0, cols // 2, cols)),
        out_shape=kept
        + [SHAPE((16 * rows, cols), BF16), SHAPE((two, 8, n, width), BF16), SHAPE((2 * HD, width), BF16)],
        in_specs=[VMEM] * 4 + [ANY] * 2,
        out_specs=[VMEM] * len(kept) + [ANY] * 3,
        scratch_shapes=fwd_scratch() + sems(GATHER_TEAM + GATHER_GROUPS + 21, 5),
        compiler_params=params(7),
        name="attn_fwd",
    )(x_all, whole, marks, drow, own_ffn, g_rows)


def ffn_in_kernel(cuts, part, x_rows, gain, own_down, hidden, ffn_all, w_down, normed, *rest):
    net = Net(*rest[-3:])
    p = net.place
    meet(team_peers(p) + group_peers(p))

    def finish(branch):
        h = x_rows[...].astype(F32) + branch
        hidden[...] = h
        scale = lax.rsqrt(jnp.mean(h * h, axis=-1, keepdims=True) + EPS_NORM)
        normed[...] = (h * scale * gain[...][None]).astype(BF16)

    def team():
        yield from scatter_team(net, part, *rest[:-3], finish)
        yield from gather_team(net, normed, ffn_all)

    interleave(team(), gather_groups(net, own_down, w_down, cuts))
    net.finish()


def ffn_in(part, x_rows, gain, own_down):
    two, n, width = x_rows.shape
    return pl.pallas_call(
        functools.partial(ffn_in_kernel, (0, width // 2, width)),
        out_shape=[
            SHAPE((two, n, width), F32),
            SHAPE((two, 8, n, width), BF16),
            SHAPE((16 * own_down.shape[0], width), BF16),
        ],
        in_specs=[VMEM, VMEM, VMEM, ANY],
        out_specs=[VMEM, ANY, ANY],
        scratch_shapes=[pltpu.VMEM((two, n, width), BF16)]
        + scatter_team_scratch(n, width)
        + sems(SCATTER_TEAM + GATHER_TEAM + GATHER_GROUPS, 2),
        compiler_params=params(3),
        name="ffn_in",
    )(part, x_rows, gain, own_down)


def norm_back(v, gain, d_normed):
    scale = lax.rsqrt(jnp.mean(v * v, axis=-1, keepdims=True) + EPS_NORM)
    unit = v * scale
    d_unit = d_normed * gain
    d_v = scale * (d_unit - unit * jnp.mean(d_unit * unit, axis=-1, keepdims=True))
    return d_v, d_normed * unit


def ffn_back_kernel(cuts, part, hidden, gain, g_rows, d_down, d_hidden, d_gain, branch_all, down_sum, branch, *rest):
    team_scratch, down_scratch = rest[:6], rest[6:12]
    net = Net(*rest[-3:])
    p = net.place
    meet(team_peers(p) + group_peers(p))

    def finish(d_normed):
        d_h, d_g = norm_back(hidden[...], gain[...][None], d_normed)
        d_h = d_h + g_rows[...].astype(F32)
        d_hidden[...] = d_h
        branch[...] = d_h.astype(BF16)
        d_gain[...] = jnp.sum(jnp.sum(d_g, axis=0), axis=0, keepdims=True)

    def team():
        yield from scatter_team(net, part, *team_scratch, finish)
        yield from gather_team(net, branch, branch_all)

    interleave(team(), scatter_groups(net, d_down, down_sum, cuts, *down_scratch))
    net.finish()


def by_group(a):
    return a.reshape(2, 4, 2, a.shape[0] // 16, a.shape[1])


def ffn_back(part, hidden, gain, g_rows, d_down):
    two, n, width = hidden.shape
    d_down = by_group(d_down)
    rows = d_down.shape[3]
    cuts = (0, width // 2, width)
    return pl.pallas_call(
        functools.partial(ffn_back_kernel, cuts),
        out_shape=[
            SHAPE((two, n, width), F32),
            SHAPE((1, width), F32),
            SHAPE((two, 8, n, width), BF16),
            SHAPE((rows, width), F32),
        ],
        in_specs=[VMEM] * 5,
        out_specs=[VMEM, VMEM, ANY, VMEM],
        scratch_shapes=[pltpu.VMEM((two, n, width), BF16)]
        + scatter_team_scratch(n, width)
        + scatter_groups_scratch(rows, cuts)
        + sems(SCATTER_TEAM + GATHER_TEAM + SCATTER_GROUPS, 1),
        compiler_params=params(4),
        name="ffn_back",
    )(part, hidden, gain, g_rows, d_down)


def trade_out_back(net, d_out, whole):
    p = net.place
    rows, middle, own = [], [], []
    cases = [(d, k) for d in (2, 1, 3, 0) for k in (1, 0)]
    for d, k in cases:
        xd, cd = p.chip(d), lax.rem(p.c + k, 2)
        for side, col in enumerate((lanes(3 * xd + 2 * cd), lanes(3 * xd + 1))):
            src = d_out.at[pl.ds(0, HD), col]
            dst = whole.at[lanes(3 * p.x + 2 * p.c), pl.ds(side * HD, HD)]
            if d + k:
                rows.append(net.send(src, dst, p.at_xc(d, k)))
            else:
                own.append(net.local(src, dst))
                own[-1].start()
    for d, k in cases:
        xd, cd = p.chip(d), lax.rem(p.c + k, 2)
        for side, col in enumerate((lanes(3 * xd + 2 * cd), lanes(3 * xd + 1))):
            src = d_out.at[pl.ds(HD, HD), col]
            dst = whole.at[lanes(3 * p.x + 1), pl.ds(side * HD, HD)]
            if d + k:
                middle.append((k, net.prepare(src, dst, p.at_xc(d, k))))
            else:
                middle.append((-1, net.local(src, dst)))

    @pl.when(p.c == 0)
    def _():
        for _, copy in middle:
            copy.start()

    yield
    for copy in rows:
        copy.wait_recv()
    for copy in own:
        copy.wait()
    for core in range(2):

        @pl.when(p.c == core)
        def _(core=core):
            for k, copy in middle:
                if k == core:
                    copy.wait_recv()

    @pl.when(p.c == 0)
    def _():
        for k, copy in middle:
            if k < 0:
                copy.wait()
            else:
                copy.wait_send()

    yield


TRADE_BACK = 28


def attn_bwd_kernel(cuts, *refs):
    given, refs = refs[:14], refs[14:]
    d_ffn, part_o, hidden, d_out, refs = *refs[:4], refs[4:]
    results, refs = refs[:2], refs[2:]
    out_rows, ffn_sum, out_sum, whole, refs = *refs[:4], refs[4:]
    bufs, o_scratch, f_scratch, w_scratch = refs[:7], refs[7:13], refs[13:19], refs[19:25]
    net = Net(*refs[-3:])
    p = net.place
    meet(team_all(p) + group_peers(p))

    def finish(branch):
        out_rows[...] = (hidden[...] + branch).astype(BF16)

    def out_grad():
        yield from trade_out_back(net, d_out, whole)
        yield from scatter_groups(net, whole, out_sum, cuts[1], *w_scratch)

    jobs = Jobs(
        scatter_groups(net, d_ffn, ffn_sum, cuts[0], *f_scratch),
        scatter_team(net, part_o, *o_scratch, finish),
        out_grad(),
    )
    jobs.poke()
    bwd_steps(jobs.poke, *given, *results, *bufs)
    jobs.drain()
    net.finish()


def attn_bwd(given, d_ffn, part_o, hidden, d_out):
    two, n, width = hidden.shape
    d_ffn = by_group(d_ffn)
    r, w = d_ffn.shape[3:]
    cuts = [(0, w // 2, w), (0, HD, 2 * HD)]
    results = bwd_shapes()
    return pl.pallas_call(
        functools.partial(attn_bwd_kernel, cuts),
        out_shape=results
        + [SHAPE((two, n, width), BF16), SHAPE((r, w), BF16), SHAPE((r, 2 * HD), BF16)],
        in_specs=[VMEM] * (len(given) + 4),
        out_specs=[VMEM] * (len(results) + 3),
        scratch_shapes=[pltpu.VMEM((width, 2 * HD), BF16)]
        + bwd_scratch()
        + scatter_team_scratch(n, width)
        + scatter_groups_scratch(r, cuts[0])
        + scatter_groups_scratch(r, cuts[1])
        + sems(SCATTER_TEAM + SCATTER_GROUPS + SCATTER_GROUPS_FLAT + TRADE_BACK, 4),
        compiler_params=params(8),
        name="attn_bwd",
    )(*given, d_ffn, part_o, hidden, d_out)


def last_kernel(cuts, part_n, x_rows, d_hidden, gain, d_heads, d_small, d_rows, heads_sum, small_sum, *rest):
    n_scratch, h_scratch, s_scratch = rest[:6], rest[6:12], rest[12:18]
    net = Net(*rest[-3:])
    p = net.place
    meet(team_peers(p) + group_peers(p))

    def finish(d_normed):
        d_x, _ = norm_back(x_rows[...].astype(F32), gain[...][None], d_normed)
        d_rows[...] = (d_x + d_hidden[...]).astype(BF16)

    interleave(
        scatter_groups(net, d_heads, heads_sum, cuts[0], *h_scratch),
        scatter_groups(net, d_small, small_sum, cuts[1], *s_scratch),
        scatter_team(net, part_n, *n_scratch, finish),
    )
    net.finish()


def last_sums(part_n, x_rows, d_hidden, gain, d_heads, d_small):
    two, n, width = d_hidden.shape
    d_heads, d_small = by_group(d_heads), by_group(d_small)
    r, w = d_heads.shape[3:]
    cuts = [(0, w // 2, w), (0, HD, HD)]
    return pl.pallas_call(
        functools.partial(last_kernel, cuts),
        out_shape=[SHAPE((two, n, width), BF16), SHAPE((r, w), BF16), SHAPE((r, HD), BF16)],
        in_specs=[VMEM] * 6,
        out_specs=[VMEM] * 3,
        scratch_shapes=scatter_team_scratch(n, width)
        + scatter_groups_scratch(r, cuts[0])
        + scatter_groups_scratch(r, cuts[1])
        + sems(SCATTER_TEAM + 2 * SCATTER_GROUPS, 0),
        compiler_params=params(5),
        name="last_sums",
    )(part_n, x_rows, d_hidden, gain, d_heads, d_small)


def end_kernel(packs, out_rows, d_rows, got, output, d_tokens, *sem):
    net = Net(*sem)
    p = net.place
    other = {"zh": 1 - p.zh}
    meet(team_all(p) + [other])
    swaps = []
    for src, dst in ((out_rows, output), (d_rows, d_tokens)):
        net.keep(src.at[p.zh], dst.at[p.zh])
        swaps.append(net.send(src.at[1 - p.zh], dst.at[p.zh], other))
    interleave(all_to_team(net, packs, got))
    for copy in swaps:
        copy.wait_recv()
    net.finish()


def end(packs, out_rows, d_rows):
    rows = SHAPE(out_rows.shape, BF16)
    return pl.pallas_call(
        end_kernel,
        out_shape=[SHAPE(packs.shape, BF16), rows, rows],
        in_specs=[ANY] * 3,
        out_specs=[ANY] * 3,
        scratch_shapes=sems(9, 3),
        compiler_params=params(6),
        name="end",
    )(packs, out_rows, d_rows)


def dot_nn(a, b):
    return lax.dot_general(a, b, (((1,), (0,)), ((), ())), preferred_element_type=F32)


def dot_nt(a, b):
    return lax.dot_general(a, b, (((1,), (1,)), ((), ())), preferred_element_type=F32)


def dot_tn(a, b):
    return lax.dot_general(a, b, (((0,), (0,)), ((), ())), preferred_element_type=F32)


def split_rows(partial):
    return partial.astype(BF16).reshape(2, 8, -1, partial.shape[1])


def pad_rows(a, rows):
    return jnp.pad(a, ((0, 0), (0, rows - a.shape[1]), (0, 0)))


HEADS_W, OUT_W, SMALL_W = 8 * HD, 2 * HD, HD


def per_device(
    tokens,
    doc_start,
    gain_attn,
    w_query,
    w_key,
    w_value,
    w_path,
    conv_path,
    w_beta,
    w_out,
    gain_ffn,
    w_gate,
    w_up,
    w_down,
    grad_out,
):
    zh, chip, core = lax.axis_index("zh"), lax.axis_index("x"), lax.axis_index("c")
    width = tokens.shape[2]
    share = w_query.shape[0]
    head_a, head_b = 3 * chip + 2 * core, 3 * chip + 1
    owns_b = core == 0

    small = jnp.concatenate([gain_attn[:, None], gain_ffn[:, None], conv_path.T, w_beta], axis=1)
    small = jnp.pad(small, ((0, 0), (0, SMALL_W - small.shape[1])))
    small = jnp.broadcast_to(small[None], (8, share, SMALL_W))
    kinds = jnp.stack([w_query, w_key, w_value, w_path, w_out], axis=1).reshape(share, 5, 4, 3, HD)
    slot_a = jnp.concatenate([kinds[:, :, :, 0:1], kinds[:, :, :, 2:3]], axis=3)
    slot_b = jnp.broadcast_to(kinds[:, :, :, 1:2], slot_a.shape)
    heads_pack = jnp.stack([slot_a, slot_b], axis=4).transpose(2, 3, 0, 1, 4, 5)
    heads_pack = heads_pack.reshape(8, share, -1)
    ffn_pack = jnp.stack([w_gate, w_up], axis=1).reshape(share, 2, 16, 8, 32)
    ffn_pack = ffn_pack.transpose(3, 0, 1, 2, 4).reshape(8, share, -1)
    packs = pad_rows(
        jnp.concatenate([heads_pack[:, :, :HEADS_W], small, heads_pack[:, :, HEADS_W:], ffn_pack], axis=2), 16
    )
    packs, x_rows, g_rows = start(packs, tokens, grad_out)
    packs = packs[:, :share].reshape(8 * share, -1)
    first_w = HEADS_W + OUT_W + SMALL_W
    x_all, whole = gather_all(x_rows, packs[:, :first_w])
    w_ext = whole[:, : HEADS_W + SMALL_W]
    gain_a, gain_f = (whole[:, HEADS_W + n].astype(F32) for n in range(2))
    doc_rows = jnp.cumsum(doc_start, axis=1)
    docs = jnp.where(zh == 0, doc_rows[0], doc_rows[1]).astype(F32)
    marks = [docs]
    for tap in range(1, TAPS):
        same = docs[: SEQ - tap] == docs[tap:]
        marks.append(jnp.concatenate([jnp.zeros((tap,), F32), same.astype(F32)]))
    drow = jnp.stack(marks + marks)
    marks = drow.T

    def own_heads(v):
        return jnp.where((jnp.arange(2 * HD) < HD) | owns_b, v, 0.0)

    normed_all, qkvp, raw, vec, o, *saved, w_ffn, g_all, w_out_t = attn_fwd(
        x_all.reshape(SEQ, width), whole, marks, drow, packs[:, first_w:], g_rows
    )
    g_all = g_all.reshape(SEQ, width)
    mixed = own_heads(o).astype(BF16)
    hidden, ffn_all, w_down_t = ffn_in(
        split_rows(dot_nn(mixed, w_out_t)), x_rows, gain_f[None], w_down
    )
    ffn_all = ffn_all.reshape(SEQ, width)
    gate_up = dot_nn(ffn_all, w_ffn)
    half = gate_up.shape[1] // 2

    def gated(pre):
        return jax.nn.silu(pre[:, :half]) * pre[:, half:]

    act_f, act_pull = jax.vjp(gated, gate_up)
    act = act_f.astype(BF16)
    out_part = split_rows(dot_nn(act, w_down_t))

    (d_gate_up,) = act_pull(dot_nt(g_all, w_down_t))
    d_gate_up = d_gate_up.astype(BF16)
    d_hidden, d_gain_ffn, branch_all, d_down = ffn_back(
        split_rows(dot_nt(d_gate_up, w_ffn)),
        hidden,
        gain_f[None],
        g_rows,
        dot_tn(act, g_all).astype(BF16),
    )
    d_ffn = dot_tn(ffn_all, d_gate_up).astype(BF16)
    branch_all = branch_all.reshape(SEQ, width)
    d_mixed = own_heads(dot_nt(branch_all, w_out_t))
    d_out = dot_tn(mixed, branch_all).astype(BF16)
    d_ext, d_conv, out_rows, ffn_sum, out_sum = attn_bwd(
        (qkvp, raw, w_ext[:, HEADS_W:], marks, vec, o, d_mixed, *saved), d_ffn, out_part, hidden, d_out
    )
    norm_part = dot_nt(d_ext, w_ext).astype(BF16)
    d_gain_attn = jnp.sum(norm_part.astype(F32) * normed_all.astype(F32), axis=0) / gain_a

    d_heads = dot_tn(normed_all, d_ext[:, :HEADS_W]).astype(BF16)
    conv_rows = jnp.zeros((width, TAPS), F32)
    conv_rows = lax.dynamic_update_slice_in_dim(conv_rows, d_conv[1, :TAPS].T, head_b * HD, 0)
    conv_rows = lax.dynamic_update_slice_in_dim(conv_rows, d_conv[0, :TAPS].T, head_a * HD, 0)
    small_back = jnp.concatenate([d_gain_attn[:, None], d_gain_ffn.T, conv_rows], axis=1)
    small_back = jnp.pad(small_back, ((0, 0), (0, SMALL_W - small_back.shape[1])))
    d_small = (dot_tn(normed_all, d_ext[:, HEADS_W:]) + small_back).astype(BF16)
    d_rows, heads_sum, small_sum = last_sums(
        split_rows(norm_part), x_rows, d_hidden, gain_a[None], d_heads, d_small
    )
    packs = jnp.concatenate([heads_sum, small_sum, out_sum, ffn_sum], axis=1).reshape(8, share, -1)
    packs, output, d_tokens = end(pad_rows(packs, 16), out_rows, d_rows)
    packs = packs[:, :share]
    at = HEADS_W + SMALL_W
    small = jnp.sum(packs[:, :, HEADS_W:at].astype(F32), axis=0)
    heads_back = jnp.concatenate([packs[:, :, :HEADS_W], packs[:, :, at : at + OUT_W]], axis=2)
    heads_back = heads_back.reshape(4, 2, share, 5, 2, HD)
    by_head = jnp.stack(
        [heads_back[:, 0, :, :, 0], heads_back[:, 0, :, :, 1], heads_back[:, 1, :, :, 0]], axis=1
    )
    by_kind = by_head.transpose(3, 2, 0, 1, 4).reshape(5, share, width).astype(F32)
    ffn_back_w = packs[:, :, at + OUT_W :].reshape(8, share, 2, 16, 32)
    ffn_back_w = ffn_back_w.transpose(2, 1, 3, 0, 4).reshape(2, share, -1).astype(F32)
    return (
        output,
        d_tokens,
        small[:, 0],
        by_kind[0],
        by_kind[1],
        by_kind[2],
        by_kind[3],
        small[:, 2:6].T,
        small[:, 6:18],
        by_kind[4],
        small[:, 1],
        ffn_back_w[0],
        ffn_back_w[1],
        d_down,
    )


def solution(mesh):
    names = ("zl", "y", "zh", "x", "c")
    fine = Mesh(mesh.devices.reshape(2, 4, 2, 4, 2), names)
    dp, ctx = names[:2], names[2:]
    rows, flat, mat, taps = P(dp, ctx, None), P(names), P(names, None), P(None, names)
    return jax.shard_map(
        per_device,
        mesh=fine,
        in_specs=(
            rows, P(dp, None), flat, mat, mat, mat, mat, taps, mat, mat, flat, mat, mat, mat, rows,
        ),
        out_specs=(
            rows, rows, flat, mat, mat, mat, mat, taps, mat, mat, flat, mat, mat, mat,
        ),
        check_vma=False,
    )
```

```python
import functools

import jax
import jax.numpy as jnp
from jax import lax
from jax.experimental import pallas as pl
from jax.experimental.pallas import tpu as pltpu
from jax.sharding import Mesh, PartitionSpec as P

F32, BF16 = jnp.float32, jnp.bfloat16
VM = 60 * 1024 * 1024

SEQ, HD, BLK = 1024, 128, 128
NB = SEQ // BLK
NQC = (NB * (NB - 1) // 2) * BLK
SCALE = HD ** (-0.5)
GROUP = 4


def mm(a, b, dims=((1,), (0,))):
    return lax.dot_general(
        a.astype(BF16), b.astype(BF16), (dims, ((), ())), preferred_element_type=F32
    )


def mm_nt(a, b):
    return mm(a, b, ((1,), (1,)))


def mm_tn(a, b):
    return mm(a, b, ((0,), (0,)))


def split(a):
    high = a.astype(BF16)
    return high, (a - high.astype(F32)).astype(BF16)


def mm3(a, b):
    ah, al = split(a)
    bh, bl = split(b)
    return mm(ah, bh) + (mm(ah, bl) + mm(al, bh))


def iota2(axis):
    return lax.broadcasted_iota(jnp.int32, (BLK, BLK), axis)


BASE = 16


def unit_inverses(lowers):
    row, col = iota2(0), iota2(1)
    eye = (row == col).astype(F32)
    in_base = (row // BASE) == (col // BASE)
    narrow = [jnp.where(in_base, low, 0.0) for low in lowers]
    inv = [eye for _ in lowers]
    for u in range(BASE - 1):
        pick = (col % BASE) == u
        coef = [jnp.sum(jnp.where(pick, low, 0.0), axis=1, keepdims=True) for low in narrow]
        for n, (t, c) in enumerate(zip(inv, coef)):
            t3 = t.reshape(BLK // BASE, BASE, BLK)
            lead = jnp.broadcast_to(t3[:, u : u + 1, :], t3.shape).reshape(BLK, BLK)
            inv[n] = t - c * lead
    size = BASE
    while size < BLK:
        off = ((row // (2 * size)) == (col // (2 * size))) & ((row // size) != (col // size))
        mid = [mm3(t, jnp.where(off, low, 0.0)) for t, low in zip(inv, lowers)]
        inv = [t - mm3(m, t) for t, m in zip(inv, mid)]
        size *= 2
    return inv


def betas_of(raw, head):
    lane = lax.broadcasted_iota(jnp.int32, raw.shape, 1)
    return 2.0 * jax.nn.sigmoid(
        jnp.sum(jnp.where(lane == head + BETA_AT, raw, 0.0), axis=1, keepdims=True)
    )


BETA_AT = 6
CONV_AT = 2
TAPS = 4


def conv_weights(small, head):
    part = small[pl.ds(pl.multiple_of(head * HD, HD), HD), :].astype(F32)
    return part.T[CONV_AT : CONV_AT + TAPS, :]


def convolve(path, taps, marks):
    total = taps[0:1, :] * path
    for m in range(1, TAPS):
        total = total + taps[m : m + 1, :] * (pltpu.roll(path, m, 0) * marks[:, m : m + 1])
    return total


def own_blocks(s, q, k, w, bcol, stores):
    t_out, a_out, z_out, m_out, kp_out, qm_buf, s_buf = stores
    row, col = iota2(0), iota2(1)
    strict, closed = row > col, row >= col
    eye = (row == col).astype(F32)

    def group(g, carry):
        sl = [pl.ds(pl.multiple_of((g * GROUP + n) * BLK, BLK), BLK) for n in range(GROUP)]
        qs = [q[r, :] for r in sl]
        ks = [k[r, :] for r in sl]
        ws = [w[r, :] for r in sl]
        bc = [jnp.broadcast_to(bcol[r, :], (BLK, BLK)) for r in sl]
        br = [b.T for b in bc]
        low = [jnp.where(strict, mm_nt(x, x), 0.0) * b for x, b in zip(ws, br)]
        inv = unit_inverses(low)
        m1 = [jnp.where(strict, mm_nt(x, y), 0.0) for x, y in zip(ws, ks)]
        gq = [jnp.where(closed, mm_nt(x, y), 0.0) * b for x, y, b in zip(qs, ws, br)]
        a = [mm(x, t) for x, t in zip(gq, inv)]
        z = [mm_tn(t, b * x.astype(F32)) for t, b, x in zip(inv, bc, ws)]
        sd = [mm_nt(x, y) - mm(p, m) for x, y, p, m in zip(qs, ks, a, m1)]
        qm = [x.astype(F32) - mm(p, y) for x, p, y in zip(qs, a, ws)]
        kmt = [x.astype(F32).T - mm_tn(zz, m) for x, zz, m in zip(ks, z, m1)]
        pm = [eye - mm_tn(zz, x) for zz, x in zip(z, ws)]
        for n, r in enumerate(sl):
            t_out[s, r, :] = inv[n].astype(t_out.dtype)
            a_out[s, r, :] = a[n].astype(a_out.dtype)
            z_out[s, r, :] = z[n].astype(z_out.dtype)
            m_out[s, r, :] = m1[n].astype(m_out.dtype)
            kp_out[s, r, :HD] = kmt[n].astype(BF16)
            kp_out[s, r, HD:] = pm[n].astype(BF16)
            qm_buf[r, :] = qm[n]
            s_buf[r, r] = sd[n]
        return carry

    lax.fori_loop(0, NB // GROUP, group, 0)


def sweep(s, qc, kp, qm_buf, x_buf, s_buf):
    at = NQC
    for j in range(NB - 2, -1, -1):
        r0 = (j + 1) * BLK
        rows = SEQ - r0
        x_buf[r0 : r0 + BLK, :] = qm_buf[r0 : r0 + BLK, :]
        x = x_buf[r0:, :].astype(BF16)
        at -= rows
        qc[s, at : at + rows, :] = x
        both = mm(x, kp[s, j * BLK : r0, :])
        s_buf[r0:, j * BLK : r0] = both[:, :HD]
        x_buf[r0:, :] = both[:, HD:]


def weigh(s, v, dcol, drow, s_buf, probs, o):
    for i in range(NB):
        lo, width = i * BLK, (i + 1) * BLK
        t = s_buf[lo:width, :width] * SCALE
        seen = dcol[lo:width, 0:1] == drow[0:1, :width]
        seen = seen & (
            lax.broadcasted_iota(jnp.int32, (BLK, width), 0) + lo
            >= lax.broadcasted_iota(jnp.int32, (BLK, width), 1)
        )
        t = jnp.where(seen, t, -1e30)
        e = jnp.exp(t - jnp.max(t, axis=1, keepdims=True))
        p = (e * (1.0 / jnp.sum(e, axis=1, keepdims=True))).astype(BF16)
        probs[s, lo:width, :width] = p
        o[lo:width, :] = mm(p, v[:width, :])


def project(x_all, whole, normed, qkvp, raw):
    rows = 256
    gain = whole[:, 8 * HD : 9 * HD].astype(F32)
    gain = jnp.concatenate(
        [gain[n * HD : (n + 1) * HD, :].T[0:1, :] for n in range(gain.shape[0] // HD)], axis=1
    )

    def block(i, carry):
        at = pl.ds(pl.multiple_of(i * rows, rows), rows)
        x = x_all[at, :].astype(F32)
        scale = lax.rsqrt(jnp.mean(x * x, axis=1, keepdims=True) + 1e-05)
        n = (x * scale * gain).astype(BF16)
        normed[at, :] = n
        y = mm(n, whole[:, : 9 * HD])
        qkvp[at, :] = y[:, : 8 * HD].astype(BF16)
        raw[at, :] = y[:, 8 * HD :]
        return carry

    lax.fori_loop(0, SEQ // rows, block, 0)


def heads_here():
    chip, core = lax.axis_index("x"), lax.axis_index("c")
    return 3 * chip + 2 * core, 3 * chip + 1


def fwd_slot(poke, s, head, small, marks, drow, qkvp, raw, vec, o, probs, qc, t_out, a_out, z_out, m_out, kp_out, s_buf, x_buf, qm_buf, b_buf):
    cols = slice(s * HD, (s + 1) * HD)
    q, k, v, path = (qkvp.at[:, (2 * n + s) * HD : (2 * n + s + 1) * HD] for n in range(4))
    taps = conv_weights(small, head)
    conved = convolve(path[...].astype(F32), taps, marks[...])
    unit = conved * lax.rsqrt(jnp.sum(conved * conved, axis=1, keepdims=True) + 1e-06)
    vec[:, cols] = unit.astype(BF16)
    b_buf[...] = betas_of(raw[...], head)
    own_blocks(s, q, k, vec.at[:, cols], b_buf, (t_out, a_out, z_out, m_out, kp_out, qm_buf, s_buf))
    poke()
    sweep(s, qc, kp_out, qm_buf, x_buf, s_buf)
    poke()
    weigh(s, v, marks, drow, s_buf, probs, o.at[:, cols])


def score_grads(s, v, o, do, probs, ds_buf, dv):
    for i in range(NB):
        lo, width = i * BLK, (i + 1) * BLK
        p = probs[s, lo:width, :width].astype(F32)
        g = do[lo:width, :]
        delta = jnp.sum(g * o[lo:width, :], axis=1, keepdims=True)
        ds = p * (mm_nt(g, v[:width, :]) - delta) * SCALE
        ds_buf[lo:width, :width] = ds.astype(BF16)
    for j in range(NB):
        lo = j * BLK
        dv[lo : lo + BLK, :] = mm_tn(probs[s, lo:, lo : lo + BLK], do[lo:, :]).astype(dv.dtype)


def sweep_back(s, qc, kp, ds_buf, x_buf, dkm_buf, dpm_buf):
    x_buf[...] = jnp.zeros_like(x_buf)
    dkm_buf[SEQ - BLK :, :] = jnp.zeros((BLK, HD), F32)
    dpm_buf[SEQ - BLK :, :] = jnp.zeros((BLK, HD), F32)
    at = 0
    for j in range(NB - 1):
        lo, r0 = j * BLK, (j + 1) * BLK
        rows = SEQ - r0
        x = x_buf[r0:, :].astype(BF16)
        ds = ds_buf[r0:, lo:r0]
        qcj = qc[s, at : at + rows, :]
        at += rows
        both = mm_tn(qcj, jnp.concatenate([x, ds], axis=1))
        dpm_buf[lo:r0, :] = both[:, :HD]
        dkm_buf[lo:r0, :] = both[:, HD:].T
        x_buf[r0:, :] = mm_nt(jnp.concatenate([ds, x], axis=1), kp[s, lo:r0, :])


def own_blocks_back(s, q, k, w, bcol, saved, bufs, dq, dk, dw, db):
    t_in, a_in, z_in, m_in = saved
    ds_buf, x_buf, dkm_buf, dpm_buf = bufs
    row, col = iota2(0), iota2(1)
    strict, closed = row > col, row >= col

    def group(g, carry):
        sl = [pl.ds(pl.multiple_of((g * GROUP + n) * BLK, BLK), BLK) for n in range(GROUP)]
        rng = range(GROUP)
        Q = [q[r, :] for r in sl]
        K = [k[r, :] for r in sl]
        W = [w[r, :] for r in sl]
        bc = [jnp.broadcast_to(bcol[r, :], (BLK, BLK)) for r in sl]
        br = [b.T for b in bc]
        E = [ds_buf[r, r] for r in sl]
        T = [t_in[s, r, :] for r in sl]
        A = [a_in[s, r, :] for r in sl]
        Z = [z_in[s, r, :] for r in sl]
        M = [m_in[s, r, :] for r in sl]
        dQm = [x_buf[r, :] for r in sl]
        dKm = [dkm_buf[r, :] for r in sl]
        dPm = [dpm_buf[r, :] for r in sl]
        i1 = [mm_nt(W[n], W[n]) for n in rng]
        qw = [jnp.where(closed, mm_nt(Q[n], W[n]), 0.0) for n in rng]
        dA = [-(mm_nt(E[n], M[n]) + mm_nt(dQm[n], W[n])) for n in rng]
        dM = [jnp.where(strict, -(mm_tn(A[n], E[n]) + mm_nt(Z[n], dKm[n])), 0.0) for n in rng]
        dZ = [-(mm(M[n], dKm[n]) + mm_nt(W[n], dPm[n])) for n in rng]
        dW = [-(mm_tn(A[n], dQm[n]) + mm(Z[n], dPm[n])) for n in rng]
        dG = [jnp.where(closed, mm_nt(dA[n], T[n]), 0.0) for n in rng]
        bw = [bc[n] * W[n].astype(F32) for n in rng]
        dT = [mm_tn(qw[n] * br[n], dA[n]) + mm_nt(bw[n], dZ[n]) for n in rng]
        dBW = [mm(T[n], dZ[n]) for n in rng]
        dL = [mm_tn(T[n], dT[n]) for n in rng]
        dL = [jnp.where(strict, -mm_nt(dL[n], T[n]), 0.0) for n in rng]
        dI = [dL[n] * br[n] for n in rng]
        R = [dG[n] * br[n] for n in rng]
        for n, r in enumerate(sl):
            db[r, :] = jnp.sum(
                (dL[n] * i1[n] + dG[n] * qw[n]).T + dBW[n] * W[n].astype(F32), axis=1, keepdims=True
            )
            dq[r, :] = (dQm[n] + mm(E[n], K[n]) + mm(R[n], W[n])).astype(dq.dtype)
            dk[r, :] = (dKm[n] + mm_tn(E[n], Q[n]) + mm_tn(dM[n], W[n])).astype(dk.dtype)
            dw[r, :] = (
                dW[n]
                + bc[n] * dBW[n]
                + mm_tn(R[n], Q[n])
                + mm(dM[n], K[n])
                + mm(dI[n] + dI[n].T, W[n])
            )
        return carry

    lax.fori_loop(0, NB // GROUP, group, 0)


def bwd_slot(poke, s, head, qkvp, raw, small, marks, vec, o, do, probs, qc, t_in, a_in, z_in, m_in, kp, d_ext, d_conv, ds_buf, x_buf, dkm_buf, dpm_buf, b_buf, db_buf, dw_buf):
    cols = slice(s * HD, (s + 1) * HD)
    q, k, v, path = (qkvp.at[:, (2 * n + s) * HD : (2 * n + s + 1) * HD] for n in range(4))
    dq, dk, dv, dpath = (d_ext.at[:, (2 * n + s) * HD : (2 * n + s + 1) * HD] for n in range(4))
    score_grads(s, v, o.at[:, cols], do.at[:, cols], probs, ds_buf, dv)
    poke()
    sweep_back(s, qc, kp, ds_buf, x_buf, dkm_buf, dpm_buf)
    poke()
    beta = betas_of(raw[...], head)
    b_buf[...] = beta
    own_blocks_back(
        s, q, k, vec.at[:, cols], b_buf, (t_in, a_in, z_in, m_in), (ds_buf, x_buf, dkm_buf, dpm_buf), dq, dk, dw_buf, db_buf
    )
    poke()
    taps = conv_weights(small, head)
    raw_path = path[...].astype(F32)
    conved = convolve(raw_path, taps, marks[...])
    scale = lax.rsqrt(jnp.sum(conved * conved, axis=1, keepdims=True) + 1e-06)
    unit = conved * scale
    dw = dw_buf[...]
    d_conved = scale * (dw - unit * jnp.sum(dw * unit, axis=1, keepdims=True))
    total = taps[0:1, :] * d_conved
    d_conv[s, 0:1, :] = jnp.sum(d_conved * raw_path, axis=0, keepdims=True)
    for m in range(1, TAPS):
        marked = d_conved * marks[:, m : m + 1]
        d_conv[s, m : m + 1, :] = jnp.sum(marked * pltpu.roll(raw_path, m, 0), axis=0, keepdims=True)
        total = total + taps[m : m + 1, :] * pltpu.roll(marked, SEQ - m, 0)
    dpath[...] = total.astype(dpath.dtype)
    lane = lax.broadcasted_iota(jnp.int32, (SEQ, HD), 1)
    return jnp.where(lane == head + BETA_AT, db_buf[...] * beta * (1.0 - 0.5 * beta), 0.0)


def fwd_shapes(width):
    return [
        ((SEQ, width), BF16),
        ((SEQ, 8 * HD), BF16),
        ((SEQ, HD), F32),
        ((SEQ, 2 * HD), BF16),
        ((SEQ, 2 * HD), F32),
        ((SEQ, 2 * HD), BF16),
        ((2, SEQ, SEQ), BF16),
        ((2, NQC, HD), BF16),
        ((2, SEQ, BLK), F32),
        ((2, SEQ, BLK), BF16),
        ((2, SEQ, BLK), BF16),
        ((2, SEQ, BLK), BF16),
        ((2, SEQ, 2 * HD), BF16),
    ]


def fwd_scratch():
    return [
        pltpu.VMEM((SEQ, SEQ), F32),
        pltpu.VMEM((SEQ, HD), F32),
        pltpu.VMEM((SEQ, HD), F32),
        pltpu.VMEM((SEQ, 1), F32),
    ]


def bwd_scratch():
    return (
        [pltpu.VMEM((SEQ, SEQ), BF16)]
        + [pltpu.VMEM((SEQ, HD), F32)] * 3
        + [pltpu.VMEM((SEQ, 1), F32)] * 2
        + [pltpu.VMEM((SEQ, HD), F32)]
    )


MESH = pl.DeviceIdType.MESH
ANY = pl.BlockSpec(memory_space=pl.ANY)
VMEM = pl.BlockSpec(memory_space=pltpu.VMEM)


class Place:
    def __init__(self):
        self.x, self.c = lax.axis_index("x"), lax.axis_index("c")
        self.y = lax.axis_index("y")
        self.zl, self.zh = lax.axis_index("zl"), lax.axis_index("zh")
        self.z = self.zh * 2 + self.zl

    def chip(self, d):
        return lax.rem(self.x + d, 4)

    def at_x(self, d):
        return {"x": lax.rem(self.x + d, 4)}

    def at_xc(self, d, k):
        return {"x": lax.rem(self.x + d, 4), "c": lax.rem(self.c + k, 2)}

    def sibling(self):
        return {"c": 1 - self.c}

    def at_y(self, d):
        return {"y": lax.rem(self.y + d, 4)}

    def at_z(self, d):
        z = lax.rem(self.z + d, 4)
        return {"zl": lax.rem(z, 2), "zh": z // 2}


class Net:
    def __init__(self, send_sem, recv_sem, local_sem):
        self.place = Place()
        self.send_sem, self.recv_sem, self.local_sem = send_sem, recv_sem, local_sem
        self.count, self.kept, self.locals, self.sent = 0, 0, [], []

    def prepare(self, src, dst, device):
        k = self.count
        self.count += 1
        return pltpu.make_async_remote_copy(
            src_ref=src,
            dst_ref=dst,
            send_sem=self.send_sem.at[k],
            recv_sem=self.recv_sem.at[k],
            device_id=device,
            device_id_type=MESH,
        )

    def send(self, src, dst, device):
        copy = self.prepare(src, dst, device)
        copy.start()
        self.sent.append(copy)
        return copy

    def local(self, src, dst):
        self.kept += 1
        return pltpu.make_async_copy(src, dst, self.local_sem.at[self.kept - 1])

    def load(self, src, dst):
        copy = self.local(src, dst)
        copy.start()
        return copy

    def keep(self, src, dst):
        self.locals.append(self.load(src, dst))

    def settle(self):
        for copy in self.locals:
            copy.wait()
        self.locals = []

    def finish(self):
        for copy in self.sent:
            copy.wait_send()
        self.settle()


def meet(devices):
    barrier = pltpu.get_barrier_semaphore()
    for device in devices:
        pl.semaphore_signal(barrier, inc=1, device_id=device, device_id_type=MESH)
    pl.semaphore_wait(barrier, len(devices))


class Jobs:
    def __init__(self, *jobs):
        self.all = list(jobs)
        self.jobs = list(jobs)

    def poke(self):
        for job in list(self.jobs):
            try:
                next(job)
            except StopIteration:
                self.jobs.remove(job)

    def step(self, *which):
        for n in which:
            next(self.all[n], None)

    def drain(self):
        while self.jobs:
            self.poke()


def interleave(*jobs):
    Jobs(*jobs).drain()


def team_peers(p):
    return [p.at_x(1), p.at_x(3), p.sibling()]


def team_all(p):
    return [p.at_xc(d, k) for d in range(4) for k in range(2) if d + k]


def group_peers(p):
    return [p.at_y(d) for d in (1, 2, 3)] + [p.at_z(d) for d in (1, 2, 3)]


def gather_team(net, own, out):
    p = net.place
    me, sib = 2 * p.x + p.c, p.sibling()
    right, left = p.at_x(1), p.at_x(3)
    t_l, t_r, t_2 = (2 * p.chip(d) + p.c for d in (3, 1, 2))
    to_r = net.send(own, out.at[:, me], right)
    to_l = net.send(own, out.at[:, me], left)
    shared = [net.send(own, out.at[:, me], sib)]
    net.keep(own, out.at[:, me])
    yield
    to_r.wait_recv()
    on_r = net.send(out.at[0, t_l], out.at[0, t_l], right)
    shared.append(net.send(out.at[:, t_l], out.at[:, t_l], sib))
    to_l.wait_recv()
    on_l = net.send(out.at[1, t_r], out.at[1, t_r], left)
    shared.append(net.send(out.at[:, t_r], out.at[:, t_r], sib))
    yield
    on_r.wait_recv()
    shared.append(net.send(out.at[0, t_2], out.at[0, t_2], sib))
    on_l.wait_recv()
    shared.append(net.send(out.at[1, t_2], out.at[1, t_2], sib))
    yield
    for copy in shared:
        copy.wait_recv()


GATHER_TEAM = 10


def add(a, b):
    return (a.astype(F32) + b.astype(F32)).astype(BF16)


def scatter_team(net, part, got, total, from_l, from_r, all_l, all_r, finish):
    p = net.place
    sib, right, left = p.sibling(), p.at_x(1), p.at_x(3)
    order = (2, 1, 3, 0)
    swaps, loads = [], []
    for d in order:
        at = p.chip(d)
        swaps.append(net.send(part.at[:, 2 * at + 1 - p.c], got.at[:, at], sib))
        loads.append(net.load(part.at[:, 2 * at + p.c], total.at[:, at]))

    def pair(n):
        swaps[n].wait_recv()
        loads[n].wait()
        at = p.chip(order[n])
        total[:, at] = add(total[:, at], got[:, at])
        return at

    yield
    x_2 = pair(0)
    half_r = net.send(total.at[0, x_2], from_l, right)
    half_l = net.send(total.at[1, x_2], from_r, left)
    x_r = pair(1)
    rest_r = net.send(total.at[1, x_r], all_l.at[1], right)
    x_l = pair(2)
    rest_l = net.send(total.at[0, x_l], all_r.at[0], left)
    pair(3)
    yield
    half_r.wait_recv()
    total[0, x_r] = add(total[0, x_r], from_l[...])
    last_r = net.send(total.at[0, x_r], all_l.at[0], right)
    half_l.wait_recv()
    total[1, x_l] = add(total[1, x_l], from_r[...])
    last_l = net.send(total.at[1, x_l], all_r.at[1], left)
    yield
    for copy in (rest_r, rest_l, last_r, last_l):
        copy.wait_recv()
    finish(total[:, p.x].astype(F32) + all_l[...].astype(F32) + all_r[...].astype(F32))


SCATTER_TEAM_LOADS = 4
SCATTER_TEAM = 10


def scatter_team_scratch(n, w):
    return [
        pltpu.VMEM((2, 4, n, w), BF16),
        pltpu.VMEM((2, 4, n, w), BF16),
        pltpu.VMEM((n, w), BF16),
        pltpu.VMEM((n, w), BF16),
        pltpu.VMEM((2, n, w), BF16),
        pltpu.VMEM((2, n, w), BF16),
    ]


def chunk_rows(y, z, rows):
    zl, zh = (z % 2, z // 2) if isinstance(z, int) else (lax.rem(z, 2), z // 2)
    return pl.ds(pl.multiple_of(((zl * 4 + y) * 2 + zh) * rows, rows), rows)


def gather_groups(net, own, out, cuts):
    p = net.place
    rows = own.shape[0]
    lo, mid, hi = cuts
    first, second = pl.ds(lo, mid - lo), pl.ds(mid, hi - mid)
    net.keep(own, out.at[chunk_rows(p.y, p.z, rows)])

    def spread(cols, y, z, devices, src=None):
        place = out.at[chunk_rows(y, z, rows), cols]
        return [net.send(place if src is None else src.at[:, cols], place, d) for d in devices]

    ys, zs = [p.at_y(d) for d in (1, 3, 2)], [p.at_z(d) for d in (1, 3, 2)]
    y_first = spread(first, p.y, p.z, ys, own)
    z_first = spread(second, p.y, p.z, zs, own)
    last = spread(first, p.y, p.z, zs, own) + spread(second, p.y, p.z, ys, own)
    yield
    for n, d in enumerate((1, 3, 2)):
        y_first[n].wait_recv()
        last += spread(first, lax.rem(p.y + 4 - d, 4), p.z, zs)
        z_first[n].wait_recv()
        last += spread(second, p.y, lax.rem(p.z + 4 - d, 4), ys)
        yield
    for copy in last:
        copy.wait_recv()


GATHER_GROUPS = 30


def scatter_groups(net, part, out, cuts, z_got, z_sum, z_last, y_got, y_sum, y_last):
    p = net.place
    lo, mid, hi = cuts
    first, second = pl.ds(lo, mid - lo), pl.ds(mid, hi - mid)
    rows = z_sum.shape[1]
    both = hi > mid
    flat = len(part.shape) == 2
    order = (2, 1, 3)
    a, b, a_own, b_own = [], [], [], []
    for n, d in enumerate(order):
        z, y = lax.rem(p.z + d, 4), lax.rem(p.y + d, 4)
        if flat:
            for k in range(4):
                a.append(net.send(part.at[chunk_rows(k, z, rows), first], z_got.at[n, k], p.at_z(d)))
                b.append(net.send(part.at[chunk_rows(y, k, rows), second], y_got.at[n, k % 2, k // 2], p.at_y(d)))
        else:
            a.append(net.send(part.at[lax.rem(z, 2), :, z // 2, :, first], z_got.at[n], p.at_z(d)))
            if both:
                b.append(net.send(part.at[:, y, :, :, second], y_got.at[n], p.at_y(d)))
    if flat:
        for k in range(4):
            a_own.append(net.load(part.at[chunk_rows(k, p.z, rows), first], z_sum.at[k]))
            b_own.append(net.load(part.at[chunk_rows(p.y, k, rows), second], y_sum.at[k % 2, k // 2]))
    else:
        a_own.append(net.load(part.at[p.zl, :, p.zh, :, first], z_sum))
        if both:
            b_own.append(net.load(part.at[:, p.y, :, :, second], y_sum))

    yield
    for copy in a_own:
        copy.wait()
    for copy in a:
        copy.wait_recv()
    for y in range(4):
        t = z_sum[y].astype(F32)
        for n in range(3):
            t = t + z_got[n, y].astype(F32)
        z_sum[y] = t.astype(BF16)
    a = [
        net.send(z_sum.at[lax.rem(p.y + d, 4)], z_last.at[n], p.at_y(d)) for n, d in enumerate(order)
    ]
    if both:
        yield
        for copy in b_own:
            copy.wait()
        for copy in b:
            copy.wait_recv()
        for zl in range(2):
            for zh in range(2):
                t = y_sum[zl, zh].astype(F32)
                for n in range(3):
                    t = t + y_got[n, zl, zh].astype(F32)
                y_sum[zl, zh] = t.astype(BF16)
        b = []
        for n, d in enumerate(order):
            z = lax.rem(p.z + d, 4)
            b.append(net.send(y_sum.at[lax.rem(z, 2), z // 2], y_last.at[n], p.at_z(d)))
    yield
    for copy in a:
        copy.wait_recv()
    t = z_sum[p.y].astype(F32)
    for n in range(3):
        t = t + z_last[n].astype(F32)
    out[:, first] = t.astype(out.dtype)
    if both:
        yield
        for copy in b:
            copy.wait_recv()
        t = y_sum[p.zl, p.zh].astype(F32)
        for n in range(3):
            t = t + y_last[n].astype(F32)
        out[:, second] = t.astype(out.dtype)


SCATTER_GROUPS_LOADS = 2
SCATTER_GROUPS_FLAT_LOADS = 8
SCATTER_GROUPS = 12
SCATTER_GROUPS_FLAT = 30


def scatter_groups_scratch(r, cuts):
    a, b = cuts[1] - cuts[0], max(cuts[2] - cuts[1], HD)
    return [
        pltpu.VMEM((3, 4, r, a), BF16),
        pltpu.VMEM((4, r, a), BF16),
        pltpu.VMEM((3, r, a), BF16),
        pltpu.VMEM((3, 2, 2, r, b), BF16),
        pltpu.VMEM((2, 2, r, b), BF16),
        pltpu.VMEM((3, r, b), BF16),
    ]


def sems(remote, local):
    return [
        pltpu.SemaphoreType.DMA((remote,)),
        pltpu.SemaphoreType.DMA((remote,)),
        pltpu.SemaphoreType.DMA((max(local, 1),)),
    ]


def params(collective_id):
    return pltpu.CompilerParams(
        collective_id=collective_id, has_side_effects=True, vmem_limit_bytes=VM
    )


EPS_NORM = 1e-05
EPS_UNIT = 1e-06
SHAPE = jax.ShapeDtypeStruct


def all_to_team(net, packs, got):
    p = net.place
    me = 2 * p.x + p.c
    net.keep(packs.at[me], got.at[me])
    copies = []
    for d in (2, 1, 3, 0):
        for k in (1, 0):
            if d + k:
                to = 2 * p.chip(d) + lax.rem(p.c + k, 2)
                copies.append(net.send(packs.at[to], got.at[me], p.at_xc(d, k)))
    yield
    for copy in copies:
        copy.wait_recv()


TO_TEAM = 7


def swap_rows(net, pairs):
    p = net.place
    copies = []
    for src, dst in pairs:
        net.keep(src.at[p.zh], dst.at[p.zh])
        copies.append(net.send(src.at[1 - p.zh], dst.at[p.zh], p.at_z(2)))
    yield
    for copy in copies:
        copy.wait_recv()


def thin_rows(rows, padded):
    out = lax.broadcasted_iota(jnp.int32, (8 * rows, 8 * padded), 0)
    at = lax.broadcasted_iota(jnp.int32, (8 * rows, 8 * padded), 1)
    return ((out // rows == at // padded) & (out % rows == at % padded)).astype(BF16)


HEADS_W, SMALL_W, OUT_W = 8 * HD, HD, 2 * HD
FIRST_W = HEADS_W + SMALL_W + OUT_W
PIECE = 32


def head_of(t, slot):
    return 3 * (t // 2) + (1 if slot else 2 * (t % 2))


def shift_pieces(tiles):
    lane = lax.broadcasted_iota(jnp.int32, tiles[0][0].shape, 1) // PIECE
    total = None
    for n, (tile, piece) in enumerate(tiles):
        turn = (PIECE * (n - piece)) % HD
        moved = pltpu.roll(tile, turn, 1) if turn else tile
        total = moved if total is None else jnp.where(lane == n, moved, total)
    return total


def pack_weights(kinds, gate_up, small, packs):
    share = small.shape[0]
    packs[...] = jnp.zeros_like(packs)
    for t in range(8):
        for n, w in enumerate(kinds):
            at = n * OUT_W + (SMALL_W if n == 4 else 0)
            for slot in range(2):
                head = head_of(t, slot)
                packs[t, :share, at + slot * HD : at + (slot + 1) * HD] = w[:, head * HD : (head + 1) * HD]
        packs[t, :share, HEADS_W : HEADS_W + SMALL_W] = small[...]
    for n, w in enumerate(gate_up):
        for t in range(8):
            for j in range(4):
                tiles = []
                for e in range(4 * j, 4 * j + 4):
                    at = (2 * e + t // 4) * HD
                    tiles.append((w[:, at : at + HD].astype(F32), t % 4))
                at = FIRST_W + n * 4 * HD + j * HD
                packs[t, :share, at : at + HD] = shift_pieces(tiles).astype(BF16)


def start_kernel(cuts, wq, wk, wv, wp, wo, gate, up, small, tokens, grad_out, x_rows, g_rows, x_all, whole, own_ffn, packs, got, own, *sem):
    net = Net(*sem)
    p = net.place
    share = small.shape[0]
    meet(team_all(p) + group_peers(p))
    swaps = swap_rows(net, ((tokens, x_rows), (grad_out, g_rows)))
    next(swaps)
    pack_weights((wq, wk, wv, wp, wo), (gate, up), small, packs)
    trade = all_to_team(net, packs, got)
    next(trade)
    interleave(trade)
    net.settle()
    pick = thin_rows(share, packs.shape[1])
    own[...] = mm(pick, got[...].reshape(pick.shape[1], got.shape[2])).astype(BF16)
    net.keep(own.at[:, pl.ds(FIRST_W, own.shape[1] - FIRST_W)], own_ffn)
    heads = gather_groups(net, own.at[:, pl.ds(0, FIRST_W)], whole, cuts)
    next(heads)
    interleave(swaps)
    interleave(gather_team(net, x_rows, x_all), heads)
    net.finish()


def start(kinds, gate, up, small, tokens, grad_out):
    share, width = kinds[0].shape
    two, n, _ = tokens.shape
    rows = SHAPE(tokens.shape, BF16)
    cols = FIRST_W + gate.shape[1] // 4
    return pl.pallas_call(
        functools.partial(start_kernel, (0, 6 * HD, FIRST_W)),
        out_shape=[
            rows,
            rows,
            SHAPE((two, 8, n, width), BF16),
            SHAPE((width, FIRST_W), BF16),
            SHAPE((8 * share, cols - FIRST_W), BF16),
        ],
        in_specs=[VMEM] * 8 + [ANY] * 2,
        out_specs=[ANY] * 5,
        scratch_shapes=[
            pltpu.VMEM((8, 16, cols), BF16),
            pltpu.VMEM((8, 16, cols), BF16),
            pltpu.VMEM((8 * share, cols), BF16),
        ]
        + sems(TO_TEAM + 2 + GATHER_TEAM + GATHER_GROUPS, 6),
        compiler_params=params(1),
        name="start",
    )(*kinds, gate, up, small, tokens, grad_out)


def lanes(at):
    return pl.ds(pl.multiple_of(at * HD, HD), HD)


OUT_AT = 9


def trade_out(net, whole, w_out):
    p = net.place
    copies, own = [], []
    for d in (2, 1, 3, 0):
        for k in (1, 0):
            xd, cd = p.chip(d), lax.rem(p.c + k, 2)
            row_a, row_b = lanes(3 * xd + 2 * cd), lanes(3 * xd + 1)
            row_c = lanes(3 * xd + jnp.where(p.c == 0, 2 * cd, 1))
            col_a, col_b = lanes(3 * p.x + 2 * p.c), lanes(3 * p.x + 1)
            moves = (
                (whole.at[row_a, pl.ds(OUT_AT * HD, HD)], w_out.at[pl.ds(0, HD), col_a]),
                (whole.at[row_b, pl.ds(OUT_AT * HD, HD)], w_out.at[pl.ds(HD, HD), col_a]),
                (whole.at[row_c, pl.ds((OUT_AT + 1) * HD, HD)], w_out.at[lanes(p.c), col_b]),
            )
            for src, dst in moves:
                if d + k:
                    copies.append(net.send(src, dst, p.at_xc(d, k)))
                else:
                    own.append(net.load(src, dst))
    yield
    for copy in own:
        copy.wait()
    for copy in copies:
        copy.wait_recv()


def attn_fwd_kernel(cuts, x_all, whole, marks, drow, own_ffn, g_rows, *rest):
    kept, (w_ffn, g_all, w_out, part), rest = rest[:13], rest[13:17], rest[17:]
    bufs, (x_buf, w_buf, wo_buf, part_buf), rest = rest[:13], rest[13:17], rest[17:]
    normed, qkvp, raw, vec, o, mixed, *saved = bufs
    net = Net(*rest[-3:])
    p = net.place
    loads = [net.load(whole.at[:, pl.ds(0, 9 * HD)], w_buf), net.load(x_all, x_buf)]
    meet(team_all(p) + group_peers(p))
    jobs = Jobs(
        gather_groups(net, own_ffn, w_ffn, cuts),
        trade_out(net, whole, wo_buf),
        gather_team(net, g_rows, g_all),
    )
    jobs.step(0, 1, 2)
    for copy in loads:
        copy.wait()
    project(x_buf, w_buf, normed, qkvp, raw)
    for n in range(3):
        net.keep(bufs[n], kept[n])
    steps = [(0,), (0, 2), (0, 2), (0, 2), (2,)]
    poke = lambda: jobs.step(*steps.pop(0)) if steps else None
    for s, head in enumerate(heads_here()):
        cols = pl.ds(s * HD, HD)
        poke()
        fwd_slot(poke, s, head, w_buf.at[:, pl.ds(8 * HD, HD)], marks, drow, qkvp, raw, vec, o, *saved, *rest[:-3])
        net.keep(vec.at[:, cols], kept[3].at[:, cols])
        net.keep(o.at[:, cols], kept[4].at[:, cols])
        for src, dst in zip(saved, kept[6:]):
            net.keep(src.at[s], dst.at[s])
    mixed[:, :HD] = o[:, :HD].astype(BF16)
    mixed[:, HD:] = jnp.where(p.c == 0, o[:, HD:], 0.0).astype(BF16)
    net.keep(mixed, kept[5])
    jobs.step(1, 1)
    net.keep(wo_buf, w_out)
    two, _, n, width = part.shape
    for h in range(two):
        for t in range(0, 8, 4):
            at = (h * 8 + t) * n
            y = mm(mixed[at : at + 4 * n, :], wo_buf[...]).astype(BF16)
            part_buf[h, t : t + 4] = y.reshape(4, n, width)
    net.keep(part_buf, part)
    jobs.drain()
    net.finish()


def attn_fwd(x_all, whole, marks, drow, own_ffn, g_rows):
    rows, cols = own_ffn.shape
    two, n, width = g_rows.shape
    kept = fwd_shapes(width)
    part = (two, 8, n, width)
    return pl.pallas_call(
        functools.partial(attn_fwd_kernel, (0, cols // 2, cols)),
        out_shape=[SHAPE(*a) for a in kept]
        + [SHAPE((16 * rows, cols), BF16), SHAPE(part, BF16), SHAPE((2 * HD, width), BF16), SHAPE(part, BF16)],
        in_specs=[ANY, ANY, VMEM, VMEM, ANY, ANY],
        out_specs=[ANY] * (len(kept) + 4),
        scratch_shapes=[pltpu.VMEM(*a) for a in kept]
        + [
            pltpu.VMEM((SEQ, width), BF16),
            pltpu.VMEM((width, 9 * HD), BF16),
            pltpu.VMEM((2 * HD, width), BF16),
            pltpu.VMEM(part, BF16),
        ]
        + fwd_scratch()
        + sems(GATHER_TEAM + GATHER_GROUPS + 21, 2 + 5 + 3 + 18 + 3),
        compiler_params=params(7),
        name="attn_fwd",
    )(x_all, whole, marks, drow, own_ffn, g_rows)


def ffn_in_kernel(cuts, part, x_rows, gain, own_down, hidden, ffn_all, w_down, normed, *rest):
    net = Net(*rest[-3:])
    p = net.place
    meet(team_peers(p) + group_peers(p))

    def finish(branch):
        h = x_rows[...].astype(F32) + branch
        hidden[...] = h
        scale = lax.rsqrt(jnp.mean(h * h, axis=-1, keepdims=True) + EPS_NORM)
        normed[...] = (h * scale * gain[...][None]).astype(BF16)

    def team():
        yield from scatter_team(net, part, *rest[:-3], finish)
        yield from gather_team(net, normed, ffn_all)

    interleave(team(), gather_groups(net, own_down, w_down, cuts))
    net.finish()


def ffn_in(part, x_rows, gain, own_down):
    two, n, width = x_rows.shape
    return pl.pallas_call(
        functools.partial(ffn_in_kernel, (0, width // 2, width)),
        out_shape=[
            SHAPE((two, n, width), F32),
            SHAPE((two, 8, n, width), BF16),
            SHAPE((16 * own_down.shape[0], width), BF16),
        ],
        in_specs=[ANY, VMEM, VMEM, ANY],
        out_specs=[VMEM, ANY, ANY],
        scratch_shapes=[pltpu.VMEM((two, n, width), BF16)]
        + scatter_team_scratch(n, width)
        + sems(SCATTER_TEAM + GATHER_TEAM + GATHER_GROUPS, 2 + SCATTER_TEAM_LOADS),
        compiler_params=params(3),
        name="ffn_in",
    )(part, x_rows, gain, own_down)


def norm_back(v, gain, d_normed):
    scale = lax.rsqrt(jnp.mean(v * v, axis=-1, keepdims=True) + EPS_NORM)
    unit = v * scale
    d_unit = d_normed * gain
    d_v = scale * (d_unit - unit * jnp.mean(d_unit * unit, axis=-1, keepdims=True))
    return d_v, d_normed * unit


def ffn_back_kernel(cuts, part, hidden, gain, g_rows, d_down, d_hidden, d_gain, branch_all, down_sum, branch, *rest):
    team_scratch, down_scratch = rest[:6], rest[6:12]
    net = Net(*rest[-3:])
    p = net.place
    meet(team_peers(p) + group_peers(p))

    def finish(d_normed):
        d_h, d_g = norm_back(hidden[...], gain[...][None], d_normed)
        d_h = d_h + g_rows[...].astype(F32)
        d_hidden[...] = d_h
        branch[...] = d_h.astype(BF16)
        d_gain[...] = jnp.sum(jnp.sum(d_g, axis=0), axis=0, keepdims=True)

    def team():
        yield from scatter_team(net, part, *team_scratch, finish)
        yield from gather_team(net, branch, branch_all)

    interleave(team(), scatter_groups(net, d_down, down_sum, cuts, *down_scratch))
    net.finish()


def by_group(a):
    return a.reshape(2, 4, 2, a.shape[0] // 16, a.shape[1])


def ffn_back(part, hidden, gain, g_rows, d_down):
    two, n, width = hidden.shape
    d_down = by_group(d_down)
    rows = d_down.shape[3]
    cuts = (0, width // 2, width)
    return pl.pallas_call(
        functools.partial(ffn_back_kernel, cuts),
        out_shape=[
            SHAPE((two, n, width), F32),
            SHAPE((1, width), F32),
            SHAPE((two, 8, n, width), BF16),
            SHAPE((rows, width), F32),
        ],
        in_specs=[ANY, VMEM, VMEM, VMEM, ANY],
        out_specs=[VMEM, VMEM, ANY, VMEM],
        scratch_shapes=[pltpu.VMEM((two, n, width), BF16)]
        + scatter_team_scratch(n, width)
        + scatter_groups_scratch(rows, cuts)
        + sems(SCATTER_TEAM + GATHER_TEAM + SCATTER_GROUPS, 1 + SCATTER_TEAM_LOADS + SCATTER_GROUPS_LOADS),
        compiler_params=params(4),
        name="ffn_back",
    )(part, hidden, gain, g_rows, d_down)


def trade_out_back(net, d_out, whole):
    p = net.place
    rows, middle, own = [], [], []
    cases = [(d, k) for d in (2, 1, 3, 0) for k in (1, 0)]
    for d, k in cases:
        xd, cd = p.chip(d), lax.rem(p.c + k, 2)
        for side, col in enumerate((lanes(3 * xd + 2 * cd), lanes(3 * xd + 1))):
            src = d_out.at[pl.ds(0, HD), col]
            dst = whole.at[lanes(3 * p.x + 2 * p.c), pl.ds(side * HD, HD)]
            if d + k:
                rows.append(net.send(src, dst, p.at_xc(d, k)))
            else:
                own.append(net.local(src, dst))
                own[-1].start()
    for d, k in cases:
        xd, cd = p.chip(d), lax.rem(p.c + k, 2)
        for side, col in enumerate((lanes(3 * xd + 2 * cd), lanes(3 * xd + 1))):
            src = d_out.at[pl.ds(HD, HD), col]
            dst = whole.at[lanes(3 * p.x + 1), pl.ds(side * HD, HD)]
            if d + k:
                middle.append((k, net.prepare(src, dst, p.at_xc(d, k))))
            else:
                middle.append((-1, net.local(src, dst)))

    @pl.when(p.c == 0)
    def _():
        for _, copy in middle:
            copy.start()

    yield
    for copy in rows:
        copy.wait_recv()
    for copy in own:
        copy.wait()
    for core in range(2):

        @pl.when(p.c == core)
        def _(core=core):
            for k, copy in middle:
                if k == core:
                    copy.wait_recv()

    @pl.when(p.c == 0)
    def _():
        for k, copy in middle:
            if k < 0:
                copy.wait()
            else:
                copy.wait_send()

    yield


TRADE_BACK = 28


def attn_bwd_kernel(cuts, *refs):
    marks, small, refs = refs[0], refs[1], refs[2:]
    given, refs = refs[:12], refs[12:]
    (d_ffn, part_o, hidden, d_out), refs = refs[:4], refs[4:]
    d_ext, d_conv, out_rows, ffn_sum, out_sum, refs = *refs[:5], refs[5:]
    bufs, refs = refs[:12], refs[12:]
    whole, own, refs = refs[0], refs[1:8], refs[8:]
    o_scratch, f_scratch, w_scratch = refs[:6], refs[6:12], refs[12:18]
    net = Net(*refs[-3:])
    p = net.place
    qkvp, raw, vec, o, do, *saved = bufs
    first, second = [], [[], []]
    for n in (0, 3, 4):
        first.append(net.load(given[n], bufs[n]))
    first.append(net.load(given[5].at[0], bufs[5].at[0]))
    for n in range(6, 12):
        second[0].append(net.load(given[n].at[0], bufs[n].at[0]))
    for n in (1, 2):
        second[0].append(net.load(given[n], bufs[n]))
    for n in range(5, 12):
        second[1].append(net.load(given[n].at[1], bufs[n].at[1]))
    meet(team_all(p) + group_peers(p))

    def finish(branch):
        out_rows[...] = (hidden[...] + branch).astype(BF16)

    def out_grad():
        yield from trade_out_back(net, d_out, whole)
        yield from scatter_groups(net, whole, out_sum, cuts[1], *w_scratch)

    jobs = Jobs(
        scatter_groups(net, d_ffn, ffn_sum, cuts[0], *f_scratch),
        scatter_team(net, part_o, *o_scratch, finish),
        out_grad(),
    )
    jobs.step(0, 1, 2)
    for copy in first:
        copy.wait()
    waits = [second[0], None, None, None, None, None]
    steps = [(1,), (), (1, 2), (0, 2), (0, 1), (2,)]

    def poke():
        jobs.step(*steps.pop(0))
        for copy in waits.pop(0) or ():
            copy.wait()

    d_raw = 0.0
    for s, head in enumerate(heads_here()):
        if s:
            for copy in second[1]:
                copy.wait()
        d_raw = d_raw + bwd_slot(poke, s, head, qkvp, raw, small, marks, vec, o, do, *saved, d_ext, d_conv, *own)
    d_ext[:, 8 * HD :] = d_raw.astype(d_ext.dtype)
    jobs.drain()
    net.finish()


def attn_bwd(marks, small, given, d_ffn, part_o, hidden, d_out):
    two, n, width = hidden.shape
    d_ffn = by_group(d_ffn)
    r, w = d_ffn.shape[3:]
    cuts = [(0, w // 2, w), (0, HD, 2 * HD)]
    return pl.pallas_call(
        functools.partial(attn_bwd_kernel, cuts),
        out_shape=[
            SHAPE((SEQ, 9 * HD), BF16),
            SHAPE((2, 8, HD), F32),
            SHAPE((two, n, width), BF16),
            SHAPE((r, w), BF16),
            SHAPE((r, 2 * HD), BF16),
        ],
        in_specs=[VMEM] * 2 + [ANY] * (len(given) + 2) + [VMEM, ANY],
        out_specs=[VMEM] * 5,
        scratch_shapes=[pltpu.VMEM(a.shape, a.dtype) for a in given]
        + [pltpu.VMEM((width, 2 * HD), BF16)]
        + bwd_scratch()
        + scatter_team_scratch(n, width)
        + scatter_groups_scratch(r, cuts[0])
        + scatter_groups_scratch(r, cuts[1])
        + sems(
            SCATTER_TEAM + SCATTER_GROUPS + SCATTER_GROUPS_FLAT + TRADE_BACK,
            4 + 8 + 7 + SCATTER_TEAM_LOADS + SCATTER_GROUPS_LOADS + SCATTER_GROUPS_FLAT_LOADS + 4,
        ),
        compiler_params=params(8),
        name="attn_bwd",
    )(marks, small, *given, d_ffn, part_o, hidden, d_out)


def last_kernel(cuts, part_n, x_rows, d_hidden, gain, d_heads, d_small, out_sum, ffn_sum, out_rows, output, d_tokens, got_heads, got_rest, d_rows, heads_sum, small_sum, packs_heads, packs_rest, *rest):
    n_scratch, h_scratch, s_scratch = rest[:6], rest[6:12], rest[12:18]
    net = Net(*rest[-3:])
    p = net.place
    meet(team_all(p) + group_peers(p))
    eight, padded, _ = packs_heads.shape
    spread = thin_rows(heads_sum.shape[0] // eight, padded).T

    def pack(sums, packs, at):
        wide = mm(spread, sums).astype(BF16)
        packs[:, :, at : at + sums.shape[1]] = wide.reshape(eight, padded, sums.shape[1])

    def finish(d_normed):
        d_x, _ = norm_back(x_rows[...].astype(F32), gain[...][None], d_normed)
        d_rows[...] = (d_x + d_hidden[...]).astype(BF16)

    def tokens():
        yield from scatter_team(net, part_n, *n_scratch, finish)
        yield from swap_rows(net, ((d_rows, d_tokens),))

    def others():
        yield from swap_rows(net, ((out_rows, output),))
        pack(out_sum[...], packs_rest, 0)
        pack(ffn_sum[...], packs_rest, out_sum.shape[1])
        yield from all_to_team(net, packs_rest, got_rest)

    jobs = Jobs(
        scatter_groups(net, d_heads, heads_sum, cuts[0], *h_scratch),
        scatter_groups(net, d_small, small_sum, cuts[1], *s_scratch),
        tokens(),
        others(),
    )
    jobs.drain()
    pack(heads_sum[...], packs_heads, 0)
    pack(small_sum[...], packs_heads, heads_sum.shape[1])
    interleave(all_to_team(net, packs_heads, got_heads))
    net.finish()


def last_sums(part_n, x_rows, d_hidden, gain, d_heads, d_small, out_sum, ffn_sum, out_rows):
    two, n, width = d_hidden.shape
    d_heads, d_small = by_group(d_heads), by_group(d_small)
    r, w = d_heads.shape[3:]
    cuts = [(0, w // 2, w), (0, HD, HD)]
    rows = SHAPE((two, n, width), BF16)
    packs = [(8, 16, w + HD), (8, 16, out_sum.shape[1] + ffn_sum.shape[1])]
    return pl.pallas_call(
        functools.partial(last_kernel, cuts),
        out_shape=[rows, rows] + [SHAPE(a, BF16) for a in packs],
        in_specs=[ANY, VMEM, VMEM, VMEM, ANY, ANY, VMEM, VMEM, ANY],
        out_specs=[ANY] * 4,
        scratch_shapes=[
            pltpu.VMEM((two, n, width), BF16),
            pltpu.VMEM((r, w), BF16),
            pltpu.VMEM((r, HD), BF16),
        ]
        + [pltpu.VMEM(a, BF16) for a in packs]
        + scatter_team_scratch(n, width)
        + scatter_groups_scratch(r, cuts[0])
        + scatter_groups_scratch(r, cuts[1])
        + sems(
            SCATTER_TEAM + 2 * SCATTER_GROUPS + 2 * TO_TEAM + 2,
            SCATTER_TEAM_LOADS + 2 * SCATTER_GROUPS_LOADS + 4,
        ),
        compiler_params=params(5),
        name="last_sums",
    )(part_n, x_rows, d_hidden, gain, d_heads, d_small, out_sum, ffn_sum, out_rows)


def unpack_kernel(heads, rest, rows_in, tokens_in, down_in, *outs):
    kinds, gate, up, small, rows, tokens, down = outs[:5], outs[5], outs[6], outs[7], outs[8], outs[9], outs[10]
    share = small.shape[0]
    for n, out in enumerate(kinds):
        src, at = (rest, 0) if n == 4 else (heads, n * OUT_W)
        for x in range(4):
            for j in range(3):
                t, col = 2 * x + j // 2, at + (j % 2) * HD
                head = 3 * x + j
                out[:, head * HD : (head + 1) * HD] = src[t, :share, col : col + HD].astype(F32)
    total = heads[0, :, HEADS_W : HEADS_W + SMALL_W].astype(F32)
    for t in range(1, 8):
        total = total + heads[t, :, HEADS_W : HEADS_W + SMALL_W].astype(F32)
    small[...] = total[:share]
    for n, out in enumerate((gate, up)):
        for tile in range(32):
            e = tile // 2
            col = OUT_W + n * 4 * HD + (e // 4) * HD
            parts = [
                (rest[t, :, col : col + HD].astype(F32), e % 4)
                for t in range(4 * (tile % 2), 4 * (tile % 2) + 4)
            ]
            out[:, tile * HD : (tile + 1) * HD] = shift_pieces(parts)[:share]
    rows[...] = rows_in[...]
    tokens[...] = tokens_in[...]
    down[...] = down_in[...]


def unpack(heads, rest, rows, tokens, down, share, ff):
    two, n, width = rows.shape
    return pl.pallas_call(
        unpack_kernel,
        out_shape=[SHAPE((share, width), F32)] * 5
        + [SHAPE((share, ff), F32)] * 2
        + [SHAPE((share, HD), F32)]
        + [SHAPE(rows.shape, BF16)] * 2
        + [SHAPE(down.shape, F32)],
        in_specs=[VMEM] * 5,
        out_specs=[VMEM] * 11,
        compiler_params=pltpu.CompilerParams(vmem_limit_bytes=VM),
        name="unpack",
    )(heads, rest, rows, tokens, down)


def dot_nn(a, b):
    return lax.dot_general(a, b, (((1,), (0,)), ((), ())), preferred_element_type=F32)


def dot_nt(a, b):
    return lax.dot_general(a, b, (((1,), (1,)), ((), ())), preferred_element_type=F32)


def dot_tn(a, b):
    return lax.dot_general(a, b, (((0,), (0,)), ((), ())), preferred_element_type=F32)


def split_rows(partial):
    return partial.astype(BF16).reshape(2, 8, -1, partial.shape[1])


def per_device(
    tokens,
    doc_start,
    gain_attn,
    w_query,
    w_key,
    w_value,
    w_path,
    conv_path,
    w_beta,
    w_out,
    gain_ffn,
    w_gate,
    w_up,
    w_down,
    grad_out,
):
    zh, chip, core = lax.axis_index("zh"), lax.axis_index("x"), lax.axis_index("c")
    width = tokens.shape[2]
    share = w_query.shape[0]
    head_a, head_b = 3 * chip + 2 * core, 3 * chip + 1
    owns_b = core == 0

    small = jnp.concatenate([gain_attn[:, None], gain_ffn[:, None], conv_path.T, w_beta], axis=1)
    small = jnp.pad(small, ((0, 0), (0, SMALL_W - small.shape[1])))
    x_rows, g_rows, x_all, whole, own_ffn = start(
        (w_query, w_key, w_value, w_path, w_out), w_gate, w_up, small, tokens, grad_out
    )
    w_ext = whole[:, : HEADS_W + SMALL_W]
    gain_a, gain_f = (whole[:, HEADS_W + n].astype(F32) for n in range(2))
    doc_rows = jnp.cumsum(doc_start, axis=1)
    docs = jnp.where(zh == 0, doc_rows[0], doc_rows[1]).astype(F32)
    marks = [docs]
    for tap in range(1, TAPS):
        same = docs[: SEQ - tap] == docs[tap:]
        marks.append(jnp.concatenate([jnp.zeros((tap,), F32), same.astype(F32)]))
    drow = jnp.stack(marks + marks)
    marks = drow.T

    def own_heads(v):
        return jnp.where((jnp.arange(2 * HD) < HD) | owns_b, v, 0.0)

    normed_all, qkvp, raw, vec, o, mixed, *saved, w_ffn, g_all, w_out_t, part = attn_fwd(
        x_all.reshape(SEQ, width), whole, marks, drow, own_ffn, g_rows
    )
    g_all = g_all.reshape(SEQ, width)
    hidden, ffn_all, w_down_t = ffn_in(part, x_rows, gain_f[None], w_down)
    ffn_all = ffn_all.reshape(SEQ, width)
    gate_up = dot_nn(ffn_all, w_ffn)
    half = gate_up.shape[1] // 2

    def gated(pre):
        return jax.nn.silu(pre[:, :half]) * pre[:, half:]

    act_f, act_pull = jax.vjp(gated, gate_up)
    act = act_f.astype(BF16)
    out_part = split_rows(dot_nn(act, w_down_t))

    (d_gate_up,) = act_pull(dot_nt(g_all, w_down_t))
    d_gate_up = d_gate_up.astype(BF16)
    d_hidden, d_gain_ffn, branch_all, d_down = ffn_back(
        split_rows(dot_nt(d_gate_up, w_ffn)),
        hidden,
        gain_f[None],
        g_rows,
        dot_tn(act, g_all).astype(BF16),
    )
    d_ffn = dot_tn(ffn_all, d_gate_up).astype(BF16)
    branch_all = branch_all.reshape(SEQ, width)
    d_mixed = own_heads(dot_nt(branch_all, w_out_t))
    d_out = dot_tn(mixed, branch_all).astype(BF16)
    d_ext, d_conv, out_rows, ffn_sum, out_sum = attn_bwd(
        marks, w_ext[:, HEADS_W:], (qkvp, raw, vec, o, d_mixed, *saved), d_ffn, out_part, hidden, d_out
    )
    norm_part = dot_nt(d_ext, w_ext).astype(BF16)
    d_gain_attn = jnp.sum(norm_part.astype(F32) * normed_all.astype(F32), axis=0) / gain_a

    d_heads = dot_tn(normed_all, d_ext[:, :HEADS_W]).astype(BF16)
    conv_rows = jnp.zeros((width, TAPS), F32)
    conv_rows = lax.dynamic_update_slice_in_dim(conv_rows, d_conv[1, :TAPS].T, head_b * HD, 0)
    conv_rows = lax.dynamic_update_slice_in_dim(conv_rows, d_conv[0, :TAPS].T, head_a * HD, 0)
    small_back = jnp.concatenate([d_gain_attn[:, None], d_gain_ffn.T, conv_rows], axis=1)
    small_back = jnp.pad(small_back, ((0, 0), (0, SMALL_W - small_back.shape[1])))
    d_small = (dot_tn(normed_all, d_ext[:, HEADS_W:]) + small_back).astype(BF16)
    output, d_tokens, heads_back, rest_back = last_sums(
        split_rows(norm_part), x_rows, d_hidden, gain_a[None], d_heads, d_small, out_sum, ffn_sum, out_rows
    )
    *kinds, d_gate_w, d_up_w, small, output, d_tokens, d_down = unpack(
        heads_back, rest_back, output, d_tokens, d_down, share, w_gate.shape[1]
    )
    return (
        output,
        d_tokens,
        small[:, 0],
        *kinds[:4],
        small[:, 2:6].T,
        small[:, 6:18],
        kinds[4],
        small[:, 1],
        d_gate_w,
        d_up_w,
        d_down,
    )


def solution(mesh):
    names = ("zl", "y", "zh", "x", "c")
    fine = Mesh(mesh.devices.reshape(2, 4, 2, 4, 2), names)
    dp, ctx = names[:2], names[2:]
    rows, flat, mat, taps = P(dp, ctx, None), P(names), P(names, None), P(None, names)
    return jax.shard_map(
        per_device,
        mesh=fine,
        in_specs=(
            rows, P(dp, None), flat, mat, mat, mat, mat, taps, mat, mat, flat, mat, mat, mat, rows,
        ),
        out_specs=(
            rows, rows, flat, mat, mat, mat, mat, taps, mat, mat, flat, mat, mat, mat,
        ),
        check_vma=False,
    )
```

```python
import functools

import jax
import jax.numpy as jnp
from jax import lax
from jax.experimental import pallas as pl
from jax.experimental.pallas import tpu as pltpu
from jax.sharding import Mesh, PartitionSpec as P

F32, BF16 = jnp.float32, jnp.bfloat16
VM = 61 * 1024 * 1024

SEQ, HD, BLK = 1024, 128, 128
NB = SEQ // BLK
NQC = (NB * (NB - 1) // 2) * BLK
SCALE = HD ** (-0.5)
GROUP = 4


def mm(a, b, dims=((1,), (0,))):
    return lax.dot_general(
        a.astype(BF16), b.astype(BF16), (dims, ((), ())), preferred_element_type=F32
    )


def mm_nt(a, b):
    return mm(a, b, ((1,), (1,)))


def mm_tn(a, b):
    return mm(a, b, ((0,), (0,)))


def split(a):
    high = a.astype(BF16)
    return high, (a - high.astype(F32)).astype(BF16)


def mm3(a, b):
    ah, al = split(a)
    bh, bl = split(b)
    return mm(ah, bh) + (mm(ah, bl) + mm(al, bh))


def iota2(axis):
    return lax.broadcasted_iota(jnp.int32, (BLK, BLK), axis)


BASE = 16


def unit_inverses(lowers):
    row, col = iota2(0), iota2(1)
    eye = (row == col).astype(F32)
    in_base = (row // BASE) == (col // BASE)
    narrow = [jnp.where(in_base, low, 0.0) for low in lowers]
    inv = [eye for _ in lowers]
    for u in range(BASE - 1):
        pick = (col % BASE) == u
        coef = [jnp.sum(jnp.where(pick, low, 0.0), axis=1, keepdims=True) for low in narrow]
        for n, (t, c) in enumerate(zip(inv, coef)):
            t3 = t.reshape(BLK // BASE, BASE, BLK)
            lead = jnp.broadcast_to(t3[:, u : u + 1, :], t3.shape).reshape(BLK, BLK)
            inv[n] = t - c * lead
    size = BASE
    while size < BLK:
        off = ((row // (2 * size)) == (col // (2 * size))) & ((row // size) != (col // size))
        mid = [mm3(t, jnp.where(off, low, 0.0)) for t, low in zip(inv, lowers)]
        inv = [t - mm3(m, t) for t, m in zip(inv, mid)]
        size *= 2
    return inv


def betas_of(raw, head):
    lane = lax.broadcasted_iota(jnp.int32, raw.shape, 1)
    return 2.0 * jax.nn.sigmoid(
        jnp.sum(jnp.where(lane == head + BETA_AT, raw, 0.0), axis=1, keepdims=True)
    )


BETA_AT = 6
CONV_AT = 2
TAPS = 4


def conv_weights(small, head):
    part = small[pl.ds(pl.multiple_of(head * HD, HD), HD), :].astype(F32)
    return part.T[CONV_AT : CONV_AT + TAPS, :]


def convolve(path, taps, marks):
    total = taps[0:1, :] * path
    for m in range(1, TAPS):
        total = total + taps[m : m + 1, :] * (pltpu.roll(path, m, 0) * marks[:, m : m + 1])
    return total


def own_blocks(s, q, k, w, bcol, stores):
    t_out, a_out, z_out, m_out, kp_out, qm_buf, s_buf = stores
    row, col = iota2(0), iota2(1)
    strict, closed = row > col, row >= col
    eye = (row == col).astype(F32)

    def group(g, carry):
        sl = [pl.ds(pl.multiple_of((g * GROUP + n) * BLK, BLK), BLK) for n in range(GROUP)]
        qs = [q[r, :] for r in sl]
        ks = [k[r, :] for r in sl]
        ws = [w[r, :] for r in sl]
        bc = [jnp.broadcast_to(bcol[r, :], (BLK, BLK)) for r in sl]
        br = [b.T for b in bc]
        low = [jnp.where(strict, mm_nt(x, x), 0.0) * b for x, b in zip(ws, br)]
        inv = unit_inverses(low)
        m1 = [jnp.where(strict, mm_nt(x, y), 0.0) for x, y in zip(ws, ks)]
        gq = [jnp.where(closed, mm_nt(x, y), 0.0) * b for x, y, b in zip(qs, ws, br)]
        a = [mm(x, t) for x, t in zip(gq, inv)]
        z = [mm_tn(t, b * x.astype(F32)) for t, b, x in zip(inv, bc, ws)]
        sd = [mm_nt(x, y) - mm(p, m) for x, y, p, m in zip(qs, ks, a, m1)]
        qm = [x.astype(F32) - mm(p, y) for x, p, y in zip(qs, a, ws)]
        kmt = [x.astype(F32).T - mm_tn(zz, m) for x, zz, m in zip(ks, z, m1)]
        pm = [eye - mm_tn(zz, x) for zz, x in zip(z, ws)]
        for n, r in enumerate(sl):
            t_out[s, r, :] = inv[n].astype(t_out.dtype)
            a_out[s, r, :] = a[n].astype(a_out.dtype)
            z_out[s, r, :] = z[n].astype(z_out.dtype)
            m_out[s, r, :] = m1[n].astype(m_out.dtype)
            kp_out[s, r, :HD] = kmt[n].astype(BF16)
            kp_out[s, r, HD:] = pm[n].astype(BF16)
            qm_buf[r, :] = qm[n]
            s_buf[r, r] = sd[n]
        return carry

    lax.fori_loop(0, NB // GROUP, group, 0)


def sweep(s, qc, kp, qm_buf, x_buf, s_buf):
    at = NQC
    for j in range(NB - 2, -1, -1):
        r0 = (j + 1) * BLK
        rows = SEQ - r0
        x_buf[r0 : r0 + BLK, :] = qm_buf[r0 : r0 + BLK, :]
        x = x_buf[r0:, :].astype(BF16)
        at -= rows
        qc[s, at : at + rows, :] = x
        both = mm(x, kp[s, j * BLK : r0, :])
        s_buf[r0:, j * BLK : r0] = both[:, :HD]
        x_buf[r0:, :] = both[:, HD:]


def weigh(s, v, dcol, drow, s_buf, probs, o):
    for i in range(NB):
        lo, width = i * BLK, (i + 1) * BLK
        t = s_buf[lo:width, :width] * SCALE
        seen = dcol[lo:width, 0:1] == drow[0:1, :width]
        seen = seen & (
            lax.broadcasted_iota(jnp.int32, (BLK, width), 0) + lo
            >= lax.broadcasted_iota(jnp.int32, (BLK, width), 1)
        )
        t = jnp.where(seen, t, -1e30)
        e = jnp.exp(t - jnp.max(t, axis=1, keepdims=True))
        p = (e * (1.0 / jnp.sum(e, axis=1, keepdims=True))).astype(BF16)
        probs[s, lo:width, :width] = p
        o[lo:width, :] = mm(p, v[:width, :])


def project(x_all, whole, gains, normed, qkvp, raw):
    rows = 256
    width = x_all.shape[1]
    for n in range(width // HD):
        cols = slice(n * HD, (n + 1) * HD)
        gains[:, cols] = whole[cols, 8 * HD : 9 * HD].astype(F32).T[:8, :]

    def block(i, carry):
        at = pl.ds(pl.multiple_of(i * rows, rows), rows)
        x = x_all[at, :].astype(F32)
        scale = lax.rsqrt(jnp.mean(x * x, axis=1, keepdims=True) + 1e-05)
        n = (x * scale * gains[0:1, :]).astype(BF16)
        normed[at, :] = n
        y = mm(n, whole[:, : 9 * HD])
        qkvp[at, :] = y[:, : 8 * HD].astype(BF16)
        raw[at, :] = y[:, 8 * HD :]
        return carry

    lax.fori_loop(0, SEQ // rows, block, 0)


def heads_here():
    chip, core = lax.axis_index("x"), lax.axis_index("c")
    return 3 * chip + 2 * core, 3 * chip + 1


def fwd_slot(poke, s, head, small, marks, drow, qkvp, raw, vec, o, probs, qc, t_out, a_out, z_out, m_out, kp_out, s_buf, x_buf, qm_buf, b_buf):
    cols = slice(s * HD, (s + 1) * HD)
    q, k, v, path = (qkvp.at[:, (4 * s + n) * HD : (4 * s + n + 1) * HD] for n in range(4))
    taps = conv_weights(small, head)
    conved = convolve(path[...].astype(F32), taps, marks[...])
    unit = conved * lax.rsqrt(jnp.sum(conved * conved, axis=1, keepdims=True) + 1e-06)
    vec[:, cols] = unit.astype(BF16)
    b_buf[...] = betas_of(raw[...], head)
    own_blocks(s, q, k, vec.at[:, cols], b_buf, (t_out, a_out, z_out, m_out, kp_out, qm_buf, s_buf))
    poke()
    sweep(s, qc, kp_out, qm_buf, x_buf, s_buf)
    poke()
    weigh(s, v, marks, drow, s_buf, probs, o.at[:, cols])


def score_grads(s, v, o, do, probs, ds_buf, dv):
    for i in range(NB):
        lo, width = i * BLK, (i + 1) * BLK
        p = probs[0, lo:width, :width].astype(F32)
        g = do[lo:width, :]
        delta = jnp.sum(g * o[lo:width, :], axis=1, keepdims=True)
        ds = p * (mm_nt(g, v[:width, :]) - delta) * SCALE
        ds_buf[lo:width, :width] = ds.astype(BF16)
    for j in range(NB):
        lo = j * BLK
        dv[lo : lo + BLK, :] = mm_tn(probs[0, lo:, lo : lo + BLK], do[lo:, :]).astype(dv.dtype)


def sweep_back(s, qc, kp, ds_buf, x_buf, dkm_buf, dpm_buf):
    x_buf[...] = jnp.zeros_like(x_buf)
    dkm_buf[SEQ - BLK :, :] = jnp.zeros((BLK, HD), F32)
    dpm_buf[SEQ - BLK :, :] = jnp.zeros((BLK, HD), F32)
    at = 0
    for j in range(NB - 1):
        lo, r0 = j * BLK, (j + 1) * BLK
        rows = SEQ - r0
        x = x_buf[r0:, :].astype(BF16)
        ds = ds_buf[r0:, lo:r0]
        qcj = qc[0, at : at + rows, :]
        at += rows
        both = mm_tn(qcj, jnp.concatenate([x, ds], axis=1))
        dpm_buf[lo:r0, :] = both[:, :HD]
        dkm_buf[lo:r0, :] = both[:, HD:].T
        x_buf[r0:, :] = mm_nt(jnp.concatenate([ds, x], axis=1), kp[0, lo:r0, :])


def own_blocks_back(s, q, k, w, bcol, saved, bufs, dq, dk, dw, db):
    t_in, a_in, z_in, m_in = saved
    ds_buf, x_buf, dkm_buf, dpm_buf = bufs
    row, col = iota2(0), iota2(1)
    strict, closed = row > col, row >= col

    def group(g, carry):
        sl = [pl.ds(pl.multiple_of((g * GROUP + n) * BLK, BLK), BLK) for n in range(GROUP)]
        rng = range(GROUP)
        Q = [q[r, :] for r in sl]
        K = [k[r, :] for r in sl]
        W = [w[r, :] for r in sl]
        bc = [jnp.broadcast_to(bcol[r, :], (BLK, BLK)) for r in sl]
        br = [b.T for b in bc]
        E = [ds_buf[r, r] for r in sl]
        T = [t_in[0, r, :] for r in sl]
        A = [a_in[0, r, :] for r in sl]
        Z = [z_in[0, r, :] for r in sl]
        M = [m_in[0, r, :] for r in sl]
        dQm = [x_buf[r, :] for r in sl]
        dKm = [dkm_buf[r, :] for r in sl]
        dPm = [dpm_buf[r, :] for r in sl]
        i1 = [mm_nt(W[n], W[n]) for n in rng]
        qw = [jnp.where(closed, mm_nt(Q[n], W[n]), 0.0) for n in rng]
        dA = [-(mm_nt(E[n], M[n]) + mm_nt(dQm[n], W[n])) for n in rng]
        dM = [jnp.where(strict, -(mm_tn(A[n], E[n]) + mm_nt(Z[n], dKm[n])), 0.0) for n in rng]
        dZ = [-(mm(M[n], dKm[n]) + mm_nt(W[n], dPm[n])) for n in rng]
        dW = [-(mm_tn(A[n], dQm[n]) + mm(Z[n], dPm[n])) for n in rng]
        dG = [jnp.where(closed, mm_nt(dA[n], T[n]), 0.0) for n in rng]
        bw = [bc[n] * W[n].astype(F32) for n in rng]
        dT = [mm_tn(qw[n] * br[n], dA[n]) + mm_nt(bw[n], dZ[n]) for n in rng]
        dBW = [mm(T[n], dZ[n]) for n in rng]
        dL = [mm_tn(T[n], dT[n]) for n in rng]
        dL = [jnp.where(strict, -mm_nt(dL[n], T[n]), 0.0) for n in rng]
        dI = [dL[n] * br[n] for n in rng]
        R = [dG[n] * br[n] for n in rng]
        for n, r in enumerate(sl):
            db[r, :] = jnp.sum(
                (dL[n] * i1[n] + dG[n] * qw[n]).T + dBW[n] * W[n].astype(F32), axis=1, keepdims=True
            )
            dq[r, :] = (dQm[n] + mm(E[n], K[n]) + mm(R[n], W[n])).astype(dq.dtype)
            dk[r, :] = (dKm[n] + mm_tn(E[n], Q[n]) + mm_tn(dM[n], W[n])).astype(dk.dtype)
            dw[r, :] = (
                dW[n]
                + bc[n] * dBW[n]
                + mm_tn(R[n], Q[n])
                + mm(dM[n], K[n])
                + mm(dI[n] + dI[n].T, W[n])
            )
        return carry

    lax.fori_loop(0, NB // GROUP, group, 0)


def bwd_slot(poke, s, head, qkvp, raw, small, marks, vec, o, do, probs, qc, t_in, a_in, z_in, m_in, kp, d_ext, d_conv, ds_buf, x_buf, dkm_buf, dpm_buf, b_buf, db_buf, dw_buf):
    cols = slice(s * HD, (s + 1) * HD)
    q, k, v, path = (qkvp.at[:, (4 * s + n) * HD : (4 * s + n + 1) * HD] for n in range(4))
    dq, dk, dv, dpath = (d_ext.at[:, (4 * s + n) * HD : (4 * s + n + 1) * HD] for n in range(4))
    score_grads(s, v, o.at[:, cols], do.at[:, cols], probs, ds_buf, dv)
    poke()
    sweep_back(s, qc, kp, ds_buf, x_buf, dkm_buf, dpm_buf)
    poke()
    beta = betas_of(raw[...], head)
    b_buf[...] = beta
    own_blocks_back(
        s, q, k, vec.at[:, cols], b_buf, (t_in, a_in, z_in, m_in), (ds_buf, x_buf, dkm_buf, dpm_buf), dq, dk, dw_buf, db_buf
    )
    poke()
    taps = conv_weights(small, head)
    raw_path = path[...].astype(F32)
    conved = convolve(raw_path, taps, marks[...])
    scale = lax.rsqrt(jnp.sum(conved * conved, axis=1, keepdims=True) + 1e-06)
    unit = conved * scale
    dw = dw_buf[...]
    d_conved = scale * (dw - unit * jnp.sum(dw * unit, axis=1, keepdims=True))
    total = taps[0:1, :] * d_conved
    d_conv[s, 0:1, :] = jnp.sum(d_conved * raw_path, axis=0, keepdims=True)
    for m in range(1, TAPS):
        marked = d_conved * marks[:, m : m + 1]
        d_conv[s, m : m + 1, :] = jnp.sum(marked * pltpu.roll(raw_path, m, 0), axis=0, keepdims=True)
        total = total + taps[m : m + 1, :] * pltpu.roll(marked, SEQ - m, 0)
    dpath[...] = total.astype(dpath.dtype)
    lane = lax.broadcasted_iota(jnp.int32, (SEQ, HD), 1)
    return jnp.where(lane == head + BETA_AT, db_buf[...] * beta * (1.0 - 0.5 * beta), 0.0)


def fwd_shapes(width):
    return [
        ((SEQ, width), BF16),
        ((SEQ, 8 * HD), BF16),
        ((SEQ, HD), F32),
        ((SEQ, 2 * HD), BF16),
        ((SEQ, 2 * HD), F32),
        ((SEQ, 2 * HD), BF16),
        ((8, width), F32),
        ((2, SEQ, SEQ), BF16),
        ((2, NQC, HD), BF16),
        ((2, SEQ, BLK), BF16),
        ((2, SEQ, BLK), BF16),
        ((2, SEQ, BLK), BF16),
        ((2, SEQ, BLK), BF16),
        ((2, SEQ, 2 * HD), BF16),
    ]


def fwd_scratch():
    return [
        pltpu.VMEM((SEQ, SEQ), F32),
        pltpu.VMEM((SEQ, HD), F32),
        pltpu.VMEM((SEQ, HD), F32),
        pltpu.VMEM((SEQ, 1), F32),
    ]


def bwd_scratch():
    return (
        [pltpu.VMEM((SEQ, SEQ), BF16)]
        + [pltpu.VMEM((SEQ, HD), F32)] * 3
        + [pltpu.VMEM((SEQ, 1), F32)] * 2
        + [pltpu.VMEM((SEQ, HD), F32)]
    )


MESH = pl.DeviceIdType.MESH
ANY = pl.BlockSpec(memory_space=pl.ANY)
VMEM = pl.BlockSpec(memory_space=pltpu.VMEM)


class Place:
    def __init__(self):
        self.x, self.c = lax.axis_index("x"), lax.axis_index("c")
        self.y = lax.axis_index("y")
        self.zl, self.zh = lax.axis_index("zl"), lax.axis_index("zh")
        self.z = self.zh * 2 + self.zl

    def chip(self, d):
        return lax.rem(self.x + d, 4)

    def at_x(self, d):
        return {"x": lax.rem(self.x + d, 4)}

    def at_xc(self, d, k):
        return {"x": lax.rem(self.x + d, 4), "c": lax.rem(self.c + k, 2)}

    def sibling(self):
        return {"c": 1 - self.c}

    def at_y(self, d):
        return {"y": lax.rem(self.y + d, 4)}

    def at_z(self, d):
        z = lax.rem(self.z + d, 4)
        return {"zl": lax.rem(z, 2), "zh": z // 2}


class Net:
    def __init__(self, send_sem, recv_sem, local_sem):
        self.place = Place()
        self.send_sem, self.recv_sem, self.local_sem = send_sem, recv_sem, local_sem
        self.count, self.kept, self.locals, self.sent = 0, 0, [], []

    def prepare(self, src, dst, device):
        k = self.count
        self.count += 1
        return pltpu.make_async_remote_copy(
            src_ref=src,
            dst_ref=dst,
            send_sem=self.send_sem.at[k],
            recv_sem=self.recv_sem.at[k],
            device_id=device,
            device_id_type=MESH,
        )

    def send(self, src, dst, device):
        copy = self.prepare(src, dst, device)
        copy.start()
        self.sent.append(copy)
        return copy

    def local(self, src, dst):
        self.kept += 1
        return pltpu.make_async_copy(src, dst, self.local_sem.at[self.kept - 1])

    def load(self, src, dst):
        copy = self.local(src, dst)
        copy.start()
        return copy

    def keep(self, src, dst):
        self.locals.append(self.load(src, dst))

    def settle(self):
        for copy in self.locals:
            copy.wait()
        self.locals = []

    def finish(self):
        for copy in self.sent:
            copy.wait_send()
        self.settle()


def meet(devices):
    barrier = pltpu.get_barrier_semaphore()
    for device in devices:
        pl.semaphore_signal(barrier, inc=1, device_id=device, device_id_type=MESH)
    pl.semaphore_wait(barrier, len(devices))


class Jobs:
    def __init__(self, *jobs):
        self.all = list(jobs)
        self.jobs = list(jobs)

    def poke(self):
        for job in list(self.jobs):
            try:
                next(job)
            except StopIteration:
                self.jobs.remove(job)

    def step(self, *which):
        for n in which:
            next(self.all[n], None)

    def drain(self):
        while self.jobs:
            self.poke()


def interleave(*jobs):
    Jobs(*jobs).drain()


def team_peers(p):
    return [p.at_x(1), p.at_x(3), p.sibling()]


def team_all(p):
    return [p.at_xc(d, k) for d in range(4) for k in range(2) if d + k]


def group_peers(p):
    return [p.at_y(d) for d in (1, 2, 3)] + [p.at_z(d) for d in (1, 2, 3)]


def gather_team(net, own, out):
    p = net.place
    me, sib = 2 * p.x + p.c, p.sibling()
    right, left = p.at_x(1), p.at_x(3)
    t_l, t_r, t_2 = (2 * p.chip(d) + p.c for d in (3, 1, 2))
    to_r = net.send(own, out.at[:, me], right)
    to_l = net.send(own, out.at[:, me], left)
    shared = [net.send(own, out.at[:, me], sib)]
    net.keep(own, out.at[:, me])
    yield
    to_r.wait_recv()
    on_r = net.send(out.at[0, t_l], out.at[0, t_l], right)
    shared.append(net.send(out.at[:, t_l], out.at[:, t_l], sib))
    to_l.wait_recv()
    on_l = net.send(out.at[1, t_r], out.at[1, t_r], left)
    shared.append(net.send(out.at[:, t_r], out.at[:, t_r], sib))
    yield
    on_r.wait_recv()
    shared.append(net.send(out.at[0, t_2], out.at[0, t_2], sib))
    on_l.wait_recv()
    shared.append(net.send(out.at[1, t_2], out.at[1, t_2], sib))
    yield
    for copy in shared:
        copy.wait_recv()


GATHER_TEAM = 10


def add(a, b):
    return (a.astype(F32) + b.astype(F32)).astype(BF16)


def scatter_team(net, part, got, total, from_l, from_r, all_l, all_r, finish):
    p = net.place
    sib, right, left = p.sibling(), p.at_x(1), p.at_x(3)
    order = (2, 1, 3, 0)
    swaps, loads = [], []
    for d in order:
        at = p.chip(d)
        swaps.append(net.send(part.at[:, 2 * at + 1 - p.c], got.at[:, at], sib))
        loads.append(net.load(part.at[:, 2 * at + p.c], total.at[:, at]))

    def pair(n):
        swaps[n].wait_recv()
        loads[n].wait()
        at = p.chip(order[n])
        total[:, at] = add(total[:, at], got[:, at])
        return at

    yield
    x_2 = pair(0)
    half_r = net.send(total.at[0, x_2], from_l, right)
    half_l = net.send(total.at[1, x_2], from_r, left)
    x_r = pair(1)
    rest_r = net.send(total.at[1, x_r], all_l.at[1], right)
    x_l = pair(2)
    rest_l = net.send(total.at[0, x_l], all_r.at[0], left)
    pair(3)
    yield
    half_r.wait_recv()
    total[0, x_r] = add(total[0, x_r], from_l[...])
    last_r = net.send(total.at[0, x_r], all_l.at[0], right)
    half_l.wait_recv()
    total[1, x_l] = add(total[1, x_l], from_r[...])
    last_l = net.send(total.at[1, x_l], all_r.at[1], left)
    yield
    for copy in (rest_r, rest_l, last_r, last_l):
        copy.wait_recv()
    finish(total[:, p.x].astype(F32) + all_l[...].astype(F32) + all_r[...].astype(F32))


SCATTER_TEAM_LOADS = 4
SCATTER_TEAM = 10


def scatter_team_scratch(n, w):
    return [
        pltpu.VMEM((2, 4, n, w), BF16),
        pltpu.VMEM((2, 4, n, w), BF16),
        pltpu.VMEM((n, w), BF16),
        pltpu.VMEM((n, w), BF16),
        pltpu.VMEM((2, n, w), BF16),
        pltpu.VMEM((2, n, w), BF16),
    ]


def chunk_rows(y, z, rows):
    zl, zh = (z % 2, z // 2) if isinstance(z, int) else (lax.rem(z, 2), z // 2)
    return pl.ds(pl.multiple_of(((zl * 4 + y) * 2 + zh) * rows, rows), rows)


def halves(cols):
    mid = cols // 2
    return [(pl.ds(0, mid),) * 2], [(pl.ds(mid, cols - mid),) * 2]


def gather_groups(net, own, out, y_pieces, z_pieces):
    p = net.place
    rows = own.shape[0]
    for src, dst in y_pieces + z_pieces:
        net.keep(own.at[:, src], out.at[chunk_rows(p.y, p.z, rows), dst])

    def spread(pieces, y, z, devices, first=False):
        copies = []
        for src, dst in pieces:
            place = out.at[chunk_rows(y, z, rows), dst]
            copies += [net.send(own.at[:, src] if first else place, place, d) for d in devices]
        return copies

    ys, zs = [p.at_y(d) for d in (1, 3, 2)], [p.at_z(d) for d in (1, 3, 2)]
    y_first = spread(y_pieces, p.y, p.z, ys, True)
    z_first = spread(z_pieces, p.y, p.z, zs, True)
    last = spread(y_pieces, p.y, p.z, zs, True) + spread(z_pieces, p.y, p.z, ys, True)
    yield
    for n, d in enumerate((1, 3, 2)):
        for copy in y_first[n::3]:
            copy.wait_recv()
        last += spread(y_pieces, lax.rem(p.y + 4 - d, 4), p.z, zs)
        for copy in z_first[n::3]:
            copy.wait_recv()
        last += spread(z_pieces, p.y, lax.rem(p.z + 4 - d, 4), ys)
        yield
    for copy in last:
        copy.wait_recv()


GATHER_GROUPS = 30


def scatter_groups(net, part, out, cuts, z_got, z_sum, z_last, y_got, y_sum, y_last):
    p = net.place
    lo, mid, hi = cuts
    first, second = pl.ds(lo, mid - lo), pl.ds(mid, hi - mid)
    rows = z_sum.shape[1]
    both = hi > mid
    flat = len(part.shape) == 2
    order = (2, 1, 3)
    a, b, a_own, b_own = [], [], [], []
    for n, d in enumerate(order):
        z, y = lax.rem(p.z + d, 4), lax.rem(p.y + d, 4)
        if flat:
            for k in range(4):
                a.append(net.send(part.at[chunk_rows(k, z, rows), first], z_got.at[n, k], p.at_z(d)))
                if both:
                    b.append(net.send(part.at[chunk_rows(y, k, rows), second], y_got.at[n, k % 2, k // 2], p.at_y(d)))
        else:
            a.append(net.send(part.at[lax.rem(z, 2), :, z // 2, :, first], z_got.at[n], p.at_z(d)))
            if both:
                b.append(net.send(part.at[:, y, :, :, second], y_got.at[n], p.at_y(d)))
    if flat:
        for k in range(4):
            a_own.append(net.load(part.at[chunk_rows(k, p.z, rows), first], z_sum.at[k]))
            if both:
                b_own.append(net.load(part.at[chunk_rows(p.y, k, rows), second], y_sum.at[k % 2, k // 2]))
    else:
        a_own.append(net.load(part.at[p.zl, :, p.zh, :, first], z_sum))
        if both:
            b_own.append(net.load(part.at[:, p.y, :, :, second], y_sum))

    yield
    for copy in a_own:
        copy.wait()
    for copy in a:
        copy.wait_recv()
    for y in range(4):
        t = z_sum[y].astype(F32)
        for n in range(3):
            t = t + z_got[n, y].astype(F32)
        z_sum[y] = t.astype(BF16)
    a = [
        net.send(z_sum.at[lax.rem(p.y + d, 4)], z_last.at[n], p.at_y(d)) for n, d in enumerate(order)
    ]
    if both:
        yield
        for copy in b_own:
            copy.wait()
        for copy in b:
            copy.wait_recv()
        for zl in range(2):
            for zh in range(2):
                t = y_sum[zl, zh].astype(F32)
                for n in range(3):
                    t = t + y_got[n, zl, zh].astype(F32)
                y_sum[zl, zh] = t.astype(BF16)
        b = []
        for n, d in enumerate(order):
            z = lax.rem(p.z + d, 4)
            b.append(net.send(y_sum.at[lax.rem(z, 2), z // 2], y_last.at[n], p.at_z(d)))
    yield
    for copy in a:
        copy.wait_recv()
    t = z_sum[p.y].astype(F32)
    for n in range(3):
        t = t + z_last[n].astype(F32)
    out[:, first] = t.astype(out.dtype)
    if both:
        yield
        for copy in b:
            copy.wait_recv()
        t = y_sum[p.zl, p.zh].astype(F32)
        for n in range(3):
            t = t + y_last[n].astype(F32)
        out[:, second] = t.astype(out.dtype)


SCATTER_GROUPS_LOADS = 2
SCATTER_GROUPS_FLAT_LOADS = 8
SCATTER_GROUPS = 12
SCATTER_GROUPS_FLAT = 30


def scatter_groups_scratch(r, cuts):
    a, b = cuts[1] - cuts[0], max(cuts[2] - cuts[1], HD)
    return [
        pltpu.VMEM((3, 4, r, a), BF16),
        pltpu.VMEM((4, r, a), BF16),
        pltpu.VMEM((3, r, a), BF16),
        pltpu.VMEM((3, 2, 2, r, b), BF16),
        pltpu.VMEM((2, 2, r, b), BF16),
        pltpu.VMEM((3, r, b), BF16),
    ]


def sems(remote, local):
    return [
        pltpu.SemaphoreType.DMA((remote,)),
        pltpu.SemaphoreType.DMA((remote,)),
        pltpu.SemaphoreType.DMA((max(local, 1),)),
    ]


def params(collective_id):
    return pltpu.CompilerParams(
        collective_id=collective_id, has_side_effects=True, vmem_limit_bytes=VM
    )


EPS_NORM = 1e-05
EPS_UNIT = 1e-06
SHAPE = jax.ShapeDtypeStruct


def all_to_team(net, packs, got):
    p = net.place
    me = 2 * p.x + p.c
    net.keep(packs.at[me], got.at[me])
    copies = []
    for d in (2, 1, 3, 0):
        for k in (1, 0):
            if d + k:
                to = 2 * p.chip(d) + lax.rem(p.c + k, 2)
                copies.append(net.send(packs.at[to], got.at[me], p.at_xc(d, k)))
    yield
    for copy in copies:
        copy.wait_recv()


TO_TEAM = 7


def swap_rows(net, pairs):
    p = net.place
    copies = []
    for src, dst in pairs:
        net.keep(src.at[p.zh], dst.at[p.zh])
        copies.append(net.send(src.at[1 - p.zh], dst.at[p.zh], p.at_z(2)))
    yield
    for copy in copies:
        copy.wait_recv()


def thin_rows(rows, padded):
    out = lax.broadcasted_iota(jnp.int32, (8 * rows, 8 * padded), 0)
    at = lax.broadcasted_iota(jnp.int32, (8 * rows, 8 * padded), 1)
    return ((out // rows == at // padded) & (out % rows == at % padded)).astype(BF16)


HEADS_W, SMALL_W = 8 * HD, HD
EXT_W = HEADS_W + SMALL_W
OUT_B, OUT_A = EXT_W, EXT_W + HD
WHOLE_W = EXT_W + 2 * HD
SHARED_W = 3 * HD
FIRST_W = 5 * HD + SHARED_W
PIECE = 32


def shift_pieces(tiles):
    lane = lax.broadcasted_iota(jnp.int32, tiles[0][0].shape, 1) // PIECE
    total = None
    for n, (tile, piece) in enumerate(tiles):
        turn = (PIECE * (n - piece)) % HD
        moved = pltpu.roll(tile, turn, 1) if turn else tile
        total = moved if total is None else jnp.where(lane == n, moved, total)
    return total


def pack_weights(kinds, gate_up, small, packs):
    share = small.shape[0]
    packs[...] = jnp.zeros_like(packs)
    for t in range(8):
        own, middle = 3 * (t // 2) + 2 * (t % 2), 3 * (t // 2) + 1
        parts = [w[:, own * HD : (own + 1) * HD] for w in kinds]
        shared = [w[:, middle * HD : (middle + 1) * HD] for w in kinds]
        shared = shared[:3] if t % 2 == 0 else [shared[3], small[...], shared[4]]
        for n, part in enumerate(parts + shared):
            packs[t, :share, n * HD : (n + 1) * HD] = part
    for n, w in enumerate(gate_up):
        for t in range(8):
            for j in range(4):
                tiles = []
                for e in range(4 * j, 4 * j + 4):
                    at = (2 * e + t // 4) * HD
                    tiles.append((w[:, at : at + HD].astype(F32), t % 4))
                at = FIRST_W + n * 4 * HD + j * HD
                packs[t, :share, at : at + HD] = shift_pieces(tiles).astype(BF16)


def start_kernel(wq, wk, wv, wp, wo, gate, up, small, tokens, grad_out, x_rows, g_rows, x_all, whole, own_ffn, packs, got, own, *sem):
    net = Net(*sem)
    p = net.place
    share = small.shape[0]
    pack_weights((wq, wk, wv, wp, wo), (gate, up), small, packs)
    meet(team_all(p) + group_peers(p))
    trade = all_to_team(net, packs, got)
    next(trade)
    swaps = swap_rows(net, ((tokens, x_rows), (grad_out, g_rows)))
    next(swaps)
    interleave(trade)
    net.settle()
    pick = thin_rows(share, packs.shape[1])
    own[...] = mm(pick, got[...].reshape(pick.shape[1], got.shape[2])).astype(BF16)
    net.keep(own.at[:, pl.ds(FIRST_W, own.shape[1] - FIRST_W)], own_ffn)
    shared = pl.ds(pl.multiple_of(4 * HD + p.c * SHARED_W, HD), SHARED_W)
    heads = gather_groups(
        net,
        own,
        whole,
        [(pl.ds(0, 4 * HD), pl.ds(0, 4 * HD))],
        [(pl.ds(4 * HD, HD), pl.ds(OUT_A, HD)), (pl.ds(5 * HD, SHARED_W), shared)],
    )
    next(heads)
    interleave(swaps)
    interleave(gather_team(net, x_rows, x_all), heads)
    net.settle()
    net.send(whole.at[:, shared], whole.at[:, shared], p.sibling()).wait_recv()
    net.finish()


def start(kinds, gate, up, small, tokens, grad_out):
    share, width = kinds[0].shape
    two, n, _ = tokens.shape
    rows = SHAPE(tokens.shape, BF16)
    cols = FIRST_W + gate.shape[1] // 4
    return pl.pallas_call(
        start_kernel,
        out_shape=[
            rows,
            rows,
            SHAPE((two, 8, n, width), BF16),
            SHAPE((width, WHOLE_W), BF16),
            SHAPE((8 * share, cols - FIRST_W), BF16),
        ],
        in_specs=[VMEM] * 8 + [ANY] * 2,
        out_specs=[ANY] * 5,
        scratch_shapes=[
            pltpu.VMEM((8, 16, cols), BF16),
            pltpu.VMEM((8, 16, cols), BF16),
            pltpu.VMEM((8 * share, cols), BF16),
        ]
        + sems(TO_TEAM + 2 + GATHER_TEAM + 3 * GATHER_GROUPS // 2 + 1, 8),
        compiler_params=params(1),
        name="start",
    )(*kinds, gate, up, small, tokens, grad_out)


def lanes(at):
    return pl.ds(pl.multiple_of(at * HD, HD), HD)


def trade_out(net, whole, w_out):
    p = net.place
    copies, own = [], []
    for d in (2, 1, 3, 0):
        for k in (1, 0):
            xd, cd = p.chip(d), lax.rem(p.c + k, 2)
            row_a, row_b = lanes(3 * xd + 2 * cd), lanes(3 * xd + 1)
            row_c = lanes(3 * xd + jnp.where(p.c == 0, 2 * cd, 1))
            col_a, col_b = lanes(3 * p.x + 2 * p.c), lanes(3 * p.x + 1)
            moves = (
                (whole.at[row_a, pl.ds(OUT_A, HD)], w_out.at[pl.ds(0, HD), col_a]),
                (whole.at[row_b, pl.ds(OUT_A, HD)], w_out.at[pl.ds(HD, HD), col_a]),
                (whole.at[row_c, pl.ds(OUT_B, HD)], w_out.at[lanes(p.c), col_b]),
            )
            for src, dst in moves:
                if d + k:
                    copies.append(net.send(src, dst, p.at_xc(d, k)))
                else:
                    own.append(net.load(src, dst))
    yield
    for copy in own:
        copy.wait()
    for copy in copies:
        copy.wait_recv()


def attn_fwd_kernel(x_all, whole, marks, drow, own_ffn, g_rows, *rest):
    kept, (w_ffn, g_all, w_out, part), rest = rest[:14], rest[14:18], rest[18:]
    bufs, (x_buf, w_buf, wo_buf, part_buf), rest = rest[:14], rest[14:18], rest[18:]
    normed, qkvp, raw, vec, o, mixed, gains, *saved = bufs
    net = Net(*rest[-3:])
    p = net.place
    loads = [net.load(whole.at[:, pl.ds(0, 9 * HD)], w_buf), net.load(x_all, x_buf)]
    meet(team_all(p) + group_peers(p))
    jobs = Jobs(
        gather_groups(net, own_ffn, w_ffn, *halves(own_ffn.shape[1])),
        trade_out(net, whole, wo_buf),
        gather_team(net, g_rows, g_all),
    )
    jobs.step(0, 1, 2)
    for copy in loads:
        copy.wait()
    project(x_buf, w_buf, gains, normed, qkvp, raw)
    for n in (0, 1, 2, 6):
        net.keep(bufs[n], kept[n])
    steps = [(0, 0, 0), (), (2,), (), (2,), (2, 0)]
    poke = lambda: jobs.step(*steps.pop(0)) if steps else None
    for s, head in enumerate(heads_here()):
        cols = pl.ds(s * HD, HD)
        poke()
        fwd_slot(poke, s, head, w_buf.at[:, pl.ds(8 * HD, HD)], marks, drow, qkvp, raw, vec, o, *saved, *rest[:-3])
        net.keep(vec.at[:, cols], kept[3].at[:, cols])
        net.keep(o.at[:, cols], kept[4].at[:, cols])
        for src, dst in zip(saved, kept[7:]):
            net.keep(src.at[s], dst.at[s])
    mixed[:, :HD] = o[:, :HD].astype(BF16)
    mixed[:, HD:] = jnp.where(p.c == 0, o[:, HD:], 0.0).astype(BF16)
    net.keep(mixed, kept[5])
    jobs.step(1, 1)
    net.keep(wo_buf, w_out)
    two, _, n, width = part.shape
    for h in range(two):
        for t in range(0, 8, 4):
            at = (h * 8 + t) * n
            y = mm(mixed[at : at + 4 * n, :], wo_buf[...]).astype(BF16)
            part_buf[h, t : t + 4] = y.reshape(4, n, width)
    net.keep(part_buf, part)
    jobs.drain()
    net.finish()


def attn_fwd(x_all, whole, marks, drow, own_ffn, g_rows):
    rows, cols = own_ffn.shape
    two, n, width = g_rows.shape
    kept = fwd_shapes(width)
    part = (two, 8, n, width)
    return pl.pallas_call(
        attn_fwd_kernel,
        out_shape=[SHAPE(*a) for a in kept]
        + [SHAPE((16 * rows, cols), BF16), SHAPE(part, BF16), SHAPE((2 * HD, width), BF16), SHAPE(part, BF16)],
        in_specs=[ANY, ANY, VMEM, VMEM, ANY, ANY],
        out_specs=[ANY] * (len(kept) + 4),
        scratch_shapes=[pltpu.VMEM(*a) for a in kept]
        + [
            pltpu.VMEM((SEQ, width), BF16),
            pltpu.VMEM((width, 9 * HD), BF16),
            pltpu.VMEM((2 * HD, width), BF16),
            pltpu.VMEM(part, BF16),
        ]
        + fwd_scratch()
        + sems(GATHER_TEAM + GATHER_GROUPS + 21, 2 + 6 + 4 + 18 + 3),
        compiler_params=params(7),
        name="attn_fwd",
    )(x_all, whole, marks, drow, own_ffn, g_rows)


def norm_back(v, gain, d_normed):
    scale = lax.rsqrt(jnp.mean(v * v, axis=-1, keepdims=True) + EPS_NORM)
    unit = v * scale
    d_unit = d_normed * gain
    d_v = scale * (d_unit - unit * jnp.mean(d_unit * unit, axis=-1, keepdims=True))
    return d_v, d_normed * unit


def by_group(a):
    return a.reshape(2, 4, 2, a.shape[0] // 16, a.shape[1])


def gather_blocks(net, own, out):
    p = net.place
    me, sib = 2 * p.x + p.c, p.sibling()
    right, left = p.at_x(1), p.at_x(3)
    t_l, t_r, t_2 = (2 * p.chip(d) + p.c for d in (3, 1, 2))
    to_r = net.send(own, out.at[:, me], right)
    to_l = net.send(own, out.at[:, me], left)
    shared = net.send(own, out.at[:, me], sib)
    kept = net.load(own, out.at[:, me])
    kept.wait()
    shared.wait_recv()
    yield 0
    to_r.wait_recv()
    on_r = net.send(out.at[0, t_l], out.at[0, t_l], right)
    from_l = net.send(out.at[:, t_l], out.at[:, t_l], sib)
    to_l.wait_recv()
    on_l = net.send(out.at[1, t_r], out.at[1, t_r], left)
    from_r = net.send(out.at[:, t_r], out.at[:, t_r], sib)
    from_l.wait_recv()
    yield 3
    from_r.wait_recv()
    yield 1
    on_r.wait_recv()
    low = net.send(out.at[0, t_2], out.at[0, t_2], sib)
    on_l.wait_recv()
    high = net.send(out.at[1, t_2], out.at[1, t_2], sib)
    low.wait_recv()
    high.wait_recv()
    yield 2


class TeamSum:
    def __init__(self, net, part, got, total, from_l, from_r, all_l, all_r):
        self.net, self.part, self.got, self.total = net, part, got, total
        self.from_l, self.from_r, self.all_l, self.all_r = from_l, from_r, all_l, all_r
        self.swaps, self.last = {}, []

    def ready(self, d):
        p = self.net.place
        at = p.chip(d)
        self.swaps[d] = self.net.send(
            self.part.at[:, 2 * at + 1 - p.c], self.got.at[:, at], p.sibling()
        )

    def pair(self, d):
        p = self.net.place
        at = p.chip(d)
        self.swaps[d].wait_recv()
        self.total[:, at] = add(self.part[:, 2 * at + p.c], self.got[:, at])
        return at

    def near(self):
        net, p = self.net, self.net.place
        self.x_r = self.pair(1)
        self.last.append(net.send(self.total.at[1, self.x_r], self.all_l.at[1], p.at_x(1)))
        self.x_l = self.pair(3)
        self.last.append(net.send(self.total.at[0, self.x_l], self.all_r.at[0], p.at_x(3)))

    def far(self):
        net, p = self.net, self.net.place
        x_2 = self.pair(2)
        self.half_r = net.send(self.total.at[0, x_2], self.from_l, p.at_x(1))
        self.half_l = net.send(self.total.at[1, x_2], self.from_r, p.at_x(3))

    def on(self):
        net, p = self.net, self.net.place
        self.half_r.wait_recv()
        self.total[0, self.x_r] = add(self.total[0, self.x_r], self.from_l[...])
        self.last.append(net.send(self.total.at[0, self.x_r], self.all_l.at[0], p.at_x(1)))
        self.half_l.wait_recv()
        self.total[1, self.x_l] = add(self.total[1, self.x_l], self.from_r[...])
        self.last.append(net.send(self.total.at[1, self.x_l], self.all_r.at[1], p.at_x(3)))

    def result(self):
        for copy in self.last:
            copy.wait_recv()
        mine = self.total[:, self.net.place.x].astype(F32)
        return mine + self.all_l[...].astype(F32) + self.all_r[...].astype(F32)


def ffn_kernel(cuts, *refs):
    (part, x_rows, g_rows, gain, own_down, w_ffn, g_all), refs = refs[:7], refs[7:]
    (hidden, d_hidden, d_gain, branch_all, out_part, ffn_sum, down_out), refs = refs[:7], refs[7:]
    (w_in, w_down, g_buf, nf_all, normed, act, d_in, back, branch, d_ffn, d_down, out_buf), refs = refs[:12], refs[12:]
    scratch = [refs[6 * n : 6 * n + 6] for n in range(3)]
    net = Net(*refs[-3:])
    p = net.place
    loads = [net.load(w_ffn, w_in), net.load(g_all, g_buf)]
    meet(team_peers(p) + group_peers(p))
    two, _, n, width = part.shape
    half = w_down.shape[0]

    def finish(sums):
        h = x_rows[...].astype(F32) + sums
        hidden[...] = h
        scale = lax.rsqrt(jnp.mean(h * h, axis=-1, keepdims=True) + EPS_NORM)
        normed[...] = (h * scale * gain[1:2, :][None]).astype(BF16)

    Jobs(
        scatter_team(net, part, *scratch[0], finish),
        gather_groups(net, own_down, w_down, *halves(width)),
    ).drain()
    for copy in loads:
        copy.wait()
    net.settle()
    sums = TeamSum(net, back, *scratch[1])

    def flat(ref, at):
        return ref[:, pl.ds(2 * at, 2)].reshape(4 * n, ref.shape[3])

    def work(at):
        pre = mm(flat(nf_all, at), w_in[...])
        gate, up = pre[:, :half], pre[:, half:]
        sig = jax.nn.sigmoid(gate)
        silu = gate * sig
        act[:, pl.ds(2 * at, 2)] = (silu * up).astype(BF16).reshape(two, 2, n, half)
        d_act = mm_nt(flat(g_buf, at), w_down[...])
        d_gate = (d_act * up * (sig + silu * (1.0 - sig))).astype(BF16)
        d_up = (d_act * silu).astype(BF16)
        d_pre = jnp.concatenate([d_gate, d_up], axis=1)
        d_in[:, pl.ds(2 * at, 2)] = d_pre.reshape(two, 2, n, 2 * half)
        back[:, pl.ds(2 * at, 2)] = mm_nt(d_pre, w_in[...]).astype(BF16).reshape(two, 2, n, width)

    for d in gather_blocks(net, normed, nf_all):
        if d == 2:
            sums.near()
        work(p.chip(d))
        sums.ready(d)
    sums.far()
    sums.pair(0)
    rows = two * 8 * n
    step = width // 4
    for k in range(4):
        cols = slice(k * step, (k + 1) * step)
        left = nf_all[:, :, :, cols].reshape(rows, step)
        d_ffn[cols, :] = mm_tn(left, d_in[...].reshape(rows, 2 * half)).astype(BF16)
        if k == 2:
            sums.on()
    jobs = Jobs(scatter_groups(net, d_ffn, ffn_sum, cuts, *scratch[2]))
    jobs.poke()
    step = half // 2
    for k in range(2):
        cols = slice(k * step, (k + 1) * step)
        left = act[:, :, :, cols].reshape(rows, step)
        d_down[cols, :] = mm_tn(left, g_buf[...].reshape(rows, width)).astype(BF16)
    d_h, d_g = norm_back(hidden[...], gain[1:2, :][None], sums.result())
    d_h = d_h + g_rows[...].astype(F32)
    d_hidden[...] = d_h
    branch[...] = d_h.astype(BF16)
    d_gain[...] = jnp.sum(jnp.sum(d_g, axis=0), axis=0, keepdims=True)
    team = gather_team(net, branch, branch_all)
    next(team)
    net.keep(d_down, down_out)
    for h in range(two):
        for t in range(0, 8, 4):
            left = act[h, t : t + 4].reshape(4 * n, half)
            out_buf[h, t : t + 4] = mm(left, w_down[...]).astype(BF16).reshape(4, n, width)
    net.keep(out_buf, out_part)
    next(team, None)
    jobs = Jobs(team, *jobs.jobs)
    jobs.drain()
    net.finish()


def ffn(part, x_rows, g_rows, gain, own_down, w_ffn, g_all):
    two, n, width = x_rows.shape
    cols = w_ffn.shape[1]
    half, rows = cols // 2, own_down.shape[0]
    every = (two, 8, n, width)
    share = width // 16
    cuts = (0, half, cols)
    return pl.pallas_call(
        functools.partial(ffn_kernel, cuts),
        out_shape=[
            SHAPE((two, n, width), F32),
            SHAPE((two, n, width), F32),
            SHAPE((1, width), F32),
            SHAPE(every, BF16),
            SHAPE(every, BF16),
            SHAPE((share, cols), BF16),
            SHAPE((16 * rows, width), BF16),
        ],
        in_specs=[ANY, VMEM, VMEM, VMEM, ANY, ANY, ANY],
        out_specs=[VMEM, VMEM, VMEM, ANY, ANY, VMEM, ANY],
        scratch_shapes=[
            pltpu.VMEM((width, cols), BF16),
            pltpu.VMEM((half, width), BF16),
            pltpu.VMEM(every, BF16),
            pltpu.VMEM(every, BF16),
            pltpu.VMEM((two, n, width), BF16),
            pltpu.VMEM((two, 8, n, half), BF16),
            pltpu.VMEM((two, 8, n, cols), BF16),
            pltpu.VMEM(every, BF16),
            pltpu.VMEM((two, n, width), BF16),
            pltpu.VMEM((width, cols), BF16),
            pltpu.VMEM((half, width), BF16),
            pltpu.VMEM(every, BF16),
        ]
        + scatter_team_scratch(n, width) * 2
        + scatter_groups_scratch(share, cuts)
        + sems(
            2 * SCATTER_TEAM + 2 * GATHER_TEAM + GATHER_GROUPS + SCATTER_GROUPS_FLAT,
            2 + SCATTER_TEAM_LOADS + 2 + 1 + 1 + 2 + SCATTER_GROUPS_FLAT_LOADS,
        ),
        compiler_params=params(3),
        name="ffn",
    )(part, x_rows, g_rows, gain, own_down, w_ffn, g_all)


def trade_out_back(net, d_out, whole):
    p = net.place
    rows, middle, own = [], [], []
    cases = [(d, k) for d in (2, 1, 3, 0) for k in (1, 0)]
    for d, k in cases:
        xd, cd = p.chip(d), lax.rem(p.c + k, 2)
        for side, col in enumerate((lanes(3 * xd + 2 * cd), lanes(3 * xd + 1))):
            src = d_out.at[pl.ds(0, HD), col]
            dst = whole.at[lanes(3 * p.x + 2 * p.c), pl.ds(side * HD, HD)]
            if d + k:
                rows.append(net.send(src, dst, p.at_xc(d, k)))
            else:
                own.append(net.local(src, dst))
                own[-1].start()
    for d, k in cases:
        xd, cd = p.chip(d), lax.rem(p.c + k, 2)
        for side, col in enumerate((lanes(3 * xd + 2 * cd), lanes(3 * xd + 1))):
            src = d_out.at[pl.ds(HD, HD), col]
            dst = whole.at[lanes(3 * p.x + 1), pl.ds(side * HD, HD)]
            if d + k:
                middle.append((k, net.prepare(src, dst, p.at_xc(d, k))))
            else:
                middle.append((-1, net.local(src, dst)))

    @pl.when(p.c == 0)
    def _():
        for _, copy in middle:
            copy.start()

    yield
    for copy in rows:
        copy.wait_recv()
    for copy in own:
        copy.wait()
    for core in range(2):

        @pl.when(p.c == core)
        def _(core=core):
            for k, copy in middle:
                if k == core:
                    copy.wait_recv()

    @pl.when(p.c == 0)
    def _():
        for k, copy in middle:
            if k < 0:
                copy.wait()
            else:
                copy.wait_send()

    yield


TRADE_BACK = 28


def back_kernel(cuts, *refs):
    (marks, gains, d_gain_f, x_rows, hidden, d_hidden, ffn_sum), refs = refs[:7], refs[7:]
    (whole, w_out, mixed, normed, branch, part_o, d_down), refs = refs[:7], refs[7:]
    given, refs = refs[:11], refs[11:]
    (output, d_tokens, got_heads, got_rest, down_sum), refs = refs[:5], refs[5:]
    bufs, refs = refs[:11], refs[11:]
    (w_buf, wo_buf, mixed_buf, normed_buf, rows_buf, do, d_out, d_ext, d_conv), refs = refs[:9], refs[9:]
    (d_head_a, d_head_b, d_small, turned, trade, out_rows, d_rows), refs = refs[:7], refs[7:]
    (sum_a, sum_b, sum_s, sum_o, packs_heads, packs_rest), refs = refs[:6], refs[6:]
    own, refs = refs[:7], refs[7:]
    scratch = [refs[6 * n : 6 * n + 6] for n in range(7)]
    net = Net(*refs[-3:])
    p = net.place
    qkvp, raw, vec, o, *saved = bufs
    two, _, n, width = rows_buf.shape
    rows = two * 8 * n
    first = [net.load(w_out, wo_buf), net.load(branch, rows_buf), net.load(mixed, mixed_buf)]
    second = [net.load(given[m], bufs[m]) for m in (0, 3)]
    second.append(net.load(given[4].at[0], bufs[4].at[0]))
    third = [net.load(given[m].at[0], bufs[m].at[0]) for m in range(5, 11)]
    third += [net.load(given[m], bufs[m]) for m in (1, 2)]
    third.append(net.load(whole.at[:, pl.ds(0, EXT_W)], w_buf))
    fourth = [net.load(normed, normed_buf)]
    later = []
    meet(team_all(p) + group_peers(p))

    def finish(sums):
        out_rows[...] = (hidden[...] + sums).astype(BF16)

    def out_grad():
        yield from trade_out_back(net, d_out, trade)
        yield from scatter_groups(net, trade, sum_o, cuts[1], *scratch[0])

    def output_rows():
        yield from scatter_team(net, part_o, *scratch[1], finish)
        yield from swap_rows(net, ((out_rows, output),))

    jobs = Jobs(
        output_rows(), out_grad(), scatter_groups(net, d_down, down_sum, cuts[0], *scratch[2])
    )
    jobs.step(0)
    for copy in first:
        copy.wait()
    branch_rows = rows_buf[...].reshape(rows, width)
    d_mixed = mm_nt(branch_rows, wo_buf[...])
    do[:, :HD] = d_mixed[:, :HD]
    do[:, HD:] = jnp.where(p.c == 0, d_mixed[:, HD:], 0.0)
    d_out[...] = mm_tn(mixed_buf[...], branch_rows).astype(BF16)
    jobs.step(1, 2)
    for copy in second:
        copy.wait()
    waits = [third, None, None, later, None, None]
    steps = [(0,), (), (0, 1), (2, 2, 0, 1), (0, 1), (2, 2)]

    def poke():
        jobs.step(*steps.pop(0))
        for copy in waits.pop(0) or ():
            copy.wait()
        if len(steps) == 5:
            fourth.append(net.load(given[4].at[1], bufs[4].at[0]))

    side = 4 * HD
    d_raw = 0.0
    sums_a = scatter_groups(net, d_head_a, sum_a, cuts[2], *scratch[3])
    sums_b = scatter_groups(net, d_head_b, sum_b, cuts[2], *scratch[4])
    for s, (head, grads, job) in enumerate(zip(heads_here(), (d_head_a, d_head_b), (sums_a, sums_b))):
        d_raw = d_raw + bwd_slot(
            poke, s, head, qkvp, raw, w_buf.at[:, pl.ds(HEADS_W, HD)], marks, vec, o, do, *saved, d_ext, d_conv, *own
        )
        if s == 0:
            later += [net.load(given[m].at[1], bufs[m].at[0]) for m in range(5, 11)]
            for copy in fourth:
                copy.wait()
        for k in range(4):
            part = slice(k * width // 4, (k + 1) * width // 4)
            grads[part, :] = mm_tn(normed_buf[:, part], d_ext[:, s * side : (s + 1) * side]).astype(BF16)
        next(job)
    d_ext[:, HEADS_W:] = d_raw.astype(d_ext.dtype)
    next(sums_a)
    next(sums_a)

    sums = TeamSum(net, rows_buf, *scratch[5])
    turned[...] = jnp.zeros_like(turned)

    def work(d):
        at = p.chip(d)
        total = 0.0
        for h in range(two):
            here = pl.ds(pl.multiple_of((h * 8 + 2 * at) * n, 2 * n), 2 * n)
            y = mm_nt(d_ext[here, :], w_buf[...])
            total = total + jnp.sum(y * normed_buf[here, :].astype(F32), axis=0, keepdims=True)
            rows_buf[h, pl.ds(2 * at, 2)] = y.astype(BF16).reshape(2, n, width)
        turned[0:1, :] += total
        sums.ready(d)

    work(2)
    work(1)
    sums.far()
    work(3)
    sums.near()
    work(0)
    sums.pair(0)
    head_a, head_b = heads_here()
    turned[0:1, :] = turned[0:1, :] / gains[0:1, :]
    turned[1:2, :] = d_gain_f[...]
    turned[CONV_AT : CONV_AT + TAPS, lanes(head_a)] = d_conv[0, :TAPS, :]
    turned[CONV_AT : CONV_AT + TAPS, lanes(head_b)] = d_conv[1, :TAPS, :]
    for k in range(width // HD):
        part = slice(k * HD, (k + 1) * HD)
        t = mm_tn(normed_buf[:, part], d_ext[:, HEADS_W:]) + turned[:, part].T
        d_small[part, :] = t.astype(BF16)
    sums_s = scatter_groups(net, d_small, sum_s, cuts[3], *scratch[6])
    next(sums_s)
    sums.on()
    Jobs(sums_a).drain()
    jobs.drain()
    eight, padded, _ = packs_heads.shape
    spread = thin_rows(sum_a.shape[0] // eight, padded).T

    def pack(part, packs, at):
        wide = mm(spread, part[...]).astype(BF16)
        packs[:, :, at : at + part.shape[1]] = wide.reshape(eight, padded, part.shape[1])

    pack(sum_a, packs_rest, 0)
    pack(sum_o, packs_rest, side)
    pack(ffn_sum, packs_rest, side + 2 * HD)
    rest = all_to_team(net, packs_rest, got_rest)
    next(rest)
    next(sums_b)
    next(sums_b)
    d_x, _ = norm_back(x_rows[...].astype(F32), gains[0:1, :][None], sums.result())
    d_rows[...] = (d_x + d_hidden[...]).astype(BF16)
    swaps = swap_rows(net, ((d_rows, d_tokens),))
    next(swaps)
    next(sums_s)
    Jobs(sums_b, sums_s).drain()
    pack(sum_b, packs_heads, 0)
    pack(sum_s, packs_heads, side)
    interleave(all_to_team(net, packs_heads, got_heads), swaps, rest)
    net.finish()


def back(values, arrays, given):
    marks, gains, d_gain_f, x_rows, hidden, d_hidden, ffn_sum = values
    whole, w_out, mixed, normed, branch, part_o, d_down = arrays
    two, n, width = hidden.shape
    r = width // 16
    down = d_down.shape[0] // 16
    side = 4 * HD
    ffn_w = ffn_sum.shape[1]
    cuts = [(0, width // 2, width), (0, HD, 2 * HD), (0, side // 2, side), (0, HD, HD)]
    rows = SHAPE((two, n, width), BF16)
    packs = [(8, 16, side + HD), (8, 16, side + 2 * HD + ffn_w)]
    vmem = pltpu.VMEM
    return pl.pallas_call(
        functools.partial(back_kernel, cuts),
        out_shape=[rows, rows] + [SHAPE(a, BF16) for a in packs] + [SHAPE((down, width), F32)],
        in_specs=[VMEM] * 7 + [ANY] * (7 + len(given)),
        out_specs=[ANY] * 4 + [VMEM],
        scratch_shapes=[vmem((1,) + a.shape[1:] if m > 3 else a.shape, a.dtype) for m, a in enumerate(given)]
        + [
            vmem((width, EXT_W), BF16),
            vmem(w_out.shape, BF16),
            vmem(mixed.shape, BF16),
            vmem(normed.shape, BF16),
            vmem(branch.shape, BF16),
            vmem((SEQ, 2 * HD), F32),
            vmem((2 * HD, width), BF16),
            vmem((SEQ, EXT_W), BF16),
            vmem((2, 8, HD), F32),
            vmem((width, side), BF16),
            vmem((width, side), BF16),
            vmem((width, HD), BF16),
            vmem((HD, width), F32),
            vmem((width, 2 * HD), BF16),
            vmem((two, n, width), BF16),
            vmem((two, n, width), BF16),
            vmem((r, side), BF16),
            vmem((r, side), BF16),
            vmem((r, HD), BF16),
            vmem((r, 2 * HD), BF16),
        ]
        + [vmem(a, BF16) for a in packs]
        + bwd_scratch()
        + scatter_groups_scratch(r, cuts[1])
        + scatter_team_scratch(n, width)
        + scatter_groups_scratch(down, cuts[0])
        + scatter_groups_scratch(r, cuts[2])
        + scatter_groups_scratch(r, cuts[2])
        + scatter_team_scratch(n, width)
        + scatter_groups_scratch(r, cuts[3])
        + sems(
            TRADE_BACK + 2 * SCATTER_TEAM + 4 * SCATTER_GROUPS_FLAT + 2 * SCATTER_GROUPS_FLAT + 2 + 2 * TO_TEAM,
            3 + 3 + 9 + 8 + 4 + SCATTER_TEAM_LOADS + 6 * SCATTER_GROUPS_FLAT_LOADS + 2 + 2,
        ),
        compiler_params=params(5),
        name="back",
    )(*values, *arrays, *given)


def unpack_kernel(heads, rest, rows_in, tokens_in, down_in, *outs):
    kinds, gate, up, small, rows, tokens, down = outs[:5], outs[5], outs[6], outs[7], outs[8], outs[9], outs[10]
    share = small.shape[0]
    side = 4 * HD
    for n, out in enumerate(kinds):
        for x in range(4):
            for j in range(3):
                t = 2 * x + j // 2
                if n < 4:
                    src, col = (heads, n * HD) if j == 1 else (rest, n * HD)
                else:
                    src, col = rest, side + (j % 2) * HD
                head = 3 * x + j
                out[:, head * HD : (head + 1) * HD] = src[t, :share, col : col + HD].astype(F32)
    total = heads[0, :, side : side + SMALL_W].astype(F32)
    for t in range(1, 8):
        total = total + heads[t, :, side : side + SMALL_W].astype(F32)
    small[...] = total[:share]
    for n, out in enumerate((gate, up)):
        for tile in range(32):
            e = tile // 2
            col = side + 2 * HD + n * 4 * HD + (e // 4) * HD
            parts = [
                (rest[t, :, col : col + HD].astype(F32), e % 4)
                for t in range(4 * (tile % 2), 4 * (tile % 2) + 4)
            ]
            out[:, tile * HD : (tile + 1) * HD] = shift_pieces(parts)[:share]
    rows[...] = rows_in[...]
    tokens[...] = tokens_in[...]
    down[...] = down_in[...]


def unpack(heads, rest, rows, tokens, down, share, ff):
    two, n, width = rows.shape
    return pl.pallas_call(
        unpack_kernel,
        out_shape=[SHAPE((share, width), F32)] * 5
        + [SHAPE((share, ff), F32)] * 2
        + [SHAPE((share, HD), F32)]
        + [SHAPE(rows.shape, BF16)] * 2
        + [SHAPE(down.shape, F32)],
        in_specs=[VMEM] * 5,
        out_specs=[VMEM] * 11,
        compiler_params=pltpu.CompilerParams(vmem_limit_bytes=VM),
        name="unpack",
    )(heads, rest, rows, tokens, down)


def per_device(
    tokens,
    doc_start,
    gain_attn,
    w_query,
    w_key,
    w_value,
    w_path,
    conv_path,
    w_beta,
    w_out,
    gain_ffn,
    w_gate,
    w_up,
    w_down,
    grad_out,
):
    zh = lax.axis_index("zh")
    width = tokens.shape[2]
    share = w_query.shape[0]
    small = jnp.concatenate([gain_attn[:, None], gain_ffn[:, None], conv_path.T, w_beta], axis=1)
    small = jnp.pad(small, ((0, 0), (0, SMALL_W - small.shape[1])))
    x_rows, g_rows, x_all, whole, own_ffn = start(
        (w_query, w_key, w_value, w_path, w_out), w_gate, w_up, small, tokens, grad_out
    )
    doc_rows = jnp.cumsum(doc_start, axis=1)
    docs = jnp.where(zh == 0, doc_rows[0], doc_rows[1]).astype(F32)
    marks = [docs]
    for tap in range(1, TAPS):
        same = docs[: SEQ - tap] == docs[tap:]
        marks.append(jnp.concatenate([jnp.zeros((tap,), F32), same.astype(F32)]))
    drow = jnp.stack(marks + marks)
    marks = drow.T

    normed, qkvp, raw, vec, o, mixed, gains, *saved, w_ffn, g_all, w_out_t, part = attn_fwd(
        x_all.reshape(SEQ, width), whole, marks, drow, own_ffn, g_rows
    )
    hidden, d_hidden, d_gain_f, branch_all, out_part, ffn_sum, d_down = ffn(
        part, x_rows, g_rows, gains, w_down, w_ffn, g_all
    )
    output, d_tokens, heads_back, rest_back, d_down = back(
        (marks, gains, d_gain_f, x_rows, hidden, d_hidden, ffn_sum),
        (whole, w_out_t, mixed, normed, branch_all, out_part, d_down),
        (qkvp, raw, vec, o, *saved),
    )
    *kinds, d_gate_w, d_up_w, small, output, d_tokens, d_down = unpack(
        heads_back, rest_back, output, d_tokens, d_down, share, w_gate.shape[1]
    )
    return (
        output,
        d_tokens,
        small[:, 0],
        *kinds[:4],
        small[:, 2:6].T,
        small[:, 6:18],
        kinds[4],
        small[:, 1],
        d_gate_w,
        d_up_w,
        d_down,
    )


def solution(mesh):
    names = ("zl", "y", "zh", "x", "c")
    fine = Mesh(mesh.devices.reshape(2, 4, 2, 4, 2), names)
    dp, ctx = names[:2], names[2:]
    rows, flat, mat, taps = P(dp, ctx, None), P(names), P(names, None), P(None, names)
    return jax.shard_map(
        per_device,
        mesh=fine,
        in_specs=(
            rows, P(dp, None), flat, mat, mat, mat, mat, taps, mat, mat, flat, mat, mat, mat, rows,
        ),
        out_specs=(
            rows, rows, flat, mat, mat, mat, mat, taps, mat, mat, flat, mat, mat, mat,
        ),
        check_vma=False,
    )
```

```python
import functools

import jax
import jax.numpy as jnp
from jax import lax
from jax.experimental import pallas as pl
from jax.experimental.pallas import tpu as pltpu
from jax.sharding import Mesh, PartitionSpec as P

F32, BF16 = jnp.float32, jnp.bfloat16
VM = 61 * 1024 * 1024

SEQ, HD, BLK = 1024, 128, 128
NB = SEQ // BLK
NQC = (NB * (NB - 1) // 2) * BLK
SCALE = HD ** (-0.5)
GROUP, GROUP_BACK = 8, 4


def mm(a, b, dims=((1,), (0,))):
    return lax.dot_general(
        a.astype(BF16), b.astype(BF16), (dims, ((), ())), preferred_element_type=F32
    )


def mm_nt(a, b):
    return mm(a, b, ((1,), (1,)))


def mm_tn(a, b):
    return mm(a, b, ((0,), (0,)))


def split(a):
    high = a.astype(BF16)
    return high, (a - high.astype(F32)).astype(BF16)


def mm3(a, b):
    ah, al = split(a)
    bh, bl = split(b)
    return mm(ah, bh) + (mm(ah, bl) + mm(al, bh))


def iota2(axis):
    return lax.broadcasted_iota(jnp.int32, (BLK, BLK), axis)


BASE = 16


def unit_inverses(lowers):
    row, col = iota2(0), iota2(1)
    eye = (row == col).astype(F32)
    in_base = (row // BASE) == (col // BASE)
    narrow = [jnp.where(in_base, low, 0.0) for low in lowers]
    inv = [eye for _ in lowers]
    for u in range(BASE - 1):
        pick = (col % BASE) == u
        coef = [jnp.sum(jnp.where(pick, low, 0.0), axis=1, keepdims=True) for low in narrow]
        for n, (t, c) in enumerate(zip(inv, coef)):
            t3 = t.reshape(BLK // BASE, BASE, BLK)
            lead = jnp.broadcast_to(t3[:, u : u + 1, :], t3.shape).reshape(BLK, BLK)
            inv[n] = t - c * lead
    size = BASE
    while size < BLK:
        off = ((row // (2 * size)) == (col // (2 * size))) & ((row // size) != (col // size))
        mid = [mm3(t, jnp.where(off, low, 0.0)) for t, low in zip(inv, lowers)]
        inv = [t - mm3(m, t) for t, m in zip(inv, mid)]
        size *= 2
    return inv


def betas_of(raw, head):
    lane = lax.broadcasted_iota(jnp.int32, raw.shape, 1)
    return 2.0 * jax.nn.sigmoid(
        jnp.sum(jnp.where(lane == head + BETA_AT, raw, 0.0), axis=1, keepdims=True)
    )


BETA_AT = 6
CONV_AT = 2
TAPS = 4


def conv_weights(small, head):
    part = small[pl.ds(pl.multiple_of(head * HD, HD), HD), :].astype(F32)
    return part.T[CONV_AT : CONV_AT + TAPS, :]


def convolve(path, taps, marks):
    total = taps[0:1, :] * path
    for m in range(1, TAPS):
        total = total + taps[m : m + 1, :] * (pltpu.roll(path, m, 0) * marks[:, m : m + 1])
    return total


def own_blocks(s, q, k, w, bcol, stores):
    t_out, a_out, z_out, m_out, kp_out, qm_buf, s_buf = stores
    row, col = iota2(0), iota2(1)
    strict, closed = row > col, row >= col
    eye = (row == col).astype(F32)

    def group(g, carry):
        sl = [pl.ds(pl.multiple_of((g * GROUP + n) * BLK, BLK), BLK) for n in range(GROUP)]
        qs = [q[r, :] for r in sl]
        ks = [k[r, :] for r in sl]
        ws = [w[r, :] for r in sl]
        bc = [jnp.broadcast_to(bcol[r, :], (BLK, BLK)) for r in sl]
        br = [b.T for b in bc]
        low = [jnp.where(strict, mm_nt(x, x), 0.0) * b for x, b in zip(ws, br)]
        inv = unit_inverses(low)
        m1 = [jnp.where(strict, mm_nt(x, y), 0.0) for x, y in zip(ws, ks)]
        gq = [jnp.where(closed, mm_nt(x, y), 0.0) * b for x, y, b in zip(qs, ws, br)]
        a = [mm(x, t) for x, t in zip(gq, inv)]
        z = [mm_tn(t, b * x.astype(F32)) for t, b, x in zip(inv, bc, ws)]
        sd = [mm_nt(x, y) - mm(p, m) for x, y, p, m in zip(qs, ks, a, m1)]
        qm = [x.astype(F32) - mm(p, y) for x, p, y in zip(qs, a, ws)]
        kmt = [x.astype(F32).T - mm_tn(zz, m) for x, zz, m in zip(ks, z, m1)]
        pm = [eye - mm_tn(zz, x) for zz, x in zip(z, ws)]
        for n, r in enumerate(sl):
            t_out[s, r, :] = inv[n].astype(t_out.dtype)
            a_out[s, r, :] = a[n].astype(a_out.dtype)
            z_out[s, r, :] = z[n].astype(z_out.dtype)
            m_out[s, r, :] = m1[n].astype(m_out.dtype)
            kp_out[s, r, :HD] = kmt[n].astype(BF16)
            kp_out[s, r, HD:] = pm[n].astype(BF16)
            qm_buf[r, :] = qm[n]
            s_buf[r, r] = sd[n]
        return carry

    lax.fori_loop(0, NB // GROUP, group, 0)


def sweep(s, qc, kp, qm_buf, x_buf, s_buf):
    at = NQC
    for j in range(NB - 2, -1, -1):
        r0 = (j + 1) * BLK
        rows = SEQ - r0
        x_buf[r0 : r0 + BLK, :] = qm_buf[r0 : r0 + BLK, :]
        x = x_buf[r0:, :].astype(BF16)
        at -= rows
        qc[s, at : at + rows, :] = x
        both = mm(x, kp[s, j * BLK : r0, :])
        s_buf[r0:, j * BLK : r0] = both[:, :HD]
        x_buf[r0:, :] = both[:, HD:]


def weigh(s, v, dcol, drow, s_buf, probs, o):
    for i in range(NB):
        lo, width = i * BLK, (i + 1) * BLK
        t = s_buf[lo:width, :width] * SCALE
        seen = dcol[lo:width, 0:1] == drow[0:1, :width]
        seen = seen & (
            lax.broadcasted_iota(jnp.int32, (BLK, width), 0) + lo
            >= lax.broadcasted_iota(jnp.int32, (BLK, width), 1)
        )
        t = jnp.where(seen, t, -1e30)
        e = jnp.exp(t - jnp.max(t, axis=1, keepdims=True))
        p = (e * (1.0 / jnp.sum(e, axis=1, keepdims=True))).astype(BF16)
        probs[s, lo:width, :width] = p
        o[lo:width, :] = mm(p, v[:width, :])


def project(x_all, whole, gains, normed, qkvp, raw):
    rows = 256
    width = x_all.shape[1]
    for n in range(width // HD):
        cols = slice(n * HD, (n + 1) * HD)
        gains[:, cols] = whole[cols, 8 * HD : 9 * HD].astype(F32).T[:8, :]

    def block(i, carry):
        at = pl.ds(pl.multiple_of(i * rows, rows), rows)
        x = x_all[at, :].astype(F32)
        scale = lax.rsqrt(jnp.mean(x * x, axis=1, keepdims=True) + 1e-05)
        n = (x * scale * gains[0:1, :]).astype(BF16)
        normed[at, :] = n
        y = mm(n, whole[:, : 9 * HD])
        qkvp[at, :] = y[:, : 8 * HD].astype(BF16)
        raw[at, :] = y[:, 8 * HD :]
        return carry

    lax.fori_loop(0, SEQ // rows, block, 0)


def heads_here():
    chip, core = lax.axis_index("x"), lax.axis_index("c")
    return 3 * chip + 2 * core, 3 * chip + 1


def fwd_slot(poke, s, head, small, marks, drow, qkvp, raw, vec, o, probs, qc, t_out, a_out, z_out, m_out, kp_out, s_buf, x_buf, qm_buf, b_buf):
    cols = slice(s * HD, (s + 1) * HD)
    q, k, v, path = (qkvp.at[:, (4 * s + n) * HD : (4 * s + n + 1) * HD] for n in range(4))
    taps = conv_weights(small, head)
    conved = convolve(path[...].astype(F32), taps, marks[...])
    unit = conved * lax.rsqrt(jnp.sum(conved * conved, axis=1, keepdims=True) + 1e-06)
    vec[:, cols] = unit.astype(BF16)
    b_buf[...] = betas_of(raw[...], head)
    own_blocks(s, q, k, vec.at[:, cols], b_buf, (t_out, a_out, z_out, m_out, kp_out, qm_buf, s_buf))
    poke()
    sweep(s, qc, kp_out, qm_buf, x_buf, s_buf)
    poke()
    weigh(s, v, marks, drow, s_buf, probs, o.at[:, cols])


def score_grads(s, v, o, do, probs, ds_buf, dv):
    for i in range(NB):
        lo, width = i * BLK, (i + 1) * BLK
        p = probs[0, lo:width, :width].astype(F32)
        g = do[lo:width, :]
        delta = jnp.sum(g * o[lo:width, :].astype(F32), axis=1, keepdims=True)
        ds = p * (mm_nt(g, v[:width, :]) - delta) * SCALE
        ds_buf[lo:width, :width] = ds.astype(BF16)
    for j in range(NB):
        lo = j * BLK
        dv[lo : lo + BLK, :] = mm_tn(probs[0, lo:, lo : lo + BLK], do[lo:, :]).astype(dv.dtype)


def sweep_back(s, qc, kp, ds_buf, x_buf, dkm_buf, dpm_buf):
    x_buf[...] = jnp.zeros_like(x_buf)
    dkm_buf[SEQ - BLK :, :] = jnp.zeros((BLK, HD), F32)
    dpm_buf[SEQ - BLK :, :] = jnp.zeros((BLK, HD), F32)
    at = 0
    for j in range(NB - 1):
        lo, r0 = j * BLK, (j + 1) * BLK
        rows = SEQ - r0
        x = x_buf[r0:, :].astype(BF16)
        ds = ds_buf[r0:, lo:r0]
        qcj = qc[0, at : at + rows, :]
        at += rows
        both = mm_tn(qcj, jnp.concatenate([x, ds], axis=1))
        dpm_buf[lo:r0, :] = both[:, :HD]
        dkm_buf[lo:r0, :] = both[:, HD:].T
        x_buf[r0:, :] = mm_nt(jnp.concatenate([ds, x], axis=1), kp[0, lo:r0, :])


def own_blocks_back(s, q, k, w, bcol, saved, bufs, dq, dk, dw, db):
    t_in, a_in, z_in, m_in = saved
    ds_buf, x_buf, dkm_buf, dpm_buf = bufs
    row, col = iota2(0), iota2(1)
    strict, closed = row > col, row >= col

    def group(g, carry):
        sl = [pl.ds(pl.multiple_of((g * GROUP_BACK + n) * BLK, BLK), BLK) for n in range(GROUP_BACK)]
        rng = range(GROUP_BACK)
        Q = [q[r, :] for r in sl]
        K = [k[r, :] for r in sl]
        W = [w[r, :] for r in sl]
        bc = [jnp.broadcast_to(bcol[r, :], (BLK, BLK)) for r in sl]
        br = [b.T for b in bc]
        E = [ds_buf[r, r] for r in sl]
        T = [t_in[0, r, :] for r in sl]
        A = [a_in[0, r, :] for r in sl]
        Z = [z_in[0, r, :] for r in sl]
        M = [m_in[0, r, :] for r in sl]
        dQm = [x_buf[r, :] for r in sl]
        dKm = [dkm_buf[r, :] for r in sl]
        dPm = [dpm_buf[r, :] for r in sl]
        i1 = [mm_nt(W[n], W[n]) for n in rng]
        qw = [jnp.where(closed, mm_nt(Q[n], W[n]), 0.0) for n in rng]
        dA = [-(mm_nt(E[n], M[n]) + mm_nt(dQm[n], W[n])) for n in rng]
        dM = [jnp.where(strict, -(mm_tn(A[n], E[n]) + mm_nt(Z[n], dKm[n])), 0.0) for n in rng]
        dZ = [-(mm(M[n], dKm[n]) + mm_nt(W[n], dPm[n])) for n in rng]
        dW = [-(mm_tn(A[n], dQm[n]) + mm(Z[n], dPm[n])) for n in rng]
        dG = [jnp.where(closed, mm_nt(dA[n], T[n]), 0.0) for n in rng]
        bw = [bc[n] * W[n].astype(F32) for n in rng]
        dT = [mm_tn(qw[n] * br[n], dA[n]) + mm_nt(bw[n], dZ[n]) for n in rng]
        dBW = [mm(T[n], dZ[n]) for n in rng]
        dL = [mm_tn(T[n], dT[n]) for n in rng]
        dL = [jnp.where(strict, -mm_nt(dL[n], T[n]), 0.0) for n in rng]
        dI = [dL[n] * br[n] for n in rng]
        R = [dG[n] * br[n] for n in rng]
        for n, r in enumerate(sl):
            db[r, :] = jnp.sum(
                (dL[n] * i1[n] + dG[n] * qw[n]).T + dBW[n] * W[n].astype(F32), axis=1, keepdims=True
            )
            dq[r, :] = (dQm[n] + mm(E[n], K[n]) + mm(R[n], W[n])).astype(dq.dtype)
            dk[r, :] = (dKm[n] + mm_tn(E[n], Q[n]) + mm_tn(dM[n], W[n])).astype(dk.dtype)
            dw[r, :] = (
                dW[n]
                + bc[n] * dBW[n]
                + mm_tn(R[n], Q[n])
                + mm(dM[n], K[n])
                + mm(dI[n] + dI[n].T, W[n])
            )
        return carry

    lax.fori_loop(0, NB // GROUP_BACK, group, 0)


def bwd_slot(poke, s, head, qkvp, raw, small, marks, vec, o, do, probs, qc, t_in, a_in, z_in, m_in, kp, d_ext, d_conv, ds_buf, x_buf, dkm_buf, dpm_buf, b_buf, db_buf, dw_buf):
    cols = slice(s * HD, (s + 1) * HD)
    q, k, v, path = (qkvp.at[:, (4 * s + n) * HD : (4 * s + n + 1) * HD] for n in range(4))
    dq, dk, dv, dpath = (d_ext.at[:, (4 * s + n) * HD : (4 * s + n + 1) * HD] for n in range(4))
    score_grads(s, v, o.at[:, cols], do.at[:, cols], probs, ds_buf, dv)
    poke()
    sweep_back(s, qc, kp, ds_buf, x_buf, dkm_buf, dpm_buf)
    poke()
    beta = betas_of(raw[...], head)
    b_buf[...] = beta
    own_blocks_back(
        s, q, k, vec.at[:, cols], b_buf, (t_in, a_in, z_in, m_in), (ds_buf, x_buf, dkm_buf, dpm_buf), dq, dk, dw_buf, db_buf
    )
    poke()
    taps = conv_weights(small, head)
    raw_path = path[...].astype(F32)
    conved = convolve(raw_path, taps, marks[...])
    scale = lax.rsqrt(jnp.sum(conved * conved, axis=1, keepdims=True) + 1e-06)
    unit = conved * scale
    dw = dw_buf[...]
    d_conved = scale * (dw - unit * jnp.sum(dw * unit, axis=1, keepdims=True))
    total = taps[0:1, :] * d_conved
    d_conv[s, 0:1, :] = jnp.sum(d_conved * raw_path, axis=0, keepdims=True)
    for m in range(1, TAPS):
        marked = d_conved * marks[:, m : m + 1]
        d_conv[s, m : m + 1, :] = jnp.sum(marked * pltpu.roll(raw_path, m, 0), axis=0, keepdims=True)
        total = total + taps[m : m + 1, :] * pltpu.roll(marked, SEQ - m, 0)
    dpath[...] = total.astype(dpath.dtype)
    lane = lax.broadcasted_iota(jnp.int32, (SEQ, HD), 1)
    return jnp.where(lane == head + BETA_AT, db_buf[...] * beta * (1.0 - 0.5 * beta), 0.0)


def fwd_shapes(width):
    return [
        ((SEQ, width), BF16),
        ((SEQ, 8 * HD), BF16),
        ((SEQ, HD), F32),
        ((SEQ, 2 * HD), BF16),
        ((SEQ, 2 * HD), BF16),
        ((8, width), F32),
        ((2, SEQ, SEQ), BF16),
        ((2, NQC, HD), BF16),
        ((2, SEQ, BLK), BF16),
        ((2, SEQ, BLK), BF16),
        ((2, SEQ, BLK), BF16),
        ((2, SEQ, BLK), BF16),
        ((2, SEQ, 2 * HD), BF16),
    ]


def fwd_scratch():
    return [
        pltpu.VMEM((SEQ, SEQ), F32),
        pltpu.VMEM((SEQ, HD), F32),
        pltpu.VMEM((SEQ, HD), F32),
        pltpu.VMEM((SEQ, 1), F32),
    ]


def bwd_scratch():
    return (
        [pltpu.VMEM((SEQ, SEQ), BF16)]
        + [pltpu.VMEM((SEQ, HD), F32)] * 3
        + [pltpu.VMEM((SEQ, 1), F32)] * 2
        + [pltpu.VMEM((SEQ, HD), F32)]
    )


MESH = pl.DeviceIdType.MESH
ANY = pl.BlockSpec(memory_space=pl.ANY)
VMEM = pl.BlockSpec(memory_space=pltpu.VMEM)


class Place:
    def __init__(self):
        self.x, self.c = lax.axis_index("x"), lax.axis_index("c")
        self.y = lax.axis_index("y")
        self.zl, self.zh = lax.axis_index("zl"), lax.axis_index("zh")
        self.z = self.zh * 2 + self.zl

    def chip(self, d):
        return lax.rem(self.x + d, 4)

    def at_x(self, d):
        return {"x": lax.rem(self.x + d, 4)}

    def at_xc(self, d, k):
        return {"x": lax.rem(self.x + d, 4), "c": lax.rem(self.c + k, 2)}

    def sibling(self):
        return {"c": 1 - self.c}

    def at_y(self, d):
        return {"y": lax.rem(self.y + d, 4)}

    def at_z(self, d):
        z = lax.rem(self.z + d, 4)
        return {"zl": lax.rem(z, 2), "zh": z // 2}


class Net:
    def __init__(self, send_sem, recv_sem, local_sem):
        self.place = Place()
        self.send_sem, self.recv_sem, self.local_sem = send_sem, recv_sem, local_sem
        self.count, self.kept, self.locals, self.sent = 0, 0, [], []

    def prepare(self, src, dst, device):
        k = self.count
        self.count += 1
        return pltpu.make_async_remote_copy(
            src_ref=src,
            dst_ref=dst,
            send_sem=self.send_sem.at[k],
            recv_sem=self.recv_sem.at[k],
            device_id=device,
            device_id_type=MESH,
        )

    def send(self, src, dst, device):
        copy = self.prepare(src, dst, device)
        copy.start()
        self.sent.append(copy)
        return copy

    def local(self, src, dst):
        self.kept += 1
        return pltpu.make_async_copy(src, dst, self.local_sem.at[self.kept - 1])

    def load(self, src, dst):
        copy = self.local(src, dst)
        copy.start()
        return copy

    def keep(self, src, dst):
        self.locals.append(self.load(src, dst))

    def settle(self):
        for copy in self.locals:
            copy.wait()
        self.locals = []

    def finish(self):
        for copy in self.sent:
            copy.wait_send()
        self.settle()


def meet(devices):
    barrier = pltpu.get_barrier_semaphore()
    for device in devices:
        pl.semaphore_signal(barrier, inc=1, device_id=device, device_id_type=MESH)
    pl.semaphore_wait(barrier, len(devices))


class Jobs:
    def __init__(self, *jobs):
        self.all = list(jobs)
        self.jobs = list(jobs)

    def poke(self):
        for job in list(self.jobs):
            try:
                next(job)
            except StopIteration:
                self.jobs.remove(job)

    def step(self, *which):
        for n in which:
            next(self.all[n], None)

    def drain(self):
        while self.jobs:
            self.poke()


def interleave(*jobs):
    Jobs(*jobs).drain()


def team_peers(p):
    return [p.at_x(1), p.at_x(3), p.sibling()]


def team_all(p):
    return [p.at_xc(d, k) for d in range(4) for k in range(2) if d + k]


def group_peers(p):
    return [p.at_y(d) for d in (1, 2, 3)] + [p.at_z(d) for d in (1, 2, 3)]


def gather_team(net, own, out):
    p = net.place
    me, sib = 2 * p.x + p.c, p.sibling()
    right, left = p.at_x(1), p.at_x(3)
    t_l, t_r, t_2 = (2 * p.chip(d) + p.c for d in (3, 1, 2))
    to_r = net.send(own, out.at[:, me], right)
    to_l = net.send(own, out.at[:, me], left)
    shared = [net.send(own, out.at[:, me], sib)]
    net.keep(own, out.at[:, me])
    yield
    to_r.wait_recv()
    on_r = net.send(out.at[0, t_l], out.at[0, t_l], right)
    shared.append(net.send(out.at[:, t_l], out.at[:, t_l], sib))
    to_l.wait_recv()
    on_l = net.send(out.at[1, t_r], out.at[1, t_r], left)
    shared.append(net.send(out.at[:, t_r], out.at[:, t_r], sib))
    yield
    on_r.wait_recv()
    shared.append(net.send(out.at[0, t_2], out.at[0, t_2], sib))
    on_l.wait_recv()
    shared.append(net.send(out.at[1, t_2], out.at[1, t_2], sib))
    yield
    for copy in shared:
        copy.wait_recv()


GATHER_TEAM = 10


def add(a, b):
    return (a.astype(F32) + b.astype(F32)).astype(BF16)


def scatter_team(net, part, got, total, from_l, from_r, all_l, all_r, finish):
    p = net.place
    sib, right, left = p.sibling(), p.at_x(1), p.at_x(3)
    order = (2, 1, 3, 0)
    swaps, loads = [], []
    for d in order:
        at = p.chip(d)
        swaps.append(net.send(part.at[:, 2 * at + 1 - p.c], got.at[:, at], sib))
        loads.append(net.load(part.at[:, 2 * at + p.c], total.at[:, at]))

    def pair(n):
        swaps[n].wait_recv()
        loads[n].wait()
        at = p.chip(order[n])
        total[:, at] = add(total[:, at], got[:, at])
        return at

    yield
    x_2 = pair(0)
    half_r = net.send(total.at[0, x_2], from_l, right)
    half_l = net.send(total.at[1, x_2], from_r, left)
    x_r = pair(1)
    rest_r = net.send(total.at[1, x_r], all_l.at[1], right)
    x_l = pair(2)
    rest_l = net.send(total.at[0, x_l], all_r.at[0], left)
    pair(3)
    yield
    half_r.wait_recv()
    total[0, x_r] = add(total[0, x_r], from_l[...])
    last_r = net.send(total.at[0, x_r], all_l.at[0], right)
    half_l.wait_recv()
    total[1, x_l] = add(total[1, x_l], from_r[...])
    last_l = net.send(total.at[1, x_l], all_r.at[1], left)
    yield
    for copy in (rest_r, rest_l, last_r, last_l):
        copy.wait_recv()
    finish(total[:, p.x].astype(F32) + all_l[...].astype(F32) + all_r[...].astype(F32))


SCATTER_TEAM_LOADS = 4
SCATTER_TEAM = 10


def scatter_team_scratch(n, w):
    return [
        pltpu.VMEM((2, 4, n, w), BF16),
        pltpu.VMEM((2, 4, n, w), BF16),
        pltpu.VMEM((n, w), BF16),
        pltpu.VMEM((n, w), BF16),
        pltpu.VMEM((2, n, w), BF16),
        pltpu.VMEM((2, n, w), BF16),
    ]


def chunk_rows(y, z, rows):
    zl, zh = (z % 2, z // 2) if isinstance(z, int) else (lax.rem(z, 2), z // 2)
    return pl.ds(pl.multiple_of(((zl * 4 + y) * 2 + zh) * rows, rows), rows)


def halves(cols):
    mid = cols // 2
    return [(pl.ds(0, mid),) * 2], [(pl.ds(mid, cols - mid),) * 2]


def gather_groups(net, own, out, y_pieces, z_pieces, share=False):
    p = net.place
    rows = own.shape[0]
    shared = []
    for src, dst in y_pieces + z_pieces:
        net.keep(own.at[:, src], out.at[chunk_rows(p.y, p.z, rows), dst])

    def spread(pieces, y, z, devices, first=False):
        copies = []
        for src, dst in pieces:
            place = out.at[chunk_rows(y, z, rows), dst]
            copies += [net.send(own.at[:, src] if first else place, place, d) for d in devices]
        return copies

    def give(y, z, first=False):
        if share:
            src, dst = z_pieces[-1]
            place = out.at[chunk_rows(y, z, rows), dst]
            shared.append(net.send(own.at[:, src] if first else place, place, p.sibling()))

    order = (1, 3, 2)
    ys, zs = [p.at_y(d) for d in order], [p.at_z(d) for d in order]
    y_first = spread(y_pieces, p.y, p.z, ys, True)
    z_first = spread(z_pieces, p.y, p.z, zs, True)
    last = spread(y_pieces, p.y, p.z, zs, True)
    via_y = [(p.z, spread(z_pieces, p.y, p.z, ys, True))]
    give(p.y, p.z, True)
    yield
    for n, d in enumerate(order):
        for copy in y_first[n::3]:
            copy.wait_recv()
        last += spread(y_pieces, lax.rem(p.y + 4 - d, 4), p.z, zs)
        for copy in z_first[n::3]:
            copy.wait_recv()
        z = lax.rem(p.z + 4 - d, 4)
        via_y.append((z, spread(z_pieces, p.y, z, ys)))
        give(p.y, z)
        yield
    for z, copies in via_y:
        for n, d in enumerate(order):
            for copy in copies[n::3]:
                copy.wait_recv()
            give(lax.rem(p.y + 4 - d, 4), z)
    for copy in last + shared:
        copy.wait_recv()


GATHER_GROUPS = 30


def scatter_groups(net, part, out, cuts, z_got, z_sum, z_last, y_got, y_sum, y_last):
    p = net.place
    lo, mid, hi = cuts
    first, second = pl.ds(lo, mid - lo), pl.ds(mid, hi - mid)
    rows = z_sum.shape[1]
    both = hi > mid
    flat = len(part.shape) == 2
    order = (2, 1, 3)
    a, b, a_own, b_own = [], [], [], []
    for n, d in enumerate(order):
        z, y = lax.rem(p.z + d, 4), lax.rem(p.y + d, 4)
        if flat:
            for k in range(4):
                a.append(net.send(part.at[chunk_rows(k, z, rows), first], z_got.at[n, k], p.at_z(d)))
                if both:
                    b.append(net.send(part.at[chunk_rows(y, k, rows), second], y_got.at[n, k % 2, k // 2], p.at_y(d)))
        else:
            a.append(net.send(part.at[lax.rem(z, 2), :, z // 2, :, first], z_got.at[n], p.at_z(d)))
            if both:
                b.append(net.send(part.at[:, y, :, :, second], y_got.at[n], p.at_y(d)))
    if flat:
        for k in range(4):
            a_own.append(net.load(part.at[chunk_rows(k, p.z, rows), first], z_sum.at[k]))
            if both:
                b_own.append(net.load(part.at[chunk_rows(p.y, k, rows), second], y_sum.at[k % 2, k // 2]))
    else:
        a_own.append(net.load(part.at[p.zl, :, p.zh, :, first], z_sum))
        if both:
            b_own.append(net.load(part.at[:, p.y, :, :, second], y_sum))

    yield
    for copy in a_own:
        copy.wait()
    for copy in a:
        copy.wait_recv()
    for y in range(4):
        t = z_sum[y].astype(F32)
        for n in range(3):
            t = t + z_got[n, y].astype(F32)
        z_sum[y] = t.astype(BF16)
    a = [
        net.send(z_sum.at[lax.rem(p.y + d, 4)], z_last.at[n], p.at_y(d)) for n, d in enumerate(order)
    ]
    if both:
        yield
        for copy in b_own:
            copy.wait()
        for copy in b:
            copy.wait_recv()
        for zl in range(2):
            for zh in range(2):
                t = y_sum[zl, zh].astype(F32)
                for n in range(3):
                    t = t + y_got[n, zl, zh].astype(F32)
                y_sum[zl, zh] = t.astype(BF16)
        b = []
        for n, d in enumerate(order):
            z = lax.rem(p.z + d, 4)
            b.append(net.send(y_sum.at[lax.rem(z, 2), z // 2], y_last.at[n], p.at_z(d)))
    yield
    for copy in a:
        copy.wait_recv()
    t = z_sum[p.y].astype(F32)
    for n in range(3):
        t = t + z_last[n].astype(F32)
    out[:, first] = t.astype(out.dtype)
    if both:
        yield
        for copy in b:
            copy.wait_recv()
        t = y_sum[p.zl, p.zh].astype(F32)
        for n in range(3):
            t = t + y_last[n].astype(F32)
        out[:, second] = t.astype(out.dtype)


SCATTER_GROUPS_LOADS = 2
SCATTER_GROUPS_FLAT_LOADS = 8
SCATTER_GROUPS = 12
SCATTER_GROUPS_FLAT = 30


def scatter_groups_scratch(r, cuts):
    a, b = cuts[1] - cuts[0], max(cuts[2] - cuts[1], HD)
    return [
        pltpu.VMEM((3, 4, r, a), BF16),
        pltpu.VMEM((4, r, a), BF16),
        pltpu.VMEM((3, r, a), BF16),
        pltpu.VMEM((3, 2, 2, r, b), BF16),
        pltpu.VMEM((2, 2, r, b), BF16),
        pltpu.VMEM((3, r, b), BF16),
    ]


def sems(remote, local):
    return [
        pltpu.SemaphoreType.DMA((remote,)),
        pltpu.SemaphoreType.DMA((remote,)),
        pltpu.SemaphoreType.DMA((max(local, 1),)),
    ]


def params(collective_id):
    return pltpu.CompilerParams(
        collective_id=collective_id, has_side_effects=True, vmem_limit_bytes=VM
    )


EPS_NORM = 1e-05
EPS_UNIT = 1e-06
SHAPE = jax.ShapeDtypeStruct


def all_to_team(net, packs, got):
    p = net.place
    me = 2 * p.x + p.c
    net.keep(packs.at[me], got.at[me])
    copies = []
    for d in (2, 1, 3, 0):
        for k in (1, 0):
            if d + k:
                to = 2 * p.chip(d) + lax.rem(p.c + k, 2)
                copies.append(net.send(packs.at[to], got.at[me], p.at_xc(d, k)))
    yield
    for copy in copies:
        copy.wait_recv()


TO_TEAM = 7


def swap_rows(net, pairs):
    p = net.place
    copies = []
    for src, dst in pairs:
        net.keep(src.at[p.zh], dst.at[p.zh])
        copies.append(net.send(src.at[1 - p.zh], dst.at[p.zh], p.at_z(2)))
    yield
    for copy in copies:
        copy.wait_recv()


def thin_rows(rows, padded):
    out = lax.broadcasted_iota(jnp.int32, (8 * rows, 8 * padded), 0)
    at = lax.broadcasted_iota(jnp.int32, (8 * rows, 8 * padded), 1)
    return ((out // rows == at // padded) & (out % rows == at % padded)).astype(BF16)


HEADS_W, SMALL_W = 8 * HD, HD
EXT_W = HEADS_W + SMALL_W
OUT_B, OUT_A = EXT_W, EXT_W + HD
WHOLE_W = EXT_W + 2 * HD
SHARED_W = 3 * HD
FIRST_W = 5 * HD + SHARED_W
PIECE = 32


def shift_pieces(tiles):
    lane = lax.broadcasted_iota(jnp.int32, tiles[0][0].shape, 1) // PIECE
    total = None
    for n, (tile, piece) in enumerate(tiles):
        turn = (PIECE * (n - piece)) % HD
        moved = pltpu.roll(tile, turn, 1) if turn else tile
        total = moved if total is None else jnp.where(lane == n, moved, total)
    return total


def pack_weights(kinds, gate_up, small, packs):
    share = small.shape[0]
    packs[...] = jnp.zeros_like(packs)
    for t in range(8):
        own, middle = 3 * (t // 2) + 2 * (t % 2), 3 * (t // 2) + 1
        parts = [w[:, own * HD : (own + 1) * HD] for w in kinds]
        shared = [w[:, middle * HD : (middle + 1) * HD] for w in kinds]
        shared = shared[:3] if t % 2 == 0 else [shared[3], small[...], shared[4]]
        for n, part in enumerate(parts + shared):
            packs[t, :share, n * HD : (n + 1) * HD] = part
    for n, w in enumerate(gate_up):
        for t in range(8):
            for j in range(4):
                tiles = []
                for e in range(4 * j, 4 * j + 4):
                    at = (2 * e + t // 4) * HD
                    tiles.append((w[:, at : at + HD].astype(F32), t % 4))
                at = FIRST_W + n * 4 * HD + j * HD
                packs[t, :share, at : at + HD] = shift_pieces(tiles).astype(BF16)


def start_kernel(wq, wk, wv, wp, wo, gate, up, small, tokens, grad_out, x_rows, g_rows, x_all, whole, own_ffn, packs, got, own, *sem):
    net = Net(*sem)
    p = net.place
    share = small.shape[0]
    pack_weights((wq, wk, wv, wp, wo), (gate, up), small, packs)
    first, second = pl.ds(0, FIRST_W), pl.ds(FIRST_W, own.shape[1] - FIRST_W)
    meet(team_all(p) + group_peers(p))
    trades = [all_to_team(net, packs.at[:, :, part], got.at[:, :, part]) for part in (first, second)]
    swaps = [swap_rows(net, (pair,)) for pair in ((tokens, x_rows), (grad_out, g_rows))]
    for n in range(2):
        next(trades[n])
        next(swaps[n])
    pick = thin_rows(share, packs.shape[1])

    def thin(part):
        wide = got[:, :, part].reshape(pick.shape[1], part.size)
        own[:, part] = mm(pick, wide).astype(BF16)

    interleave(trades[0])
    net.settle()
    thin(first)
    shared = pl.ds(pl.multiple_of(4 * HD + p.c * SHARED_W, HD), SHARED_W)
    heads = gather_groups(
        net,
        own,
        whole,
        [(pl.ds(0, 4 * HD), pl.ds(0, 4 * HD))],
        [(pl.ds(4 * HD, HD), pl.ds(OUT_A, HD)), (pl.ds(5 * HD, SHARED_W), shared)],
        True,
    )
    next(heads)
    interleave(swaps[0])
    x_team = gather_team(net, x_rows, x_all)
    next(x_team)
    for _ in range(3):
        next(heads)
    next(x_team)
    interleave(trades[1])
    thin(second)
    net.keep(own.at[:, second], own_ffn)
    interleave(x_team, heads, swaps[1])
    net.finish()


def start(kinds, gate, up, small, tokens, grad_out):
    share, width = kinds[0].shape
    two, n, _ = tokens.shape
    rows = SHAPE(tokens.shape, BF16)
    cols = FIRST_W + gate.shape[1] // 4
    return pl.pallas_call(
        start_kernel,
        out_shape=[
            rows,
            rows,
            SHAPE((two, 8, n, width), BF16),
            SHAPE((width, WHOLE_W), BF16),
            SHAPE((8 * share, cols - FIRST_W), BF16),
        ],
        in_specs=[VMEM] * 8 + [ANY] * 2,
        out_specs=[ANY] * 5,
        scratch_shapes=[
            pltpu.VMEM((8, 16, cols), BF16),
            pltpu.VMEM((8, 16, cols), BF16),
            pltpu.VMEM((8 * share, cols), BF16),
        ]
        + sems(2 * TO_TEAM + 2 + GATHER_TEAM + 3 * GATHER_GROUPS // 2 + 16, 9),
        compiler_params=params(1),
        name="start",
    )(*kinds, gate, up, small, tokens, grad_out)


def lanes(at):
    return pl.ds(pl.multiple_of(at * HD, HD), HD)


def trade_out(net, whole, w_out):
    p = net.place
    copies, own = [], []
    for d in (2, 1, 3, 0):
        for k in (1, 0):
            xd, cd = p.chip(d), lax.rem(p.c + k, 2)
            row_a, row_b = lanes(3 * xd + 2 * cd), lanes(3 * xd + 1)
            row_c = lanes(3 * xd + jnp.where(p.c == 0, 2 * cd, 1))
            col_a, col_b = lanes(3 * p.x + 2 * p.c), lanes(3 * p.x + 1)
            moves = (
                (whole.at[row_a, pl.ds(OUT_A, HD)], w_out.at[pl.ds(0, HD), col_a]),
                (whole.at[row_b, pl.ds(OUT_A, HD)], w_out.at[pl.ds(HD, HD), col_a]),
                (whole.at[row_c, pl.ds(OUT_B, HD)], w_out.at[lanes(p.c), col_b]),
            )
            for src, dst in moves:
                if d + k:
                    copies.append(net.send(src, dst, p.at_xc(d, k)))
                else:
                    own.append(net.load(src, dst))
    yield
    for copy in own:
        copy.wait()
    for copy in copies:
        copy.wait_recv()


def attn_fwd_kernel(x_all, whole, marks, drow, own_ffn, g_rows, *rest):
    kept, (w_ffn, g_all, w_out, part), rest = rest[:13], rest[13:17], rest[17:]
    bufs, (x_buf, w_buf, wo_buf, part_buf), rest = rest[:14], rest[14:18], rest[18:]
    normed, qkvp, raw, vec, mixed, gains, *saved, o = bufs
    net = Net(*rest[-3:])
    p = net.place
    loads = [net.load(whole.at[:, pl.ds(0, 9 * HD)], w_buf), net.load(x_all, x_buf)]
    meet(team_all(p) + group_peers(p))
    jobs = Jobs(
        gather_groups(net, own_ffn, w_ffn, *halves(own_ffn.shape[1])),
        trade_out(net, whole, wo_buf),
        gather_team(net, g_rows, g_all),
    )
    jobs.step(0, 1, 2)
    for copy in loads:
        copy.wait()
    project(x_buf, w_buf, gains, normed, qkvp, raw)
    for n in (0, 1, 2, 5):
        net.keep(bufs[n], kept[n])
    steps = [(0, 0, 0), (), (), (), (2,), ()]
    poke = lambda: jobs.step(*steps.pop(0)) if steps else None
    for s, head in enumerate(heads_here()):
        cols = pl.ds(s * HD, HD)
        poke()
        fwd_slot(poke, s, head, w_buf.at[:, pl.ds(8 * HD, HD)], marks, drow, qkvp, raw, vec, o, *saved, *rest[:-3])
        net.keep(vec.at[:, cols], kept[3].at[:, cols])
        for src, dst in zip(saved, kept[6:]):
            net.keep(src.at[s], dst.at[s])
    mixed[:, :HD] = o[:, :HD].astype(BF16)
    mixed[:, HD:] = jnp.where(p.c == 0, o[:, HD:], 0.0).astype(BF16)
    net.keep(mixed, kept[4])
    jobs.step(1, 1)
    net.keep(wo_buf, w_out)
    two, _, n, width = part.shape
    for h in range(two):
        for t in range(0, 8, 4):
            at = (h * 8 + t) * n
            y = mm(mixed[at : at + 4 * n, :], wo_buf[...]).astype(BF16)
            part_buf[h, t : t + 4] = y.reshape(4, n, width)
    net.keep(part_buf, part)
    jobs.drain()
    net.finish()


def attn_fwd(x_all, whole, marks, drow, own_ffn, g_rows):
    rows, cols = own_ffn.shape
    two, n, width = g_rows.shape
    kept = fwd_shapes(width)
    part = (two, 8, n, width)
    return pl.pallas_call(
        attn_fwd_kernel,
        out_shape=[SHAPE(*a) for a in kept]
        + [SHAPE((16 * rows, cols), BF16), SHAPE(part, BF16), SHAPE((2 * HD, width), BF16), SHAPE(part, BF16)],
        in_specs=[ANY, ANY, VMEM, VMEM, ANY, ANY],
        out_specs=[ANY] * (len(kept) + 4),
        scratch_shapes=[pltpu.VMEM(*a) for a in kept]
        + [
            pltpu.VMEM((SEQ, 2 * HD), F32),
            pltpu.VMEM((SEQ, width), BF16),
            pltpu.VMEM((width, 9 * HD), BF16),
            pltpu.VMEM((2 * HD, width), BF16),
            pltpu.VMEM(part, BF16),
        ]
        + fwd_scratch()
        + sems(GATHER_TEAM + GATHER_GROUPS + 21, 2 + 6 + 4 + 18 + 3),
        compiler_params=params(7),
        name="attn_fwd",
    )(x_all, whole, marks, drow, own_ffn, g_rows)


def norm_back(v, gain, d_normed):
    scale = lax.rsqrt(jnp.mean(v * v, axis=-1, keepdims=True) + EPS_NORM)
    unit = v * scale
    d_unit = d_normed * gain
    d_v = scale * (d_unit - unit * jnp.mean(d_unit * unit, axis=-1, keepdims=True))
    return d_v, d_normed * unit


def by_group(a):
    return a.reshape(2, 4, 2, a.shape[0] // 16, a.shape[1])


class TeamBlocks:
    def __init__(self, net, own, out):
        self.net, self.own, self.out = net, own, out

    def start(self):
        net, p, out = self.net, self.net.place, self.out
        place = out.at[:, 2 * p.x + p.c]
        self.to_r = net.send(self.own, place, p.at_x(1))
        self.to_l = net.send(self.own, place, p.at_x(3))
        self.shared = net.send(self.own, place, p.sibling())
        self.kept = net.load(self.own, place)

    def mine(self):
        self.kept.wait()
        self.shared.wait_recv()

    def hand_on(self):
        net, p, out = self.net, self.net.place, self.out
        left, right = 2 * p.chip(3) + p.c, 2 * p.chip(1) + p.c
        self.to_r.wait_recv()
        self.on_r = net.send(out.at[0, left], out.at[0, left], p.at_x(1))
        self.from_l = net.send(out.at[:, left], out.at[:, left], p.sibling())
        self.to_l.wait_recv()
        self.on_l = net.send(out.at[1, right], out.at[1, right], p.at_x(3))
        self.from_r = net.send(out.at[:, right], out.at[:, right], p.sibling())

    def opposite(self):
        net, p, out = self.net, self.net.place, self.out
        far = 2 * p.chip(2) + p.c
        self.far = []
        for n, copy in enumerate((self.on_r, self.on_l)):
            copy.wait_recv()
            self.far.append(net.send(out.at[n, far], out.at[n, far], p.sibling()))


class TeamSum:
    def __init__(self, net, part, got, total, from_l, from_r, all_l, all_r):
        self.net, self.part, self.got, self.total = net, part, got, total
        self.from_l, self.from_r, self.all_l, self.all_r = from_l, from_r, all_l, all_r
        self.swaps, self.last = {}, []

    def ready(self, d):
        p = self.net.place
        at = p.chip(d)
        self.swaps[d] = self.net.send(
            self.part.at[:, 2 * at + 1 - p.c], self.got.at[:, at], p.sibling()
        )

    def pair(self, d):
        p = self.net.place
        at = p.chip(d)
        self.swaps[d].wait_recv()
        self.total[:, at] = add(self.part[:, 2 * at + p.c], self.got[:, at])
        return at

    def near(self):
        net, p = self.net, self.net.place
        self.x_r = self.pair(1)
        self.last.append(net.send(self.total.at[1, self.x_r], self.all_l.at[1], p.at_x(1)))
        self.x_l = self.pair(3)
        self.last.append(net.send(self.total.at[0, self.x_l], self.all_r.at[0], p.at_x(3)))

    def far(self):
        net, p = self.net, self.net.place
        x_2 = self.pair(2)
        self.half_r = net.send(self.total.at[0, x_2], self.from_l, p.at_x(1))
        self.half_l = net.send(self.total.at[1, x_2], self.from_r, p.at_x(3))

    def on(self):
        net, p = self.net, self.net.place
        self.half_r.wait_recv()
        self.total[0, self.x_r] = add(self.total[0, self.x_r], self.from_l[...])
        self.last.append(net.send(self.total.at[0, self.x_r], self.all_l.at[0], p.at_x(1)))
        self.half_l.wait_recv()
        self.total[1, self.x_l] = add(self.total[1, self.x_l], self.from_r[...])
        self.last.append(net.send(self.total.at[1, self.x_l], self.all_r.at[1], p.at_x(3)))

    def result(self):
        for copy in self.last:
            copy.wait_recv()
        mine = self.total[:, self.net.place.x].astype(F32)
        return mine + self.all_l[...].astype(F32) + self.all_r[...].astype(F32)


def ffn_kernel(cuts, *refs):
    (part, x_rows, g_rows, gain, own_down, w_ffn, g_all), refs = refs[:7], refs[7:]
    (hidden, d_hidden, d_gain, branch_all, out_part, ffn_sum, down_out), refs = refs[:7], refs[7:]
    (w_in, w_down, g_buf, nf_all, normed, act, d_in, back, branch, d_ffn, d_down, out_buf), refs = refs[:12], refs[12:]
    scratch = [refs[6 * n : 6 * n + 6] for n in range(5)]
    net = Net(*refs[-3:])
    p = net.place
    loads = [net.load(w_ffn, w_in), net.load(g_all, g_buf)]
    meet(team_peers(p) + group_peers(p))
    two, _, n, width = part.shape
    half = w_down.shape[0]
    pieces = [pl.ds(m * n // 2, n // 2) for m in range(2)]

    def finish_rows(piece):
        def finish(sums):
            h = x_rows[:, piece].astype(F32) + sums
            hidden[:, piece] = h
            scale = lax.rsqrt(jnp.mean(h * h, axis=-1, keepdims=True) + EPS_NORM)
            normed[:, piece] = (h * scale * gain[1:2, :][None]).astype(BF16)

        return finish

    jobs = Jobs(
        *[
            scatter_team(net, part.at[:, :, piece], *scratch[m], finish_rows(piece))
            for m, piece in enumerate(pieces)
        ],
        gather_groups(net, own_down, w_down, *halves(width)),
    )
    blocks = [TeamBlocks(net, normed.at[:, piece], nf_all.at[:, :, piece]) for piece in pieces]
    jobs.step(0, 1, 2, 0, 1, 2, 2, 2, 0, 1)
    for m in range(2):
        jobs.step(m)
        blocks[m].start()
    jobs.drain()
    for copy in loads:
        copy.wait()
    net.settle()
    sums = [
        TeamSum(net, back.at[:, :, piece], *scratch[2 + m]) for m, piece in enumerate(pieces)
    ]

    def flat(ref, at):
        return ref[:, pl.ds(2 * at, 2)].reshape(4 * n, ref.shape[3])

    def work(d):
        at = p.chip(d)
        pre = mm(flat(nf_all, at), w_in[...])
        gate, up = pre[:, :half], pre[:, half:]
        sig = jax.nn.sigmoid(gate)
        silu = gate * sig
        act[:, pl.ds(2 * at, 2)] = (silu * up).astype(BF16).reshape(two, 2, n, half)
        d_act = mm_nt(flat(g_buf, at), w_down[...])
        d_gate = (d_act * up * (sig + silu * (1.0 - sig))).astype(BF16)
        d_up = (d_act * silu).astype(BF16)
        d_pre = jnp.concatenate([d_gate, d_up], axis=1)
        d_in[:, pl.ds(2 * at, 2)] = d_pre.reshape(two, 2, n, 2 * half)
        back[:, pl.ds(2 * at, 2)] = mm_nt(d_pre, w_in[...]).astype(BF16).reshape(two, 2, n, width)
        for s in sums:
            s.ready(d)

    for b in blocks:
        b.mine()
    work(0)
    for b in blocks:
        b.hand_on()
    for b in blocks:
        b.from_l.wait_recv()
    work(3)
    for b in blocks:
        b.opposite()
    for b in blocks:
        b.from_r.wait_recv()
    work(1)
    for s in sums:
        s.near()
    for b in blocks:
        for copy in b.far:
            copy.wait_recv()
    work(2)
    for s in sums:
        s.far()
    for s in sums:
        s.pair(0)
    rows = two * 8 * n
    step = width // 4
    for k in range(4):
        cols = slice(k * step, (k + 1) * step)
        left = nf_all[:, :, :, cols].reshape(rows, step)
        d_ffn[cols, :] = mm_tn(left, d_in[...].reshape(rows, 2 * half)).astype(BF16)
        if k in (1, 2):
            sums[k - 1].on()
    group = scatter_groups(net, d_ffn, ffn_sum, cuts, *scratch[4])
    next(group)
    d_gain[...] = jnp.zeros_like(d_gain)
    teams = []
    for s, piece in zip(sums, pieces):
        d_h, d_g = norm_back(hidden[:, piece], gain[1:2, :][None], s.result())
        d_h = d_h + g_rows[:, piece].astype(F32)
        d_hidden[:, piece] = d_h
        branch[:, piece] = d_h.astype(BF16)
        d_gain[...] += jnp.sum(jnp.sum(d_g, axis=0), axis=0, keepdims=True)
        teams.append(gather_team(net, branch.at[:, piece], branch_all.at[:, :, piece]))
        next(teams[-1])
    step = half // 2
    for k in range(2):
        cols = slice(k * step, (k + 1) * step)
        left = act[:, :, :, cols].reshape(rows, step)
        d_down[cols, :] = mm_tn(left, g_buf[...].reshape(rows, width)).astype(BF16)
    net.keep(d_down, down_out)
    for h in range(two):
        for t in range(0, 8, 4):
            left = act[h, t : t + 4].reshape(4 * n, half)
            out_buf[h, t : t + 4] = mm(left, w_down[...]).astype(BF16).reshape(4, n, width)
    net.keep(out_buf, out_part)
    for team in teams:
        next(team)
    next(group)
    next(group)
    jobs = Jobs(*teams, group)
    jobs.drain()
    net.finish()


def ffn(part, x_rows, g_rows, gain, own_down, w_ffn, g_all):
    two, n, width = x_rows.shape
    cols = w_ffn.shape[1]
    half, rows = cols // 2, own_down.shape[0]
    every = (two, 8, n, width)
    share = width // 16
    cuts = (0, half, cols)
    return pl.pallas_call(
        functools.partial(ffn_kernel, cuts),
        out_shape=[
            SHAPE((two, n, width), F32),
            SHAPE((two, n, width), F32),
            SHAPE((1, width), F32),
            SHAPE(every, BF16),
            SHAPE(every, BF16),
            SHAPE((share, cols), BF16),
            SHAPE((16 * rows, width), BF16),
        ],
        in_specs=[ANY, VMEM, VMEM, VMEM, ANY, ANY, ANY],
        out_specs=[VMEM, VMEM, VMEM, ANY, ANY, VMEM, ANY],
        scratch_shapes=[
            pltpu.VMEM((width, cols), BF16),
            pltpu.VMEM((half, width), BF16),
            pltpu.VMEM(every, BF16),
            pltpu.VMEM(every, BF16),
            pltpu.VMEM((two, n, width), BF16),
            pltpu.VMEM((two, 8, n, half), BF16),
            pltpu.VMEM((two, 8, n, cols), BF16),
            pltpu.VMEM(every, BF16),
            pltpu.VMEM((two, n, width), BF16),
            pltpu.VMEM((width, cols), BF16),
            pltpu.VMEM((half, width), BF16),
            pltpu.VMEM(every, BF16),
        ]
        + scatter_team_scratch(n // 2, width) * 4
        + scatter_groups_scratch(share, cuts)
        + sems(
            4 * SCATTER_TEAM + 4 * GATHER_TEAM + GATHER_GROUPS + SCATTER_GROUPS_FLAT,
            2 + 2 * SCATTER_TEAM_LOADS + 2 + 2 + 2 + 2 + SCATTER_GROUPS_FLAT_LOADS,
        ),
        compiler_params=params(3),
        name="ffn",
    )(part, x_rows, g_rows, gain, own_down, w_ffn, g_all)


def trade_out_back(net, d_out, whole):
    p = net.place
    rows, middle, own = [], [], []
    cases = [(d, k) for d in (2, 1, 3, 0) for k in (1, 0)]
    for d, k in cases:
        xd, cd = p.chip(d), lax.rem(p.c + k, 2)
        for side, col in enumerate((lanes(3 * xd + 2 * cd), lanes(3 * xd + 1))):
            src = d_out.at[pl.ds(0, HD), col]
            dst = whole.at[lanes(3 * p.x + 2 * p.c), pl.ds(side * HD, HD)]
            if d + k:
                rows.append(net.send(src, dst, p.at_xc(d, k)))
            else:
                own.append(net.local(src, dst))
                own[-1].start()
    for d, k in cases:
        xd, cd = p.chip(d), lax.rem(p.c + k, 2)
        for side, col in enumerate((lanes(3 * xd + 2 * cd), lanes(3 * xd + 1))):
            src = d_out.at[pl.ds(HD, HD), col]
            dst = whole.at[lanes(3 * p.x + 1), pl.ds(side * HD, HD)]
            if d + k:
                middle.append((k, net.prepare(src, dst, p.at_xc(d, k))))
            else:
                middle.append((-1, net.local(src, dst)))

    @pl.when(p.c == 0)
    def _():
        for _, copy in middle:
            copy.start()

    yield
    for copy in rows:
        copy.wait_recv()
    for copy in own:
        copy.wait()
    for core in range(2):

        @pl.when(p.c == core)
        def _(core=core):
            for k, copy in middle:
                if k == core:
                    copy.wait_recv()

    @pl.when(p.c == 0)
    def _():
        for k, copy in middle:
            if k < 0:
                copy.wait()
            else:
                copy.wait_send()

    yield


TRADE_BACK = 28


def back_kernel(cuts, *refs):
    (marks, gains, d_gain_f, x_rows, hidden, d_hidden, ffn_sum), refs = refs[:7], refs[7:]
    (whole, w_out, mixed, normed, branch, part_o, d_down), refs = refs[:7], refs[7:]
    given, refs = refs[:10], refs[10:]
    (output, d_tokens, got_heads, got_rest, down_sum), refs = refs[:5], refs[5:]
    bufs, refs = refs[:10], refs[10:]
    (w_buf, wo_buf, mixed_buf, normed_buf, rows_buf, do, d_out, d_ext, d_conv), refs = refs[:9], refs[9:]
    (d_head_a, d_head_b, d_small, turned, trade, out_rows, d_rows), refs = refs[:7], refs[7:]
    (sum_a, sum_b, sum_s, sum_o, packs_heads, packs_rest), refs = refs[:6], refs[6:]
    own, refs = refs[:7], refs[7:]
    scratch = [refs[6 * n : 6 * n + 6] for n in range(7)]
    net = Net(*refs[-3:])
    p = net.place
    qkvp, raw, vec, *saved = bufs
    two, _, n, width = rows_buf.shape
    rows = two * 8 * n
    first = [net.load(w_out, wo_buf), net.load(branch, rows_buf), net.load(mixed, mixed_buf)]
    second = [net.load(given[m], bufs[m]) for m in (0,)]
    second.append(net.load(given[3].at[0], bufs[3].at[0]))
    meet(team_all(p) + group_peers(p))

    def finish(sums):
        out_rows[...] = (hidden[...] + sums).astype(BF16)

    def out_grad():
        yield from trade_out_back(net, d_out, trade)
        yield from scatter_groups(net, trade, sum_o, cuts[1], *scratch[0])

    def output_rows():
        yield from scatter_team(net, part_o, *scratch[1], finish)
        yield from swap_rows(net, ((out_rows, output),))

    jobs = Jobs(
        output_rows(), out_grad(), scatter_groups(net, d_down, down_sum, cuts[0], *scratch[2])
    )
    jobs.step(0)
    for copy in first:
        copy.wait()
    third = [net.load(given[m].at[0], bufs[m].at[0]) for m in range(4, 10)]
    third += [net.load(given[m], bufs[m]) for m in (1, 2)]
    third.append(net.load(whole.at[:, pl.ds(0, EXT_W)], w_buf))
    branch_rows = rows_buf[...].reshape(rows, width)
    d_mixed = mm_nt(branch_rows, wo_buf[...])
    do[:, :HD] = d_mixed[:, :HD]
    do[:, HD:] = jnp.where(p.c == 0, d_mixed[:, HD:], 0.0)
    d_out[...] = mm_tn(mixed_buf[...], branch_rows).astype(BF16)
    jobs.step(1, 2)
    fourth = [net.load(normed, normed_buf)]
    later = []
    for copy in second:
        copy.wait()
    waits = [third, None, None, None, later, None, None, None]
    steps = [(0,), (), (), (0,), (2, 2), (), (1,), (1,)]

    def poke():
        jobs.step(*steps.pop(0))
        for copy in waits.pop(0) or ():
            copy.wait()
        if len(steps) == 7:
            fourth.append(net.load(given[3].at[1], bufs[3].at[0]))

    side = 4 * HD
    d_raw = 0.0
    sums_a = scatter_groups(net, d_head_a, sum_a, cuts[2], *scratch[3])
    sums_b = scatter_groups(net, d_head_b, sum_b, cuts[2], *scratch[4])
    for s, (head, grads, job) in enumerate(zip(heads_here(), (d_head_a, d_head_b), (sums_a, sums_b))):
        d_raw = d_raw + bwd_slot(
            poke, s, head, qkvp, raw, w_buf.at[:, pl.ds(HEADS_W, HD)], marks, vec, mixed_buf, do, *saved, d_ext, d_conv, *own
        )
        if s == 0:
            later += [net.load(given[m].at[1], bufs[m].at[0]) for m in range(4, 10)]
            for copy in fourth:
                copy.wait()
        for k in range(4):
            part = slice(k * width // 4, (k + 1) * width // 4)
            grads[part, :] = mm_tn(normed_buf[:, part], d_ext[:, s * side : (s + 1) * side]).astype(BF16)
        next(job)
        poke()
    d_ext[:, HEADS_W:] = d_raw.astype(d_ext.dtype)
    next(sums_a)
    next(sums_a)

    sums = TeamSum(net, rows_buf, *scratch[5])
    turned[...] = jnp.zeros_like(turned)

    def work(d):
        at = p.chip(d)
        total = 0.0
        for h in range(two):
            here = pl.ds(pl.multiple_of((h * 8 + 2 * at) * n, 2 * n), 2 * n)
            y = mm_nt(d_ext[here, :], w_buf[...])
            total = total + jnp.sum(y * normed_buf[here, :].astype(F32), axis=0, keepdims=True)
            rows_buf[h, pl.ds(2 * at, 2)] = y.astype(BF16).reshape(2, n, width)
        turned[0:1, :] += total
        sums.ready(d)

    work(2)
    work(1)
    sums.far()
    work(3)
    sums.near()
    work(0)
    sums.pair(0)
    head_a, head_b = heads_here()
    turned[0:1, :] = turned[0:1, :] / gains[0:1, :]
    turned[1:2, :] = d_gain_f[...]
    turned[CONV_AT : CONV_AT + TAPS, lanes(head_a)] = d_conv[0, :TAPS, :]
    turned[CONV_AT : CONV_AT + TAPS, lanes(head_b)] = d_conv[1, :TAPS, :]
    for k in range(width // HD):
        part = slice(k * HD, (k + 1) * HD)
        t = mm_tn(normed_buf[:, part], d_ext[:, HEADS_W:]) + turned[:, part].T
        d_small[part, :] = t.astype(BF16)
    sums_s = scatter_groups(net, d_small, sum_s, cuts[3], *scratch[6])
    next(sums_s)
    next(sums_b)
    next(sums_b)
    sums.on()
    jobs.step(0, 1, 1)
    Jobs(sums_a).drain()
    jobs.drain()
    eight, padded, _ = packs_heads.shape
    spread = thin_rows(sum_a.shape[0] // eight, padded).T

    def pack(part, packs, at):
        wide = mm(spread, part[...]).astype(BF16)
        packs[:, :, at : at + part.shape[1]] = wide.reshape(eight, padded, part.shape[1])

    pack(sum_a, packs_rest, 0)
    pack(sum_o, packs_rest, side)
    pack(ffn_sum, packs_rest, side + 2 * HD)
    rest = all_to_team(net, packs_rest, got_rest)
    next(rest)
    next(sums_s)
    d_x, _ = norm_back(x_rows[...].astype(F32), gains[0:1, :][None], sums.result())
    d_rows[...] = (d_x + d_hidden[...]).astype(BF16)
    swaps = swap_rows(net, ((d_rows, d_tokens),))
    next(swaps)
    Jobs(sums_b, sums_s).drain()
    pack(sum_b, packs_heads, 0)
    pack(sum_s, packs_heads, side)
    interleave(all_to_team(net, packs_heads, got_heads), swaps, rest)
    net.finish()


def back(values, arrays, given):
    marks, gains, d_gain_f, x_rows, hidden, d_hidden, ffn_sum = values
    whole, w_out, mixed, normed, branch, part_o, d_down = arrays
    two, n, width = hidden.shape
    r = width // 16
    down = d_down.shape[0] // 16
    side = 4 * HD
    ffn_w = ffn_sum.shape[1]
    cuts = [(0, width // 2, width), (0, HD, 2 * HD), (0, side // 2, side), (0, HD, HD)]
    rows = SHAPE((two, n, width), BF16)
    packs = [(8, 16, side + HD), (8, 16, side + 2 * HD + ffn_w)]
    vmem = pltpu.VMEM
    return pl.pallas_call(
        functools.partial(back_kernel, cuts),
        out_shape=[rows, rows] + [SHAPE(a, BF16) for a in packs] + [SHAPE((down, width), F32)],
        in_specs=[VMEM] * 7 + [ANY] * (7 + len(given)),
        out_specs=[ANY] * 4 + [VMEM],
        scratch_shapes=[vmem((1,) + a.shape[1:] if m > 2 else a.shape, a.dtype) for m, a in enumerate(given)]
        + [
            vmem((width, EXT_W), BF16),
            vmem(w_out.shape, BF16),
            vmem(mixed.shape, BF16),
            vmem(normed.shape, BF16),
            vmem(branch.shape, BF16),
            vmem((SEQ, 2 * HD), F32),
            vmem((2 * HD, width), BF16),
            vmem((SEQ, EXT_W), BF16),
            vmem((2, 8, HD), F32),
            vmem((width, side), BF16),
            vmem((width, side), BF16),
            vmem((width, HD), BF16),
            vmem((HD, width), F32),
            vmem((width, 2 * HD), BF16),
            vmem((two, n, width), BF16),
            vmem((two, n, width), BF16),
            vmem((r, side), BF16),
            vmem((r, side), BF16),
            vmem((r, HD), BF16),
            vmem((r, 2 * HD), BF16),
        ]
        + [vmem(a, BF16) for a in packs]
        + bwd_scratch()
        + scatter_groups_scratch(r, cuts[1])
        + scatter_team_scratch(n, width)
        + scatter_groups_scratch(down, cuts[0])
        + scatter_groups_scratch(r, cuts[2])
        + scatter_groups_scratch(r, cuts[2])
        + scatter_team_scratch(n, width)
        + scatter_groups_scratch(r, cuts[3])
        + sems(
            TRADE_BACK + 2 * SCATTER_TEAM + 4 * SCATTER_GROUPS_FLAT + 2 * SCATTER_GROUPS_FLAT + 2 + 2 * TO_TEAM,
            3 + 3 + 9 + 8 + 4 + SCATTER_TEAM_LOADS + 6 * SCATTER_GROUPS_FLAT_LOADS + 2 + 2,
        ),
        compiler_params=params(5),
        name="back",
    )(*values, *arrays, *given)


def unpack_kernel(heads, rest, rows_in, tokens_in, down_in, *outs):
    kinds, gate, up, small, rows, tokens, down = outs[:5], outs[5], outs[6], outs[7], outs[8], outs[9], outs[10]
    share = small.shape[0]
    side = 4 * HD
    for n, out in enumerate(kinds):
        for x in range(4):
            for j in range(3):
                t = 2 * x + j // 2
                if n < 4:
                    src, col = (heads, n * HD) if j == 1 else (rest, n * HD)
                else:
                    src, col = rest, side + (j % 2) * HD
                head = 3 * x + j
                out[:, head * HD : (head + 1) * HD] = src[t, :share, col : col + HD].astype(F32)
    total = heads[0, :, side : side + SMALL_W].astype(F32)
    for t in range(1, 8):
        total = total + heads[t, :, side : side + SMALL_W].astype(F32)
    small[...] = total[:share]
    for n, out in enumerate((gate, up)):
        for tile in range(32):
            e = tile // 2
            col = side + 2 * HD + n * 4 * HD + (e // 4) * HD
            parts = [
                (rest[t, :, col : col + HD].astype(F32), e % 4)
                for t in range(4 * (tile % 2), 4 * (tile % 2) + 4)
            ]
            out[:, tile * HD : (tile + 1) * HD] = shift_pieces(parts)[:share]
    rows[...] = rows_in[...]
    tokens[...] = tokens_in[...]
    down[...] = down_in[...]


def unpack(heads, rest, rows, tokens, down, share, ff):
    two, n, width = rows.shape
    return pl.pallas_call(
        unpack_kernel,
        out_shape=[SHAPE((share, width), F32)] * 5
        + [SHAPE((share, ff), F32)] * 2
        + [SHAPE((share, HD), F32)]
        + [SHAPE(rows.shape, BF16)] * 2
        + [SHAPE(down.shape, F32)],
        in_specs=[VMEM] * 5,
        out_specs=[VMEM] * 11,
        compiler_params=pltpu.CompilerParams(vmem_limit_bytes=VM),
        name="unpack",
    )(heads, rest, rows, tokens, down)


def per_device(
    tokens,
    doc_start,
    gain_attn,
    w_query,
    w_key,
    w_value,
    w_path,
    conv_path,
    w_beta,
    w_out,
    gain_ffn,
    w_gate,
    w_up,
    w_down,
    grad_out,
):
    zh = lax.axis_index("zh")
    width = tokens.shape[2]
    share = w_query.shape[0]
    small = jnp.concatenate([gain_attn[:, None], gain_ffn[:, None], conv_path.T, w_beta], axis=1)
    small = jnp.pad(small, ((0, 0), (0, SMALL_W - small.shape[1])))
    x_rows, g_rows, x_all, whole, own_ffn = start(
        (w_query, w_key, w_value, w_path, w_out), w_gate, w_up, small, tokens, grad_out
    )
    doc_rows = jnp.cumsum(doc_start, axis=1)
    docs = jnp.where(zh == 0, doc_rows[0], doc_rows[1]).astype(F32)
    marks = [docs]
    for tap in range(1, TAPS):
        same = docs[: SEQ - tap] == docs[tap:]
        marks.append(jnp.concatenate([jnp.zeros((tap,), F32), same.astype(F32)]))
    drow = jnp.stack(marks + marks)
    marks = drow.T

    normed, qkvp, raw, vec, mixed, gains, *saved, w_ffn, g_all, w_out_t, part = attn_fwd(
        x_all.reshape(SEQ, width), whole, marks, drow, own_ffn, g_rows
    )
    hidden, d_hidden, d_gain_f, branch_all, out_part, ffn_sum, d_down = ffn(
        part, x_rows, g_rows, gains, w_down, w_ffn, g_all
    )
    output, d_tokens, heads_back, rest_back, d_down = back(
        (marks, gains, d_gain_f, x_rows, hidden, d_hidden, ffn_sum),
        (whole, w_out_t, mixed, normed, branch_all, out_part, d_down),
        (qkvp, raw, vec, *saved),
    )
    *kinds, d_gate_w, d_up_w, small, output, d_tokens, d_down = unpack(
        heads_back, rest_back, output, d_tokens, d_down, share, w_gate.shape[1]
    )
    return (
        output,
        d_tokens,
        small[:, 0],
        *kinds[:4],
        small[:, 2:6].T,
        small[:, 6:18],
        kinds[4],
        small[:, 1],
        d_gate_w,
        d_up_w,
        d_down,
    )


def solution(mesh):
    names = ("zl", "y", "zh", "x", "c")
    fine = Mesh(mesh.devices.reshape(2, 4, 2, 4, 2), names)
    dp, ctx = names[:2], names[2:]
    rows, flat, mat, taps = P(dp, ctx, None), P(names), P(names, None), P(None, names)
    return jax.shard_map(
        per_device,
        mesh=fine,
        in_specs=(
            rows, P(dp, None), flat, mat, mat, mat, mat, taps, mat, mat, flat, mat, mat, mat, rows,
        ),
        out_specs=(
            rows, rows, flat, mat, mat, mat, mat, taps, mat, mat, flat, mat, mat, mat,
        ),
        check_vma=False,
    )
```

```python
import functools

import jax
import jax.numpy as jnp
from jax import lax
from jax.experimental import pallas as pl
from jax.experimental.pallas import tpu as pltpu
from jax.sharding import Mesh, PartitionSpec as P

F32, BF16 = jnp.float32, jnp.bfloat16
VM = 61 * 1024 * 1024

SEQ, HD, BLK = 1024, 128, 128
NB = SEQ // BLK
NQC = (NB * (NB - 1) // 2) * BLK
SCALE = HD ** (-0.5)
GROUP, GROUP_BACK = 8, 4


def mm(a, b, dims=((1,), (0,))):
    return lax.dot_general(
        a.astype(BF16), b.astype(BF16), (dims, ((), ())), preferred_element_type=F32
    )


def mm_nt(a, b):
    return mm(a, b, ((1,), (1,)))


def mm_tn(a, b):
    return mm(a, b, ((0,), (0,)))


def split(a):
    high = a.astype(BF16)
    return high, (a - high.astype(F32)).astype(BF16)


def mm3(a, b):
    ah, al = split(a)
    bh, bl = split(b)
    return mm(ah, bh) + (mm(ah, bl) + mm(al, bh))


def iota2(axis):
    return lax.broadcasted_iota(jnp.int32, (BLK, BLK), axis)


BASE = 16


def unit_inverses(lowers):
    row, col = iota2(0), iota2(1)
    eye = (row == col).astype(F32)
    in_base = (row // BASE) == (col // BASE)
    narrow = [jnp.where(in_base, low, 0.0) for low in lowers]
    inv = [eye for _ in lowers]
    for u in range(BASE - 1):
        pick = (col % BASE) == u
        coef = [jnp.sum(jnp.where(pick, low, 0.0), axis=1, keepdims=True) for low in narrow]
        for n, (t, c) in enumerate(zip(inv, coef)):
            t3 = t.reshape(BLK // BASE, BASE, BLK)
            lead = jnp.broadcast_to(t3[:, u : u + 1, :], t3.shape).reshape(BLK, BLK)
            inv[n] = t - c * lead
    size = BASE
    while size < BLK:
        off = ((row // (2 * size)) == (col // (2 * size))) & ((row // size) != (col // size))
        mid = [mm3(t, jnp.where(off, low, 0.0)) for t, low in zip(inv, lowers)]
        inv = [t - mm3(m, t) for t, m in zip(inv, mid)]
        size *= 2
    return inv


def betas_of(raw, head):
    lane = lax.broadcasted_iota(jnp.int32, raw.shape, 1)
    return 2.0 * jax.nn.sigmoid(
        jnp.sum(jnp.where(lane == head + BETA_AT, raw, 0.0), axis=1, keepdims=True)
    )


BETA_AT = 6
CONV_AT = 2
TAPS = 4


def conv_weights(small, head):
    part = small[pl.ds(pl.multiple_of(head * HD, HD), HD), :].astype(F32)
    return part.T[CONV_AT : CONV_AT + TAPS, :]


def convolve(path, taps, marks):
    total = taps[0:1, :] * path
    for m in range(1, TAPS):
        total = total + taps[m : m + 1, :] * (pltpu.roll(path, m, 0) * marks[:, m : m + 1])
    return total


def own_blocks(s, q, k, w, bcol, stores):
    t_out, a_out, z_out, m_out, kp_out, qm_buf, s_buf = stores
    row, col = iota2(0), iota2(1)
    strict, closed = row > col, row >= col
    eye = (row == col).astype(F32)

    def group(g, carry):
        sl = [pl.ds(pl.multiple_of((g * GROUP + n) * BLK, BLK), BLK) for n in range(GROUP)]
        qs = [q[r, :] for r in sl]
        ks = [k[r, :] for r in sl]
        ws = [w[r, :] for r in sl]
        bc = [jnp.broadcast_to(bcol[r, :], (BLK, BLK)) for r in sl]
        br = [b.T for b in bc]
        low = [jnp.where(strict, mm_nt(x, x), 0.0) * b for x, b in zip(ws, br)]
        inv = unit_inverses(low)
        m1 = [jnp.where(strict, mm_nt(x, y), 0.0) for x, y in zip(ws, ks)]
        gq = [jnp.where(closed, mm_nt(x, y), 0.0) * b for x, y, b in zip(qs, ws, br)]
        a = [mm(x, t) for x, t in zip(gq, inv)]
        z = [mm_tn(t, b * x.astype(F32)) for t, b, x in zip(inv, bc, ws)]
        sd = [mm_nt(x, y) - mm(p, m) for x, y, p, m in zip(qs, ks, a, m1)]
        qm = [x.astype(F32) - mm(p, y) for x, p, y in zip(qs, a, ws)]
        kmt = [x.astype(F32).T - mm_tn(zz, m) for x, zz, m in zip(ks, z, m1)]
        pm = [eye - mm_tn(zz, x) for zz, x in zip(z, ws)]
        for n, r in enumerate(sl):
            t_out[s, r, :] = inv[n].astype(t_out.dtype)
            a_out[s, r, :] = a[n].astype(a_out.dtype)
            z_out[s, r, :] = z[n].astype(z_out.dtype)
            m_out[s, r, :] = m1[n].astype(m_out.dtype)
            kp_out[s, r, :HD] = kmt[n].astype(BF16)
            kp_out[s, r, HD:] = pm[n].astype(BF16)
            qm_buf[r, :] = qm[n]
            s_buf[r, r] = sd[n]
        return carry

    lax.fori_loop(0, NB // GROUP, group, 0)


def sweep(s, qc, kp, qm_buf, x_buf, s_buf):
    at = NQC
    for j in range(NB - 2, -1, -1):
        r0 = (j + 1) * BLK
        rows = SEQ - r0
        x_buf[r0 : r0 + BLK, :] = qm_buf[r0 : r0 + BLK, :]
        x = x_buf[r0:, :].astype(BF16)
        at -= rows
        qc[s, at : at + rows, :] = x
        both = mm(x, kp[s, j * BLK : r0, :])
        s_buf[r0:, j * BLK : r0] = both[:, :HD]
        x_buf[r0:, :] = both[:, HD:]


def weigh(s, v, dcol, drow, s_buf, probs, o):
    for i in range(NB):
        lo, width = i * BLK, (i + 1) * BLK
        t = s_buf[lo:width, :width] * SCALE
        seen = dcol[lo:width, 0:1] == drow[0:1, :width]
        seen = seen & (
            lax.broadcasted_iota(jnp.int32, (BLK, width), 0) + lo
            >= lax.broadcasted_iota(jnp.int32, (BLK, width), 1)
        )
        t = jnp.where(seen, t, -1e30)
        e = jnp.exp(t - jnp.max(t, axis=1, keepdims=True))
        p = (e * (1.0 / jnp.sum(e, axis=1, keepdims=True))).astype(BF16)
        probs[s, lo:width, :width] = p
        o[lo:width, :] = mm(p, v[:width, :])


def project(x_all, whole, gains, normed, qkvp, raw):
    rows = 256
    width = x_all.shape[1]
    for n in range(width // HD):
        cols = slice(n * HD, (n + 1) * HD)
        gains[:, cols] = whole[cols, 8 * HD : 9 * HD].astype(F32).T[:8, :]

    def block(i, carry):
        at = pl.ds(pl.multiple_of(i * rows, rows), rows)
        x = x_all[at, :].astype(F32)
        scale = lax.rsqrt(jnp.mean(x * x, axis=1, keepdims=True) + 1e-05)
        n = (x * scale * gains[0:1, :]).astype(BF16)
        normed[at, :] = n
        y = mm(n, whole[:, : 9 * HD])
        qkvp[at, :] = y[:, : 8 * HD].astype(BF16)
        raw[at, :] = y[:, 8 * HD :]
        return carry

    lax.fori_loop(0, SEQ // rows, block, 0)


def heads_here():
    chip, core = lax.axis_index("x"), lax.axis_index("c")
    return 3 * chip + 2 * core, 3 * chip + 1


def fwd_slot(poke, s, head, small, marks, drow, qkvp, raw, vec, o, probs, qc, t_out, a_out, z_out, m_out, kp_out, s_buf, x_buf, qm_buf, b_buf):
    cols = slice(s * HD, (s + 1) * HD)
    q, k, v, path = (qkvp.at[:, (4 * s + n) * HD : (4 * s + n + 1) * HD] for n in range(4))
    taps = conv_weights(small, head)
    conved = convolve(path[...].astype(F32), taps, marks[...])
    unit = conved * lax.rsqrt(jnp.sum(conved * conved, axis=1, keepdims=True) + 1e-06)
    vec[:, cols] = unit.astype(BF16)
    b_buf[...] = betas_of(raw[...], head)
    own_blocks(s, q, k, vec.at[:, cols], b_buf, (t_out, a_out, z_out, m_out, kp_out, qm_buf, s_buf))
    poke()
    sweep(s, qc, kp_out, qm_buf, x_buf, s_buf)
    poke()
    weigh(s, v, marks, drow, s_buf, probs, o.at[:, cols])


def score_grads(s, v, o, do, probs, ds_buf, dv):
    for i in range(NB):
        lo, width = i * BLK, (i + 1) * BLK
        p = probs[0, lo:width, :width].astype(F32)
        g = do[lo:width, :]
        delta = jnp.sum(g * o[lo:width, :].astype(F32), axis=1, keepdims=True)
        ds = p * (mm_nt(g, v[:width, :]) - delta) * SCALE
        ds_buf[lo:width, :width] = ds.astype(BF16)
    for j in range(NB):
        lo = j * BLK
        dv[lo : lo + BLK, :] = mm_tn(probs[0, lo:, lo : lo + BLK], do[lo:, :]).astype(dv.dtype)


def sweep_back(s, qc, kp, ds_buf, x_buf, dkm_buf, dpm_buf):
    x_buf[...] = jnp.zeros_like(x_buf)
    dkm_buf[SEQ - BLK :, :] = jnp.zeros((BLK, HD), F32)
    dpm_buf[SEQ - BLK :, :] = jnp.zeros((BLK, HD), F32)
    at = 0
    for j in range(NB - 1):
        lo, r0 = j * BLK, (j + 1) * BLK
        rows = SEQ - r0
        x = x_buf[r0:, :].astype(BF16)
        ds = ds_buf[r0:, lo:r0]
        qcj = qc[0, at : at + rows, :]
        at += rows
        both = mm_tn(qcj, jnp.concatenate([x, ds], axis=1))
        dpm_buf[lo:r0, :] = both[:, :HD]
        dkm_buf[lo:r0, :] = both[:, HD:].T
        x_buf[r0:, :] = mm_nt(jnp.concatenate([ds, x], axis=1), kp[0, lo:r0, :])


def own_blocks_back(s, q, k, w, bcol, saved, bufs, dq, dk, dw, db):
    t_in, a_in, z_in, m_in = saved
    ds_buf, x_buf, dkm_buf, dpm_buf = bufs
    row, col = iota2(0), iota2(1)
    strict, closed = row > col, row >= col

    def group(g, carry):
        sl = [pl.ds(pl.multiple_of((g * GROUP_BACK + n) * BLK, BLK), BLK) for n in range(GROUP_BACK)]
        rng = range(GROUP_BACK)
        Q = [q[r, :] for r in sl]
        K = [k[r, :] for r in sl]
        W = [w[r, :] for r in sl]
        bc = [jnp.broadcast_to(bcol[r, :], (BLK, BLK)) for r in sl]
        br = [b.T for b in bc]
        E = [ds_buf[r, r] for r in sl]
        T = [t_in[0, r, :] for r in sl]
        A = [a_in[0, r, :] for r in sl]
        Z = [z_in[0, r, :] for r in sl]
        M = [m_in[0, r, :] for r in sl]
        dQm = [x_buf[r, :] for r in sl]
        dKm = [dkm_buf[r, :] for r in sl]
        dPm = [dpm_buf[r, :] for r in sl]
        i1 = [mm_nt(W[n], W[n]) for n in rng]
        qw = [jnp.where(closed, mm_nt(Q[n], W[n]), 0.0) for n in rng]
        dA = [-(mm_nt(E[n], M[n]) + mm_nt(dQm[n], W[n])) for n in rng]
        dM = [jnp.where(strict, -(mm_tn(A[n], E[n]) + mm_nt(Z[n], dKm[n])), 0.0) for n in rng]
        dZ = [-(mm(M[n], dKm[n]) + mm_nt(W[n], dPm[n])) for n in rng]
        dW = [-(mm_tn(A[n], dQm[n]) + mm(Z[n], dPm[n])) for n in rng]
        dG = [jnp.where(closed, mm_nt(dA[n], T[n]), 0.0) for n in rng]
        bw = [bc[n] * W[n].astype(F32) for n in rng]
        dT = [mm_tn(qw[n] * br[n], dA[n]) + mm_nt(bw[n], dZ[n]) for n in rng]
        dBW = [mm(T[n], dZ[n]) for n in rng]
        dL = [mm_tn(T[n], dT[n]) for n in rng]
        dL = [jnp.where(strict, -mm_nt(dL[n], T[n]), 0.0) for n in rng]
        dI = [dL[n] * br[n] for n in rng]
        R = [dG[n] * br[n] for n in rng]
        for n, r in enumerate(sl):
            db[r, :] = jnp.sum(
                (dL[n] * i1[n] + dG[n] * qw[n]).T + dBW[n] * W[n].astype(F32), axis=1, keepdims=True
            )
            dq[r, :] = (dQm[n] + mm(E[n], K[n]) + mm(R[n], W[n])).astype(dq.dtype)
            dk[r, :] = (dKm[n] + mm_tn(E[n], Q[n]) + mm_tn(dM[n], W[n])).astype(dk.dtype)
            dw[r, :] = (
                dW[n]
                + bc[n] * dBW[n]
                + mm_tn(R[n], Q[n])
                + mm(dM[n], K[n])
                + mm(dI[n] + dI[n].T, W[n])
            )
        return carry

    lax.fori_loop(0, NB // GROUP_BACK, group, 0)


def bwd_slot(poke, s, head, qkvp, raw, small, marks, vec, o, do, probs, qc, t_in, a_in, z_in, m_in, kp, d_ext, d_conv, ds_buf, x_buf, dkm_buf, dpm_buf, b_buf, db_buf, dw_buf):
    cols = slice(s * HD, (s + 1) * HD)
    q, k, v, path = (qkvp.at[:, (4 * s + n) * HD : (4 * s + n + 1) * HD] for n in range(4))
    dq, dk, dv, dpath = (d_ext.at[:, (4 * s + n) * HD : (4 * s + n + 1) * HD] for n in range(4))
    score_grads(s, v, o.at[:, cols], do.at[:, cols], probs, ds_buf, dv)
    poke()
    sweep_back(s, qc, kp, ds_buf, x_buf, dkm_buf, dpm_buf)
    poke()
    beta = betas_of(raw[...], head)
    b_buf[...] = beta
    own_blocks_back(
        s, q, k, vec.at[:, cols], b_buf, (t_in, a_in, z_in, m_in), (ds_buf, x_buf, dkm_buf, dpm_buf), dq, dk, dw_buf, db_buf
    )
    poke()
    taps = conv_weights(small, head)
    raw_path = path[...].astype(F32)
    conved = convolve(raw_path, taps, marks[...])
    scale = lax.rsqrt(jnp.sum(conved * conved, axis=1, keepdims=True) + 1e-06)
    unit = conved * scale
    dw = dw_buf[...]
    d_conved = scale * (dw - unit * jnp.sum(dw * unit, axis=1, keepdims=True))
    total = taps[0:1, :] * d_conved
    d_conv[s, 0:1, :] = jnp.sum(d_conved * raw_path, axis=0, keepdims=True)
    for m in range(1, TAPS):
        marked = d_conved * marks[:, m : m + 1]
        d_conv[s, m : m + 1, :] = jnp.sum(marked * pltpu.roll(raw_path, m, 0), axis=0, keepdims=True)
        total = total + taps[m : m + 1, :] * pltpu.roll(marked, SEQ - m, 0)
    dpath[...] = total.astype(dpath.dtype)
    lane = lax.broadcasted_iota(jnp.int32, (SEQ, HD), 1)
    return jnp.where(lane == head + BETA_AT, db_buf[...] * beta * (1.0 - 0.5 * beta), 0.0)


def fwd_shapes(width):
    return [
        ((SEQ, width), BF16),
        ((SEQ, 8 * HD), BF16),
        ((SEQ, HD), F32),
        ((SEQ, 2 * HD), BF16),
        ((SEQ, 2 * HD), BF16),
        ((8, width), F32),
        ((2, SEQ, SEQ), BF16),
        ((2, NQC, HD), BF16),
        ((2, SEQ, BLK), BF16),
        ((2, SEQ, BLK), BF16),
        ((2, SEQ, BLK), BF16),
        ((2, SEQ, BLK), BF16),
        ((2, SEQ, 2 * HD), BF16),
    ]


def fwd_scratch():
    return [
        pltpu.VMEM((SEQ, SEQ), F32),
        pltpu.VMEM((SEQ, HD), F32),
        pltpu.VMEM((SEQ, HD), F32),
        pltpu.VMEM((SEQ, 1), F32),
    ]


def bwd_scratch():
    return (
        [pltpu.VMEM((SEQ, SEQ), BF16)]
        + [pltpu.VMEM((SEQ, HD), F32)] * 3
        + [pltpu.VMEM((SEQ, 1), F32)] * 2
        + [pltpu.VMEM((SEQ, HD), F32)]
    )


MESH = pl.DeviceIdType.MESH
ANY = pl.BlockSpec(memory_space=pl.ANY)
VMEM = pl.BlockSpec(memory_space=pltpu.VMEM)


class Place:
    def __init__(self):
        self.x, self.c = lax.axis_index("x"), lax.axis_index("c")
        self.y = lax.axis_index("y")
        self.zl, self.zh = lax.axis_index("zl"), lax.axis_index("zh")
        self.z = self.zh * 2 + self.zl

    def chip(self, d):
        return lax.rem(self.x + d, 4)

    def at_x(self, d):
        return {"x": lax.rem(self.x + d, 4)}

    def at_xc(self, d, k):
        return {"x": lax.rem(self.x + d, 4), "c": lax.rem(self.c + k, 2)}

    def sibling(self):
        return {"c": 1 - self.c}

    def at_y(self, d):
        return {"y": lax.rem(self.y + d, 4)}

    def at_z(self, d):
        z = lax.rem(self.z + d, 4)
        return {"zl": lax.rem(z, 2), "zh": z // 2}


class Net:
    def __init__(self, send_sem, recv_sem, local_sem):
        self.place = Place()
        self.send_sem, self.recv_sem, self.local_sem = send_sem, recv_sem, local_sem
        self.count, self.kept, self.locals, self.sent = 0, 0, [], []

    def prepare(self, src, dst, device):
        k = self.count
        self.count += 1
        return pltpu.make_async_remote_copy(
            src_ref=src,
            dst_ref=dst,
            send_sem=self.send_sem.at[k],
            recv_sem=self.recv_sem.at[k],
            device_id=device,
            device_id_type=MESH,
        )

    def send(self, src, dst, device):
        copy = self.prepare(src, dst, device)
        copy.start()
        self.sent.append(copy)
        return copy

    def local(self, src, dst):
        self.kept += 1
        return pltpu.make_async_copy(src, dst, self.local_sem.at[self.kept - 1])

    def load(self, src, dst):
        copy = self.local(src, dst)
        copy.start()
        return copy

    def keep(self, src, dst):
        self.locals.append(self.load(src, dst))

    def settle(self):
        for copy in self.locals:
            copy.wait()
        self.locals = []

    def finish(self):
        for copy in self.sent:
            copy.wait_send()
        self.settle()


def meet(devices):
    barrier = pltpu.get_barrier_semaphore()
    for device in devices:
        pl.semaphore_signal(barrier, inc=1, device_id=device, device_id_type=MESH)
    pl.semaphore_wait(barrier, len(devices))


class Jobs:
    def __init__(self, *jobs):
        self.all = list(jobs)
        self.jobs = list(jobs)

    def poke(self):
        for job in list(self.jobs):
            try:
                next(job)
            except StopIteration:
                self.jobs.remove(job)

    def step(self, *which):
        for n in which:
            next(self.all[n], None)

    def drain(self):
        while self.jobs:
            self.poke()


def interleave(*jobs):
    Jobs(*jobs).drain()


def team_peers(p):
    return [p.at_x(1), p.at_x(3), p.sibling()]


def team_all(p):
    return [p.at_xc(d, k) for d in range(4) for k in range(2) if d + k]


def group_peers(p):
    return [p.at_y(d) for d in (1, 2, 3)] + [p.at_z(d) for d in (1, 2, 3)]


def gather_team(net, own, out):
    p = net.place
    me, sib = 2 * p.x + p.c, p.sibling()
    right, left = p.at_x(1), p.at_x(3)
    t_l, t_r, t_2 = (2 * p.chip(d) + p.c for d in (3, 1, 2))
    to_r = net.send(own, out.at[:, me], right)
    to_l = net.send(own, out.at[:, me], left)
    shared = [net.send(own, out.at[:, me], sib)]
    net.keep(own, out.at[:, me])
    yield
    to_r.wait_recv()
    on_r = net.send(out.at[0, t_l], out.at[0, t_l], right)
    shared.append(net.send(out.at[:, t_l], out.at[:, t_l], sib))
    to_l.wait_recv()
    on_l = net.send(out.at[1, t_r], out.at[1, t_r], left)
    shared.append(net.send(out.at[:, t_r], out.at[:, t_r], sib))
    yield
    on_r.wait_recv()
    shared.append(net.send(out.at[0, t_2], out.at[0, t_2], sib))
    on_l.wait_recv()
    shared.append(net.send(out.at[1, t_2], out.at[1, t_2], sib))
    yield
    for copy in shared:
        copy.wait_recv()


GATHER_TEAM = 10


def add(a, b):
    return (a.astype(F32) + b.astype(F32)).astype(BF16)


def scatter_team(net, part, got, total, from_l, from_r, all_l, all_r, finish):
    p = net.place
    sib, right, left = p.sibling(), p.at_x(1), p.at_x(3)
    order = (2, 1, 3, 0)
    swaps, loads = [], []
    for d in order:
        at = p.chip(d)
        swaps.append(net.send(part.at[:, 2 * at + 1 - p.c], got.at[:, at], sib))
        loads.append(net.load(part.at[:, 2 * at + p.c], total.at[:, at]))

    def pair(n):
        swaps[n].wait_recv()
        loads[n].wait()
        at = p.chip(order[n])
        total[:, at] = add(total[:, at], got[:, at])
        return at

    yield
    x_2 = pair(0)
    half_r = net.send(total.at[0, x_2], from_l, right)
    half_l = net.send(total.at[1, x_2], from_r, left)
    x_r = pair(1)
    rest_r = net.send(total.at[1, x_r], all_l.at[1], right)
    x_l = pair(2)
    rest_l = net.send(total.at[0, x_l], all_r.at[0], left)
    pair(3)
    yield
    half_r.wait_recv()
    total[0, x_r] = add(total[0, x_r], from_l[...])
    last_r = net.send(total.at[0, x_r], all_l.at[0], right)
    half_l.wait_recv()
    total[1, x_l] = add(total[1, x_l], from_r[...])
    last_l = net.send(total.at[1, x_l], all_r.at[1], left)
    yield
    for copy in (rest_r, rest_l, last_r, last_l):
        copy.wait_recv()
    finish(total[:, p.x].astype(F32) + all_l[...].astype(F32) + all_r[...].astype(F32))


SCATTER_TEAM_LOADS = 4
SCATTER_TEAM = 10


def scatter_team_scratch(n, w):
    return [
        pltpu.VMEM((2, 4, n, w), BF16),
        pltpu.VMEM((2, 4, n, w), BF16),
        pltpu.VMEM((n, w), BF16),
        pltpu.VMEM((n, w), BF16),
        pltpu.VMEM((2, n, w), BF16),
        pltpu.VMEM((2, n, w), BF16),
    ]


def chunk_rows(y, z, rows):
    zl, zh = (z % 2, z // 2) if isinstance(z, int) else (lax.rem(z, 2), z // 2)
    return pl.ds(pl.multiple_of(((zl * 4 + y) * 2 + zh) * rows, rows), rows)


def halves(cols):
    mid = cols // 2
    return [(pl.ds(0, mid),) * 2], [(pl.ds(mid, cols - mid),) * 2]


def gather_groups(net, own, out, y_pieces, z_pieces, share=False):
    p = net.place
    rows = own.shape[0]
    shared = []
    for src, dst in y_pieces + z_pieces:
        net.keep(own.at[:, src], out.at[chunk_rows(p.y, p.z, rows), dst])

    def spread(pieces, y, z, devices, first=False):
        copies = []
        for src, dst in pieces:
            place = out.at[chunk_rows(y, z, rows), dst]
            copies += [net.send(own.at[:, src] if first else place, place, d) for d in devices]
        return copies

    def give(y, z, first=False):
        if share:
            src, dst = z_pieces[-1]
            place = out.at[chunk_rows(y, z, rows), dst]
            shared.append(net.send(own.at[:, src] if first else place, place, p.sibling()))

    order = (1, 3, 2)
    ys, zs = [p.at_y(d) for d in order], [p.at_z(d) for d in order]
    y_first = spread(y_pieces, p.y, p.z, ys, True)
    z_first = spread(z_pieces, p.y, p.z, zs, True)
    last = spread(y_pieces, p.y, p.z, zs, True)
    via_y = [(p.z, spread(z_pieces, p.y, p.z, ys, True))]
    give(p.y, p.z, True)
    yield
    for n, d in enumerate(order):
        for copy in y_first[n::3]:
            copy.wait_recv()
        last += spread(y_pieces, lax.rem(p.y + 4 - d, 4), p.z, zs)
        for copy in z_first[n::3]:
            copy.wait_recv()
        z = lax.rem(p.z + 4 - d, 4)
        via_y.append((z, spread(z_pieces, p.y, z, ys)))
        give(p.y, z)
        yield
    for z, copies in via_y:
        for n, d in enumerate(order):
            for copy in copies[n::3]:
                copy.wait_recv()
            give(lax.rem(p.y + 4 - d, 4), z)
    for copy in last + shared:
        copy.wait_recv()


GATHER_GROUPS = 30


def scatter_groups(net, part, out, cuts, z_got, z_sum, z_last, y_got, y_sum, y_last):
    p = net.place
    lo, mid, hi = cuts
    first, second = pl.ds(lo, mid - lo), pl.ds(mid, hi - mid)
    rows = z_sum.shape[1]
    both = hi > mid
    flat = len(part.shape) == 2
    order = (2, 1, 3)
    a, b, a_own, b_own = [], [], [], []
    for n, d in enumerate(order):
        z, y = lax.rem(p.z + d, 4), lax.rem(p.y + d, 4)
        if flat:
            for k in range(4):
                a.append(net.send(part.at[chunk_rows(k, z, rows), first], z_got.at[n, k], p.at_z(d)))
                if both:
                    b.append(net.send(part.at[chunk_rows(y, k, rows), second], y_got.at[n, k % 2, k // 2], p.at_y(d)))
        else:
            a.append(net.send(part.at[lax.rem(z, 2), :, z // 2, :, first], z_got.at[n], p.at_z(d)))
            if both:
                b.append(net.send(part.at[:, y, :, :, second], y_got.at[n], p.at_y(d)))
    if flat:
        for k in range(4):
            a_own.append(net.load(part.at[chunk_rows(k, p.z, rows), first], z_sum.at[k]))
            if both:
                b_own.append(net.load(part.at[chunk_rows(p.y, k, rows), second], y_sum.at[k % 2, k // 2]))
    else:
        a_own.append(net.load(part.at[p.zl, :, p.zh, :, first], z_sum))
        if both:
            b_own.append(net.load(part.at[:, p.y, :, :, second], y_sum))

    yield
    for copy in a_own:
        copy.wait()
    for copy in a:
        copy.wait_recv()
    for y in range(4):
        t = z_sum[y].astype(F32)
        for n in range(3):
            t = t + z_got[n, y].astype(F32)
        z_sum[y] = t.astype(BF16)
    a = [
        net.send(z_sum.at[lax.rem(p.y + d, 4)], z_last.at[n], p.at_y(d)) for n, d in enumerate(order)
    ]
    if both:
        yield
        for copy in b_own:
            copy.wait()
        for copy in b:
            copy.wait_recv()
        for zl in range(2):
            for zh in range(2):
                t = y_sum[zl, zh].astype(F32)
                for n in range(3):
                    t = t + y_got[n, zl, zh].astype(F32)
                y_sum[zl, zh] = t.astype(BF16)
        b = []
        for n, d in enumerate(order):
            z = lax.rem(p.z + d, 4)
            b.append(net.send(y_sum.at[lax.rem(z, 2), z // 2], y_last.at[n], p.at_z(d)))
    yield
    for copy in a:
        copy.wait_recv()
    t = z_sum[p.y].astype(F32)
    for n in range(3):
        t = t + z_last[n].astype(F32)
    out[:, first] = t.astype(out.dtype)
    if both:
        yield
        for copy in b:
            copy.wait_recv()
        t = y_sum[p.zl, p.zh].astype(F32)
        for n in range(3):
            t = t + y_last[n].astype(F32)
        out[:, second] = t.astype(out.dtype)


SCATTER_GROUPS_LOADS = 2
SCATTER_GROUPS_FLAT_LOADS = 8
SCATTER_GROUPS = 12
SCATTER_GROUPS_FLAT = 30


def scatter_groups_scratch(r, cuts):
    a, b = cuts[1] - cuts[0], max(cuts[2] - cuts[1], HD)
    return [
        pltpu.VMEM((3, 4, r, a), BF16),
        pltpu.VMEM((4, r, a), BF16),
        pltpu.VMEM((3, r, a), BF16),
        pltpu.VMEM((3, 2, 2, r, b), BF16),
        pltpu.VMEM((2, 2, r, b), BF16),
        pltpu.VMEM((3, r, b), BF16),
    ]


def sems(remote, local):
    return [
        pltpu.SemaphoreType.DMA((remote,)),
        pltpu.SemaphoreType.DMA((remote,)),
        pltpu.SemaphoreType.DMA((max(local, 1),)),
    ]


def params(collective_id):
    return pltpu.CompilerParams(
        collective_id=collective_id, has_side_effects=True, vmem_limit_bytes=VM
    )


EPS_NORM = 1e-05
EPS_UNIT = 1e-06
SHAPE = jax.ShapeDtypeStruct


def all_to_team(net, packs, got):
    p = net.place
    me = 2 * p.x + p.c
    net.keep(packs.at[me], got.at[me])
    copies = []
    for d in (2, 1, 3, 0):
        for k in (1, 0):
            if d + k:
                to = 2 * p.chip(d) + lax.rem(p.c + k, 2)
                copies.append(net.send(packs.at[to], got.at[me], p.at_xc(d, k)))
    yield
    for copy in copies:
        copy.wait_recv()


TO_TEAM = 7


def swap_rows(net, pairs):
    p = net.place
    copies = []
    for src, dst in pairs:
        net.keep(src.at[p.zh], dst.at[p.zh])
        copies.append(net.send(src.at[1 - p.zh], dst.at[p.zh], p.at_z(2)))
    yield
    for copy in copies:
        copy.wait_recv()


def thin_rows(rows, padded):
    out = lax.broadcasted_iota(jnp.int32, (8 * rows, 8 * padded), 0)
    at = lax.broadcasted_iota(jnp.int32, (8 * rows, 8 * padded), 1)
    return ((out // rows == at // padded) & (out % rows == at % padded)).astype(BF16)


HEADS_W, SMALL_W = 8 * HD, HD
EXT_W = HEADS_W + SMALL_W
OUT_B, OUT_A = EXT_W, EXT_W + HD
WHOLE_W = EXT_W + 2 * HD
SHARED_W = 3 * HD
FIRST_W = 5 * HD + SHARED_W
PIECE = 32


def shift_pieces(tiles):
    lane = lax.broadcasted_iota(jnp.int32, tiles[0][0].shape, 1) // PIECE
    total = None
    for n, (tile, piece) in enumerate(tiles):
        turn = (PIECE * (n - piece)) % HD
        moved = pltpu.roll(tile, turn, 1) if turn else tile
        total = moved if total is None else jnp.where(lane == n, moved, total)
    return total


def small_columns(gain_a, gain_f, conv, w_beta, rows_buf, beta_buf):
    share = w_beta.shape[0]
    rows_buf[...] = jnp.zeros_like(rows_buf)
    beta_buf[...] = jnp.zeros_like(beta_buf)
    rows_buf[0:1, :share] = gain_a[...].astype(F32)
    rows_buf[1:2, :share] = gain_f[...].astype(F32)
    rows_buf[CONV_AT : CONV_AT + TAPS, :share] = conv[...].astype(F32)
    beta_buf[:share, : w_beta.shape[1]] = w_beta[...].astype(F32)
    columns = rows_buf[...].T[: beta_buf.shape[0], :]
    return (columns + pltpu.roll(beta_buf[...], BETA_AT, 1))[:share].astype(BF16)


def mark_documents(starts, zh, drow, marks):
    row, col = iota2(0), iota2(1)
    upto = (row <= col).astype(BF16)
    starts = jnp.broadcast_to(starts[pl.ds(zh, 1), :].astype(F32), drow.shape)
    before = 0.0
    for k in range(NB):
        cols = slice(k * BLK, (k + 1) * BLK)
        docs = mm(starts[:, cols], upto) + before
        before = docs[:, BLK - 1 :]
        drow[:, cols] = docs
    docs = drow[...]
    lane = lax.broadcasted_iota(jnp.int32, docs.shape, 1)
    kind = lax.broadcasted_iota(jnp.int32, docs.shape, 0) % TAPS
    total = docs
    for m in range(1, TAPS):
        same = ((pltpu.roll(docs, m, 1) == docs) & (lane >= m)).astype(F32)
        total = jnp.where(kind == m, same, total)
    drow[...] = total
    for k in range(NB):
        cols = slice(k * BLK, (k + 1) * BLK)
        tall = jnp.concatenate([total[:, cols]] * (BLK // total.shape[0]), axis=0)
        marks[cols, :] = tall.T[:, : marks.shape[1]]


def pack_weights(kinds, gate_up, small, packs):
    share = small.shape[0]
    packs[...] = jnp.zeros_like(packs)
    for t in range(8):
        own, middle = 3 * (t // 2) + 2 * (t % 2), 3 * (t // 2) + 1
        parts = [w[:, own * HD : (own + 1) * HD] for w in kinds]
        shared = [w[:, middle * HD : (middle + 1) * HD] for w in kinds]
        shared = shared[:3] if t % 2 == 0 else [shared[3], small, shared[4]]
        for n, part in enumerate(parts + shared):
            packs[t, :share, n * HD : (n + 1) * HD] = part
    for n, w in enumerate(gate_up):
        for t in range(8):
            for j in range(4):
                tiles = []
                for e in range(4 * j, 4 * j + 4):
                    at = (2 * e + t // 4) * HD
                    tiles.append((w[:, at : at + HD].astype(F32), t % 4))
                at = FIRST_W + n * 4 * HD + j * HD
                packs[t, :share, at : at + HD] = shift_pieces(tiles).astype(BF16)


def start_kernel(wq, wk, wv, wp, wo, gate, up, gain_a, gain_f, conv, w_beta, starts, tokens, grad_out, x_rows, g_rows, x_all, whole, own_ffn, drow, marks, packs, got, own, rows_buf, beta_buf, *sem):
    net = Net(*sem)
    p = net.place
    share = w_beta.shape[0]
    small = small_columns(gain_a, gain_f, conv, w_beta, rows_buf, beta_buf)
    pack_weights((wq, wk, wv, wp, wo), (gate, up), small, packs)
    first, second = pl.ds(0, FIRST_W), pl.ds(FIRST_W, own.shape[1] - FIRST_W)
    meet(team_all(p) + group_peers(p))
    trades = [all_to_team(net, packs.at[:, :, part], got.at[:, :, part]) for part in (first, second)]
    swaps = [swap_rows(net, (pair,)) for pair in ((tokens, x_rows), (grad_out, g_rows))]
    for n in range(2):
        next(trades[n])
        next(swaps[n])
    pick = thin_rows(share, packs.shape[1])

    def thin(part):
        wide = got[:, :, part].reshape(pick.shape[1], part.size)
        own[:, part] = mm(pick, wide).astype(BF16)

    interleave(trades[0])
    net.settle()
    thin(first)
    shared = pl.ds(pl.multiple_of(4 * HD + p.c * SHARED_W, HD), SHARED_W)
    heads = gather_groups(
        net,
        own,
        whole,
        [(pl.ds(0, 4 * HD), pl.ds(0, 4 * HD))],
        [(pl.ds(4 * HD, HD), pl.ds(OUT_A, HD)), (pl.ds(5 * HD, SHARED_W), shared)],
        True,
    )
    next(heads)
    mark_documents(starts, p.zh, drow, marks)
    interleave(swaps[0])
    x_team = gather_team(net, x_rows, x_all)
    next(x_team)
    for _ in range(3):
        next(heads)
    next(x_team)
    interleave(trades[1])
    thin(second)
    net.keep(own.at[:, second], own_ffn)
    interleave(x_team, heads, swaps[1])
    net.finish()


def start(kinds, gate, up, gain_a, gain_f, conv, w_beta, starts, tokens, grad_out):
    share, width = kinds[0].shape
    two, n, _ = tokens.shape
    rows = SHAPE(tokens.shape, BF16)
    cols = FIRST_W + gate.shape[1] // 4
    return pl.pallas_call(
        start_kernel,
        out_shape=[
            rows,
            rows,
            SHAPE((two, 8, n, width), BF16),
            SHAPE((width, WHOLE_W), BF16),
            SHAPE((8 * share, cols - FIRST_W), BF16),
            SHAPE((8, SEQ), F32),
            SHAPE((SEQ, 8), F32),
        ],
        in_specs=[VMEM] * 12 + [ANY] * 2,
        out_specs=[ANY] * 5 + [VMEM] * 2,
        scratch_shapes=[
            pltpu.VMEM((8, 16, cols), BF16),
            pltpu.VMEM((8, 16, cols), BF16),
            pltpu.VMEM((8 * share, cols), BF16),
            pltpu.VMEM((HD, HD), F32),
            pltpu.VMEM((16, HD), F32),
        ]
        + sems(2 * TO_TEAM + 2 + GATHER_TEAM + 3 * GATHER_GROUPS // 2 + 16, 9),
        compiler_params=params(1),
        name="start",
    )(*kinds, gate, up, gain_a, gain_f, conv, w_beta, starts, tokens, grad_out)


def lanes(at):
    return pl.ds(pl.multiple_of(at * HD, HD), HD)


def trade_out(net, whole, w_out):
    p = net.place
    copies, own = [], []
    for d in (2, 1, 3, 0):
        for k in (1, 0):
            xd, cd = p.chip(d), lax.rem(p.c + k, 2)
            row_a, row_b = lanes(3 * xd + 2 * cd), lanes(3 * xd + 1)
            row_c = lanes(3 * xd + jnp.where(p.c == 0, 2 * cd, 1))
            col_a, col_b = lanes(3 * p.x + 2 * p.c), lanes(3 * p.x + 1)
            moves = (
                (whole.at[row_a, pl.ds(OUT_A, HD)], w_out.at[pl.ds(0, HD), col_a]),
                (whole.at[row_b, pl.ds(OUT_A, HD)], w_out.at[pl.ds(HD, HD), col_a]),
                (whole.at[row_c, pl.ds(OUT_B, HD)], w_out.at[lanes(p.c), col_b]),
            )
            for src, dst in moves:
                if d + k:
                    copies.append(net.send(src, dst, p.at_xc(d, k)))
                else:
                    own.append(net.load(src, dst))
    yield
    for copy in own:
        copy.wait()
    for copy in copies:
        copy.wait_recv()


def attn_fwd_kernel(x_all, whole, marks, drow, own_ffn, g_rows, *rest):
    kept, (w_ffn, g_all, w_out, part), rest = rest[:13], rest[13:17], rest[17:]
    bufs, (x_buf, w_buf, wo_buf, part_buf), rest = rest[:14], rest[14:18], rest[18:]
    normed, qkvp, raw, vec, mixed, gains, *saved, o = bufs
    net = Net(*rest[-3:])
    p = net.place
    loads = [net.load(whole.at[:, pl.ds(0, 9 * HD)], w_buf), net.load(x_all, x_buf)]
    meet(team_all(p) + group_peers(p))
    jobs = Jobs(
        gather_groups(net, own_ffn, w_ffn, *halves(own_ffn.shape[1])),
        trade_out(net, whole, wo_buf),
        gather_team(net, g_rows, g_all),
    )
    jobs.step(0, 1, 2)
    for copy in loads:
        copy.wait()
    project(x_buf, w_buf, gains, normed, qkvp, raw)
    for n in (0, 1, 2, 5):
        net.keep(bufs[n], kept[n])
    steps = [(0, 0, 0), (), (), (), (2,), ()]
    poke = lambda: jobs.step(*steps.pop(0)) if steps else None
    for s, head in enumerate(heads_here()):
        cols = pl.ds(s * HD, HD)
        poke()
        fwd_slot(poke, s, head, w_buf.at[:, pl.ds(8 * HD, HD)], marks, drow, qkvp, raw, vec, o, *saved, *rest[:-3])
        net.keep(vec.at[:, cols], kept[3].at[:, cols])
        for src, dst in zip(saved, kept[6:]):
            net.keep(src.at[s], dst.at[s])
    mixed[:, :HD] = o[:, :HD].astype(BF16)
    mixed[:, HD:] = jnp.where(p.c == 0, o[:, HD:], 0.0).astype(BF16)
    net.keep(mixed, kept[4])
    jobs.step(1, 1)
    net.keep(wo_buf, w_out)
    two, _, n, width = part.shape
    for h in range(two):
        for t in range(0, 8, 4):
            at = (h * 8 + t) * n
            y = mm(mixed[at : at + 4 * n, :], wo_buf[...]).astype(BF16)
            part_buf[h, t : t + 4] = y.reshape(4, n, width)
    net.keep(part_buf, part)
    jobs.drain()
    net.finish()


def attn_fwd(x_all, whole, marks, drow, own_ffn, g_rows):
    rows, cols = own_ffn.shape
    two, n, width = g_rows.shape
    kept = fwd_shapes(width)
    part = (two, 8, n, width)
    return pl.pallas_call(
        attn_fwd_kernel,
        out_shape=[SHAPE(*a) for a in kept]
        + [SHAPE((16 * rows, cols), BF16), SHAPE(part, BF16), SHAPE((2 * HD, width), BF16), SHAPE(part, BF16)],
        in_specs=[ANY, ANY, VMEM, VMEM, ANY, ANY],
        out_specs=[ANY] * (len(kept) + 4),
        scratch_shapes=[pltpu.VMEM(*a) for a in kept]
        + [
            pltpu.VMEM((SEQ, 2 * HD), F32),
            pltpu.VMEM((SEQ, width), BF16),
            pltpu.VMEM((width, 9 * HD), BF16),
            pltpu.VMEM((2 * HD, width), BF16),
            pltpu.VMEM(part, BF16),
        ]
        + fwd_scratch()
        + sems(GATHER_TEAM + GATHER_GROUPS + 21, 2 + 6 + 4 + 18 + 3),
        compiler_params=params(7),
        name="attn_fwd",
    )(x_all, whole, marks, drow, own_ffn, g_rows)


def norm_back(v, gain, d_normed):
    scale = lax.rsqrt(jnp.mean(v * v, axis=-1, keepdims=True) + EPS_NORM)
    unit = v * scale
    d_unit = d_normed * gain
    d_v = scale * (d_unit - unit * jnp.mean(d_unit * unit, axis=-1, keepdims=True))
    return d_v, d_normed * unit


def by_group(a):
    return a.reshape(2, 4, 2, a.shape[0] // 16, a.shape[1])


class TeamBlocks:
    def __init__(self, net, own, out):
        self.net, self.own, self.out = net, own, out

    def start(self):
        net, p, out = self.net, self.net.place, self.out
        place = out.at[:, 2 * p.x + p.c]
        self.to_r = net.send(self.own, place, p.at_x(1))
        self.to_l = net.send(self.own, place, p.at_x(3))
        self.shared = net.send(self.own, place, p.sibling())
        self.kept = net.load(self.own, place)

    def mine(self):
        self.kept.wait()
        self.shared.wait_recv()

    def hand_on(self):
        net, p, out = self.net, self.net.place, self.out
        left, right = 2 * p.chip(3) + p.c, 2 * p.chip(1) + p.c
        self.to_r.wait_recv()
        self.on_r = net.send(out.at[0, left], out.at[0, left], p.at_x(1))
        self.from_l = net.send(out.at[:, left], out.at[:, left], p.sibling())
        self.to_l.wait_recv()
        self.on_l = net.send(out.at[1, right], out.at[1, right], p.at_x(3))
        self.from_r = net.send(out.at[:, right], out.at[:, right], p.sibling())

    def opposite(self):
        net, p, out = self.net, self.net.place, self.out
        far = 2 * p.chip(2) + p.c
        self.far = []
        for n, copy in enumerate((self.on_r, self.on_l)):
            copy.wait_recv()
            self.far.append(net.send(out.at[n, far], out.at[n, far], p.sibling()))


class TeamSum:
    def __init__(self, net, part, got, total, from_l, from_r, all_l, all_r):
        self.net, self.part, self.got, self.total = net, part, got, total
        self.from_l, self.from_r, self.all_l, self.all_r = from_l, from_r, all_l, all_r
        self.swaps, self.last = {}, []

    def ready(self, d):
        p = self.net.place
        at = p.chip(d)
        self.swaps[d] = self.net.send(
            self.part.at[:, 2 * at + 1 - p.c], self.got.at[:, at], p.sibling()
        )

    def pair(self, d):
        p = self.net.place
        at = p.chip(d)
        self.swaps[d].wait_recv()
        self.total[:, at] = add(self.part[:, 2 * at + p.c], self.got[:, at])
        return at

    def near(self):
        net, p = self.net, self.net.place
        self.x_r = self.pair(1)
        self.last.append(net.send(self.total.at[1, self.x_r], self.all_l.at[1], p.at_x(1)))
        self.x_l = self.pair(3)
        self.last.append(net.send(self.total.at[0, self.x_l], self.all_r.at[0], p.at_x(3)))

    def far(self):
        net, p = self.net, self.net.place
        x_2 = self.pair(2)
        self.half_r = net.send(self.total.at[0, x_2], self.from_l, p.at_x(1))
        self.half_l = net.send(self.total.at[1, x_2], self.from_r, p.at_x(3))

    def on(self):
        net, p = self.net, self.net.place
        self.half_r.wait_recv()
        self.total[0, self.x_r] = add(self.total[0, self.x_r], self.from_l[...])
        self.last.append(net.send(self.total.at[0, self.x_r], self.all_l.at[0], p.at_x(1)))
        self.half_l.wait_recv()
        self.total[1, self.x_l] = add(self.total[1, self.x_l], self.from_r[...])
        self.last.append(net.send(self.total.at[1, self.x_l], self.all_r.at[1], p.at_x(3)))

    def result(self):
        for copy in self.last:
            copy.wait_recv()
        mine = self.total[:, self.net.place.x].astype(F32)
        return mine + self.all_l[...].astype(F32) + self.all_r[...].astype(F32)


def ffn_kernel(cuts, *refs):
    (part, x_rows, g_rows, gain, own_down, w_ffn, g_all), refs = refs[:7], refs[7:]
    (hidden, d_hidden, d_gain, branch_all, out_part, ffn_sum, down_out), refs = refs[:7], refs[7:]
    (w_in, w_down, g_buf, nf_all, normed, act, d_in, back, branch, d_ffn, d_down, out_buf), refs = refs[:12], refs[12:]
    scratch = [refs[6 * n : 6 * n + 6] for n in range(5)]
    net = Net(*refs[-3:])
    p = net.place
    loads = [net.load(w_ffn, w_in), net.load(g_all, g_buf)]
    meet(team_peers(p) + group_peers(p))
    two, _, n, width = part.shape
    half = w_down.shape[0]
    pieces = [pl.ds(m * n // 2, n // 2) for m in range(2)]

    def finish_rows(piece):
        def finish(sums):
            h = x_rows[:, piece].astype(F32) + sums
            hidden[:, piece] = h
            scale = lax.rsqrt(jnp.mean(h * h, axis=-1, keepdims=True) + EPS_NORM)
            normed[:, piece] = (h * scale * gain[1:2, :][None]).astype(BF16)

        return finish

    jobs = Jobs(
        *[
            scatter_team(net, part.at[:, :, piece], *scratch[m], finish_rows(piece))
            for m, piece in enumerate(pieces)
        ],
        gather_groups(net, own_down, w_down, *halves(width)),
    )
    blocks = [TeamBlocks(net, normed.at[:, piece], nf_all.at[:, :, piece]) for piece in pieces]
    jobs.step(0, 1, 2, 0, 1, 2, 2, 2, 0, 1)
    for m in range(2):
        jobs.step(m)
        blocks[m].start()
    jobs.drain()
    for copy in loads:
        copy.wait()
    net.settle()
    sums = [
        TeamSum(net, back.at[:, :, piece], *scratch[2 + m]) for m, piece in enumerate(pieces)
    ]

    def flat(ref, at):
        return ref[:, pl.ds(2 * at, 2)].reshape(4 * n, ref.shape[3])

    def work(d):
        at = p.chip(d)
        pre = mm(flat(nf_all, at), w_in[...])
        gate, up = pre[:, :half], pre[:, half:]
        sig = jax.nn.sigmoid(gate)
        silu = gate * sig
        act[:, pl.ds(2 * at, 2)] = (silu * up).astype(BF16).reshape(two, 2, n, half)
        d_act = mm_nt(flat(g_buf, at), w_down[...])
        d_gate = (d_act * up * (sig + silu * (1.0 - sig))).astype(BF16)
        d_up = (d_act * silu).astype(BF16)
        d_pre = jnp.concatenate([d_gate, d_up], axis=1)
        d_in[:, pl.ds(2 * at, 2)] = d_pre.reshape(two, 2, n, 2 * half)
        back[:, pl.ds(2 * at, 2)] = mm_nt(d_pre, w_in[...]).astype(BF16).reshape(two, 2, n, width)
        for s in sums:
            s.ready(d)

    for b in blocks:
        b.mine()
    work(0)
    for b in blocks:
        b.hand_on()
    for b in blocks:
        b.from_l.wait_recv()
    work(3)
    for b in blocks:
        b.opposite()
    for b in blocks:
        b.from_r.wait_recv()
    work(1)
    for s in sums:
        s.near()
    for b in blocks:
        for copy in b.far:
            copy.wait_recv()
    work(2)
    for s in sums:
        s.far()
    for s in sums:
        s.pair(0)
    rows = two * 8 * n
    step = width // 4
    for k in range(4):
        cols = slice(k * step, (k + 1) * step)
        left = nf_all[:, :, :, cols].reshape(rows, step)
        d_ffn[cols, :] = mm_tn(left, d_in[...].reshape(rows, 2 * half)).astype(BF16)
        if k in (1, 2):
            sums[k - 1].on()
    group = scatter_groups(net, d_ffn, ffn_sum, cuts, *scratch[4])
    next(group)
    d_gain[...] = jnp.zeros_like(d_gain)
    teams = []
    for s, piece in zip(sums, pieces):
        d_h, d_g = norm_back(hidden[:, piece], gain[1:2, :][None], s.result())
        d_h = d_h + g_rows[:, piece].astype(F32)
        d_hidden[:, piece] = d_h
        branch[:, piece] = d_h.astype(BF16)
        d_gain[...] += jnp.sum(jnp.sum(d_g, axis=0), axis=0, keepdims=True)
        teams.append(gather_team(net, branch.at[:, piece], branch_all.at[:, :, piece]))
        next(teams[-1])
    step = half // 2
    for k in range(2):
        cols = slice(k * step, (k + 1) * step)
        left = act[:, :, :, cols].reshape(rows, step)
        d_down[cols, :] = mm_tn(left, g_buf[...].reshape(rows, width)).astype(BF16)
    net.keep(d_down, down_out)
    for h in range(two):
        for t in range(0, 8, 4):
            left = act[h, t : t + 4].reshape(4 * n, half)
            out_buf[h, t : t + 4] = mm(left, w_down[...]).astype(BF16).reshape(4, n, width)
    net.keep(out_buf, out_part)
    for team in teams:
        next(team)
    next(group)
    next(group)
    jobs = Jobs(*teams, group)
    jobs.drain()
    net.finish()


def ffn(part, x_rows, g_rows, gain, own_down, w_ffn, g_all):
    two, n, width = x_rows.shape
    cols = w_ffn.shape[1]
    half, rows = cols // 2, own_down.shape[0]
    every = (two, 8, n, width)
    share = width // 16
    cuts = (0, half, cols)
    return pl.pallas_call(
        functools.partial(ffn_kernel, cuts),
        out_shape=[
            SHAPE((two, n, width), F32),
            SHAPE((two, n, width), F32),
            SHAPE((1, width), F32),
            SHAPE(every, BF16),
            SHAPE(every, BF16),
            SHAPE((share, cols), BF16),
            SHAPE((16 * rows, width), BF16),
        ],
        in_specs=[ANY, VMEM, VMEM, VMEM, ANY, ANY, ANY],
        out_specs=[VMEM, VMEM, VMEM, ANY, ANY, VMEM, ANY],
        scratch_shapes=[
            pltpu.VMEM((width, cols), BF16),
            pltpu.VMEM((half, width), BF16),
            pltpu.VMEM(every, BF16),
            pltpu.VMEM(every, BF16),
            pltpu.VMEM((two, n, width), BF16),
            pltpu.VMEM((two, 8, n, half), BF16),
            pltpu.VMEM((two, 8, n, cols), BF16),
            pltpu.VMEM(every, BF16),
            pltpu.VMEM((two, n, width), BF16),
            pltpu.VMEM((width, cols), BF16),
            pltpu.VMEM((half, width), BF16),
            pltpu.VMEM(every, BF16),
        ]
        + scatter_team_scratch(n // 2, width) * 4
        + scatter_groups_scratch(share, cuts)
        + sems(
            4 * SCATTER_TEAM + 4 * GATHER_TEAM + GATHER_GROUPS + SCATTER_GROUPS_FLAT,
            2 + 2 * SCATTER_TEAM_LOADS + 2 + 2 + 2 + 2 + SCATTER_GROUPS_FLAT_LOADS,
        ),
        compiler_params=params(3),
        name="ffn",
    )(part, x_rows, g_rows, gain, own_down, w_ffn, g_all)


def trade_out_back(net, d_out, whole):
    p = net.place
    rows, middle, own = [], [], []
    cases = [(d, k) for d in (2, 1, 3, 0) for k in (1, 0)]
    for d, k in cases:
        xd, cd = p.chip(d), lax.rem(p.c + k, 2)
        for side, col in enumerate((lanes(3 * xd + 2 * cd), lanes(3 * xd + 1))):
            src = d_out.at[pl.ds(0, HD), col]
            dst = whole.at[lanes(3 * p.x + 2 * p.c), pl.ds(side * HD, HD)]
            if d + k:
                rows.append(net.send(src, dst, p.at_xc(d, k)))
            else:
                own.append(net.local(src, dst))
                own[-1].start()
    for d, k in cases:
        xd, cd = p.chip(d), lax.rem(p.c + k, 2)
        for side, col in enumerate((lanes(3 * xd + 2 * cd), lanes(3 * xd + 1))):
            src = d_out.at[pl.ds(HD, HD), col]
            dst = whole.at[lanes(3 * p.x + 1), pl.ds(side * HD, HD)]
            if d + k:
                middle.append((k, net.prepare(src, dst, p.at_xc(d, k))))
            else:
                middle.append((-1, net.local(src, dst)))

    @pl.when(p.c == 0)
    def _():
        for _, copy in middle:
            copy.start()

    yield
    for copy in rows:
        copy.wait_recv()
    for copy in own:
        copy.wait()
    for core in range(2):

        @pl.when(p.c == core)
        def _(core=core):
            for k, copy in middle:
                if k == core:
                    copy.wait_recv()

    @pl.when(p.c == 0)
    def _():
        for k, copy in middle:
            if k < 0:
                copy.wait()
            else:
                copy.wait_send()

    yield


TRADE_BACK = 28


def back_kernel(cuts, *refs):
    (marks, gains, d_gain_f, x_rows, hidden, d_hidden, ffn_sum), refs = refs[:7], refs[7:]
    (whole, w_out, mixed, normed, branch, part_o, d_down), refs = refs[:7], refs[7:]
    given, refs = refs[:10], refs[10:]
    (output, d_tokens, got_heads, got_rest, got_ffn, down_sum), refs = refs[:6], refs[6:]
    bufs, refs = refs[:10], refs[10:]
    (w_buf, wo_buf, mixed_buf, normed_buf, rows_buf, do, d_out, d_ext, d_conv), refs = refs[:9], refs[9:]
    (d_head_a, d_head_b, d_small, turned, trade, out_rows, d_rows), refs = refs[:7], refs[7:]
    (sum_a, sum_b, sum_s, sum_o, packs_heads, packs_rest, packs_ffn), refs = refs[:7], refs[7:]
    own, refs = refs[:7], refs[7:]
    scratch = [refs[6 * n : 6 * n + 6] for n in range(8)]
    net = Net(*refs[-3:])
    p = net.place
    qkvp, raw, vec, *saved = bufs
    two, _, n, width = rows_buf.shape
    rows = two * 8 * n
    first = [net.load(w_out, wo_buf), net.load(branch, rows_buf), net.load(mixed, mixed_buf)]
    second = [net.load(given[m], bufs[m]) for m in (0,)]
    second.append(net.load(given[3].at[0], bufs[3].at[0]))
    meet(team_all(p) + group_peers(p))

    def finish(sums):
        out_rows[...] = (hidden[...] + sums).astype(BF16)

    def out_grad():
        yield from trade_out_back(net, d_out, trade)
        yield from scatter_groups(net, trade, sum_o, cuts[1], *scratch[0])

    def output_rows():
        yield from scatter_team(net, part_o, *scratch[1], finish)
        yield from swap_rows(net, ((out_rows, output),))

    jobs = Jobs(
        output_rows(), out_grad(), scatter_groups(net, d_down, down_sum, cuts[0], *scratch[2])
    )
    eight, padded, _ = packs_heads.shape
    spread = thin_rows(ffn_sum.shape[0] // eight, padded).T

    def pack(part, packs, at):
        wide = mm(spread, part[...]).astype(BF16)
        packs[:, :, at : at + part.shape[1]] = wide.reshape(eight, padded, part.shape[1])

    jobs.step(0)
    pack(ffn_sum, packs_ffn, 0)
    early = all_to_team(net, packs_ffn, got_ffn)
    next(early)
    for copy in first:
        copy.wait()
    third = [net.load(given[m].at[0], bufs[m].at[0]) for m in range(4, 10)]
    third += [net.load(given[m], bufs[m]) for m in (1, 2)]
    third.append(net.load(whole.at[:, pl.ds(0, EXT_W)], w_buf))
    branch_rows = rows_buf[...].reshape(rows, width)
    d_mixed = mm_nt(branch_rows, wo_buf[...])
    do[:, :HD] = d_mixed[:, :HD]
    do[:, HD:] = jnp.where(p.c == 0, d_mixed[:, HD:], 0.0)
    d_out[...] = mm_tn(mixed_buf[...], branch_rows).astype(BF16)
    jobs.step(1, 2)
    fourth = [net.load(normed, normed_buf)]
    later = []
    for copy in second:
        copy.wait()
    waits = [third, None, None, None, later, None, None, None]
    steps = [(0,), (), (), (0,), (2, 2), (), (0, 1), (1,)]

    def poke():
        jobs.step(*steps.pop(0))
        for copy in waits.pop(0) or ():
            copy.wait()
        if len(steps) == 7:
            fourth.append(net.load(given[3].at[1], bufs[3].at[0]))

    side = 4 * HD
    d_raw = 0.0
    sums_a = scatter_groups(net, d_head_a, sum_a, cuts[2], *scratch[3])
    sums_b = scatter_groups(net, d_head_b, sum_b, cuts[2], *scratch[4])
    for s, (head, grads, job) in enumerate(zip(heads_here(), (d_head_a, d_head_b), (sums_a, sums_b))):
        d_raw = d_raw + bwd_slot(
            poke, s, head, qkvp, raw, w_buf.at[:, pl.ds(HEADS_W, HD)], marks, vec, mixed_buf, do, *saved, d_ext, d_conv, *own
        )
        if s == 0:
            later += [net.load(given[m].at[1], bufs[m].at[0]) for m in range(4, 10)]
            for copy in fourth:
                copy.wait()
        for k in range(4):
            part = slice(k * width // 4, (k + 1) * width // 4)
            grads[part, :] = mm_tn(normed_buf[:, part], d_ext[:, s * side : (s + 1) * side]).astype(BF16)
        next(job)
        poke()
    d_ext[:, HEADS_W:] = d_raw.astype(d_ext.dtype)
    next(sums_a)
    next(sums_a)

    pieces = [pl.ds(m * n // 2, n // 2) for m in range(2)]
    sums = [
        TeamSum(net, rows_buf.at[:, :, piece], *scratch[5 + m]) for m, piece in enumerate(pieces)
    ]
    turned[...] = jnp.zeros_like(turned)

    def work(d):
        at = p.chip(d)
        parts = [
            d_ext[pl.ds(pl.multiple_of((h * 8 + 2 * at) * n, 2 * n), 2 * n), :] for h in range(two)
        ]
        y = mm_nt(jnp.concatenate(parts, axis=0), w_buf[...]).astype(BF16)
        rows_buf[:, pl.ds(2 * at, 2)] = y.reshape(two, 2, n, width)
        for s in sums:
            s.ready(d)

    work(2)
    work(1)
    for s in sums:
        s.far()
    work(3)
    for s in sums:
        s.near()
    work(0)
    for s in sums:
        s.pair(0)
    total = 0.0
    for h in range(two):
        for t in range(0, 8, 2):
            here = slice((h * 8 + t) * n, (h * 8 + t + 2) * n)
            y = rows_buf[h, t : t + 2].reshape(2 * n, width).astype(F32)
            total = total + jnp.sum(y * normed_buf[here, :].astype(F32), axis=0, keepdims=True)
    turned[0:1, :] = total
    head_a, head_b = heads_here()
    turned[0:1, :] = turned[0:1, :] / gains[0:1, :]
    turned[1:2, :] = d_gain_f[...]
    turned[CONV_AT : CONV_AT + TAPS, lanes(head_a)] = d_conv[0, :TAPS, :]
    turned[CONV_AT : CONV_AT + TAPS, lanes(head_b)] = d_conv[1, :TAPS, :]
    for k in range(width // HD):
        part = slice(k * HD, (k + 1) * HD)
        t = mm_tn(normed_buf[:, part], d_ext[:, HEADS_W:]) + turned[:, part].T
        d_small[part, :] = t.astype(BF16)
    sums_s = scatter_groups(net, d_small, sum_s, cuts[3], *scratch[7])
    next(sums_s)
    for s in sums:
        s.on()
    next(sums_b)
    next(sums_b)
    swaps = []
    for s, piece in zip(sums, pieces):
        d_x, _ = norm_back(x_rows[:, piece].astype(F32), gains[0:1, :][None], s.result())
        d_rows[:, piece] = (d_x + d_hidden[:, piece]).astype(BF16)
        swaps.append(swap_rows(net, ((d_rows.at[:, piece], d_tokens.at[:, piece]),)))
        next(swaps[-1])
    next(sums_s)
    jobs.step(1, 1)
    Jobs(sums_a).drain()
    jobs.drain()
    pack(sum_a, packs_rest, 0)
    pack(sum_o, packs_rest, side)
    rest = all_to_team(net, packs_rest, got_rest)
    next(rest)
    Jobs(sums_b, sums_s).drain()
    pack(sum_b, packs_heads, 0)
    pack(sum_s, packs_heads, side)
    interleave(all_to_team(net, packs_heads, got_heads), *swaps, rest, early)
    net.finish()


def back(values, arrays, given):
    marks, gains, d_gain_f, x_rows, hidden, d_hidden, ffn_sum = values
    whole, w_out, mixed, normed, branch, part_o, d_down = arrays
    two, n, width = hidden.shape
    r = width // 16
    down = d_down.shape[0] // 16
    side = 4 * HD
    ffn_w = ffn_sum.shape[1]
    cuts = [(0, width // 2, width), (0, HD, 2 * HD), (0, side // 2, side), (0, HD, HD)]
    rows = SHAPE((two, n, width), BF16)
    packs = [(8, 16, side + HD), (8, 16, side + 2 * HD), (8, 16, ffn_w)]
    vmem = pltpu.VMEM
    return pl.pallas_call(
        functools.partial(back_kernel, cuts),
        out_shape=[rows, rows] + [SHAPE(a, BF16) for a in packs] + [SHAPE((down, width), F32)],
        in_specs=[VMEM] * 7 + [ANY] * (7 + len(given)),
        out_specs=[ANY] * 5 + [VMEM],
        scratch_shapes=[vmem((1,) + a.shape[1:] if m > 2 else a.shape, a.dtype) for m, a in enumerate(given)]
        + [
            vmem((width, EXT_W), BF16),
            vmem(w_out.shape, BF16),
            vmem(mixed.shape, BF16),
            vmem(normed.shape, BF16),
            vmem(branch.shape, BF16),
            vmem((SEQ, 2 * HD), F32),
            vmem((2 * HD, width), BF16),
            vmem((SEQ, EXT_W), BF16),
            vmem((2, 8, HD), F32),
            vmem((width, side), BF16),
            vmem((width, side), BF16),
            vmem((width, HD), BF16),
            vmem((HD, width), F32),
            vmem((width, 2 * HD), BF16),
            vmem((two, n, width), BF16),
            vmem((two, n, width), BF16),
            vmem((r, side), BF16),
            vmem((r, side), BF16),
            vmem((r, HD), BF16),
            vmem((r, 2 * HD), BF16),
        ]
        + [vmem(a, BF16) for a in packs]
        + bwd_scratch()
        + scatter_groups_scratch(r, cuts[1])
        + scatter_team_scratch(n, width)
        + scatter_groups_scratch(down, cuts[0])
        + scatter_groups_scratch(r, cuts[2])
        + scatter_groups_scratch(r, cuts[2])
        + scatter_team_scratch(n // 2, width) * 2
        + scatter_groups_scratch(r, cuts[3])
        + sems(
            TRADE_BACK + 3 * SCATTER_TEAM + 6 * SCATTER_GROUPS_FLAT + 3 + 3 * TO_TEAM,
            3 + 3 + 9 + 8 + 4 + SCATTER_TEAM_LOADS + 6 * SCATTER_GROUPS_FLAT_LOADS + 3 + 3,
        ),
        compiler_params=params(5),
        name="back",
    )(*values, *arrays, *given)


def unpack_kernel(heads, rest, ffn_in, rows_in, tokens_in, down_in, *outs):
    kinds, (gate, up, gain_a, gain_f, conv, beta, rows, tokens, down) = outs[:5], outs[5:]
    share = beta.shape[0]
    side = 4 * HD
    for n, out in enumerate(kinds):
        for x in range(4):
            for j in range(3):
                t = 2 * x + j // 2
                if n < 4:
                    src, col = (heads, n * HD) if j == 1 else (rest, n * HD)
                else:
                    src, col = rest, side + (j % 2) * HD
                head = 3 * x + j
                out[:, head * HD : (head + 1) * HD] = src[t, :share, col : col + HD].astype(F32)
    total = heads[0, :, side : side + SMALL_W].astype(F32)
    for t in range(1, 8):
        total = total + heads[t, :, side : side + SMALL_W].astype(F32)
    turned = jnp.concatenate([total] * (HD // total.shape[0]), axis=0).T
    gain_a[...] = turned[0:1, :share]
    gain_f[...] = turned[1:2, :share]
    conv[...] = turned[CONV_AT : CONV_AT + TAPS, :share]
    beta[...] = pltpu.roll(total, HD - BETA_AT, 1)[:share, : beta.shape[1]]
    for n, out in enumerate((gate, up)):
        for tile in range(32):
            e = tile // 2
            col = n * 4 * HD + (e // 4) * HD
            parts = [
                (ffn_in[t, :, col : col + HD].astype(F32), e % 4)
                for t in range(4 * (tile % 2), 4 * (tile % 2) + 4)
            ]
            out[:, tile * HD : (tile + 1) * HD] = shift_pieces(parts)[:share]
    rows[...] = rows_in[...]
    tokens[...] = tokens_in[...]
    down[...] = down_in[...]


def unpack(heads, rest, ffn_sum, rows, tokens, down, share, ff):
    two, n, width = rows.shape
    return pl.pallas_call(
        unpack_kernel,
        out_shape=[SHAPE((share, width), F32)] * 5
        + [SHAPE((share, ff), F32)] * 2
        + [SHAPE((1, share), F32)] * 2
        + [SHAPE((TAPS, share), F32), SHAPE((share, 12), F32)]
        + [SHAPE(rows.shape, BF16)] * 2
        + [SHAPE(down.shape, F32)],
        in_specs=[VMEM] * 6,
        out_specs=[VMEM] * 14,
        compiler_params=pltpu.CompilerParams(vmem_limit_bytes=VM),
        name="unpack",
    )(heads, rest, ffn_sum, rows, tokens, down)


def per_device(
    tokens,
    doc_start,
    gain_attn,
    w_query,
    w_key,
    w_value,
    w_path,
    conv_path,
    w_beta,
    w_out,
    gain_ffn,
    w_gate,
    w_up,
    w_down,
    grad_out,
):
    width = tokens.shape[2]
    share = w_query.shape[0]
    x_rows, g_rows, x_all, whole, own_ffn, drow, marks = start(
        (w_query, w_key, w_value, w_path, w_out),
        w_gate,
        w_up,
        gain_attn[None],
        gain_ffn[None],
        conv_path,
        w_beta,
        doc_start,
        tokens,
        grad_out,
    )
    normed, qkvp, raw, vec, mixed, gains, *saved, w_ffn, g_all, w_out_t, part = attn_fwd(
        x_all.reshape(SEQ, width), whole, marks, drow, own_ffn, g_rows
    )
    hidden, d_hidden, d_gain_f, branch_all, out_part, ffn_sum, d_down = ffn(
        part, x_rows, g_rows, gains, w_down, w_ffn, g_all
    )
    output, d_tokens, heads_back, rest_back, ffn_back, d_down = back(
        (marks, gains, d_gain_f, x_rows, hidden, d_hidden, ffn_sum),
        (whole, w_out_t, mixed, normed, branch_all, out_part, d_down),
        (qkvp, raw, vec, *saved),
    )
    *kinds, d_gate_w, d_up_w, d_gain_a, d_gain_f, d_conv, d_beta_w, output, d_tokens, d_down = unpack(
        heads_back, rest_back, ffn_back, output, d_tokens, d_down, share, w_gate.shape[1]
    )
    return (
        output,
        d_tokens,
        d_gain_a[0],
        *kinds[:4],
        d_conv,
        d_beta_w,
        kinds[4],
        d_gain_f[0],
        d_gate_w,
        d_up_w,
        d_down,
    )


def solution(mesh):
    names = ("zl", "y", "zh", "x", "c")
    fine = Mesh(mesh.devices.reshape(2, 4, 2, 4, 2), names)
    dp, ctx = names[:2], names[2:]
    rows, flat, mat, taps = P(dp, ctx, None), P(names), P(names, None), P(None, names)
    return jax.shard_map(
        per_device,
        mesh=fine,
        in_specs=(
            rows, P(dp, None), flat, mat, mat, mat, mat, taps, mat, mat, flat, mat, mat, mat, rows,
        ),
        out_specs=(
            rows, rows, flat, mat, mat, mat, mat, taps, mat, mat, flat, mat, mat, mat,
        ),
        check_vma=False,
    )
```

```python
import functools

import jax
import jax.numpy as jnp
from jax import lax
from jax.experimental import pallas as pl
from jax.experimental.pallas import tpu as pltpu
from jax.sharding import Mesh, PartitionSpec as P

F32, BF16 = jnp.float32, jnp.bfloat16
VM = 61 * 1024 * 1024

SEQ, HD, BLK = 1024, 128, 128
NB = SEQ // BLK
NQC = (NB * (NB - 1) // 2) * BLK
SCALE = HD ** (-0.5)
GROUP, GROUP_BACK = 8, 4


def mm(a, b, dims=((1,), (0,))):
    return lax.dot_general(
        a.astype(BF16), b.astype(BF16), (dims, ((), ())), preferred_element_type=F32
    )


def mm_nt(a, b):
    return mm(a, b, ((1,), (1,)))


def mm_tn(a, b):
    return mm(a, b, ((0,), (0,)))


def split(a):
    high = a.astype(BF16)
    return high, (a - high.astype(F32)).astype(BF16)


def mm3(a, b):
    ah, al = split(a)
    bh, bl = split(b)
    return mm(ah, bh) + (mm(ah, bl) + mm(al, bh))


def iota2(axis):
    return lax.broadcasted_iota(jnp.int32, (BLK, BLK), axis)


BASE = 16


def unit_inverses(lowers):
    row, col = iota2(0), iota2(1)
    eye = (row == col).astype(F32)
    in_base = (row // BASE) == (col // BASE)
    narrow = [jnp.where(in_base, low, 0.0) for low in lowers]
    inv = [eye for _ in lowers]
    for u in range(BASE - 1):
        pick = (col % BASE) == u
        coef = [jnp.sum(jnp.where(pick, low, 0.0), axis=1, keepdims=True) for low in narrow]
        for n, (t, c) in enumerate(zip(inv, coef)):
            t3 = t.reshape(BLK // BASE, BASE, BLK)
            lead = jnp.broadcast_to(t3[:, u : u + 1, :], t3.shape).reshape(BLK, BLK)
            inv[n] = t - c * lead
    size = BASE
    while size < BLK:
        off = ((row // (2 * size)) == (col // (2 * size))) & ((row // size) != (col // size))
        mid = [mm3(t, jnp.where(off, low, 0.0)) for t, low in zip(inv, lowers)]
        inv = [t - mm3(m, t) for t, m in zip(inv, mid)]
        size *= 2
    return inv


def betas_of(raw, head):
    lane = lax.broadcasted_iota(jnp.int32, raw.shape, 1)
    return 2.0 * jax.nn.sigmoid(
        jnp.sum(jnp.where(lane == head + BETA_AT, raw, 0.0), axis=1, keepdims=True)
    )


BETA_AT = 6
CONV_AT = 2
TAPS = 4


def conv_weights(small, head):
    part = small[pl.ds(pl.multiple_of(head * HD, HD), HD), :].astype(F32)
    return part.T[CONV_AT : CONV_AT + TAPS, :]


def convolve(path, taps, marks):
    total = taps[0:1, :] * path
    for m in range(1, TAPS):
        total = total + taps[m : m + 1, :] * (pltpu.roll(path, m, 0) * marks[:, m : m + 1])
    return total


def own_blocks(s, q, k, w, bcol, stores):
    t_out, a_out, z_out, m_out, kp_out, qm_buf, s_buf = stores
    row, col = iota2(0), iota2(1)
    strict, closed = row > col, row >= col
    eye = (row == col).astype(F32)

    def group(g, carry):
        sl = [pl.ds(pl.multiple_of((g * GROUP + n) * BLK, BLK), BLK) for n in range(GROUP)]
        qs = [q[r, :] for r in sl]
        ks = [k[r, :] for r in sl]
        ws = [w[r, :] for r in sl]
        bc = [jnp.broadcast_to(bcol[r, :], (BLK, BLK)) for r in sl]
        br = [b.T for b in bc]
        low = [jnp.where(strict, mm_nt(x, x), 0.0) * b for x, b in zip(ws, br)]
        inv = unit_inverses(low)
        m1 = [jnp.where(strict, mm_nt(x, y), 0.0) for x, y in zip(ws, ks)]
        gq = [jnp.where(closed, mm_nt(x, y), 0.0) * b for x, y, b in zip(qs, ws, br)]
        a = [mm(x, t) for x, t in zip(gq, inv)]
        z = [mm_tn(t, b * x.astype(F32)) for t, b, x in zip(inv, bc, ws)]
        sd = [mm_nt(x, y) - mm(p, m) for x, y, p, m in zip(qs, ks, a, m1)]
        qm = [x.astype(F32) - mm(p, y) for x, p, y in zip(qs, a, ws)]
        kmt = [x.astype(F32).T - mm_tn(zz, m) for x, zz, m in zip(ks, z, m1)]
        pm = [eye - mm_tn(zz, x) for zz, x in zip(z, ws)]
        for n, r in enumerate(sl):
            t_out[s, r, :] = inv[n].astype(t_out.dtype)
            a_out[s, r, :] = a[n].astype(a_out.dtype)
            z_out[s, r, :] = z[n].astype(z_out.dtype)
            m_out[s, r, :] = m1[n].astype(m_out.dtype)
            kp_out[s, r, :HD] = kmt[n].astype(BF16)
            kp_out[s, r, HD:] = pm[n].astype(BF16)
            qm_buf[r, :] = qm[n]
            s_buf[r, r] = sd[n]
        return carry

    lax.fori_loop(0, NB // GROUP, group, 0)


def sweep(s, qc, kp, qm_buf, x_buf, s_buf):
    at = NQC
    for j in range(NB - 2, -1, -1):
        r0 = (j + 1) * BLK
        rows = SEQ - r0
        x_buf[r0 : r0 + BLK, :] = qm_buf[r0 : r0 + BLK, :]
        x = x_buf[r0:, :].astype(BF16)
        at -= rows
        qc[s, at : at + rows, :] = x
        both = mm(x, kp[s, j * BLK : r0, :])
        s_buf[r0:, j * BLK : r0] = both[:, :HD]
        x_buf[r0:, :] = both[:, HD:]


def weigh(s, v, dcol, drow, s_buf, probs, o):
    for i in range(NB):
        lo, width = i * BLK, (i + 1) * BLK
        t = s_buf[lo:width, :width] * SCALE
        seen = dcol[lo:width, 0:1] == drow[0:1, :width]
        seen = seen & (
            lax.broadcasted_iota(jnp.int32, (BLK, width), 0) + lo
            >= lax.broadcasted_iota(jnp.int32, (BLK, width), 1)
        )
        t = jnp.where(seen, t, -1e30)
        e = jnp.exp(t - jnp.max(t, axis=1, keepdims=True))
        p = (e * (1.0 / jnp.sum(e, axis=1, keepdims=True))).astype(BF16)
        probs[s, lo:width, :width] = p
        o[lo:width, :] = mm(p, v[:width, :])


def project(x_all, whole, gains, normed, qkvp, raw):
    rows = 256
    width = x_all.shape[1]
    for n in range(width // HD):
        cols = slice(n * HD, (n + 1) * HD)
        gains[:, cols] = whole[cols, 8 * HD : 9 * HD].astype(F32).T[:8, :]

    def block(i, carry):
        at = pl.ds(pl.multiple_of(i * rows, rows), rows)
        x = x_all[at, :].astype(F32)
        scale = lax.rsqrt(jnp.mean(x * x, axis=1, keepdims=True) + 1e-05)
        n = (x * scale * gains[0:1, :]).astype(BF16)
        normed[at, :] = n
        y = mm(n, whole[:, : 9 * HD])
        qkvp[at, :] = y[:, : 8 * HD].astype(BF16)
        raw[at, :] = y[:, 8 * HD :]
        return carry

    lax.fori_loop(0, SEQ // rows, block, 0)


def heads_here():
    chip, core = lax.axis_index("x"), lax.axis_index("c")
    return 3 * chip + 2 * core, 3 * chip + 1


def fwd_slot(poke, s, head, small, marks, drow, qkvp, raw, vec, o, probs, qc, t_out, a_out, z_out, m_out, kp_out, s_buf, x_buf, qm_buf, b_buf):
    cols = slice(s * HD, (s + 1) * HD)
    q, k, v, path = (qkvp.at[:, (4 * s + n) * HD : (4 * s + n + 1) * HD] for n in range(4))
    taps = conv_weights(small, head)
    conved = convolve(path[...].astype(F32), taps, marks[...])
    unit = conved * lax.rsqrt(jnp.sum(conved * conved, axis=1, keepdims=True) + 1e-06)
    vec[:, cols] = unit.astype(BF16)
    b_buf[...] = betas_of(raw[...], head)
    own_blocks(s, q, k, vec.at[:, cols], b_buf, (t_out, a_out, z_out, m_out, kp_out, qm_buf, s_buf))
    poke()
    sweep(s, qc, kp_out, qm_buf, x_buf, s_buf)
    poke()
    weigh(s, v, marks, drow, s_buf, probs, o.at[:, cols])


def score_grads(s, v, o, do, probs, ds_buf, dv):
    for i in range(NB):
        lo, width = i * BLK, (i + 1) * BLK
        p = probs[0, lo:width, :width].astype(F32)
        g = do[lo:width, :]
        delta = jnp.sum(g * o[lo:width, :].astype(F32), axis=1, keepdims=True)
        ds = p * (mm_nt(g, v[:width, :]) - delta) * SCALE
        ds_buf[lo:width, :width] = ds.astype(BF16)
    for j in range(NB):
        lo = j * BLK
        dv[lo : lo + BLK, :] = mm_tn(probs[0, lo:, lo : lo + BLK], do[lo:, :]).astype(dv.dtype)


def sweep_back(s, qc, kp, ds_buf, x_buf, dkm_buf, dpm_buf):
    x_buf[...] = jnp.zeros_like(x_buf)
    dkm_buf[SEQ - BLK :, :] = jnp.zeros((BLK, HD), F32)
    dpm_buf[SEQ - BLK :, :] = jnp.zeros((BLK, HD), F32)
    at = 0
    for j in range(NB - 1):
        lo, r0 = j * BLK, (j + 1) * BLK
        rows = SEQ - r0
        x = x_buf[r0:, :].astype(BF16)
        ds = ds_buf[r0:, lo:r0]
        qcj = qc[0, at : at + rows, :]
        at += rows
        both = mm_tn(qcj, jnp.concatenate([x, ds], axis=1))
        dpm_buf[lo:r0, :] = both[:, :HD]
        dkm_buf[lo:r0, :] = both[:, HD:].T
        x_buf[r0:, :] = mm_nt(jnp.concatenate([ds, x], axis=1), kp[0, lo:r0, :])


def own_blocks_back(s, q, k, w, bcol, saved, bufs, dq, dk, dw, db):
    t_in, a_in, z_in, m_in = saved
    ds_buf, x_buf, dkm_buf, dpm_buf = bufs
    row, col = iota2(0), iota2(1)
    strict, closed = row > col, row >= col

    def group(g, carry):
        sl = [pl.ds(pl.multiple_of((g * GROUP_BACK + n) * BLK, BLK), BLK) for n in range(GROUP_BACK)]
        rng = range(GROUP_BACK)
        Q = [q[r, :] for r in sl]
        K = [k[r, :] for r in sl]
        W = [w[r, :] for r in sl]
        bc = [jnp.broadcast_to(bcol[r, :], (BLK, BLK)) for r in sl]
        br = [b.T for b in bc]
        E = [ds_buf[r, r] for r in sl]
        T = [t_in[0, r, :] for r in sl]
        A = [a_in[0, r, :] for r in sl]
        Z = [z_in[0, r, :] for r in sl]
        M = [m_in[0, r, :] for r in sl]
        dQm = [x_buf[r, :] for r in sl]
        dKm = [dkm_buf[r, :] for r in sl]
        dPm = [dpm_buf[r, :] for r in sl]
        i1 = [mm_nt(W[n], W[n]) for n in rng]
        qw = [jnp.where(closed, mm_nt(Q[n], W[n]), 0.0) for n in rng]
        dA = [-(mm_nt(E[n], M[n]) + mm_nt(dQm[n], W[n])) for n in rng]
        dM = [jnp.where(strict, -(mm_tn(A[n], E[n]) + mm_nt(Z[n], dKm[n])), 0.0) for n in rng]
        dZ = [-(mm(M[n], dKm[n]) + mm_nt(W[n], dPm[n])) for n in rng]
        dW = [-(mm_tn(A[n], dQm[n]) + mm(Z[n], dPm[n])) for n in rng]
        dG = [jnp.where(closed, mm_nt(dA[n], T[n]), 0.0) for n in rng]
        bw = [bc[n] * W[n].astype(F32) for n in rng]
        dT = [mm_tn(qw[n] * br[n], dA[n]) + mm_nt(bw[n], dZ[n]) for n in rng]
        dBW = [mm(T[n], dZ[n]) for n in rng]
        dL = [mm_tn(T[n], dT[n]) for n in rng]
        dL = [jnp.where(strict, -mm_nt(dL[n], T[n]), 0.0) for n in rng]
        dI = [dL[n] * br[n] for n in rng]
        R = [dG[n] * br[n] for n in rng]
        for n, r in enumerate(sl):
            db[r, :] = jnp.sum(
                (dL[n] * i1[n] + dG[n] * qw[n]).T + dBW[n] * W[n].astype(F32), axis=1, keepdims=True
            )
            dq[r, :] = (dQm[n] + mm(E[n], K[n]) + mm(R[n], W[n])).astype(dq.dtype)
            dk[r, :] = (dKm[n] + mm_tn(E[n], Q[n]) + mm_tn(dM[n], W[n])).astype(dk.dtype)
            dw[r, :] = (
                dW[n]
                + bc[n] * dBW[n]
                + mm_tn(R[n], Q[n])
                + mm(dM[n], K[n])
                + mm(dI[n] + dI[n].T, W[n])
            )
        return carry

    lax.fori_loop(0, NB // GROUP_BACK, group, 0)


def bwd_slot(poke, s, head, qkvp, raw, small, marks, vec, o, do, probs, qc, t_in, a_in, z_in, m_in, kp, d_ext, d_conv, ds_buf, x_buf, dkm_buf, dpm_buf, b_buf, db_buf, dw_buf):
    cols = slice(s * HD, (s + 1) * HD)
    q, k, v, path = (qkvp.at[:, (4 * s + n) * HD : (4 * s + n + 1) * HD] for n in range(4))
    dq, dk, dv, dpath = (d_ext.at[:, (4 * s + n) * HD : (4 * s + n + 1) * HD] for n in range(4))
    score_grads(s, v, o.at[:, cols], do.at[:, cols], probs, ds_buf, dv)
    poke()
    sweep_back(s, qc, kp, ds_buf, x_buf, dkm_buf, dpm_buf)
    poke()
    beta = betas_of(raw[...], head)
    b_buf[...] = beta
    own_blocks_back(
        s, q, k, vec.at[:, cols], b_buf, (t_in, a_in, z_in, m_in), (ds_buf, x_buf, dkm_buf, dpm_buf), dq, dk, dw_buf, db_buf
    )
    poke()
    taps = conv_weights(small, head)
    raw_path = path[...].astype(F32)
    conved = convolve(raw_path, taps, marks[...])
    scale = lax.rsqrt(jnp.sum(conved * conved, axis=1, keepdims=True) + 1e-06)
    unit = conved * scale
    dw = dw_buf[...]
    d_conved = scale * (dw - unit * jnp.sum(dw * unit, axis=1, keepdims=True))
    total = taps[0:1, :] * d_conved
    d_conv[s, 0:1, :] = jnp.sum(d_conved * raw_path, axis=0, keepdims=True)
    for m in range(1, TAPS):
        marked = d_conved * marks[:, m : m + 1]
        d_conv[s, m : m + 1, :] = jnp.sum(marked * pltpu.roll(raw_path, m, 0), axis=0, keepdims=True)
        total = total + taps[m : m + 1, :] * pltpu.roll(marked, SEQ - m, 0)
    dpath[...] = total.astype(dpath.dtype)
    lane = lax.broadcasted_iota(jnp.int32, (SEQ, HD), 1)
    return jnp.where(lane == head + BETA_AT, db_buf[...] * beta * (1.0 - 0.5 * beta), 0.0)


def fwd_shapes(width):
    return [
        ((SEQ, width), BF16),
        ((SEQ, 8 * HD), BF16),
        ((SEQ, HD), F32),
        ((SEQ, 2 * HD), BF16),
        ((SEQ, 2 * HD), BF16),
        ((8, width), F32),
        ((2, SEQ, SEQ), BF16),
        ((2, NQC, HD), BF16),
        ((2, SEQ, BLK), BF16),
        ((2, SEQ, BLK), BF16),
        ((2, SEQ, BLK), BF16),
        ((2, SEQ, BLK), BF16),
        ((2, SEQ, 2 * HD), BF16),
    ]


def fwd_scratch():
    return [
        pltpu.VMEM((SEQ, SEQ), F32),
        pltpu.VMEM((SEQ, HD), F32),
        pltpu.VMEM((SEQ, HD), F32),
        pltpu.VMEM((SEQ, 1), F32),
    ]


def bwd_scratch():
    return (
        [pltpu.VMEM((SEQ, SEQ), BF16)]
        + [pltpu.VMEM((SEQ, HD), F32)] * 3
        + [pltpu.VMEM((SEQ, 1), F32)] * 2
        + [pltpu.VMEM((SEQ, HD), F32)]
    )


MESH = pl.DeviceIdType.MESH
ANY = pl.BlockSpec(memory_space=pl.ANY)
VMEM = pl.BlockSpec(memory_space=pltpu.VMEM)


class Place:
    def __init__(self):
        self.x, self.c = lax.axis_index("x"), lax.axis_index("c")
        self.y = lax.axis_index("y")
        self.zl, self.zh = lax.axis_index("zl"), lax.axis_index("zh")
        self.z = self.zh * 2 + self.zl

    def chip(self, d):
        return lax.rem(self.x + d, 4)

    def at_x(self, d):
        return {"x": lax.rem(self.x + d, 4)}

    def at_xc(self, d, k):
        return {"x": lax.rem(self.x + d, 4), "c": lax.rem(self.c + k, 2)}

    def sibling(self):
        return {"c": 1 - self.c}

    def at_y(self, d):
        return {"y": lax.rem(self.y + d, 4)}

    def at_z(self, d):
        z = lax.rem(self.z + d, 4)
        return {"zl": lax.rem(z, 2), "zh": z // 2}


class Net:
    def __init__(self, send_sem, recv_sem, local_sem):
        self.place = Place()
        self.send_sem, self.recv_sem, self.local_sem = send_sem, recv_sem, local_sem
        self.count, self.kept, self.locals, self.sent = 0, 0, [], []

    def prepare(self, src, dst, device):
        k = self.count
        self.count += 1
        return pltpu.make_async_remote_copy(
            src_ref=src,
            dst_ref=dst,
            send_sem=self.send_sem.at[k],
            recv_sem=self.recv_sem.at[k],
            device_id=device,
            device_id_type=MESH,
        )

    def send(self, src, dst, device):
        copy = self.prepare(src, dst, device)
        copy.start()
        self.sent.append(copy)
        return copy

    def local(self, src, dst):
        self.kept += 1
        return pltpu.make_async_copy(src, dst, self.local_sem.at[self.kept - 1])

    def load(self, src, dst):
        copy = self.local(src, dst)
        copy.start()
        return copy

    def keep(self, src, dst):
        self.locals.append(self.load(src, dst))

    def settle(self):
        for copy in self.locals:
            copy.wait()
        self.locals = []

    def finish(self):
        for copy in self.sent:
            copy.wait_send()
        self.settle()


def meet(devices):
    barrier = pltpu.get_barrier_semaphore()
    for device in devices:
        pl.semaphore_signal(barrier, inc=1, device_id=device, device_id_type=MESH)
    pl.semaphore_wait(barrier, len(devices))


class Jobs:
    def __init__(self, *jobs):
        self.all = list(jobs)
        self.jobs = list(jobs)

    def poke(self):
        for job in list(self.jobs):
            try:
                next(job)
            except StopIteration:
                self.jobs.remove(job)

    def step(self, *which):
        for n in which:
            next(self.all[n], None)

    def drain(self):
        while self.jobs:
            self.poke()


def interleave(*jobs):
    Jobs(*jobs).drain()


def team_peers(p):
    return [p.at_x(1), p.at_x(3), p.sibling()]


def team_all(p):
    return [p.at_xc(d, k) for d in range(4) for k in range(2) if d + k]


def group_peers(p):
    return [p.at_y(d) for d in (1, 2, 3)] + [p.at_z(d) for d in (1, 2, 3)]


def gather_team(net, own, out):
    p = net.place
    me, sib = 2 * p.x + p.c, p.sibling()
    right, left = p.at_x(1), p.at_x(3)
    t_l, t_r, t_2 = (2 * p.chip(d) + p.c for d in (3, 1, 2))
    to_r = net.send(own, out.at[:, me], right)
    to_l = net.send(own, out.at[:, me], left)
    shared = [net.send(own, out.at[:, me], sib)]
    net.keep(own, out.at[:, me])
    yield
    to_r.wait_recv()
    on_r = net.send(out.at[0, t_l], out.at[0, t_l], right)
    shared.append(net.send(out.at[:, t_l], out.at[:, t_l], sib))
    to_l.wait_recv()
    on_l = net.send(out.at[1, t_r], out.at[1, t_r], left)
    shared.append(net.send(out.at[:, t_r], out.at[:, t_r], sib))
    yield
    on_r.wait_recv()
    shared.append(net.send(out.at[0, t_2], out.at[0, t_2], sib))
    on_l.wait_recv()
    shared.append(net.send(out.at[1, t_2], out.at[1, t_2], sib))
    yield
    for copy in shared:
        copy.wait_recv()


GATHER_TEAM = 10


def add(a, b):
    return (a.astype(F32) + b.astype(F32)).astype(BF16)


def scatter_team(net, part, got, total, from_l, from_r, all_l, all_r, finish):
    p = net.place
    sib, right, left = p.sibling(), p.at_x(1), p.at_x(3)
    order = (2, 1, 3, 0)
    swaps, loads = [], []
    for d in order:
        at = p.chip(d)
        swaps.append(net.send(part.at[:, 2 * at + 1 - p.c], got.at[:, at], sib))
        loads.append(net.load(part.at[:, 2 * at + p.c], total.at[:, at]))

    def pair(n):
        swaps[n].wait_recv()
        loads[n].wait()
        at = p.chip(order[n])
        total[:, at] = add(total[:, at], got[:, at])
        return at

    yield
    x_2 = pair(0)
    half_r = net.send(total.at[0, x_2], from_l, right)
    half_l = net.send(total.at[1, x_2], from_r, left)
    x_r = pair(1)
    rest_r = net.send(total.at[1, x_r], all_l.at[1], right)
    x_l = pair(2)
    rest_l = net.send(total.at[0, x_l], all_r.at[0], left)
    pair(3)
    yield
    half_r.wait_recv()
    total[0, x_r] = add(total[0, x_r], from_l[...])
    last_r = net.send(total.at[0, x_r], all_l.at[0], right)
    half_l.wait_recv()
    total[1, x_l] = add(total[1, x_l], from_r[...])
    last_l = net.send(total.at[1, x_l], all_r.at[1], left)
    yield
    for copy in (rest_r, rest_l, last_r, last_l):
        copy.wait_recv()
    finish(total[:, p.x].astype(F32) + all_l[...].astype(F32) + all_r[...].astype(F32))


SCATTER_TEAM_LOADS = 4
SCATTER_TEAM = 10


def scatter_team_scratch(n, w):
    return [
        pltpu.VMEM((2, 4, n, w), BF16),
        pltpu.VMEM((2, 4, n, w), BF16),
        pltpu.VMEM((n, w), BF16),
        pltpu.VMEM((n, w), BF16),
        pltpu.VMEM((2, n, w), BF16),
        pltpu.VMEM((2, n, w), BF16),
    ]


def chunk_rows(y, z, rows):
    zl, zh = (z % 2, z // 2) if isinstance(z, int) else (lax.rem(z, 2), z // 2)
    return pl.ds(pl.multiple_of(((zl * 4 + y) * 2 + zh) * rows, rows), rows)


def halves(cols):
    mid = cols // 2
    return [(pl.ds(0, mid),) * 2], [(pl.ds(mid, cols - mid),) * 2]


def gather_groups(net, own, out, y_pieces, z_pieces, share=False):
    p = net.place
    rows = own.shape[0]
    shared = []
    for src, dst in y_pieces + z_pieces:
        net.keep(own.at[:, src], out.at[chunk_rows(p.y, p.z, rows), dst])

    def spread(pieces, y, z, devices, first=False):
        copies = []
        for src, dst in pieces:
            place = out.at[chunk_rows(y, z, rows), dst]
            copies += [net.send(own.at[:, src] if first else place, place, d) for d in devices]
        return copies

    def give(y, z, first=False):
        if share:
            src, dst = z_pieces[-1]
            place = out.at[chunk_rows(y, z, rows), dst]
            shared.append(net.send(own.at[:, src] if first else place, place, p.sibling()))

    order = (1, 3, 2)
    ys, zs = [p.at_y(d) for d in order], [p.at_z(d) for d in order]
    y_first = spread(y_pieces, p.y, p.z, ys, True)
    z_first = spread(z_pieces, p.y, p.z, zs, True)
    last = spread(y_pieces, p.y, p.z, zs, True)
    via_y = [(p.z, spread(z_pieces, p.y, p.z, ys, True))]
    give(p.y, p.z, True)
    yield
    for n, d in enumerate(order):
        for copy in y_first[n::3]:
            copy.wait_recv()
        last += spread(y_pieces, lax.rem(p.y + 4 - d, 4), p.z, zs)
        for copy in z_first[n::3]:
            copy.wait_recv()
        z = lax.rem(p.z + 4 - d, 4)
        via_y.append((z, spread(z_pieces, p.y, z, ys)))
        give(p.y, z)
        yield
    for z, copies in via_y:
        for n, d in enumerate(order):
            for copy in copies[n::3]:
                copy.wait_recv()
            give(lax.rem(p.y + 4 - d, 4), z)
    for copy in last + shared:
        copy.wait_recv()


GATHER_GROUPS = 30


def scatter_groups(net, part, out, cuts, z_got, z_sum, z_last, y_got, y_sum, y_last):
    p = net.place
    lo, mid, hi = cuts
    first, second = pl.ds(lo, mid - lo), pl.ds(mid, hi - mid)
    rows = z_sum.shape[1]
    both = hi > mid
    flat = len(part.shape) == 2
    order = (2, 1, 3)
    a, b, a_own, b_own = [], [], [], []
    for n, d in enumerate(order):
        z, y = lax.rem(p.z + d, 4), lax.rem(p.y + d, 4)
        if flat:
            for k in range(4):
                a.append(net.send(part.at[chunk_rows(k, z, rows), first], z_got.at[n, k], p.at_z(d)))
                if both:
                    b.append(net.send(part.at[chunk_rows(y, k, rows), second], y_got.at[n, k % 2, k // 2], p.at_y(d)))
        else:
            a.append(net.send(part.at[lax.rem(z, 2), :, z // 2, :, first], z_got.at[n], p.at_z(d)))
            if both:
                b.append(net.send(part.at[:, y, :, :, second], y_got.at[n], p.at_y(d)))
    if flat:
        for k in range(4):
            a_own.append(net.load(part.at[chunk_rows(k, p.z, rows), first], z_sum.at[k]))
            if both:
                b_own.append(net.load(part.at[chunk_rows(p.y, k, rows), second], y_sum.at[k % 2, k // 2]))
    else:
        a_own.append(net.load(part.at[p.zl, :, p.zh, :, first], z_sum))
        if both:
            b_own.append(net.load(part.at[:, p.y, :, :, second], y_sum))

    yield
    for copy in a_own:
        copy.wait()
    for copy in a:
        copy.wait_recv()
    for y in range(4):
        t = z_sum[y].astype(F32)
        for n in range(3):
            t = t + z_got[n, y].astype(F32)
        z_sum[y] = t.astype(BF16)
    a = [
        net.send(z_sum.at[lax.rem(p.y + d, 4)], z_last.at[n], p.at_y(d)) for n, d in enumerate(order)
    ]
    if both:
        yield
        for copy in b_own:
            copy.wait()
        for copy in b:
            copy.wait_recv()
        for zl in range(2):
            for zh in range(2):
                t = y_sum[zl, zh].astype(F32)
                for n in range(3):
                    t = t + y_got[n, zl, zh].astype(F32)
                y_sum[zl, zh] = t.astype(BF16)
        b = []
        for n, d in enumerate(order):
            z = lax.rem(p.z + d, 4)
            b.append(net.send(y_sum.at[lax.rem(z, 2), z // 2], y_last.at[n], p.at_z(d)))
    yield
    for copy in a:
        copy.wait_recv()
    t = z_sum[p.y].astype(F32)
    for n in range(3):
        t = t + z_last[n].astype(F32)
    out[:, first] = t.astype(out.dtype)
    if both:
        yield
        for copy in b:
            copy.wait_recv()
        t = y_sum[p.zl, p.zh].astype(F32)
        for n in range(3):
            t = t + y_last[n].astype(F32)
        out[:, second] = t.astype(out.dtype)


SCATTER_GROUPS_LOADS = 2
SCATTER_GROUPS_FLAT_LOADS = 8
SCATTER_GROUPS = 12
SCATTER_GROUPS_FLAT = 30


def scatter_groups_scratch(r, cuts):
    a, b = cuts[1] - cuts[0], max(cuts[2] - cuts[1], HD)
    return [
        pltpu.VMEM((3, 4, r, a), BF16),
        pltpu.VMEM((4, r, a), BF16),
        pltpu.VMEM((3, r, a), BF16),
        pltpu.VMEM((3, 2, 2, r, b), BF16),
        pltpu.VMEM((2, 2, r, b), BF16),
        pltpu.VMEM((3, r, b), BF16),
    ]


def sems(remote, local):
    return [
        pltpu.SemaphoreType.DMA((remote,)),
        pltpu.SemaphoreType.DMA((remote,)),
        pltpu.SemaphoreType.DMA((max(local, 1),)),
    ]


def params(collective_id):
    return pltpu.CompilerParams(
        collective_id=collective_id, has_side_effects=True, vmem_limit_bytes=VM
    )


EPS_NORM = 1e-05
EPS_UNIT = 1e-06
SHAPE = jax.ShapeDtypeStruct


def all_to_team(net, packs, got):
    p = net.place
    me = 2 * p.x + p.c
    net.keep(packs.at[me], got.at[me])
    copies = []
    for d in (2, 1, 3, 0):
        for k in (1, 0):
            if d + k:
                to = 2 * p.chip(d) + lax.rem(p.c + k, 2)
                copies.append(net.send(packs.at[to], got.at[me], p.at_xc(d, k)))
    yield
    for copy in copies:
        copy.wait_recv()


TO_TEAM = 7


def swap_rows(net, pairs):
    p = net.place
    copies = []
    for src, dst in pairs:
        net.keep(src.at[p.zh], dst.at[p.zh])
        copies.append(net.send(src.at[1 - p.zh], dst.at[p.zh], p.at_z(2)))
    yield
    for copy in copies:
        copy.wait_recv()


def thin_rows(rows, padded):
    out = lax.broadcasted_iota(jnp.int32, (8 * rows, 8 * padded), 0)
    at = lax.broadcasted_iota(jnp.int32, (8 * rows, 8 * padded), 1)
    return ((out // rows == at // padded) & (out % rows == at % padded)).astype(BF16)


HEADS_W, SMALL_W = 8 * HD, HD
EXT_W = HEADS_W + SMALL_W
OUT_B, OUT_A = EXT_W, EXT_W + HD
WHOLE_W = EXT_W + 2 * HD
SHARED_W = 3 * HD
FIRST_W = 5 * HD + SHARED_W
PIECE = 32


def shift_pieces(tiles):
    lane = lax.broadcasted_iota(jnp.int32, tiles[0][0].shape, 1) // PIECE
    total = None
    for n, (tile, piece) in enumerate(tiles):
        turn = (PIECE * (n - piece)) % HD
        moved = pltpu.roll(tile, turn, 1) if turn else tile
        total = moved if total is None else jnp.where(lane == n, moved, total)
    return total


def small_columns(gain_a, gain_f, conv, w_beta, rows_buf, beta_buf):
    share = w_beta.shape[0]
    rows_buf[...] = jnp.zeros_like(rows_buf)
    beta_buf[...] = jnp.zeros_like(beta_buf)
    rows_buf[0:1, :share] = gain_a[...].astype(F32)
    rows_buf[1:2, :share] = gain_f[...].astype(F32)
    rows_buf[CONV_AT : CONV_AT + TAPS, :share] = conv[...].astype(F32)
    beta_buf[:share, : w_beta.shape[1]] = w_beta[...].astype(F32)
    columns = rows_buf[...].T[: beta_buf.shape[0], :]
    return (columns + pltpu.roll(beta_buf[...], BETA_AT, 1))[:share].astype(BF16)


def mark_documents(starts, zh, drow, marks):
    row, col = iota2(0), iota2(1)
    upto = (row <= col).astype(BF16)
    starts = jnp.broadcast_to(starts[pl.ds(zh, 1), :].astype(F32), drow.shape)
    before = 0.0
    for k in range(NB):
        cols = slice(k * BLK, (k + 1) * BLK)
        docs = mm(starts[:, cols], upto) + before
        before = docs[:, BLK - 1 :]
        drow[:, cols] = docs
    docs = drow[...]
    lane = lax.broadcasted_iota(jnp.int32, docs.shape, 1)
    kind = lax.broadcasted_iota(jnp.int32, docs.shape, 0) % TAPS
    total = docs
    for m in range(1, TAPS):
        same = ((pltpu.roll(docs, m, 1) == docs) & (lane >= m)).astype(F32)
        total = jnp.where(kind == m, same, total)
    drow[...] = total
    for k in range(NB):
        cols = slice(k * BLK, (k + 1) * BLK)
        tall = jnp.concatenate([total[:, cols]] * (BLK // total.shape[0]), axis=0)
        marks[cols, :] = tall.T[:, : marks.shape[1]]


def pack_weights(kinds, gate_up, small, packs):
    share = small.shape[0]
    packs[...] = jnp.zeros_like(packs)
    for t in range(8):
        own, middle = 3 * (t // 2) + 2 * (t % 2), 3 * (t // 2) + 1
        parts = [w[:, own * HD : (own + 1) * HD] for w in kinds]
        shared = [w[:, middle * HD : (middle + 1) * HD] for w in kinds]
        shared = shared[:3] if t % 2 == 0 else [shared[3], small, shared[4]]
        for n, part in enumerate(parts + shared):
            packs[t, :share, n * HD : (n + 1) * HD] = part
    for n, w in enumerate(gate_up):
        for t in range(8):
            for j in range(4):
                tiles = []
                for e in range(4 * j, 4 * j + 4):
                    at = (2 * e + t // 4) * HD
                    tiles.append((w[:, at : at + HD].astype(F32), t % 4))
                at = FIRST_W + n * 4 * HD + j * HD
                packs[t, :share, at : at + HD] = shift_pieces(tiles).astype(BF16)


def start_kernel(wq, wk, wv, wp, wo, gate, up, gain_a, gain_f, conv, w_beta, starts, tokens, grad_out, x_rows, g_rows, x_all, whole, own_ffn, drow, marks, packs, got, own, rows_buf, beta_buf, *sem):
    net = Net(*sem)
    p = net.place
    share = w_beta.shape[0]
    small = small_columns(gain_a, gain_f, conv, w_beta, rows_buf, beta_buf)
    pack_weights((wq, wk, wv, wp, wo), (gate, up), small, packs)
    first, second = pl.ds(0, FIRST_W), pl.ds(FIRST_W, own.shape[1] - FIRST_W)
    meet(team_all(p) + group_peers(p))
    trades = [all_to_team(net, packs.at[:, :, part], got.at[:, :, part]) for part in (first, second)]
    swaps = [swap_rows(net, (pair,)) for pair in ((tokens, x_rows), (grad_out, g_rows))]
    next(trades[0])
    next(swaps[0])
    pick = thin_rows(share, packs.shape[1])

    def thin(part):
        wide = got[:, :, part].reshape(pick.shape[1], part.size)
        own[:, part] = mm(pick, wide).astype(BF16)

    interleave(trades[0])
    net.settle()
    thin(first)
    shared = pl.ds(pl.multiple_of(4 * HD + p.c * SHARED_W, HD), SHARED_W)
    heads = gather_groups(
        net,
        own,
        whole,
        [(pl.ds(0, 4 * HD), pl.ds(0, 4 * HD))],
        [(pl.ds(4 * HD, HD), pl.ds(OUT_A, HD)), (pl.ds(5 * HD, SHARED_W), shared)],
        True,
    )
    next(heads)
    mark_documents(starts, p.zh, drow, marks)
    interleave(swaps[0])
    x_team = gather_team(net, x_rows, x_all)
    next(x_team)
    next(trades[1])
    next(swaps[1])
    for _ in range(3):
        next(heads)
    next(x_team)
    interleave(trades[1])
    net.settle()
    thin(second)
    net.keep(own.at[:, second], own_ffn)
    interleave(x_team, heads, swaps[1])
    net.finish()


def start(kinds, gate, up, gain_a, gain_f, conv, w_beta, starts, tokens, grad_out):
    share, width = kinds[0].shape
    two, n, _ = tokens.shape
    rows = SHAPE(tokens.shape, BF16)
    cols = FIRST_W + gate.shape[1] // 4
    return pl.pallas_call(
        start_kernel,
        out_shape=[
            rows,
            rows,
            SHAPE((two, 8, n, width), BF16),
            SHAPE((width, WHOLE_W), BF16),
            SHAPE((8 * share, cols - FIRST_W), BF16),
            SHAPE((8, SEQ), F32),
            SHAPE((SEQ, 8), F32),
        ],
        in_specs=[VMEM] * 12 + [ANY] * 2,
        out_specs=[ANY] * 5 + [VMEM] * 2,
        scratch_shapes=[
            pltpu.VMEM((8, 16, cols), BF16),
            pltpu.VMEM((8, 16, cols), BF16),
            pltpu.VMEM((8 * share, cols), BF16),
            pltpu.VMEM((HD, HD), F32),
            pltpu.VMEM((16, HD), F32),
        ]
        + sems(2 * TO_TEAM + 2 + GATHER_TEAM + 3 * GATHER_GROUPS // 2 + 16, 9),
        compiler_params=params(1),
        name="start",
    )(*kinds, gate, up, gain_a, gain_f, conv, w_beta, starts, tokens, grad_out)


def lanes(at):
    return pl.ds(pl.multiple_of(at * HD, HD), HD)


def trade_out(net, whole, w_out):
    p = net.place
    copies, own = [], []
    for d in (2, 1, 3, 0):
        for k in (1, 0):
            xd, cd = p.chip(d), lax.rem(p.c + k, 2)
            row_a, row_b = lanes(3 * xd + 2 * cd), lanes(3 * xd + 1)
            row_c = lanes(3 * xd + jnp.where(p.c == 0, 2 * cd, 1))
            col_a, col_b = lanes(3 * p.x + 2 * p.c), lanes(3 * p.x + 1)
            moves = (
                (whole.at[row_a, pl.ds(OUT_A, HD)], w_out.at[pl.ds(0, HD), col_a]),
                (whole.at[row_b, pl.ds(OUT_A, HD)], w_out.at[pl.ds(HD, HD), col_a]),
                (whole.at[row_c, pl.ds(OUT_B, HD)], w_out.at[lanes(p.c), col_b]),
            )
            for src, dst in moves:
                if d + k:
                    copies.append(net.send(src, dst, p.at_xc(d, k)))
                else:
                    own.append(net.load(src, dst))
    yield
    for copy in own:
        copy.wait()
    for copy in copies:
        copy.wait_recv()


def attn_fwd_kernel(x_all, whole, marks, drow, own_ffn, g_rows, *rest):
    kept, (w_ffn, g_all, w_out, part), rest = rest[:13], rest[13:17], rest[17:]
    bufs, (x_buf, w_buf, wo_buf, part_buf), rest = rest[:14], rest[14:18], rest[18:]
    normed, qkvp, raw, vec, mixed, gains, *saved, o = bufs
    net = Net(*rest[-3:])
    p = net.place
    loads = [net.load(whole.at[:, pl.ds(0, 9 * HD)], w_buf), net.load(x_all, x_buf)]
    meet(team_all(p) + group_peers(p))
    jobs = Jobs(
        gather_groups(net, own_ffn, w_ffn, *halves(own_ffn.shape[1])),
        trade_out(net, whole, wo_buf),
        gather_team(net, g_rows, g_all),
    )
    jobs.step(0, 1, 2)
    for copy in loads:
        copy.wait()
    project(x_buf, w_buf, gains, normed, qkvp, raw)
    for n in (0, 1, 2, 5):
        net.keep(bufs[n], kept[n])
    steps = [(0, 0, 0), (), (), (), (2,), ()]
    poke = lambda: jobs.step(*steps.pop(0)) if steps else None
    for s, head in enumerate(heads_here()):
        cols = pl.ds(s * HD, HD)
        poke()
        fwd_slot(poke, s, head, w_buf.at[:, pl.ds(8 * HD, HD)], marks, drow, qkvp, raw, vec, o, *saved, *rest[:-3])
        net.keep(vec.at[:, cols], kept[3].at[:, cols])
        for src, dst in zip(saved, kept[6:]):
            net.keep(src.at[s], dst.at[s])
    mixed[:, :HD] = o[:, :HD].astype(BF16)
    mixed[:, HD:] = jnp.where(p.c == 0, o[:, HD:], 0.0).astype(BF16)
    net.keep(mixed, kept[4])
    jobs.step(1, 1)
    net.keep(wo_buf, w_out)
    two, _, n, width = part.shape
    for h in range(two):
        for t in range(0, 8, 4):
            at = (h * 8 + t) * n
            y = mm(mixed[at : at + 4 * n, :], wo_buf[...]).astype(BF16)
            part_buf[h, t : t + 4] = y.reshape(4, n, width)
    net.keep(part_buf, part)
    jobs.drain()
    net.finish()


def attn_fwd(x_all, whole, marks, drow, own_ffn, g_rows):
    rows, cols = own_ffn.shape
    two, n, width = g_rows.shape
    kept = fwd_shapes(width)
    part = (two, 8, n, width)
    return pl.pallas_call(
        attn_fwd_kernel,
        out_shape=[SHAPE(*a) for a in kept]
        + [SHAPE((16 * rows, cols), BF16), SHAPE(part, BF16), SHAPE((2 * HD, width), BF16), SHAPE(part, BF16)],
        in_specs=[ANY, ANY, VMEM, VMEM, ANY, ANY],
        out_specs=[ANY] * (len(kept) + 4),
        scratch_shapes=[pltpu.VMEM(*a) for a in kept]
        + [
            pltpu.VMEM((SEQ, 2 * HD), F32),
            pltpu.VMEM((SEQ, width), BF16),
            pltpu.VMEM((width, 9 * HD), BF16),
            pltpu.VMEM((2 * HD, width), BF16),
            pltpu.VMEM(part, BF16),
        ]
        + fwd_scratch()
        + sems(GATHER_TEAM + GATHER_GROUPS + 21, 2 + 6 + 4 + 18 + 3),
        compiler_params=params(7),
        name="attn_fwd",
    )(x_all, whole, marks, drow, own_ffn, g_rows)


def norm_back(v, gain, d_normed):
    scale = lax.rsqrt(jnp.mean(v * v, axis=-1, keepdims=True) + EPS_NORM)
    unit = v * scale
    d_unit = d_normed * gain
    d_v = scale * (d_unit - unit * jnp.mean(d_unit * unit, axis=-1, keepdims=True))
    return d_v, d_normed * unit


def by_group(a):
    return a.reshape(2, 4, 2, a.shape[0] // 16, a.shape[1])


class TeamBlocks:
    def __init__(self, net, own, out):
        self.net, self.own, self.out = net, own, out

    def start(self):
        net, p, out = self.net, self.net.place, self.out
        place = out.at[:, 2 * p.x + p.c]
        self.to_r = net.send(self.own, place, p.at_x(1))
        self.to_l = net.send(self.own, place, p.at_x(3))
        self.shared = net.send(self.own, place, p.sibling())
        self.kept = net.load(self.own, place)

    def mine(self):
        self.kept.wait()
        self.shared.wait_recv()

    def hand_on(self):
        net, p, out = self.net, self.net.place, self.out
        left, right = 2 * p.chip(3) + p.c, 2 * p.chip(1) + p.c
        self.to_r.wait_recv()
        self.on_r = net.send(out.at[0, left], out.at[0, left], p.at_x(1))
        self.from_l = net.send(out.at[:, left], out.at[:, left], p.sibling())
        self.to_l.wait_recv()
        self.on_l = net.send(out.at[1, right], out.at[1, right], p.at_x(3))
        self.from_r = net.send(out.at[:, right], out.at[:, right], p.sibling())

    def opposite(self):
        net, p, out = self.net, self.net.place, self.out
        far = 2 * p.chip(2) + p.c
        self.far = []
        for n, copy in enumerate((self.on_r, self.on_l)):
            copy.wait_recv()
            self.far.append(net.send(out.at[n, far], out.at[n, far], p.sibling()))


class TeamSum:
    def __init__(self, net, part, got, total, from_l, from_r, all_l, all_r):
        self.net, self.part, self.got, self.total = net, part, got, total
        self.from_l, self.from_r, self.all_l, self.all_r = from_l, from_r, all_l, all_r
        self.swaps, self.last = {}, []

    def ready(self, d):
        p = self.net.place
        at = p.chip(d)
        self.swaps[d] = self.net.send(
            self.part.at[:, 2 * at + 1 - p.c], self.got.at[:, at], p.sibling()
        )

    def pair(self, d):
        p = self.net.place
        at = p.chip(d)
        self.swaps[d].wait_recv()
        self.total[:, at] = add(self.part[:, 2 * at + p.c], self.got[:, at])
        return at

    def near(self):
        net, p = self.net, self.net.place
        self.x_r = self.pair(1)
        self.last.append(net.send(self.total.at[1, self.x_r], self.all_l.at[1], p.at_x(1)))
        self.x_l = self.pair(3)
        self.last.append(net.send(self.total.at[0, self.x_l], self.all_r.at[0], p.at_x(3)))

    def far(self):
        net, p = self.net, self.net.place
        x_2 = self.pair(2)
        self.half_r = net.send(self.total.at[0, x_2], self.from_l, p.at_x(1))
        self.half_l = net.send(self.total.at[1, x_2], self.from_r, p.at_x(3))

    def on(self):
        net, p = self.net, self.net.place
        self.half_r.wait_recv()
        self.total[0, self.x_r] = add(self.total[0, self.x_r], self.from_l[...])
        self.last.append(net.send(self.total.at[0, self.x_r], self.all_l.at[0], p.at_x(1)))
        self.half_l.wait_recv()
        self.total[1, self.x_l] = add(self.total[1, self.x_l], self.from_r[...])
        self.last.append(net.send(self.total.at[1, self.x_l], self.all_r.at[1], p.at_x(3)))

    def result(self):
        for copy in self.last:
            copy.wait_recv()
        mine = self.total[:, self.net.place.x].astype(F32)
        return mine + self.all_l[...].astype(F32) + self.all_r[...].astype(F32)


def ffn_kernel(cuts, *refs):
    (part, x_rows, g_rows, gain, own_down, w_ffn, g_all), refs = refs[:7], refs[7:]
    (hidden, d_hidden, d_gain, branch_all, out_part, ffn_sum, down_out), refs = refs[:7], refs[7:]
    (w_in, w_down, g_buf, nf_all, normed, act, d_in, back, branch, d_ffn, d_down, out_buf), refs = refs[:12], refs[12:]
    scratch = [refs[6 * n : 6 * n + 6] for n in range(6)]
    net = Net(*refs[-3:])
    p = net.place
    loads = [net.load(w_ffn, w_in), net.load(g_all, g_buf)]
    meet(team_peers(p) + group_peers(p))
    two, _, n, width = part.shape
    half = w_down.shape[0]
    pieces = [pl.ds(m * n // 2, n // 2) for m in range(2)]

    def finish_rows(piece):
        def finish(sums):
            h = x_rows[:, piece].astype(F32) + sums
            hidden[:, piece] = h
            scale = lax.rsqrt(jnp.mean(h * h, axis=-1, keepdims=True) + EPS_NORM)
            normed[:, piece] = (h * scale * gain[1:2, :][None]).astype(BF16)

        return finish

    jobs = Jobs(
        *[
            scatter_team(net, part.at[:, :, piece], *scratch[m], finish_rows(piece))
            for m, piece in enumerate(pieces)
        ],
        gather_groups(net, own_down, w_down, *halves(width)),
    )
    blocks = [TeamBlocks(net, normed.at[:, piece], nf_all.at[:, :, piece]) for piece in pieces]
    jobs.step(0, 1, 2, 0, 1, 2, 2, 2, 0, 1)
    for m in range(2):
        jobs.step(m)
        blocks[m].start()
    jobs.drain()
    for copy in loads:
        copy.wait()
    net.settle()
    sums = [
        TeamSum(net, back.at[:, :, piece], *scratch[2 + m]) for m, piece in enumerate(pieces)
    ]

    def flat(ref, at):
        return ref[:, pl.ds(2 * at, 2)].reshape(4 * n, ref.shape[3])

    def work(d):
        at = p.chip(d)
        pre = mm(flat(nf_all, at), w_in[...])
        gate, up = pre[:, :half], pre[:, half:]
        sig = jax.nn.sigmoid(gate)
        silu = gate * sig
        act[:, pl.ds(2 * at, 2)] = (silu * up).astype(BF16).reshape(two, 2, n, half)
        d_act = mm_nt(flat(g_buf, at), w_down[...])
        d_gate = (d_act * up * (sig + silu * (1.0 - sig))).astype(BF16)
        d_up = (d_act * silu).astype(BF16)
        d_pre = jnp.concatenate([d_gate, d_up], axis=1)
        d_in[:, pl.ds(2 * at, 2)] = d_pre.reshape(two, 2, n, 2 * half)
        back[:, pl.ds(2 * at, 2)] = mm_nt(d_pre, w_in[...]).astype(BF16).reshape(two, 2, n, width)
        for s in sums:
            s.ready(d)

    for b in blocks:
        b.mine()
    work(0)
    for b in blocks:
        b.hand_on()
    for b in blocks:
        b.from_l.wait_recv()
    work(3)
    for b in blocks:
        b.opposite()
    for b in blocks:
        b.from_r.wait_recv()
    work(1)
    for s in sums:
        s.near()
    for b in blocks:
        for copy in b.far:
            copy.wait_recv()
    work(2)
    for s in sums:
        s.far()
    for s in sums:
        s.pair(0)
    rows = two * 8 * n
    step = width // 4
    groups = []
    for side in range(2):
        right = d_in[:, :, :, side * half : (side + 1) * half].reshape(rows, half)
        for k in range(4):
            cols = slice(k * step, (k + 1) * step)
            left = nf_all[:, :, :, cols].reshape(rows, step)
            d_ffn[side, cols, :] = mm_tn(left, right).astype(BF16)
        place = ffn_sum.at[:, pl.ds(side * half, half)]
        groups.append(scatter_groups(net, d_ffn.at[side], place, cuts, *scratch[4 + side]))
        next(groups[-1])
        sums[side].on()
    d_gain[...] = jnp.zeros_like(d_gain)
    teams = []
    for s, piece in zip(sums, pieces):
        d_h, d_g = norm_back(hidden[:, piece], gain[1:2, :][None], s.result())
        d_h = d_h + g_rows[:, piece].astype(F32)
        d_hidden[:, piece] = d_h
        branch[:, piece] = d_h.astype(BF16)
        d_gain[...] += jnp.sum(jnp.sum(d_g, axis=0), axis=0, keepdims=True)
        teams.append(gather_team(net, branch.at[:, piece], branch_all.at[:, :, piece]))
        next(teams[-1])
    step = half // 2
    for k in range(2):
        cols = slice(k * step, (k + 1) * step)
        left = act[:, :, :, cols].reshape(rows, step)
        d_down[cols, :] = mm_tn(left, g_buf[...].reshape(rows, width)).astype(BF16)
    net.keep(d_down, down_out)
    for h in range(two):
        for t in range(0, 8, 4):
            left = act[h, t : t + 4].reshape(4 * n, half)
            out_buf[h, t : t + 4] = mm(left, w_down[...]).astype(BF16).reshape(4, n, width)
    net.keep(out_buf, out_part)
    for team in teams:
        next(team)
    for _ in range(2):
        for group in groups:
            next(group)
    jobs = Jobs(*teams, *groups)
    jobs.drain()
    net.finish()


def ffn(part, x_rows, g_rows, gain, own_down, w_ffn, g_all):
    two, n, width = x_rows.shape
    cols = w_ffn.shape[1]
    half, rows = cols // 2, own_down.shape[0]
    every = (two, 8, n, width)
    share = width // 16
    cuts = (0, half // 2, half)
    return pl.pallas_call(
        functools.partial(ffn_kernel, cuts),
        out_shape=[
            SHAPE((two, n, width), F32),
            SHAPE((two, n, width), F32),
            SHAPE((1, width), F32),
            SHAPE(every, BF16),
            SHAPE(every, BF16),
            SHAPE((share, cols), BF16),
            SHAPE((16 * rows, width), BF16),
        ],
        in_specs=[ANY, VMEM, VMEM, VMEM, ANY, ANY, ANY],
        out_specs=[VMEM, VMEM, VMEM, ANY, ANY, VMEM, ANY],
        scratch_shapes=[
            pltpu.VMEM((width, cols), BF16),
            pltpu.VMEM((half, width), BF16),
            pltpu.VMEM(every, BF16),
            pltpu.VMEM(every, BF16),
            pltpu.VMEM((two, n, width), BF16),
            pltpu.VMEM((two, 8, n, half), BF16),
            pltpu.VMEM((two, 8, n, cols), BF16),
            pltpu.VMEM(every, BF16),
            pltpu.VMEM((two, n, width), BF16),
            pltpu.VMEM((2, width, half), BF16),
            pltpu.VMEM((half, width), BF16),
            pltpu.VMEM(every, BF16),
        ]
        + scatter_team_scratch(n // 2, width) * 4
        + scatter_groups_scratch(share, cuts) * 2
        + sems(
            4 * SCATTER_TEAM + 4 * GATHER_TEAM + GATHER_GROUPS + 2 * SCATTER_GROUPS_FLAT,
            2 + 2 * SCATTER_TEAM_LOADS + 2 + 2 + 2 + 2 + 2 * SCATTER_GROUPS_FLAT_LOADS,
        ),
        compiler_params=params(3),
        name="ffn",
    )(part, x_rows, g_rows, gain, own_down, w_ffn, g_all)


def trade_out_back(net, d_out, whole):
    p = net.place
    rows, middle, own = [], [], []
    cases = [(d, k) for d in (2, 1, 3, 0) for k in (1, 0)]
    for d, k in cases:
        xd, cd = p.chip(d), lax.rem(p.c + k, 2)
        for side, col in enumerate((lanes(3 * xd + 2 * cd), lanes(3 * xd + 1))):
            src = d_out.at[pl.ds(0, HD), col]
            dst = whole.at[lanes(3 * p.x + 2 * p.c), pl.ds(side * HD, HD)]
            if d + k:
                rows.append(net.send(src, dst, p.at_xc(d, k)))
            else:
                own.append(net.local(src, dst))
                own[-1].start()
    for d, k in cases:
        xd, cd = p.chip(d), lax.rem(p.c + k, 2)
        for side, col in enumerate((lanes(3 * xd + 2 * cd), lanes(3 * xd + 1))):
            src = d_out.at[pl.ds(HD, HD), col]
            dst = whole.at[lanes(3 * p.x + 1), pl.ds(side * HD, HD)]
            if d + k:
                middle.append((k, net.prepare(src, dst, p.at_xc(d, k))))
            else:
                middle.append((-1, net.local(src, dst)))

    @pl.when(p.c == 0)
    def _():
        for _, copy in middle:
            copy.start()

    yield
    for copy in rows:
        copy.wait_recv()
    for copy in own:
        copy.wait()
    for core in range(2):

        @pl.when(p.c == core)
        def _(core=core):
            for k, copy in middle:
                if k == core:
                    copy.wait_recv()

    @pl.when(p.c == 0)
    def _():
        for k, copy in middle:
            if k < 0:
                copy.wait()
            else:
                copy.wait_send()

    yield


TRADE_BACK = 28


def back_kernel(cuts, *refs):
    (marks, gains, d_gain_f, x_rows, hidden, d_hidden, ffn_sum), refs = refs[:7], refs[7:]
    (whole, w_out, mixed, normed, branch, part_o, d_down), refs = refs[:7], refs[7:]
    given, refs = refs[:10], refs[10:]
    (output, d_tokens, got_heads, got_rest, got_ffn, down_sum), refs = refs[:6], refs[6:]
    bufs, refs = refs[:10], refs[10:]
    (w_buf, wo_buf, mixed_buf, normed_buf, rows_buf, do, d_out, d_ext, d_conv), refs = refs[:9], refs[9:]
    (d_head_a, d_head_b, d_small, turned, trade, out_rows, d_rows), refs = refs[:7], refs[7:]
    (sum_a, sum_b, sum_s, sum_o, packs_heads, packs_rest, packs_ffn), refs = refs[:7], refs[7:]
    own, refs = refs[:7], refs[7:]
    scratch = [refs[6 * n : 6 * n + 6] for n in range(8)]
    net = Net(*refs[-3:])
    p = net.place
    qkvp, raw, vec, *saved = bufs
    two, _, n, width = rows_buf.shape
    rows = two * 8 * n
    first = [net.load(w_out, wo_buf), net.load(branch, rows_buf), net.load(mixed, mixed_buf)]
    second = [net.load(given[m], bufs[m]) for m in (0,)]
    second.append(net.load(given[3].at[0], bufs[3].at[0]))
    meet(team_all(p) + group_peers(p))

    def finish(sums):
        out_rows[...] = (hidden[...] + sums).astype(BF16)

    def out_grad():
        yield from trade_out_back(net, d_out, trade)
        yield from scatter_groups(net, trade, sum_o, cuts[1], *scratch[0])

    def output_rows():
        yield from scatter_team(net, part_o, *scratch[1], finish)
        yield from swap_rows(net, ((out_rows, output),))

    jobs = Jobs(
        output_rows(), out_grad(), scatter_groups(net, d_down, down_sum, cuts[0], *scratch[2])
    )
    eight, padded, _ = packs_heads.shape
    spread = thin_rows(ffn_sum.shape[0] // eight, padded).T

    def pack(part, packs, at):
        wide = mm(spread, part[...]).astype(BF16)
        packs[:, :, at : at + part.shape[1]] = wide.reshape(eight, padded, part.shape[1])

    jobs.step(0)
    pack(ffn_sum, packs_ffn, 0)
    early = all_to_team(net, packs_ffn, got_ffn)
    next(early)
    for copy in first:
        copy.wait()
    third = [net.load(given[m].at[0], bufs[m].at[0]) for m in range(4, 10)]
    third += [net.load(given[m], bufs[m]) for m in (1, 2)]
    third.append(net.load(whole.at[:, pl.ds(0, EXT_W)], w_buf))
    branch_rows = rows_buf[...].reshape(rows, width)
    d_mixed = mm_nt(branch_rows, wo_buf[...])
    do[:, :HD] = d_mixed[:, :HD]
    do[:, HD:] = jnp.where(p.c == 0, d_mixed[:, HD:], 0.0)
    d_out[...] = mm_tn(mixed_buf[...], branch_rows).astype(BF16)
    jobs.step(2)
    fourth = [net.load(normed, normed_buf)]
    later = []
    for copy in second:
        copy.wait()
    waits = [third, None, None, None, later, None, None, None]
    steps = [(0,), (), (), (0, 1), (2, 2), (), (0,), (1, 1)]

    def poke():
        jobs.step(*steps.pop(0))
        for copy in waits.pop(0) or ():
            copy.wait()
        if len(steps) == 7:
            fourth.append(net.load(given[3].at[1], bufs[3].at[0]))

    side = 4 * HD
    d_raw = 0.0
    sums_a = scatter_groups(net, d_head_a, sum_a, cuts[2], *scratch[3])
    sums_b = scatter_groups(net, d_head_b, sum_b, cuts[2], *scratch[4])
    for s, (head, grads, job) in enumerate(zip(heads_here(), (d_head_a, d_head_b), (sums_a, sums_b))):
        d_raw = d_raw + bwd_slot(
            poke, s, head, qkvp, raw, w_buf.at[:, pl.ds(HEADS_W, HD)], marks, vec, mixed_buf, do, *saved, d_ext, d_conv, *own
        )
        if s == 0:
            later += [net.load(given[m].at[1], bufs[m].at[0]) for m in range(4, 10)]
            for copy in fourth:
                copy.wait()
        for k in range(4):
            part = slice(k * width // 4, (k + 1) * width // 4)
            grads[part, :] = mm_tn(normed_buf[:, part], d_ext[:, s * side : (s + 1) * side]).astype(BF16)
        next(job)
        poke()
    d_ext[:, HEADS_W:] = d_raw.astype(d_ext.dtype)
    next(sums_a)
    next(sums_a)

    pieces = [pl.ds(m * n // 2, n // 2) for m in range(2)]
    sums = [
        TeamSum(net, rows_buf.at[:, :, piece], *scratch[5 + m]) for m, piece in enumerate(pieces)
    ]
    turned[...] = jnp.zeros_like(turned)

    def work(d):
        at = p.chip(d)
        parts = [
            d_ext[pl.ds(pl.multiple_of((h * 8 + 2 * at) * n, 2 * n), 2 * n), :] for h in range(two)
        ]
        y = mm_nt(jnp.concatenate(parts, axis=0), w_buf[...]).astype(BF16)
        rows_buf[:, pl.ds(2 * at, 2)] = y.reshape(two, 2, n, width)
        for s in sums:
            s.ready(d)

    work(2)
    work(1)
    for s in sums:
        s.far()
    work(3)
    for s in sums:
        s.near()
    work(0)
    for s in sums:
        s.pair(0)
    total = 0.0
    for h in range(two):
        for t in range(0, 8, 2):
            here = slice((h * 8 + t) * n, (h * 8 + t + 2) * n)
            y = rows_buf[h, t : t + 2].reshape(2 * n, width).astype(F32)
            total = total + jnp.sum(y * normed_buf[here, :].astype(F32), axis=0, keepdims=True)
    turned[0:1, :] = total
    head_a, head_b = heads_here()
    turned[0:1, :] = turned[0:1, :] / gains[0:1, :]
    turned[1:2, :] = d_gain_f[...]
    turned[CONV_AT : CONV_AT + TAPS, lanes(head_a)] = d_conv[0, :TAPS, :]
    turned[CONV_AT : CONV_AT + TAPS, lanes(head_b)] = d_conv[1, :TAPS, :]
    for k in range(width // HD):
        part = slice(k * HD, (k + 1) * HD)
        t = mm_tn(normed_buf[:, part], d_ext[:, HEADS_W:]) + turned[:, part].T
        d_small[part, :] = t.astype(BF16)
    sums_s = scatter_groups(net, d_small, sum_s, cuts[3], *scratch[7])
    next(sums_s)
    for s in sums:
        s.on()
    next(sums_b)
    next(sums_b)
    swaps = []
    for s, piece in zip(sums, pieces):
        d_x, _ = norm_back(x_rows[:, piece].astype(F32), gains[0:1, :][None], s.result())
        d_rows[:, piece] = (d_x + d_hidden[:, piece]).astype(BF16)
        swaps.append(swap_rows(net, ((d_rows.at[:, piece], d_tokens.at[:, piece]),)))
        next(swaps[-1])
    next(sums_s)
    jobs.step(1, 1)
    Jobs(sums_a).drain()
    jobs.drain()
    pack(sum_a, packs_rest, 0)
    pack(sum_o, packs_rest, side)
    rest = all_to_team(net, packs_rest, got_rest)
    next(rest)
    Jobs(sums_b, sums_s).drain()
    pack(sum_b, packs_heads, 0)
    pack(sum_s, packs_heads, side)
    interleave(all_to_team(net, packs_heads, got_heads), *swaps, rest, early)
    net.finish()


def back(values, arrays, given):
    marks, gains, d_gain_f, x_rows, hidden, d_hidden, ffn_sum = values
    whole, w_out, mixed, normed, branch, part_o, d_down = arrays
    two, n, width = hidden.shape
    r = width // 16
    down = d_down.shape[0] // 16
    side = 4 * HD
    ffn_w = ffn_sum.shape[1]
    cuts = [(0, width // 2, width), (0, HD, 2 * HD), (0, side // 2, side), (0, HD, HD)]
    rows = SHAPE((two, n, width), BF16)
    packs = [(8, 16, side + HD), (8, 16, side + 2 * HD), (8, 16, ffn_w)]
    vmem = pltpu.VMEM
    return pl.pallas_call(
        functools.partial(back_kernel, cuts),
        out_shape=[rows, rows] + [SHAPE(a, BF16) for a in packs] + [SHAPE((down, width), F32)],
        in_specs=[VMEM] * 7 + [ANY] * (7 + len(given)),
        out_specs=[ANY] * 5 + [VMEM],
        scratch_shapes=[vmem((1,) + a.shape[1:] if m > 2 else a.shape, a.dtype) for m, a in enumerate(given)]
        + [
            vmem((width, EXT_W), BF16),
            vmem(w_out.shape, BF16),
            vmem(mixed.shape, BF16),
            vmem(normed.shape, BF16),
            vmem(branch.shape, BF16),
            vmem((SEQ, 2 * HD), F32),
            vmem((2 * HD, width), BF16),
            vmem((SEQ, EXT_W), BF16),
            vmem((2, 8, HD), F32),
            vmem((width, side), BF16),
            vmem((width, side), BF16),
            vmem((width, HD), BF16),
            vmem((HD, width), F32),
            vmem((width, 2 * HD), BF16),
            vmem((two, n, width), BF16),
            vmem((two, n, width), BF16),
            vmem((r, side), BF16),
            vmem((r, side), BF16),
            vmem((r, HD), BF16),
            vmem((r, 2 * HD), BF16),
        ]
        + [vmem(a, BF16) for a in packs]
        + bwd_scratch()
        + scatter_groups_scratch(r, cuts[1])
        + scatter_team_scratch(n, width)
        + scatter_groups_scratch(down, cuts[0])
        + scatter_groups_scratch(r, cuts[2])
        + scatter_groups_scratch(r, cuts[2])
        + scatter_team_scratch(n // 2, width) * 2
        + scatter_groups_scratch(r, cuts[3])
        + sems(
            TRADE_BACK + 3 * SCATTER_TEAM + 6 * SCATTER_GROUPS_FLAT + 3 + 3 * TO_TEAM,
            3 + 3 + 9 + 8 + 4 + SCATTER_TEAM_LOADS + 6 * SCATTER_GROUPS_FLAT_LOADS + 3 + 3,
        ),
        compiler_params=params(5),
        name="back",
    )(*values, *arrays, *given)


def unpack_kernel(heads, rest, ffn_in, rows_in, tokens_in, down_in, *outs):
    kinds, (gate, up, gain_a, gain_f, conv, beta, rows, tokens, down) = outs[:5], outs[5:]
    share = beta.shape[0]
    side = 4 * HD
    for n, out in enumerate(kinds):
        for x in range(4):
            for j in range(3):
                t = 2 * x + j // 2
                if n < 4:
                    src, col = (heads, n * HD) if j == 1 else (rest, n * HD)
                else:
                    src, col = rest, side + (j % 2) * HD
                head = 3 * x + j
                out[:, head * HD : (head + 1) * HD] = src[t, :share, col : col + HD].astype(F32)
    total = heads[0, :, side : side + SMALL_W].astype(F32)
    for t in range(1, 8):
        total = total + heads[t, :, side : side + SMALL_W].astype(F32)
    turned = jnp.concatenate([total] * (HD // total.shape[0]), axis=0).T
    gain_a[...] = turned[0:1, :share]
    gain_f[...] = turned[1:2, :share]
    conv[...] = turned[CONV_AT : CONV_AT + TAPS, :share]
    beta[...] = pltpu.roll(total, HD - BETA_AT, 1)[:share, : beta.shape[1]]
    for n, out in enumerate((gate, up)):
        for tile in range(32):
            e = tile // 2
            col = n * 4 * HD + (e // 4) * HD
            parts = [
                (ffn_in[t, :, col : col + HD].astype(F32), e % 4)
                for t in range(4 * (tile % 2), 4 * (tile % 2) + 4)
            ]
            out[:, tile * HD : (tile + 1) * HD] = shift_pieces(parts)[:share]
    rows[...] = rows_in[...]
    tokens[...] = tokens_in[...]
    down[...] = down_in[...]


def unpack(heads, rest, ffn_sum, rows, tokens, down, share, ff):
    two, n, width = rows.shape
    return pl.pallas_call(
        unpack_kernel,
        out_shape=[SHAPE((share, width), F32)] * 5
        + [SHAPE((share, ff), F32)] * 2
        + [SHAPE((1, share), F32)] * 2
        + [SHAPE((TAPS, share), F32), SHAPE((share, 12), F32)]
        + [SHAPE(rows.shape, BF16)] * 2
        + [SHAPE(down.shape, F32)],
        in_specs=[VMEM] * 6,
        out_specs=[VMEM] * 14,
        compiler_params=pltpu.CompilerParams(vmem_limit_bytes=VM),
        name="unpack",
    )(heads, rest, ffn_sum, rows, tokens, down)


def per_device(
    tokens,
    doc_start,
    gain_attn,
    w_query,
    w_key,
    w_value,
    w_path,
    conv_path,
    w_beta,
    w_out,
    gain_ffn,
    w_gate,
    w_up,
    w_down,
    grad_out,
):
    width = tokens.shape[2]
    share = w_query.shape[0]
    x_rows, g_rows, x_all, whole, own_ffn, drow, marks = start(
        (w_query, w_key, w_value, w_path, w_out),
        w_gate,
        w_up,
        gain_attn[None],
        gain_ffn[None],
        conv_path,
        w_beta,
        doc_start,
        tokens,
        grad_out,
    )
    normed, qkvp, raw, vec, mixed, gains, *saved, w_ffn, g_all, w_out_t, part = attn_fwd(
        x_all.reshape(SEQ, width), whole, marks, drow, own_ffn, g_rows
    )
    hidden, d_hidden, d_gain_f, branch_all, out_part, ffn_sum, d_down = ffn(
        part, x_rows, g_rows, gains, w_down, w_ffn, g_all
    )
    output, d_tokens, heads_back, rest_back, ffn_back, d_down = back(
        (marks, gains, d_gain_f, x_rows, hidden, d_hidden, ffn_sum),
        (whole, w_out_t, mixed, normed, branch_all, out_part, d_down),
        (qkvp, raw, vec, *saved),
    )
    *kinds, d_gate_w, d_up_w, d_gain_a, d_gain_f, d_conv, d_beta_w, output, d_tokens, d_down = unpack(
        heads_back, rest_back, ffn_back, output, d_tokens, d_down, share, w_gate.shape[1]
    )
    return (
        output,
        d_tokens,
        d_gain_a[0],
        *kinds[:4],
        d_conv,
        d_beta_w,
        kinds[4],
        d_gain_f[0],
        d_gate_w,
        d_up_w,
        d_down,
    )


def solution(mesh):
    names = ("zl", "y", "zh", "x", "c")
    fine = Mesh(mesh.devices.reshape(2, 4, 2, 4, 2), names)
    dp, ctx = names[:2], names[2:]
    rows, flat, mat, taps = P(dp, ctx, None), P(names), P(names, None), P(None, names)
    return jax.shard_map(
        per_device,
        mesh=fine,
        in_specs=(
            rows, P(dp, None), flat, mat, mat, mat, mat, taps, mat, mat, flat, mat, mat, mat, rows,
        ),
        out_specs=(
            rows, rows, flat, mat, mat, mat, mat, taps, mat, mat, flat, mat, mat, mat,
        ),
        check_vma=False,
    )
```
